32 devices in a mesh: dp: 32 (over z, y, x, core).
Axes of the slice: x: 2, y: 2, z: 4, core: 2. Of those that a mesh axis runs over, the one named last changes fastest.
Arguments:
- block_in: bfloat16 [32, 1024, 1024], P('dp'), may hold values from -6 to 6
- condition: float32 [32, 1024], P('dp'), may hold values from -6 to 6
- out_grad: bfloat16 [32, 1024, 1024], P('dp'), may hold values from -6 to 6
- weights: float32 [1024, 18432], P('dp'), may hold values from -2 to 2, as said below
- biases: float32 [14336], P('dp'), may hold values from -0.75 to 0.75
- first_moment: float32 [1024, 18432], P('dp'), may hold values from -32 to 32
- second_moment: float32 [1024, 18432], P('dp'), may hold values from 131.072 to 983.04
- bias_first: float32 [14336], P('dp'), may hold values from -32 to 32
- bias_second: float32 [14336], P('dp'), may hold values from 131.072 to 983.04
Outputs:
- block_out: bfloat16 [32, 1024, 1024], P('dp')
- input_grad: float32 [32, 1024, 1024], P('dp')
- condition_grad: float32 [32, 1024], P('dp')
- weight_grad: float32 [1024, 18432], P('dp')
- bias_grad: float32 [14336], P('dp')
- new_weights: float32 [1024, 18432], P('dp')
- new_biases: float32 [14336], P('dp')
- new_first: float32 [1024, 18432], P('dp')
- new_second: float32 [1024, 18432], P('dp')
- new_bias_first: float32 [14336], P('dp')
- new_bias_second: float32 [14336], P('dp')
The draws below stay inside these ranges and needn't reach their ends.
Inputs may be any that keep to these rules, and one draw needn't show every extreme that they name: `weights`: columns as described in the first step.
All inputs are finite; a program needn't handle non-finite values.
Results may differ from the reference program's by a relative error of at most 0.017.
The reference program's roundings to bfloat16 on the way count: a program that leaves them out, or rounds other values in their place, can miss the bound.
Values may be sent and summed in bfloat16 or wider, within the bound.
A program may use at most 320 MiB of HBM per device.

```python
import math
import jax
import jax.numpy as jnp
from jax import lax

D = 1024
HEADS = 16
HEAD = 64
FF = 4096
SEQ = 1024
STEP = 3
LATENTS = 32
WCOLS = 18432
BIAS = 14336


def noise_block(key, rows_count, cols_count, spread):
    return jnp.clip(jax.random.normal(key, (rows_count, cols_count), jnp.float32), -6.0, 6.0) * spread


def draw_weights(key, part):
    keys = jax.random.split(jax.random.fold_in(key, 11), 7)
    base = D ** (-0.5)
    query_proj = noise_block(keys[0], D, D, 1.5 * base)
    key_proj = noise_block(keys[1], D, D, 1.5 * base)
    value_proj = noise_block(keys[2], D, D, base)
    out_proj = noise_block(keys[3], D, D, 2.0 * base)
    up_proj = noise_block(keys[4], D, FF, base)
    down_proj = noise_block(keys[5], D, FF, FF ** (-0.5))
    ada_proj = noise_block(keys[6], D, 6 * D, base)
    return jnp.concatenate([query_proj, key_proj, value_proj, out_proj, up_proj, down_proj, ada_proj], axis=1)


def shard_levels(own_key, dims, cuts, smallest, top_value):
    factor_of = 1.0
    for axis_at, parts in cuts:
        heights = jax.random.uniform(jax.random.fold_in(jax.random.fold_in(own_key, 6), axis_at), (parts,), jnp.float32, smallest / len(cuts), top_value / len(cuts))
        factor_of = factor_of * jnp.repeat(jnp.exp(heights), dims[axis_at] // parts).reshape((-1,) + (1,) * (len(dims) - 1 - axis_at))
    return factor_of


def normal_values(stream_key, extent, scale, bound, shards=(), kind=jnp.bfloat16):
    drawn = scale * jax.random.normal(stream_key, extent, jnp.float32)
    if shards:
        drawn = drawn * shard_levels(stream_key, extent, shards, -0.22, 0.18)
    return jnp.clip(drawn, -bound, bound).astype(kind)


def setup_inputs(seed: int = 0) -> dict:
    streams_of = jax.random.split(jax.random.key(seed), 10)
    return {
        "block_in": normal_values(streams_of[0], (LATENTS, SEQ, D), 1.0, 6.0, ((0, 32),)),
        "condition": normal_values(streams_of[1], (LATENTS, D), 1.0, 6.0, ((0, 32),), jnp.float32),
        "out_grad": normal_values(streams_of[2], (LATENTS, SEQ, D), 1.0, 6.0, ((0, 32),)),
        "weights": draw_weights(jax.random.fold_in(streams_of[9], 71), 0),
        "biases": normal_values(streams_of[4], (BIAS,), 0.05, 0.75, ((0, 32),), jnp.float32),
        "first_moment": normal_values(streams_of[5], (D, WCOLS), (0.03 * (LATENTS * SEQ) ** 0.5), 32.0, ((0, 32),), jnp.float32),
        "second_moment": jnp.clip(jnp.exp(math.log(983.04) - 2.014903 * jax.random.uniform(streams_of[6], (D, WCOLS), jnp.float32) ** shard_levels(streams_of[6], (D, WCOLS), ((0, 32),), -0.2, 0.2)), 131.072, 983.04),
        "bias_first": normal_values(streams_of[7], (BIAS,), (0.03 * (LATENTS * SEQ) ** 0.5), 32.0, ((0, 32),), jnp.float32),
        "bias_second": jnp.clip(jnp.exp(math.log(983.04) - 2.014903 * jax.random.uniform(streams_of[8], (BIAS,), jnp.float32) ** shard_levels(streams_of[8], (BIAS,), ((0, 32),), -0.2, 0.2)), 131.072, 983.04),
    }


norm_eps = 1e-06
gelu_coef = 0.7978845608028654
learn_rate = 0.01
beta_first = 0.9
beta_second = 0.95
adam_eps = 1e-08
weight_decay = 0.05
contract_rows = (((0,), (0,)), ((), ()))
contract_cols = (((1,), (1,)), ((), ()))
highest = lax.Precision.HIGHEST

def rounded(values):
    return lax.optimization_barrier(values.astype(jnp.bfloat16)).astype(jnp.float32)

def norm_rows(values):
    center = values - lax.optimization_barrier(jnp.mean(values, axis=-1, keepdims=True))
    inv_std = lax.rsqrt(lax.optimization_barrier(jnp.mean(center * center, axis=-1, keepdims=True)) + norm_eps)
    return (center * inv_std, inv_std)

def norm_back(grad_hat, normed, inv_std):
    return inv_std * (grad_hat - lax.optimization_barrier(jnp.mean(grad_hat, axis=-1, keepdims=True)) - normed * lax.optimization_barrier(jnp.mean(grad_hat * normed, axis=-1, keepdims=True)))

def gelu_pair(inner):
    tangent = jnp.tanh(gelu_coef * (inner + 0.044715 * inner * inner * inner))
    value = 0.5 * inner * (1.0 + tangent)
    slope = 0.5 * (1.0 + tangent) + 0.5 * inner * (1.0 - tangent * tangent) * gelu_coef * (1.0 + 3.0 * 0.044715 * inner * inner)
    return (value, slope)

def attend(query, keys, values):
    seq_len = query.shape[0]
    rows_per = min(512, seq_len)
    scale = HEAD ** (-0.5)
    key_heads = keys.reshape(seq_len, HEADS, HEAD).astype(jnp.float32)
    value_heads = values.reshape(seq_len, HEADS, HEAD).astype(jnp.float32)
    query_blocks = query.reshape(seq_len // rows_per, rows_per, HEADS, HEAD)

    def one_block(query_block):
        scores = jnp.einsum('qhd,khd->hqk', query_block.astype(jnp.float32), key_heads, precision=highest) * scale
        row_max = lax.optimization_barrier(jnp.max(scores, axis=-1, keepdims=True))
        log_total = row_max + jnp.log(lax.optimization_barrier(jnp.sum(jnp.exp(scores - row_max), axis=-1, keepdims=True)))
        probs = rounded(jnp.exp(scores - log_total))
        mixed = jnp.einsum('hqk,khd->qhd', probs, value_heads, precision=highest)
        return (mixed.astype(jnp.bfloat16).reshape(rows_per, HEADS * HEAD), log_total[..., 0])
    mixed, log_total = lax.map(one_block, query_blocks)
    return (mixed.reshape(seq_len, HEADS * HEAD), log_total)

def attend_back(query, keys, values, log_total, grad_mixed):
    seq_len = query.shape[0]
    rows_per = min(512, seq_len)
    block_count = seq_len // rows_per
    scale = HEAD ** (-0.5)
    key_heads = keys.reshape(seq_len, HEADS, HEAD).astype(jnp.float32)
    value_heads = values.reshape(seq_len, HEADS, HEAD).astype(jnp.float32)
    query_blocks = query.reshape(block_count, rows_per, HEADS, HEAD)
    grad_blocks = grad_mixed.reshape(block_count, rows_per, HEADS, HEAD)

    def one_block(carry, inputs):
        query_block, grad_block, total_block = inputs
        query_f = query_block.astype(jnp.float32)
        grad_f = grad_block.astype(jnp.float32)
        scores = jnp.einsum('qhd,khd->hqk', query_f, key_heads, precision=highest) * scale
        probs = jnp.exp(scores - total_block[..., None])
        grad_probs = jnp.einsum('qhd,khd->hqk', grad_f, value_heads, precision=highest)
        grad_scores = rounded(probs * (grad_probs - lax.optimization_barrier(jnp.sum(probs * grad_probs, axis=-1, keepdims=True))) * scale)
        grad_query = jnp.einsum('hqk,khd->qhd', grad_scores, key_heads, precision=highest)
        grad_keys = carry[0] + jnp.einsum('hqk,qhd->khd', grad_scores, query_f, precision=highest)
        grad_values = carry[1] + jnp.einsum('hqk,qhd->khd', rounded(probs), grad_f, precision=highest)
        return ((grad_keys, grad_values), grad_query.reshape(rows_per, HEADS * HEAD))
    empty = jnp.zeros((seq_len, HEADS, HEAD), jnp.float32)
    (grad_keys, grad_values), grad_query = lax.scan(one_block, (empty, empty), (query_blocks, grad_blocks, log_total))
    width = HEADS * HEAD
    return (grad_query.reshape(seq_len, width), grad_keys.reshape(seq_len, width), grad_values.reshape(seq_len, width))

def forward_latent(tokens, mod_row, mats, bias_full):
    w_qkv, w_out, w_up, w_down = mats
    shift_one, scale_one, gate_one, shift_two, scale_two, gate_two = jnp.split(mod_row, 6)
    tokens_f = tokens.astype(jnp.float32)
    normed_one, inv_one = norm_rows(tokens_f)
    hidden_one = (normed_one * (1.0 + scale_one) + shift_one).astype(jnp.bfloat16)
    qkv_bias = jnp.concatenate([bias_full[0:D], jnp.zeros((D,), jnp.float32), bias_full[D:2 * D]])
    qkv_all = (jnp.dot(hidden_one, w_qkv, preferred_element_type=jnp.float32) + qkv_bias).astype(jnp.bfloat16)
    query, keys, values = (qkv_all[:, :D], qkv_all[:, D:2 * D], qkv_all[:, 2 * D:])
    mixed, log_total = attend(query, keys, values)
    branch = jnp.dot(mixed, w_out, preferred_element_type=jnp.float32) + bias_full[2 * D:3 * D]
    middle = tokens_f + gate_one * branch
    normed_two, inv_two = norm_rows(middle)
    hidden_two = (normed_two * (1.0 + scale_two) + shift_two).astype(jnp.bfloat16)
    inner = jnp.dot(hidden_two, w_up, preferred_element_type=jnp.float32) + bias_full[3 * D:3 * D + FF]
    value, slope = gelu_pair(inner)
    activ = value.astype(jnp.bfloat16)
    down = lax.dot_general(activ, w_down, contract_cols, preferred_element_type=jnp.float32) + bias_full[3 * D + FF:4 * D + FF]
    result = (middle + gate_two * down).astype(jnp.bfloat16)
    saved = (normed_one, inv_one, hidden_one, query, keys, values, mixed, log_total, branch, normed_two, inv_two, hidden_two, slope, activ, down)
    return (result, saved)

def backward_latent(grad_out, mod_row, saved, mats):
    w_qkv, w_out, w_up, w_down = mats
    normed_one, inv_one, hidden_one, query, keys, values, mixed, log_total, branch, normed_two, inv_two, hidden_two, slope, activ, down = saved
    shift_one, scale_one, gate_one, shift_two, scale_two, gate_two = jnp.split(mod_row, 6)
    grad_f = grad_out.astype(jnp.float32)
    grad_down = grad_f * gate_two
    grad_gate_two = lax.optimization_barrier(jnp.sum(grad_f * down, axis=0))
    down_b = grad_down.astype(jnp.bfloat16)
    grad_w_down = lax.dot_general(down_b, activ, contract_rows, preferred_element_type=jnp.float32)
    grad_inner = jnp.dot(down_b, w_down, preferred_element_type=jnp.float32) * slope
    inner_b = grad_inner.astype(jnp.bfloat16)
    grad_w_up = lax.dot_general(hidden_two, inner_b, contract_rows, preferred_element_type=jnp.float32)
    grad_hidden_two = lax.dot_general(inner_b, w_up, contract_cols, preferred_element_type=jnp.float32)
    grad_shift_two = lax.optimization_barrier(jnp.sum(grad_hidden_two, axis=0))
    grad_scale_two = lax.optimization_barrier(jnp.sum(grad_hidden_two * normed_two, axis=0))
    grad_middle = grad_f + norm_back(grad_hidden_two * (1.0 + scale_two), normed_two, inv_two)
    grad_branch = grad_middle * gate_one
    grad_gate_one = lax.optimization_barrier(jnp.sum(grad_middle * branch, axis=0))
    branch_b = grad_branch.astype(jnp.bfloat16)
    grad_w_out = lax.dot_general(mixed, branch_b, contract_rows, preferred_element_type=jnp.float32)
    grad_mixed = lax.dot_general(branch_b, w_out, contract_cols, preferred_element_type=jnp.float32).astype(jnp.bfloat16)
    grad_query, grad_keys, grad_values = attend_back(query, keys, values, log_total, grad_mixed)
    qkv_b = jnp.concatenate([grad_query, grad_keys, grad_values], axis=1).astype(jnp.bfloat16)
    grad_w_qkv = lax.dot_general(hidden_one, qkv_b, contract_rows, preferred_element_type=jnp.float32)
    grad_hidden_one = lax.dot_general(qkv_b, w_qkv, contract_cols, preferred_element_type=jnp.float32)
    grad_shift_one = lax.optimization_barrier(jnp.sum(grad_hidden_one, axis=0))
    grad_scale_one = lax.optimization_barrier(jnp.sum(grad_hidden_one * normed_one, axis=0))
    grad_input = grad_middle + norm_back(grad_hidden_one * (1.0 + scale_one), normed_one, inv_one)
    grad_mod = jnp.concatenate([grad_shift_one, grad_scale_one, grad_gate_one, grad_shift_two, grad_scale_two, grad_gate_two])
    bias_row = jnp.concatenate([lax.optimization_barrier(jnp.sum(grad_query, axis=0)), lax.optimization_barrier(jnp.sum(grad_values, axis=0)), lax.optimization_barrier(jnp.sum(grad_branch, axis=0)), lax.optimization_barrier(jnp.sum(grad_inner, axis=0)), lax.optimization_barrier(jnp.sum(grad_down, axis=0)), grad_mod])
    return (grad_input, grad_mod, (grad_w_qkv, grad_w_out, grad_w_up, grad_w_down), bias_row)

def adam_step(param, grad, first, second, decay):
    new_first = beta_first * first + (1.0 - beta_first) * grad
    new_second = beta_second * second + (1.0 - beta_second) * grad * grad
    step_size = learn_rate / (1.0 - beta_first ** STEP)
    denom = jnp.sqrt(new_second / (1.0 - beta_second ** STEP)) + adam_eps
    new_param = param - step_size * new_first / denom - learn_rate * decay * param
    return (new_param, new_first, new_second)

def reference(block_in, condition, out_grad, weights, biases, first_moment, second_moment, bias_first, bias_second):
    weights_b = weights.astype(jnp.bfloat16)
    w_qkv = weights_b[:, :3 * D]
    w_out = weights_b[:, 3 * D:4 * D]
    w_up = weights_b[:, 4 * D:4 * D + FF]
    w_down = weights_b[:, 4 * D + FF:4 * D + 2 * FF]
    w_ada = weights_b[:, 4 * D + 2 * FF:]
    bias_full = rounded(biases)
    cond_act = jax.nn.silu(condition).astype(jnp.bfloat16)
    mod = jnp.dot(cond_act, w_ada, preferred_element_type=jnp.float32) + bias_full[4 * D + FF:]
    mats = (w_qkv, w_out, w_up, w_down)

    def one_latent(carry, inputs):
        tokens, mod_row, grad_out = inputs
        result, saved = forward_latent(tokens, mod_row, mats, bias_full)
        grad_input, grad_mod, grads, bias_row = backward_latent(grad_out, mod_row, saved, mats)
        summed = tuple((total + part for total, part in zip(carry[0], grads)))
        return ((summed, carry[1] + bias_row), (result, grad_input, grad_mod))
    init = (tuple((jnp.zeros(mat.shape, jnp.float32) for mat in mats)), jnp.zeros((10 * D + FF,), jnp.float32))
    (grads, bias_grad), (block_out, input_grad, grad_mod) = lax.scan(one_latent, init, (block_in, mod, out_grad))
    mod_b = grad_mod.astype(jnp.bfloat16)
    grad_ada = lax.dot_general(cond_act, mod_b, contract_rows, preferred_element_type=jnp.float32)
    sigma = jax.nn.sigmoid(condition)
    condition_grad = lax.dot_general(mod_b, w_ada, contract_cols, preferred_element_type=jnp.float32) * (sigma * (1.0 + condition * (1.0 - sigma)))
    weight_grad = jnp.concatenate([grads[0], grads[1], grads[2], grads[3], grad_ada], axis=1)
    new_weights, new_first, new_second = adam_step(weights, weight_grad, first_moment, second_moment, weight_decay)
    new_biases, new_bias_first, new_bias_second = adam_step(biases, bias_grad, bias_first, bias_second, 0.0)
    return (block_out, input_grad, condition_grad, weight_grad, bias_grad, new_weights, new_biases, new_first, new_second, new_bias_first, new_bias_second)
```

```python
import functools

import jax
import jax.numpy as jnp
from jax import lax
from jax.experimental import pallas as pl
from jax.experimental.pallas import tpu as pltpu
from jax.sharding import PartitionSpec as P

D = 1024
FF = 4096
S = 1024
STEP = 3
CH = 512
NJ = FF // CH
learn_rate = 0.01
beta_first = 0.9
beta_second = 0.95
adam_eps = 1e-08
weight_decay = 0.05
gc = 0.7978845608028654
LOG2E = 1.4426950408889634
f32 = jnp.float32
bf = jnp.bfloat16
NT = (((1,), (1,)), ((), ()))
TN = (((0,), (0,)), ((), ()))
V = pl.BlockSpec(memory_space=pltpu.VMEM)
A = pl.BlockSpec(memory_space=pl.ANY)
sd = jax.ShapeDtypeStruct


def dot(a,b,dn=None):
    if dn is None: return jnp.dot(a,b,preferred_element_type=f32)
    return lax.dot_general(a,b,dn,preferred_element_type=f32)

def lane_half(x, hh):
    lane=lax.broadcasted_iota(jnp.int32, x.shape, 1)
    keep=(lane<64) if hh==0 else (lane>=64)
    return jnp.where(keep, x, jnp.zeros_like(x))

def gelu_pair(u):
    u2=u*u
    t=jnp.tanh(gc*(u+0.044715*u2*u))
    return 0.5*u*(1.0+t), 0.5*(1.0+t)+0.5*u*(1.0-t*t)*gc*(1.0+3.0*0.044715*u2)
def nrm(v):
    c=v-jnp.mean(v,axis=-1,keepdims=True)
    r=lax.rsqrt(jnp.mean(c*c,axis=-1,keepdims=True)+1e-6)
    return c*r,r
def rows_loop(n, R, f):
    def body(i,_):
        f(pl.ds(pl.multiple_of(i*R,R),R)); return 0
    lax.fori_loop(0,n//R,body,0)

def kb_kernel(R, tok, gout, attnT, mod, bias, bup, wout_h, wup_h, wdn_h,
      bo_ref, dx1_ref, dat_ref, dw_h, dwout_ref, dmod_ref, db_ref, dbup_ref,
      h2, h2T, dzb, dzT, z, dh2, o_s, wout, wbuf, act, du, dwst, wsem, osem, wosem):
    pltpu.make_async_copy(wout_h, wout, wosem).start()
    def fetch(j, slot):
        pltpu.make_async_copy(wup_h.at[j], wbuf.at[slot,0], wsem.at[slot,0]).start()
        pltpu.make_async_copy(wdn_h.at[j], wbuf.at[slot,1], wsem.at[slot,1]).start()
    fetch(0,0)
    shift1=mod[0:1];scale1=mod[1:2];gate1=mod[2:3];shift2=mod[3:4];scale2=mod[4:5];gate2=mod[5:6]
    db_ref[...]=jnp.zeros_like(db_ref); dmod_ref[...]=jnp.zeros_like(dmod_ref)
    pltpu.make_async_copy(wout_h, wout, wosem).wait()
    def pre(r):
        o=dot(attnT[:,r],wout[...],TN)+bias[2:3]
        o_s[r,:]=o
        x1=tok[r,:].astype(f32)+gate1*o
        xh,_=nrm(x1)
        h2[r,:]=(xh*(1.0+scale2)+shift2).astype(bf)
        dz=gout[r,:].astype(f32)*gate2
        dzb[r,:]=dz.astype(bf)
        db_ref[3:4]+=jnp.sum(dz,axis=0,keepdims=True)
    rows_loop(S,256,pre)
    for i in range(4):
        r=slice(i*256,(i+1)*256)
        h2T[:,r]=h2[r,:].T
        dzT[:,r]=dzb[r,:].T
    z[...]=jnp.zeros_like(z); dh2[...]=jnp.zeros_like(dh2)
    def chunk(j,_):
        slot=lax.rem(j,2)
        @pl.when(j+1<NJ)
        def _(): fetch(j+1,1-slot)
        pltpu.make_async_copy(wup_h.at[j], wbuf.at[slot,0], wsem.at[slot,0]).wait()
        pltpu.make_async_copy(wdn_h.at[j], wbuf.at[slot,1], wsem.at[slot,1]).wait()
        dbup_ref[j]=jnp.zeros((1,CH),f32)
        def row(r):
            u=dot(h2[r,:],wbuf[slot,0])+bup[j]
            a,sl=gelu_pair(u)
            ab=a.astype(bf); act[r,:]=ab
            da=dot(dzb[r,:],wbuf[slot,1])
            d=da*sl
            dbup_ref[j]+=jnp.sum(d,axis=0,keepdims=True)
            db_=d.astype(bf); du[r,:]=db_
            z[r,:]+=dot(ab,wbuf[slot,1],NT)
            dh2[r,:]+=dot(db_,wbuf[slot,0],NT)
        rows_loop(S,R,row)
        @pl.when(j>=2)
        def _():
            pltpu.make_async_copy(dwst.at[slot], dw_h.at[j], osem.at[slot]).wait()
        def wrow(r):
            dwst[slot,0,r,:]=dot(h2T[r,:],du[...])
            dwst[slot,1,r,:]=dot(dzT[r,:],act[...])
        rows_loop(D,256,wrow)
        pltpu.make_async_copy(dwst.at[slot], dw_h.at[j], osem.at[slot]).start()
        return 0
    lax.fori_loop(0,NJ,chunk,0)
    for s in range(2): pltpu.make_async_copy(dwst.at[s], dw_h.at[s], osem.at[s]).wait()
    def post(r):
        g=gout[r,:].astype(f32); o=o_s[r,:]
        x1=tok[r,:].astype(f32)+gate1*o
        xh,rstd=nrm(x1)
        zz=z[r,:]+bias[3:4]
        bo_ref[r,:]=(x1+gate2*zz).astype(bf)
        dmod_ref[5:6]+=jnp.sum(g*zz,axis=0,keepdims=True)
        dh=dh2[r,:]
        dmod_ref[3:4]+=jnp.sum(dh,axis=0,keepdims=True)
        dmod_ref[4:5]+=jnp.sum(dh*xh,axis=0,keepdims=True)
        gg=dh*(1.0+scale2)
        dx1=g+rstd*(gg-jnp.mean(gg,axis=-1,keepdims=True)-xh*jnp.mean(gg*xh,axis=-1,keepdims=True))
        dx1_ref[r,:]=dx1
        dmod_ref[2:3]+=jnp.sum(dx1*o,axis=0,keepdims=True)
        do=dx1*gate1
        db_ref[2:3]+=jnp.sum(do,axis=0,keepdims=True)
        dob=do.astype(bf)
        dzb[r,:]=dob
        t=dot(dob,wout[...],NT).astype(bf)
        for g4 in range(4): dat_ref[g4,r,:]=t[:,g4*256:(g4+1)*256]
    rows_loop(S,128,post)
    def wo(r):
        dwout_ref[r,:]=dot(attnT[r,:],dzb[...])
    rows_loop(D,256,wo)

def kb(R,*a):
    V=pl.BlockSpec(memory_space=pltpu.VMEM); A=pl.BlockSpec(memory_space=pl.ANY)
    sd=jax.ShapeDtypeStruct
    return pl.pallas_call(functools.partial(kb_kernel,R),
      out_shape=(sd((S,D),bf),sd((S,D),f32),sd((4,S,256),bf),sd((NJ,2,D,CH),f32),sd((D,D),f32),sd((8,D),f32),sd((8,D),f32),sd((NJ,1,CH),f32)),
      in_specs=[V]*6+[A]*3, out_specs=[V,V,V,A,V,V,V,V],
      scratch_shapes=[pltpu.VMEM((S,D),bf)]*4+[pltpu.VMEM((S,D),f32)]*3+[pltpu.VMEM((D,D),bf),pltpu.VMEM((2,2,D,CH),bf),pltpu.VMEM((S,CH),bf),pltpu.VMEM((S,CH),bf),
         pltpu.VMEM((2,2,D,CH),f32),pltpu.SemaphoreType.DMA((2,2)),pltpu.SemaphoreType.DMA((2,)),pltpu.SemaphoreType.DMA],
      compiler_params=pltpu.CompilerParams(vmem_limit_bytes=62*2**20), name=f"kb{R}")(*a)

def ka_kernel(QB, tok, mod, bqkv, w_h, qkv, attnT, lse, h1T, h1, wbuf, wsem):
    c=LOG2E/8.0
    def cp(g,slot): return pltpu.make_async_copy(w_h.at[g], wbuf.at[slot], wsem.at[slot])
    cp(0,0).start()
    shift1=mod[0:1]; scale1=mod[1:2]
    def ln(r):
        xh,_=nrm(tok[r,:].astype(f32))
        h1[r,:]=(xh*(1.0+scale1)+shift1).astype(bf)
    rows_loop(S,128,ln)
    for i in range(4):
        r=slice(i*256,(i+1)*256); h1T[:,r]=h1[r,:].T
    def group(g,_):
        slot=lax.rem(g,2)
        @pl.when(g<3)
        def _(): cp(g+1,1-slot).start()
        cp(g,slot).wait()
        def proj(r):
            qkv[g,r,:]=(dot(h1[r,:],wbuf[slot])+bqkv[g]).astype(bf)
        rows_loop(S,256,proj)
        for p in range(2):
            kp=qkv[g,:,256+p*128:256+(p+1)*128]; vp=qkv[g,:,512+p*128:512+(p+1)*128]
            ks=[lane_half(kp,h) for h in range(2)]; vT=vp.T
            for i in range(S//QB):
                q=qkv[g,i*QB:(i+1)*QB,p*128:(p+1)*128]
                for h in range(2):
                    s=dot(ks[h],q,NT)
                    m=jnp.max(s,axis=0,keepdims=True)
                    e=jnp.exp2((s-m)*c)
                    l=jnp.sum(e,axis=0,keepdims=True)
                    pr=(e*(1.0/l)).astype(bf)
                    o=dot(vT[h*64:(h+1)*64],pr)
                    lse[g,p*2+h:p*2+h+1,i*QB:(i+1)*QB]=m*0.125+jnp.log(l)
                    attnT[pl.ds(pl.multiple_of(g*256+(p*128+h*64),64),64),i*QB:(i+1)*QB]=o.astype(bf)
        return 0
    lax.fori_loop(0,4,group,0)
def ka(QB,*a):
    return pl.pallas_call(functools.partial(ka_kernel,QB),
      out_shape=(sd((4,S,768),bf),sd((D,S),bf),sd((4,4,S),f32),sd((D,S),bf)),
      in_specs=[V,V,V,A], out_specs=[V]*4,
      scratch_shapes=[pltpu.VMEM((S,D),bf),pltpu.VMEM((2,D,768),bf),pltpu.SemaphoreType.DMA((2,))],
      compiler_params=pltpu.CompilerParams(vmem_limit_bytes=60*2**20), name=f"ka{QB}")(*a)
def kc_kernel(QB, tok, mod, qkv, dat, lse, dx1, h1T, w_h, ig, dw_h, dmod, dbq, dqkv, dk_s, dv_s, dqT_s, dh1, wbuf, dwst, wsem, osem):
    c=LOG2E/8.0
    def cp(g,slot): return pltpu.make_async_copy(w_h.at[g], wbuf.at[slot], wsem.at[slot])
    def co(g,slot): return pltpu.make_async_copy(dwst.at[slot], dw_h.at[g], osem.at[slot])
    cp(0,0).start()
    dh1[...]=jnp.zeros_like(dh1); dmod[...]=jnp.zeros_like(dmod); dbq[...]=jnp.zeros_like(dbq)
    def group(g,_):
        slot=lax.rem(g,2)
        @pl.when(g<3)
        def _(): cp(g+1,1-slot).start()
        for p in range(2):
            sl=slice(p*128,(p+1)*128); slk=slice(256+p*128,256+(p+1)*128); slv=slice(512+p*128,512+(p+1)*128)
            kp=qkv[g,:,slk]; vp=qkv[g,:,slv]
            ks=[lane_half(kp,h) for h in range(2)]; vs=[lane_half(vp,h) for h in range(2)]
            kT=kp.T
            dk_s[...]=jnp.zeros_like(dk_s); dv_s[...]=jnp.zeros_like(dv_s)
            def qblk(i,_):
                r=pl.ds(pl.multiple_of(i*QB,QB),QB)
                q=qkv[g,r,sl]; da=dat[g,r,sl]
                for h in range(2):
                    s=dot(ks[h],q,NT)
                    pT=jnp.exp2(s*c-lse[g,p*2+h:p*2+h+1,r]*LOG2E)
                    dp=dot(vs[h],da,NT)
                    delta=jnp.sum(pT*dp,axis=0,keepdims=True)
                    ds=(pT*(dp-delta)).astype(bf)
                    dv_s[...]+=dot(pT.astype(bf),lane_half(da,h))
                    dk_s[...]+=dot(ds,lane_half(q,h))
                    dqT_s[h*64:(h+1)*64,r]=dot(kT[h*64:(h+1)*64],ds)
                return 0
            lax.fori_loop(0,S//QB,qblk,0)
            dq=dqT_s[...].T*0.125
            dbq[g,:,sl]=jnp.sum(dq,axis=0,keepdims=True)
            dqkv[:,sl]=dq.astype(bf)
            dqkv[:,slk]=(dk_s[...]*0.125).astype(bf)
            dbq[g,:,slv]=jnp.sum(dv_s[...],axis=0,keepdims=True)
            dqkv[:,slv]=dv_s[...].astype(bf)
        cp(g,slot).wait()
        @pl.when(g>=2)
        def _(): co(g,slot).wait()
        def wrow(r):
            dwst[slot,r,:]=dot(h1T[r,:],dqkv[...])
            dh1[r,:]+=dot(dqkv[r,:],wbuf[slot],NT)
        rows_loop(D,256,wrow)
        co(g,slot).start()
        return 0
    lax.fori_loop(0,4,group,0)
    for s_ in range(2): co(s_,s_).wait()
    scale1=mod[1:2]
    def post(r):
        xh,rstd=nrm(tok[r,:].astype(f32))
        dh=dh1[r,:]
        dmod[0:1]+=jnp.sum(dh,axis=0,keepdims=True)
        dmod[1:2]+=jnp.sum(dh*xh,axis=0,keepdims=True)
        gg=dh*(1.0+scale1)
        ig[r,:]=dx1[r,:]+rstd*(gg-jnp.mean(gg,axis=-1,keepdims=True)-xh*jnp.mean(gg*xh,axis=-1,keepdims=True))
    rows_loop(S,128,post)
def kc(QB,*a):
    return pl.pallas_call(functools.partial(kc_kernel,QB),
      out_shape=(sd((S,D),f32),sd((4,D,768),f32),sd((8,D),f32),sd((4,1,768),f32)),
      in_specs=[V]*7+[A], out_specs=[V,A,V,V],
      scratch_shapes=[pltpu.VMEM((S,768),bf),pltpu.VMEM((S,128),f32),pltpu.VMEM((S,128),f32),pltpu.VMEM((128,S),f32),pltpu.VMEM((S,D),f32),
        pltpu.VMEM((2,D,768),bf),pltpu.VMEM((2,D,768),f32),pltpu.SemaphoreType.DMA((2,)),pltpu.SemaphoreType.DMA((2,))],
      compiler_params=pltpu.CompilerParams(vmem_limit_bytes=60*2**20), name=f"kc{QB}")(*a)

def adam_step(param, grad, first, second, decay):
    new_first = beta_first * first + (1.0 - beta_first) * grad
    new_second = beta_second * second + (1.0 - beta_second) * grad * grad
    step_size = learn_rate / (1.0 - beta_first**STEP)
    denom = jnp.sqrt(new_second / (1.0 - beta_second**STEP)) + adam_eps
    new_param = param - step_size * new_first / denom - learn_rate * decay * param
    return (new_param, new_first, new_second)


def on_device(n, block_in, condition, out_grad, weights, biases, first_moment, second_moment, bias_first, bias_second):
    me = lax.axis_index("dp")
    rows = D // n
    wb = weights.astype(bf)
    qkv_l = wb[:, : 3 * D].reshape(rows, 3, 4, 256).transpose(2, 0, 1, 3).reshape(4, rows, 768)
    up_l = wb[:, 4 * D : 4 * D + FF].reshape(rows, NJ, CH).transpose(1, 0, 2)
    dn_l = wb[:, 4 * D + FF : 4 * D + 2 * FF].reshape(rows, NJ, CH).transpose(1, 0, 2)
    ada_l = wb[:, 4 * D + 2 * FF :]
    bias_full = lax.all_gather(biases.astype(bf), "dp", axis=0, tiled=True).astype(f32)
    cond_act = jax.nn.silu(condition).astype(bf)
    cond_all = lax.all_gather(cond_act, "dp", axis=0, tiled=True)
    cond_cols = lax.dynamic_slice_in_dim(cond_all, me * rows, rows, 1)
    mod_part = jnp.dot(cond_cols, ada_l, preferred_element_type=f32)
    mod = lax.psum_scatter(mod_part, "dp", scatter_dimension=0, tiled=True) + bias_full[4 * D + FF :]
    mod = jnp.concatenate([mod.reshape(6, D), jnp.zeros((2, D), f32)], axis=0)
    w_qkv = lax.all_gather(qkv_l, "dp", axis=1, tiled=True)
    w_out = lax.all_gather(wb[:, 3 * D : 4 * D], "dp", axis=0, tiled=True)
    w_up = lax.all_gather(up_l, "dp", axis=1, tiled=True)
    w_dn = lax.all_gather(dn_l, "dp", axis=1, tiled=True)
    zrow = jnp.zeros((D,), f32)
    bqkv = jnp.stack([bias_full[:D], zrow, bias_full[D : 2 * D]]).reshape(3, 4, 256).transpose(1, 0, 2).reshape(4, 1, 768)
    brows = jnp.stack([zrow, zrow, bias_full[2 * D : 3 * D], bias_full[3 * D + FF : 4 * D + FF], zrow, zrow, zrow, zrow])
    bup = bias_full[3 * D : 3 * D + FF].reshape(NJ, 1, CH)
    tok = block_in[0]
    gout = out_grad[0]
    qkv, attn_t, lse, h1t = ka(1024, tok, mod, bqkv, w_qkv)
    bo, dx1, dat, dw_mlp, dw_out, dmod_b, db, db_up = kb(512, tok, gout, attn_t, mod, brows, bup, w_out, w_up, w_dn)
    ig, dw_qkv, dmod_a, db_qkv = kc(1024, tok, mod, qkv, dat, lse, dx1, h1t, w_qkv)
    dmod = (dmod_a + dmod_b)[:6].reshape(1, 6 * D)
    g_mlp = lax.psum_scatter(dw_mlp, "dp", scatter_dimension=2, tiled=True)
    g_out = lax.psum_scatter(dw_out, "dp", scatter_dimension=0, tiled=True)
    g_qkv = lax.psum_scatter(dw_qkv, "dp", scatter_dimension=1, tiled=True)
    db_qkv = db_qkv.reshape(4, 3, 256).transpose(1, 0, 2).reshape(3, D)
    bias_row = jnp.concatenate([db_qkv[0], db_qkv[2], db[2], db_up.reshape(FF), db[3], dmod[0]])
    bias_grad = lax.psum_scatter(bias_row, "dp", scatter_dimension=0, tiled=True)
    dmod_all = lax.all_gather(dmod.astype(bf), "dp", axis=0, tiled=True)
    g_ada = lax.dot_general(cond_cols, dmod_all, TN, preferred_element_type=f32)
    cond_part = lax.dot_general(dmod_all, ada_l, NT, preferred_element_type=f32)
    cond_grad = lax.all_to_all(cond_part, "dp", split_axis=0, concat_axis=1, tiled=True)
    sigma = jax.nn.sigmoid(condition)
    cond_grad = cond_grad * (sigma * (1.0 + condition * (1.0 - sigma)))
    g_qkv = g_qkv.reshape(4, rows, 3, 256).transpose(1, 2, 0, 3).reshape(rows, 3 * D)
    g_mlp = g_mlp.transpose(2, 1, 0, 3).reshape(rows, 2 * FF)
    weight_grad = jnp.concatenate([g_qkv, g_out, g_mlp, g_ada], axis=1)
    new_weights, new_first, new_second = adam_step(weights, weight_grad, first_moment, second_moment, weight_decay)
    new_biases, new_bias_first, new_bias_second = adam_step(biases, bias_grad, bias_first, bias_second, 0.0)
    return (bo[None], ig[None], cond_grad, weight_grad, bias_grad, new_weights, new_biases, new_first, new_second, new_bias_first, new_bias_second)


def solution(mesh):
    three, two, one = P("dp", None, None), P("dp", None), P("dp")
    return jax.shard_map(
        functools.partial(on_device, mesh.shape["dp"]),
        mesh=mesh,
        in_specs=(three, two, three, two, one, two, two, one, one),
        out_specs=(three, three, two, two, one, two, one, two, two, one, one),
        check_vma=False,
    )
```

```python
import functools

import jax
import jax.numpy as jnp
from jax import lax
from jax.experimental import pallas as pl
from jax.experimental.pallas import tpu as pltpu
from jax.sharding import PartitionSpec as P

D = 1024
FF = 4096
S = 1024
STEP = 3
CH = 512
NJ = FF // CH
learn_rate = 0.01
beta_first = 0.9
beta_second = 0.95
adam_eps = 1e-08
weight_decay = 0.05
gc = 0.7978845608028654
LOG2E = 1.4426950408889634
f32 = jnp.float32
bf = jnp.bfloat16
NT = (((1,), (1,)), ((), ()))
TN = (((0,), (0,)), ((), ()))
V = pl.BlockSpec(memory_space=pltpu.VMEM)
A = pl.BlockSpec(memory_space=pl.ANY)
sd = jax.ShapeDtypeStruct
MESH = pl.DeviceIdType.MESH


def mesh_signal(sem, dev):
    pl.semaphore_signal(sem, inc=1, device_id=(dev,), device_id_type=MESH)


def remote(src, dst, send, recv, dev):
    return pltpu.make_async_remote_copy(src_ref=src, dst_ref=dst, send_sem=send, recv_sem=recv, device_id=(dev,), device_id_type=MESH)


def greet_all(n, me):
    barrier = pltpu.get_barrier_semaphore()

    def go(k, _):
        mesh_signal(barrier, lax.rem(me + k, n))
        return 0

    lax.fori_loop(1, n, go, 0)
    pl.semaphore_wait(barrier, n - 1)


def each_peer(n, me, f):
    def go(k, _):
        f(k, lax.rem(me + k, n), lax.rem(me + n - k, n))
        return 0

    lax.fori_loop(1, n, go, 0)


def first_kernel(n, rows, small, ada, mod, gat, wz, part, rec, s0, r0, s1, r1):
    me = lax.axis_index("dp")
    greet_all(n, me)
    each_peer(n, me, lambda k, to, fr: remote(small, gat.at[me], s0.at[k], r0.at[k], to).start())
    gat[pl.ds(me, 1)] = small[...].reshape(1, 16, 128)
    wz[...] = jnp.zeros_like(wz)
    per = 128 // rows
    wz[pl.ds(pl.multiple_of(lax.rem(me, per) * rows, rows), rows), :] = ada[...]
    each_peer(n, me, lambda k, to, fr: remote(small, gat.at[fr], s0.at[k], r0.at[k], to).wait())
    cond = gat[:, pl.ds(me // per, 1), :].reshape(n, 128).astype(bf)
    for c in range(12):
        cols = slice(c * 512, (c + 1) * 512)
        part[:, :, cols] = dot(cond, wz[:, cols]).reshape(n, 1, 512)
    each_peer(n, me, lambda k, to, fr: remote(part.at[to], rec.at[me], s1.at[k], r1.at[k], to).start())
    rec[pl.ds(me, 1)] = part[pl.ds(me, 1)]
    each_peer(n, me, lambda k, to, fr: remote(part.at[to], rec.at[fr], s1.at[k], r1.at[k], to).wait())
    for c in range(12):
        cols = slice(c * 512, (c + 1) * 512)
        mod[:, cols] = jnp.sum(rec[:, :, cols], axis=0)


def first(n, rows, small, ada):
    return pl.pallas_call(
        functools.partial(first_kernel, n, rows),
        out_shape=(sd((1, 6 * D), f32), sd((n, 16, 128), f32)),
        in_specs=[V, V],
        out_specs=[V, V],
        scratch_shapes=[pltpu.VMEM((128, 6 * D), bf), pltpu.VMEM((n, 1, 6 * D), f32), pltpu.VMEM((n, 1, 6 * D), f32)] + [pltpu.SemaphoreType.DMA((n,))] * 4,
        compiler_params=pltpu.CompilerParams(collective_id=0, has_side_effects=True, vmem_limit_bytes=40 * 2**20),
        name="first",
    )(small, ada)


def last_kernel(n, brow, dm, bsum, dall, rec, s0, r0, s1, r1):
    me = lax.axis_index("dp")
    greet_all(n, me)
    each_peer(n, me, lambda k, to, fr: remote(dm, dall.at[me], s0.at[k], r0.at[k], to).start())
    each_peer(n, me, lambda k, to, fr: remote(brow.at[to], rec.at[me], s1.at[k], r1.at[k], to).start())
    dall[pl.ds(me, 1)] = dm[...].reshape(1, 48, 128)
    rec[pl.ds(me, 1)] = brow[pl.ds(me, 1)]
    each_peer(n, me, lambda k, to, fr: remote(dm, dall.at[fr], s0.at[k], r0.at[k], to).wait())
    each_peer(n, me, lambda k, to, fr: remote(brow.at[to], rec.at[fr], s1.at[k], r1.at[k], to).wait())
    bsum[...] = jnp.sum(rec[...], axis=0)


def last(n, brow, dm):
    return pl.pallas_call(
        functools.partial(last_kernel, n),
        out_shape=(sd((8, 128), f32), sd((n, 48, 128), bf)),
        in_specs=[V, V],
        out_specs=[V, V],
        scratch_shapes=[pltpu.VMEM((n, 8, 128), f32)] + [pltpu.SemaphoreType.DMA((n,))] * 4,
        compiler_params=pltpu.CompilerParams(collective_id=1, has_side_effects=True),
        name="last",
    )(brow, dm)


def swap_kernel(n, cp, out, s0, r0):
    me = lax.axis_index("dp")
    greet_all(n, me)
    each_peer(n, me, lambda k, to, fr: remote(cp.at[to], out.at[me], s0.at[k], r0.at[k], to).start())
    out[pl.ds(me, 1)] = cp[pl.ds(me, 1)]
    each_peer(n, me, lambda k, to, fr: remote(cp.at[to], out.at[fr], s0.at[k], r0.at[k], to).wait())


def swap(n, cp):
    return pl.pallas_call(
        functools.partial(swap_kernel, n),
        out_shape=sd(cp.shape, f32),
        in_specs=[V],
        out_specs=V,
        scratch_shapes=[pltpu.SemaphoreType.DMA((n,))] * 2,
        compiler_params=pltpu.CompilerParams(collective_id=2, has_side_effects=True),
        name="swap",
    )(cp)


class Place:
    def __init__(self):
        me = lax.axis_index("dp")
        self.me = me
        self.z = me // 8
        self.y = lax.rem(me // 4, 2)
        self.x = lax.rem(me // 2, 2)
        self.c = lax.rem(me, 2)
        self.to_c = me + 1 - 2 * self.c
        self.to_x = me + 2 - 4 * self.x
        self.to_y = me + 4 - 8 * self.y

    def to_z(self, k):
        return lax.rem(self.z + k, 4) * 8 + lax.rem(self.me, 8)

    def greet(self):
        barrier = pltpu.get_barrier_semaphore()
        for k in (1, 2, 3):
            mesh_signal(barrier, self.to_z(k))
        for dev in (self.to_c, self.to_x, self.to_y):
            mesh_signal(barrier, dev)
        pl.semaphore_wait(barrier, 6)


class Gather:
    def __init__(self, at, src, buf, local, send, recv, count):
        self.at, self.src, self.buf, self.local, self.send, self.recv, self.count = at, src, buf, local, send, recv, count

    def step_refs(self, i, step, c):
        at, b = self.at, self.buf.at[i]
        y, x = at.y, at.x
        lo, hi = pl.ds(0, 16), pl.ds(16, 16)
        if step == 1:
            return [b.at[:, y, x, c]]
        if step == 2:
            return [b.at[:, y, 1 - x, c, lo], b.at[:, 1 - y, x, c, hi]]
        return [b.at[:, 1 - y, :, c, lo], b.at[:, :, 1 - x, c, hi]]

    def z_copy(self, i, k):
        at = self.at
        return remote(self.src.at[i], self.buf.at[i, at.z, at.y, at.x, at.c], self.send.at[i, k - 1], self.recv.at[i, k - 1], at.to_z(k))

    def z_landed(self, i, k):
        at = self.at
        zz = lax.rem(at.z + 4 - k, 4)
        return remote(self.src.at[i], self.buf.at[i, zz, at.y, at.x, at.c], self.send.at[i, k - 1], self.recv.at[i, k - 1], at.to_z(k))

    def own(self, i):
        at = self.at
        return pltpu.make_async_copy(self.src.at[i], self.buf.at[i, at.z, at.y, at.x, at.c], self.local.at[i])

    def xy_copies(self, i, step):
        at, b = self.at, self.buf.at[i]
        y, x, c = at.y, at.x, at.c
        lo, hi = pl.ds(0, 16), pl.ds(16, 16)
        if step == 2:
            a, d = b.at[:, y, x, c, lo], b.at[:, y, x, c, hi]
            return [
                remote(a, a, self.send.at[i, 3], self.recv.at[i, 3], at.to_x),
                remote(d, d, self.send.at[i, 4], self.recv.at[i, 4], at.to_y),
            ]
        a, d = b.at[:, y, :, c, lo], b.at[:, :, x, c, hi]
        return [
            remote(a, a, self.send.at[i, 5], self.recv.at[i, 5], at.to_y),
            remote(d, d, self.send.at[i, 6], self.recv.at[i, 6], at.to_x),
        ]

    def xy_landed(self, i, step):
        at, b = self.at, self.buf.at[i]
        refs = self.step_refs(i, step, at.c)
        base = 3 if step == 2 else 5
        return [remote(r, r, self.send.at[i, base + q], self.recv.at[i, base + q], at.to_x) for q, r in enumerate(refs)]

    def core_copies(self, i, step):
        at = self.at
        base = {1: 7, 2: 8, 3: 10}[step]
        return [remote(r, r, self.send.at[i, base + q], self.recv.at[i, base + q], at.to_c) for q, r in enumerate(self.step_refs(i, step, at.c))]

    def core_landed(self, i, step):
        at = self.at
        base = {1: 7, 2: 8, 3: 10}[step]
        return [remote(r, r, self.send.at[i, base + q], self.recv.at[i, base + q], at.to_c) for q, r in enumerate(self.step_refs(i, step, 1 - at.c))]

    def start(self):
        def go(i, _):
            self.own(i).start()
            return 0

        lax.fori_loop(0, self.count, go, 0)

    def tick(self, t):
        def when(i, f):
            @pl.when((i >= 0) & (i < self.count))
            def _():
                f()

        def one():
            for k in (1, 2, 3):
                self.z_copy(t, k).start()

        def two():
            i = t - 1
            for k in (1, 2, 3):
                self.z_landed(i, k).wait_recv()
            self.own(i).wait()
            for cp in self.xy_copies(i, 2) + self.core_copies(i, 1):
                cp.start()

        def three():
            i = t - 2
            for cp in self.xy_landed(i, 2):
                cp.wait_recv()
            for cp in self.xy_copies(i, 3) + self.core_copies(i, 2):
                cp.start()

        def four():
            i = t - 3
            for cp in self.xy_landed(i, 3):
                cp.wait_recv()
            for cp in self.core_copies(i, 3):
                cp.start()

        def five():
            i = t - 4
            for step in (1, 2, 3):
                for cp in self.core_landed(i, step):
                    cp.wait_recv()

        when(t - 3, four)
        when(t - 2, three)
        when(t - 1, two)
        when(t, one)
        when(t - 4, five)

    def finish(self):
        def go(i, _):
            for k in (1, 2, 3):
                self.z_copy(i, k).wait_send()
            for step in (2, 3):
                for cp in self.xy_copies(i, step):
                    cp.wait_send()
            for step in (1, 2, 3):
                for cp in self.core_copies(i, step):
                    cp.wait_send()
            return 0

        lax.fori_loop(0, self.count, go, 0)


def dot(a,b,dn=None):
    if dn is None: return jnp.dot(a,b,preferred_element_type=f32)
    return lax.dot_general(a,b,dn,preferred_element_type=f32)

def lane_half(x, hh):
    lane=lax.broadcasted_iota(jnp.int32, x.shape, 1)
    keep=(lane<64) if hh==0 else (lane>=64)
    return jnp.where(keep, x, jnp.zeros_like(x))

def gelu_pair(u):
    u2=u*u
    t=jnp.tanh(gc*(u+0.044715*u2*u))
    return 0.5*u*(1.0+t), 0.5*(1.0+t)+0.5*u*(1.0-t*t)*gc*(1.0+3.0*0.044715*u2)
def nrm(v):
    c=v-jnp.mean(v,axis=-1,keepdims=True)
    r=lax.rsqrt(jnp.mean(c*c,axis=-1,keepdims=True)+1e-6)
    return c*r,r
def rows_loop(n, R, f):
    def body(i,_):
        f(pl.ds(pl.multiple_of(i*R,R),R)); return 0
    lax.fori_loop(0,n//R,body,0)

def kb_kernel(R, tok, gout, attnT, mod, bias, bup, wall,
      bo_ref, dx1_ref, dat_ref, dw_h, dwout_ref, dmod_ref, db_ref, dbup_ref,
      h2, h2T, dzb, dzT, z, dh2, o_s, wout, wbuf, act, du, dwst, wsem, osem, wosem):
    def co(g): return pltpu.make_async_copy(wall.at[g, :, 768:1024], wout.at[:, g*256:(g+1)*256], wosem.at[g])
    for g in range(4): co(g).start()
    def fetch(j, slot):
        pltpu.make_async_copy(wall.at[4 + j], wbuf.at[slot], wsem.at[slot]).start()
    fetch(0,0)
    shift1=mod[0:1];scale1=mod[1:2];gate1=mod[2:3];shift2=mod[3:4];scale2=mod[4:5];gate2=mod[5:6]
    db_ref[...]=jnp.zeros_like(db_ref); dmod_ref[...]=jnp.zeros_like(dmod_ref)
    for g in range(4): co(g).wait()
    def pre(r):
        o=dot(attnT[:,r],wout[...],TN)+bias[2:3]
        o_s[r,:]=o
        x1=tok[r,:].astype(f32)+gate1*o
        xh,_=nrm(x1)
        h2[r,:]=(xh*(1.0+scale2)+shift2).astype(bf)
        dz=gout[r,:].astype(f32)*gate2
        dzb[r,:]=dz.astype(bf)
        db_ref[3:4]+=jnp.sum(dz,axis=0,keepdims=True)
    rows_loop(S,256,pre)
    for i in range(4):
        r=slice(i*256,(i+1)*256)
        h2T[:,r]=h2[r,:].T
        dzT[:,r]=dzb[r,:].T
    z[...]=jnp.zeros_like(z); dh2[...]=jnp.zeros_like(dh2)
    def chunk(j,_):
        slot=lax.rem(j,2)
        @pl.when(j+1<NJ)
        def _(): fetch(j+1,1-slot)
        pltpu.make_async_copy(wall.at[4 + j], wbuf.at[slot], wsem.at[slot]).wait()
        dbup_ref[j]=jnp.zeros((1,CH),f32)
        def row(r):
            u=dot(h2[r,:],wbuf[slot,:,:CH])+bup[j]
            a,sl=gelu_pair(u)
            ab=a.astype(bf); act[r,:]=ab
            da=dot(dzb[r,:],wbuf[slot,:,CH:])
            d=da*sl
            dbup_ref[j]+=jnp.sum(d,axis=0,keepdims=True)
            db_=d.astype(bf); du[r,:]=db_
            z[r,:]+=dot(ab,wbuf[slot,:,CH:],NT)
            dh2[r,:]+=dot(db_,wbuf[slot,:,:CH],NT)
        rows_loop(S,R,row)
        @pl.when(j>=2)
        def _():
            pltpu.make_async_copy(dwst.at[slot], dw_h.at[j], osem.at[slot]).wait()
        def wrow(r):
            dwst[slot,0,r,:]=dot(h2T[r,:],du[...])
            dwst[slot,1,r,:]=dot(dzT[r,:],act[...])
        rows_loop(D,256,wrow)
        pltpu.make_async_copy(dwst.at[slot], dw_h.at[j], osem.at[slot]).start()
        return 0
    lax.fori_loop(0,NJ,chunk,0)
    for s in range(2): pltpu.make_async_copy(dwst.at[s], dw_h.at[s], osem.at[s]).wait()
    def post(r):
        g=gout[r,:].astype(f32); o=o_s[r,:]
        x1=tok[r,:].astype(f32)+gate1*o
        xh,rstd=nrm(x1)
        zz=z[r,:]+bias[3:4]
        bo_ref[r,:]=(x1+gate2*zz).astype(bf)
        dmod_ref[5:6]+=jnp.sum(g*zz,axis=0,keepdims=True)
        dh=dh2[r,:]
        dmod_ref[3:4]+=jnp.sum(dh,axis=0,keepdims=True)
        dmod_ref[4:5]+=jnp.sum(dh*xh,axis=0,keepdims=True)
        gg=dh*(1.0+scale2)
        dx1=g+rstd*(gg-jnp.mean(gg,axis=-1,keepdims=True)-xh*jnp.mean(gg*xh,axis=-1,keepdims=True))
        dx1_ref[r,:]=dx1
        dmod_ref[2:3]+=jnp.sum(dx1*o,axis=0,keepdims=True)
        do=dx1*gate1
        db_ref[2:3]+=jnp.sum(do,axis=0,keepdims=True)
        dob=do.astype(bf)
        dzb[r,:]=dob
        t=dot(dob,wout[...],NT).astype(bf)
        for g4 in range(4): dat_ref[g4,r,:]=t[:,g4*256:(g4+1)*256]
    rows_loop(S,128,post)
    def wo(r):
        dwout_ref[r,:]=dot(attnT[r,:],dzb[...])
    rows_loop(D,256,wo)

def kb(R,*a):
    V=pl.BlockSpec(memory_space=pltpu.VMEM); A=pl.BlockSpec(memory_space=pl.ANY)
    sd=jax.ShapeDtypeStruct
    return pl.pallas_call(functools.partial(kb_kernel,R),
      out_shape=(sd((S,D),bf),sd((S,D),f32),sd((4,S,256),bf),sd((NJ,2,D,CH),f32),sd((D,D),f32),sd((8,D),f32),sd((8,D),f32),sd((NJ,1,CH),f32)),
      in_specs=[V]*6+[A], out_specs=[V,V,V,A,V,V,V,V],
      scratch_shapes=[pltpu.VMEM((S,D),bf)]*4+[pltpu.VMEM((S,D),f32)]*3+[pltpu.VMEM((D,D),bf),pltpu.VMEM((2,D,2*CH),bf),pltpu.VMEM((S,CH),bf),pltpu.VMEM((S,CH),bf),
         pltpu.VMEM((2,2,D,CH),f32),pltpu.SemaphoreType.DMA((2,)),pltpu.SemaphoreType.DMA((2,)),pltpu.SemaphoreType.DMA((4,))],
      compiler_params=pltpu.CompilerParams(vmem_limit_bytes=62*2**20), name=f"kb{R}")(*a)

def ka_kernel(comm, tok, mod, bqkv, w_in, qkv, attnT, lse, h1T, *rest):
    c = LOG2E / 8.0
    if comm:
        wall, h1, wbuf, wsem, local, send, recv = rest
        at = Place()
        at.greet()
        gather = Gather(at, w_in, wall, local, send, recv, 12)
        gather.start()
        gather.tick(0)
    else:
        wall = w_in
        h1, wbuf, wsem = rest

    def cp(g, slot):
        return pltpu.make_async_copy(wall.at[g, :, :, :, :, :, 0:768], wbuf.at[slot], wsem.at[slot])

    shift1 = mod[0:1]
    scale1 = mod[1:2]

    def ln(r):
        xh, _ = nrm(tok[r, :].astype(f32))
        h1[r, :] = (xh * (1.0 + scale1) + shift1).astype(bf)

    rows_loop(S, 128, ln)
    if comm:
        gather.tick(1)
    for i in range(4):
        r = slice(i * 256, (i + 1) * 256)
        h1T[:, r] = h1[r, :].T
    if comm:
        for t in (2, 3, 4):
            gather.tick(t)
    cp(0, 0).start()

    def group(g, _):
        slot = lax.rem(g, 2)
        if comm:
            gather.tick(5 + 2 * g)

        @pl.when(g < 3)
        def _():
            cp(g + 1, 1 - slot).start()

        cp(g, slot).wait()

        def proj(r):
            qkv[g, r, :] = (dot(h1[r, :], wbuf[slot].reshape(D, 768)) + bqkv[g]).astype(bf)

        rows_loop(S, 256, proj)
        for p in range(2):
            if comm and p == 1:
                gather.tick(6 + 2 * g)
            kp = qkv[g, :, 256 + p * 128 : 256 + (p + 1) * 128]
            vp = qkv[g, :, 512 + p * 128 : 512 + (p + 1) * 128]
            q = qkv[g, :, p * 128 : (p + 1) * 128]
            vT = vp.T
            for h in range(2):
                s = dot(lane_half(kp, h), q, NT)
                m = jnp.max(s, axis=0, keepdims=True)
                e = jnp.exp2((s - m) * c)
                l = jnp.sum(e, axis=0, keepdims=True)
                pr = (e * (1.0 / l)).astype(bf)
                o = dot(vT[h * 64 : (h + 1) * 64], pr)
                lse[g, p * 2 + h : p * 2 + h + 1, :] = m * 0.125 + jnp.log(l)
                attnT[pl.ds(pl.multiple_of(g * 256 + (p * 128 + h * 64), 64), 64), :] = o.astype(bf)
        return 0

    lax.fori_loop(0, 4, group, 0)
    if comm:
        for t in (13, 14, 15):
            gather.tick(t)
        gather.finish()


def ka(comm, *a):
    out = (sd((4, S, 768), bf), sd((D, S), bf), sd((4, 4, S), f32), sd((D, S), bf))
    scratch = [pltpu.VMEM((S, D), bf), pltpu.VMEM((2, 4, 2, 2, 2, 32, 768), bf), pltpu.SemaphoreType.DMA((2,))]
    params = dict(vmem_limit_bytes=60 * 2**20)
    specs = [V] * 4
    if comm:
        out += (sd((12, 4, 2, 2, 2, 32, 1024), bf),)
        specs += [A]
        scratch += [pltpu.SemaphoreType.DMA((12,)), pltpu.SemaphoreType.DMA((12, 12)), pltpu.SemaphoreType.DMA((12, 12))]
        params.update(collective_id=3, has_side_effects=True)
    return pl.pallas_call(
        functools.partial(ka_kernel, comm),
        out_shape=out,
        in_specs=[V, V, V, A],
        out_specs=specs,
        scratch_shapes=scratch,
        compiler_params=pltpu.CompilerParams(**params),
        name="attention_forward",
    )(*a)


def kc_kernel(QB, tok, mod, qkv, dat, lse, dx1, h1T, w_h, ig, dw_h, dmod, dbq, dqkv, dk_s, dv_s, dqT_s, dh1, wbuf, dwst, wsem, osem):
    c=LOG2E/8.0
    def cp(g,slot): return pltpu.make_async_copy(w_h.at[g, :, 0:768], wbuf.at[slot], wsem.at[slot])
    def co(g,slot): return pltpu.make_async_copy(dwst.at[slot], dw_h.at[g], osem.at[slot])
    cp(0,0).start()
    dh1[...]=jnp.zeros_like(dh1); dmod[...]=jnp.zeros_like(dmod); dbq[...]=jnp.zeros_like(dbq)
    def group(g,_):
        slot=lax.rem(g,2)
        @pl.when(g<3)
        def _(): cp(g+1,1-slot).start()
        for p in range(2):
            sl=slice(p*128,(p+1)*128); slk=slice(256+p*128,256+(p+1)*128); slv=slice(512+p*128,512+(p+1)*128)
            kp=qkv[g,:,slk]; vp=qkv[g,:,slv]
            ks=[lane_half(kp,h) for h in range(2)]; vs=[lane_half(vp,h) for h in range(2)]
            kT=kp.T
            dk_s[...]=jnp.zeros_like(dk_s); dv_s[...]=jnp.zeros_like(dv_s)
            def qblk(i,_):
                r=pl.ds(pl.multiple_of(i*QB,QB),QB)
                q=qkv[g,r,sl]; da=dat[g,r,sl]
                for h in range(2):
                    s=dot(ks[h],q,NT)
                    pT=jnp.exp2(s*c-lse[g,p*2+h:p*2+h+1,r]*LOG2E)
                    dp=dot(vs[h],da,NT)
                    delta=jnp.sum(pT*dp,axis=0,keepdims=True)
                    ds=(pT*(dp-delta)).astype(bf)
                    dv_s[...]+=dot(pT.astype(bf),lane_half(da,h))
                    dk_s[...]+=dot(ds,lane_half(q,h))
                    dqT_s[h*64:(h+1)*64,r]=dot(kT[h*64:(h+1)*64],ds)
                return 0
            lax.fori_loop(0,S//QB,qblk,0)
            dq=dqT_s[...].T*0.125
            dbq[g,:,sl]=jnp.sum(dq,axis=0,keepdims=True)
            dqkv[:,sl]=dq.astype(bf)
            dqkv[:,slk]=(dk_s[...]*0.125).astype(bf)
            dbq[g,:,slv]=jnp.sum(dv_s[...],axis=0,keepdims=True)
            dqkv[:,slv]=dv_s[...].astype(bf)
        cp(g,slot).wait()
        @pl.when(g>=2)
        def _(): co(g,slot).wait()
        def wrow(r):
            dwst[slot,r,:]=dot(h1T[r,:],dqkv[...])
            dh1[r,:]+=dot(dqkv[r,:],wbuf[slot],NT)
        rows_loop(D,256,wrow)
        co(g,slot).start()
        return 0
    lax.fori_loop(0,4,group,0)
    for s_ in range(2): co(s_,s_).wait()
    scale1=mod[1:2]
    def post(r):
        xh,rstd=nrm(tok[r,:].astype(f32))
        dh=dh1[r,:]
        dmod[0:1]+=jnp.sum(dh,axis=0,keepdims=True)
        dmod[1:2]+=jnp.sum(dh*xh,axis=0,keepdims=True)
        gg=dh*(1.0+scale1)
        ig[r,:]=dx1[r,:]+rstd*(gg-jnp.mean(gg,axis=-1,keepdims=True)-xh*jnp.mean(gg*xh,axis=-1,keepdims=True))
    rows_loop(S,128,post)
def kc(QB,*a):
    return pl.pallas_call(functools.partial(kc_kernel,QB),
      out_shape=(sd((S,D),f32),sd((4,D,768),f32),sd((8,D),f32),sd((4,1,768),f32)),
      in_specs=[V]*7+[A], out_specs=[V,A,V,V],
      scratch_shapes=[pltpu.VMEM((S,768),bf),pltpu.VMEM((S,128),f32),pltpu.VMEM((S,128),f32),pltpu.VMEM((128,S),f32),pltpu.VMEM((S,D),f32),
        pltpu.VMEM((2,D,768),bf),pltpu.VMEM((2,D,768),f32),pltpu.SemaphoreType.DMA((2,)),pltpu.SemaphoreType.DMA((2,))],
      compiler_params=pltpu.CompilerParams(vmem_limit_bytes=60*2**20), name=f"kc{QB}")(*a)

def adam_step(param, grad, first, second, decay):
    new_first = beta_first * first + (1.0 - beta_first) * grad
    new_second = beta_second * second + (1.0 - beta_second) * grad * grad
    step_size = learn_rate / (1.0 - beta_first**STEP)
    denom = jnp.sqrt(new_second / (1.0 - beta_second**STEP)) + adam_eps
    new_param = param - step_size * new_first / denom - learn_rate * decay * param
    return (new_param, new_first, new_second)


def on_device(n, block_in, condition, out_grad, weights, biases, first_moment, second_moment, bias_first, bias_second):
    me = lax.axis_index("dp")
    rows = D // n
    chips = n == 32
    wb = weights.astype(bf)
    qkvo = wb[:, : 4 * D].reshape(rows, 4, 4, 256).transpose(2, 0, 1, 3).reshape(4, rows, 1024)
    updn = wb[:, 4 * D : 4 * D + 2 * FF].reshape(rows, 2, NJ, CH).transpose(2, 0, 1, 3).reshape(NJ, rows, 1024)
    mine = jnp.concatenate([qkvo, updn], axis=0)
    ada_l = wb[:, 4 * D + 2 * FF :]
    cond_act = jax.nn.silu(condition).astype(bf)
    if chips:
        small = jnp.concatenate([cond_act.astype(f32).reshape(-1), lax.reduce_precision(biases, 8, 7), jnp.zeros((576,), f32)])
        mod, gat = first(n, rows, small.reshape(16, 128), ada_l)
        bias_full = gat[:, 8:12].reshape(n, 512)[:, : biases.shape[0]].reshape(-1)
        cond_all = gat[:, :8].reshape(n, D).astype(bf)
    else:
        bias_full = lax.all_gather(biases.astype(bf), "dp", axis=0, tiled=True).astype(f32)
        cond_all = lax.all_gather(cond_act, "dp", axis=0, tiled=True)
    cond_cols = lax.dynamic_slice_in_dim(cond_all, me * rows, rows, 1)
    if not chips:
        mod = lax.psum_scatter(jnp.dot(cond_cols, ada_l, preferred_element_type=f32), "dp", scatter_dimension=0, tiled=True)
    mod = mod + bias_full[4 * D + FF :]
    mod = jnp.concatenate([mod.reshape(6, D), jnp.zeros((2, D), f32)], axis=0)
    zrow = jnp.zeros((D,), f32)
    bqkv = jnp.stack([bias_full[:D], zrow, bias_full[D : 2 * D]]).reshape(3, 4, 256).transpose(1, 0, 2).reshape(4, 1, 768)
    brows = jnp.stack([zrow, zrow, bias_full[2 * D : 3 * D], bias_full[3 * D + FF : 4 * D + FF], zrow, zrow, zrow, zrow])
    bup = bias_full[3 * D : 3 * D + FF].reshape(NJ, 1, CH)
    tok = block_in[0]
    gout = out_grad[0]
    if chips:
        qkv, attn_t, lse, h1t, wall = ka(True, tok, mod, bqkv, mine)
    else:
        wall = lax.all_gather(mine, "dp", axis=1, tiled=True).reshape(12, 4, 2, 2, 2, 32, 1024)
        qkv, attn_t, lse, h1t = ka(False, tok, mod, bqkv, wall)
    wall = wall.reshape(12, D, 1024)
    bo, dx1, dat, dw_mlp, dw_out, dmod_b, db, db_up = kb(512, tok, gout, attn_t, mod, brows, bup, wall)
    ig, dw_qkv, dmod_a, db_qkv = kc(1024, tok, mod, qkv, dat, lse, dx1, h1t, wall)
    dmod = (dmod_a + dmod_b)[:6].reshape(1, 6 * D)
    g_mlp = lax.psum_scatter(dw_mlp, "dp", scatter_dimension=2, tiled=True)
    g_out = lax.psum_scatter(dw_out, "dp", scatter_dimension=0, tiled=True)
    g_qkv = lax.psum_scatter(dw_qkv, "dp", scatter_dimension=1, tiled=True)
    db_qkv = db_qkv.reshape(4, 3, 256).transpose(1, 0, 2).reshape(3, D)
    bias_row = jnp.concatenate([db_qkv[0], db_qkv[2], db[2], db_up.reshape(FF), db[3], dmod[0]])
    dmod_bf = dmod.astype(bf)
    if chips:
        own = biases.shape[0]
        blocks = jnp.pad(bias_row.reshape(n, own), ((0, 0), (0, 1024 - own))).reshape(n, 8, 128)
        bias_grad, dmod_all = last(n, blocks, dmod_bf.reshape(48, 128))
        bias_grad = bias_grad.reshape(-1)[:own]
        dmod_all = dmod_all.reshape(n, 6 * D)
    else:
        bias_grad = lax.psum_scatter(bias_row, "dp", scatter_dimension=0, tiled=True)
        dmod_all = lax.all_gather(dmod_bf, "dp", axis=0, tiled=True)
    g_ada = lax.dot_general(cond_cols, dmod_all, TN, preferred_element_type=f32)
    cond_part = lax.dot_general(dmod_all, ada_l, NT, preferred_element_type=f32)
    if chips:
        cond_grad = swap(n, jnp.pad(cond_part, ((0, 0), (0, 128 - rows))).reshape(n, 1, 128))[:, 0, :rows].reshape(1, D)
    else:
        cond_grad = lax.all_to_all(cond_part, "dp", split_axis=0, concat_axis=1, tiled=True)
    sigma = jax.nn.sigmoid(condition)
    cond_grad = cond_grad * (sigma * (1.0 + condition * (1.0 - sigma)))
    g_qkv = g_qkv.reshape(4, rows, 3, 256).transpose(1, 2, 0, 3).reshape(rows, 3 * D)
    g_mlp = g_mlp.transpose(2, 1, 0, 3).reshape(rows, 2 * FF)
    weight_grad = jnp.concatenate([g_qkv, g_out, g_mlp, g_ada], axis=1)
    new_weights, new_first, new_second = adam_step(weights, weight_grad, first_moment, second_moment, weight_decay)
    new_biases, new_bias_first, new_bias_second = adam_step(biases, bias_grad, bias_first, bias_second, 0.0)
    return (bo[None], ig[None], cond_grad, weight_grad, bias_grad, new_weights, new_biases, new_first, new_second, new_bias_first, new_bias_second)


def solution(mesh):
    three, two, one = P("dp", None, None), P("dp", None), P("dp")
    return jax.shard_map(
        functools.partial(on_device, mesh.shape["dp"]),
        mesh=mesh,
        in_specs=(three, two, three, two, one, two, two, one, one),
        out_specs=(three, three, two, two, one, two, one, two, two, one, one),
        check_vma=False,
    )
```

```python
import functools

import jax
import jax.numpy as jnp
from jax import lax
from jax.experimental import pallas as pl
from jax.experimental.pallas import tpu as pltpu
from jax.sharding import PartitionSpec as P

D = 1024
FF = 4096
S = 1024
STEP = 3
CH = 512
NJ = FF // CH
learn_rate = 0.01
beta_first = 0.9
beta_second = 0.95
adam_eps = 1e-08
weight_decay = 0.05
gc = 0.7978845608028654
LOG2E = 1.4426950408889634
f32 = jnp.float32
bf = jnp.bfloat16
NT = (((1,), (1,)), ((), ()))
TN = (((0,), (0,)), ((), ()))
V = pl.BlockSpec(memory_space=pltpu.VMEM)
A = pl.BlockSpec(memory_space=pl.ANY)
sd = jax.ShapeDtypeStruct
MESH = pl.DeviceIdType.MESH


def mesh_signal(sem, dev):
    pl.semaphore_signal(sem, inc=1, device_id=(dev,), device_id_type=MESH)


def remote(src, dst, send, recv, dev):
    return pltpu.make_async_remote_copy(src_ref=src, dst_ref=dst, send_sem=send, recv_sem=recv, device_id=(dev,), device_id_type=MESH)


def greet_all(n, me):
    barrier = pltpu.get_barrier_semaphore()

    def go(k, _):
        mesh_signal(barrier, lax.rem(me + k, n))
        return 0

    lax.fori_loop(1, n, go, 0)
    pl.semaphore_wait(barrier, n - 1)


def each_peer(n, me, f):
    def go(k, _):
        f(k, lax.rem(me + k, n), lax.rem(me + n - k, n))
        return 0

    lax.fori_loop(1, n, go, 0)


def first_kernel(n, rows, small, ada, mod, gat, wz, part, rec, s0, r0, s1, r1):
    me = lax.axis_index("dp")
    greet_all(n, me)
    each_peer(n, me, lambda k, to, fr: remote(small, gat.at[me], s0.at[k], r0.at[k], to).start())
    gat[pl.ds(me, 1)] = small[...].reshape(1, 16, 128)
    wz[...] = jnp.zeros_like(wz)
    per = 128 // rows
    wz[pl.ds(pl.multiple_of(lax.rem(me, per) * rows, rows), rows), :] = ada[...]
    each_peer(n, me, lambda k, to, fr: remote(small, gat.at[fr], s0.at[k], r0.at[k], to).wait())
    cond = gat[:, pl.ds(me // per, 1), :].reshape(n, 128).astype(bf)
    for c in range(12):
        cols = slice(c * 512, (c + 1) * 512)
        part[:, :, cols] = dot(cond, wz[:, cols]).reshape(n, 1, 512)
    each_peer(n, me, lambda k, to, fr: remote(part.at[to], rec.at[me], s1.at[k], r1.at[k], to).start())
    rec[pl.ds(me, 1)] = part[pl.ds(me, 1)]
    each_peer(n, me, lambda k, to, fr: remote(part.at[to], rec.at[fr], s1.at[k], r1.at[k], to).wait())
    for c in range(12):
        cols = slice(c * 512, (c + 1) * 512)
        mod[:, cols] = jnp.sum(rec[:, :, cols], axis=0)


def first(n, rows, small, ada):
    return pl.pallas_call(
        functools.partial(first_kernel, n, rows),
        out_shape=(sd((1, 6 * D), f32), sd((n, 16, 128), f32)),
        in_specs=[V, V],
        out_specs=[V, V],
        scratch_shapes=[pltpu.VMEM((128, 6 * D), bf), pltpu.VMEM((n, 1, 6 * D), f32), pltpu.VMEM((n, 1, 6 * D), f32)] + [pltpu.SemaphoreType.DMA((n,))] * 4,
        compiler_params=pltpu.CompilerParams(collective_id=0, has_side_effects=True, vmem_limit_bytes=40 * 2**20),
        name="first",
    )(small, ada)


def last_kernel(n, brow, dm, bsum, dall, rec, s0, r0, s1, r1):
    me = lax.axis_index("dp")
    greet_all(n, me)
    each_peer(n, me, lambda k, to, fr: remote(dm, dall.at[me], s0.at[k], r0.at[k], to).start())
    each_peer(n, me, lambda k, to, fr: remote(brow.at[to], rec.at[me], s1.at[k], r1.at[k], to).start())
    dall[pl.ds(me, 1)] = dm[...].reshape(1, 48, 128)
    rec[pl.ds(me, 1)] = brow[pl.ds(me, 1)]
    each_peer(n, me, lambda k, to, fr: remote(dm, dall.at[fr], s0.at[k], r0.at[k], to).wait())
    each_peer(n, me, lambda k, to, fr: remote(brow.at[to], rec.at[fr], s1.at[k], r1.at[k], to).wait())
    bsum[...] = jnp.sum(rec[...], axis=0)


def last(n, brow, dm):
    return pl.pallas_call(
        functools.partial(last_kernel, n),
        out_shape=(sd((8, 128), f32), sd((n, 48, 128), bf)),
        in_specs=[V, V],
        out_specs=[V, V],
        scratch_shapes=[pltpu.VMEM((n, 8, 128), f32)] + [pltpu.SemaphoreType.DMA((n,))] * 4,
        compiler_params=pltpu.CompilerParams(collective_id=1, has_side_effects=True),
        name="last",
    )(brow, dm)


def swap_kernel(n, cp, out, s0, r0):
    me = lax.axis_index("dp")
    greet_all(n, me)
    each_peer(n, me, lambda k, to, fr: remote(cp.at[to], out.at[me], s0.at[k], r0.at[k], to).start())
    out[pl.ds(me, 1)] = cp[pl.ds(me, 1)]
    each_peer(n, me, lambda k, to, fr: remote(cp.at[to], out.at[fr], s0.at[k], r0.at[k], to).wait())


def swap(n, cp):
    return pl.pallas_call(
        functools.partial(swap_kernel, n),
        out_shape=sd(cp.shape, f32),
        in_specs=[V],
        out_specs=V,
        scratch_shapes=[pltpu.SemaphoreType.DMA((n,))] * 2,
        compiler_params=pltpu.CompilerParams(collective_id=2, has_side_effects=True),
        name="swap",
    )(cp)


class Place:
    def __init__(self):
        me = lax.axis_index("dp")
        self.me = me
        self.z = me // 8
        self.y = lax.rem(me // 4, 2)
        self.x = lax.rem(me // 2, 2)
        self.c = lax.rem(me, 2)
        self.to_c = me + 1 - 2 * self.c
        self.to_x = me + 2 - 4 * self.x
        self.to_y = me + 4 - 8 * self.y

    def to_z(self, k):
        return lax.rem(self.z + k, 4) * 8 + lax.rem(self.me, 8)

    def greet(self):
        barrier = pltpu.get_barrier_semaphore()
        for k in (1, 2, 3):
            mesh_signal(barrier, self.to_z(k))
        for dev in (self.to_c, self.to_x, self.to_y):
            mesh_signal(barrier, dev)
        pl.semaphore_wait(barrier, 6)


class Gather:
    def __init__(self, at, src, buf, local, send, recv, count):
        self.at, self.src, self.buf, self.local, self.send, self.recv, self.count = at, src, buf, local, send, recv, count

    def step_refs(self, i, step, c):
        at, b = self.at, self.buf.at[i]
        y, x = at.y, at.x
        lo, hi = pl.ds(0, 16), pl.ds(16, 16)
        if step == 1:
            return [b.at[:, y, x, c]]
        if step == 2:
            return [b.at[:, y, 1 - x, c, lo], b.at[:, 1 - y, x, c, hi]]
        return [b.at[:, 1 - y, :, c, lo], b.at[:, :, 1 - x, c, hi]]

    def z_copy(self, i, k):
        at = self.at
        return remote(self.src.at[i], self.buf.at[i, at.z, at.y, at.x, at.c], self.send.at[i, k - 1], self.recv.at[i, k - 1], at.to_z(k))

    def z_landed(self, i, k):
        at = self.at
        zz = lax.rem(at.z + 4 - k, 4)
        return remote(self.src.at[i], self.buf.at[i, zz, at.y, at.x, at.c], self.send.at[i, k - 1], self.recv.at[i, k - 1], at.to_z(k))

    def own(self, i):
        at = self.at
        return pltpu.make_async_copy(self.src.at[i], self.buf.at[i, at.z, at.y, at.x, at.c], self.local.at[i])

    def xy_copies(self, i, step):
        at, b = self.at, self.buf.at[i]
        y, x, c = at.y, at.x, at.c
        lo, hi = pl.ds(0, 16), pl.ds(16, 16)
        if step == 2:
            a, d = b.at[:, y, x, c, lo], b.at[:, y, x, c, hi]
            return [
                remote(a, a, self.send.at[i, 3], self.recv.at[i, 3], at.to_x),
                remote(d, d, self.send.at[i, 4], self.recv.at[i, 4], at.to_y),
            ]
        a, d = b.at[:, y, :, c, lo], b.at[:, :, x, c, hi]
        return [
            remote(a, a, self.send.at[i, 5], self.recv.at[i, 5], at.to_y),
            remote(d, d, self.send.at[i, 6], self.recv.at[i, 6], at.to_x),
        ]

    def xy_landed(self, i, step):
        at, b = self.at, self.buf.at[i]
        refs = self.step_refs(i, step, at.c)
        base = 3 if step == 2 else 5
        return [remote(r, r, self.send.at[i, base + q], self.recv.at[i, base + q], at.to_x) for q, r in enumerate(refs)]

    def core_copies(self, i, step):
        at = self.at
        base = {1: 7, 2: 8, 3: 10}[step]
        return [remote(r, r, self.send.at[i, base + q], self.recv.at[i, base + q], at.to_c) for q, r in enumerate(self.step_refs(i, step, at.c))]

    def core_landed(self, i, step):
        at = self.at
        base = {1: 7, 2: 8, 3: 10}[step]
        return [remote(r, r, self.send.at[i, base + q], self.recv.at[i, base + q], at.to_c) for q, r in enumerate(self.step_refs(i, step, 1 - at.c))]

    def start(self):
        def go(i, _):
            self.own(i).start()
            return 0

        lax.fori_loop(0, self.count, go, 0)

    def tick(self, t):
        def when(i, f):
            @pl.when((i >= 0) & (i < self.count))
            def _():
                f()

        def one():
            for k in (1, 2, 3):
                self.z_copy(t, k).start()

        def two():
            i = t - 1
            for k in (1, 2, 3):
                self.z_landed(i, k).wait_recv()
            self.own(i).wait()
            for cp in self.xy_copies(i, 2) + self.core_copies(i, 1):
                cp.start()

        def three():
            i = t - 2
            for cp in self.xy_landed(i, 2):
                cp.wait_recv()
            for cp in self.xy_copies(i, 3) + self.core_copies(i, 2):
                cp.start()

        def four():
            i = t - 3
            for cp in self.xy_landed(i, 3):
                cp.wait_recv()
            for cp in self.core_copies(i, 3):
                cp.start()

        def five():
            i = t - 4
            for step in (1, 2, 3):
                for cp in self.core_landed(i, step):
                    cp.wait_recv()

        when(t - 3, four)
        when(t - 2, three)
        when(t - 1, two)
        when(t, one)
        when(t - 4, five)

    def finish(self):
        def go(i, _):
            for k in (1, 2, 3):
                self.z_copy(i, k).wait_send()
            for step in (2, 3):
                for cp in self.xy_copies(i, step):
                    cp.wait_send()
            for step in (1, 2, 3):
                for cp in self.core_copies(i, step):
                    cp.wait_send()
            return 0

        lax.fori_loop(0, self.count, go, 0)


def dot(a,b,dn=None):
    if dn is None: return jnp.dot(a,b,preferred_element_type=f32)
    return lax.dot_general(a,b,dn,preferred_element_type=f32)

def lane_half(x, hh):
    lane=lax.broadcasted_iota(jnp.int32, x.shape, 1)
    keep=(lane<64) if hh==0 else (lane>=64)
    return jnp.where(keep, x, jnp.zeros_like(x))

def gelu_pair(u):
    u2=u*u
    t=jnp.tanh(gc*(u+0.044715*u2*u))
    return 0.5*u*(1.0+t), 0.5*(1.0+t)+0.5*u*(1.0-t*t)*gc*(1.0+3.0*0.044715*u2)
def nrm(v):
    c=v-jnp.mean(v,axis=-1,keepdims=True)
    r=lax.rsqrt(jnp.mean(c*c,axis=-1,keepdims=True)+1e-6)
    return c*r,r
def rows_loop(n, R, f):
    def body(i,_):
        f(pl.ds(pl.multiple_of(i*R,R),R)); return 0
    lax.fori_loop(0,n//R,body,0)

def kb_kernel(R, tok, gout, attnT, mod, bias, bup, wall,
      bo_ref, dx1_ref, dat_ref, dw_h, dwout_ref, dmod_ref, db_ref, dbup_ref,
      h2, h2T, dzb, dzT, z, dh2, o_s, wout, wbuf, act, du, dwst, wsem, osem, wosem):
    def co(g): return pltpu.make_async_copy(wall.at[g, :, 768:1024], wout.at[:, g*256:(g+1)*256], wosem.at[g])
    for g in range(4): co(g).start()
    def fetch(j, slot):
        pltpu.make_async_copy(wall.at[4 + j], wbuf.at[slot], wsem.at[slot]).start()
    fetch(0,0)
    shift1=mod[0:1];scale1=mod[1:2];gate1=mod[2:3];shift2=mod[3:4];scale2=mod[4:5];gate2=mod[5:6]
    db_ref[...]=jnp.zeros_like(db_ref); dmod_ref[...]=jnp.zeros_like(dmod_ref)
    for g in range(4): co(g).wait()
    def pre(r):
        o=dot(attnT[:,r],wout[...],TN)+bias[2:3]
        o_s[r,:]=o
        x1=tok[r,:].astype(f32)+gate1*o
        xh,_=nrm(x1)
        h2[r,:]=(xh*(1.0+scale2)+shift2).astype(bf)
        dz=gout[r,:].astype(f32)*gate2
        dzb[r,:]=dz.astype(bf)
        db_ref[3:4]+=jnp.sum(dz,axis=0,keepdims=True)
    rows_loop(S,256,pre)
    for i in range(4):
        r=slice(i*256,(i+1)*256)
        h2T[:,r]=h2[r,:].T
        dzT[:,r]=dzb[r,:].T
    z[...]=jnp.zeros_like(z); dh2[...]=jnp.zeros_like(dh2)
    def chunk(j,_):
        slot=lax.rem(j,2)
        @pl.when(j+1<NJ)
        def _(): fetch(j+1,1-slot)
        pltpu.make_async_copy(wall.at[4 + j], wbuf.at[slot], wsem.at[slot]).wait()
        dbup_ref[j]=jnp.zeros((1,CH),f32)
        def row(r):
            u=dot(h2[r,:],wbuf[slot,:,:CH])+bup[j]
            a,sl=gelu_pair(u)
            ab=a.astype(bf); act[r,:]=ab
            da=dot(dzb[r,:],wbuf[slot,:,CH:])
            d=da*sl
            dbup_ref[j]+=jnp.sum(d,axis=0,keepdims=True)
            db_=d.astype(bf); du[r,:]=db_
            z[r,:]+=dot(ab,wbuf[slot,:,CH:],NT)
            dh2[r,:]+=dot(db_,wbuf[slot,:,:CH],NT)
        rows_loop(S,R,row)
        @pl.when(j>=2)
        def _():
            pltpu.make_async_copy(dwst.at[slot], dw_h.at[j], osem.at[slot]).wait()
        def wrow(r):
            dwst[slot,0,r,:]=dot(h2T[r,:],du[...])
            dwst[slot,1,r,:]=dot(dzT[r,:],act[...])
        rows_loop(D,256,wrow)
        pltpu.make_async_copy(dwst.at[slot], dw_h.at[j], osem.at[slot]).start()
        return 0
    lax.fori_loop(0,NJ,chunk,0)
    for s in range(2): pltpu.make_async_copy(dwst.at[s], dw_h.at[s], osem.at[s]).wait()
    def post(r):
        g=gout[r,:].astype(f32); o=o_s[r,:]
        x1=tok[r,:].astype(f32)+gate1*o
        xh,rstd=nrm(x1)
        zz=z[r,:]+bias[3:4]
        bo_ref[r,:]=(x1+gate2*zz).astype(bf)
        dmod_ref[5:6]+=jnp.sum(g*zz,axis=0,keepdims=True)
        dh=dh2[r,:]
        dmod_ref[3:4]+=jnp.sum(dh,axis=0,keepdims=True)
        dmod_ref[4:5]+=jnp.sum(dh*xh,axis=0,keepdims=True)
        gg=dh*(1.0+scale2)
        dx1=g+rstd*(gg-jnp.mean(gg,axis=-1,keepdims=True)-xh*jnp.mean(gg*xh,axis=-1,keepdims=True))
        dx1_ref[r,:]=dx1
        dmod_ref[2:3]+=jnp.sum(dx1*o,axis=0,keepdims=True)
        do=dx1*gate1
        db_ref[2:3]+=jnp.sum(do,axis=0,keepdims=True)
        dob=do.astype(bf)
        dzb[r,:]=dob
        t=dot(dob,wout[...],NT).astype(bf)
        for g4 in range(4): dat_ref[g4,r,:]=t[:,g4*256:(g4+1)*256]
    rows_loop(S,128,post)
    def wo(r):
        dwout_ref[r,:]=dot(attnT[r,:],dzb[...])
    rows_loop(D,256,wo)

def kb(R,*a):
    V=pl.BlockSpec(memory_space=pltpu.VMEM); A=pl.BlockSpec(memory_space=pl.ANY)
    sd=jax.ShapeDtypeStruct
    return pl.pallas_call(functools.partial(kb_kernel,R),
      out_shape=(sd((S,D),bf),sd((S,D),f32),sd((4,S,256),bf),sd((NJ,2,D,CH),f32),sd((D,D),f32),sd((8,D),f32),sd((8,D),f32),sd((NJ,1,CH),f32)),
      in_specs=[V]*6+[A], out_specs=[V,V,V,A,V,V,V,V],
      scratch_shapes=[pltpu.VMEM((S,D),bf)]*4+[pltpu.VMEM((S,D),f32)]*3+[pltpu.VMEM((D,D),bf),pltpu.VMEM((2,D,2*CH),bf),pltpu.VMEM((S,CH),bf),pltpu.VMEM((S,CH),bf),
         pltpu.VMEM((2,2,D,CH),f32),pltpu.SemaphoreType.DMA((2,)),pltpu.SemaphoreType.DMA((2,)),pltpu.SemaphoreType.DMA((4,))],
      compiler_params=pltpu.CompilerParams(vmem_limit_bytes=62*2**20), name=f"kb{R}")(*a)

def ka_kernel(comm, tok, mod, bqkv, w_in, qkv, attnT, lse, h1T, *rest):
    c = LOG2E / 8.0
    if comm:
        wall, h1, wbuf, wsem, local, send, recv = rest
        at = Place()
        at.greet()
        gather = Gather(at, w_in, wall, local, send, recv, 12)
        gather.start()
        gather.tick(0)
    else:
        wall = w_in
        h1, wbuf, wsem = rest

    def cp(g, slot):
        return pltpu.make_async_copy(wall.at[g, :, :, :, :, :, 0:768], wbuf.at[slot], wsem.at[slot])

    shift1 = mod[0:1]
    scale1 = mod[1:2]

    def ln(r):
        xh, _ = nrm(tok[r, :].astype(f32))
        h1[r, :] = (xh * (1.0 + scale1) + shift1).astype(bf)

    rows_loop(S, 128, ln)
    if comm:
        gather.tick(1)
    for i in range(4):
        r = slice(i * 256, (i + 1) * 256)
        h1T[:, r] = h1[r, :].T
    if comm:
        for t in (2, 3, 4):
            gather.tick(t)
    cp(0, 0).start()

    def group(g, _):
        slot = lax.rem(g, 2)
        if comm:
            gather.tick(5 + 2 * g)

        @pl.when(g < 3)
        def _():
            cp(g + 1, 1 - slot).start()

        cp(g, slot).wait()

        def proj(r):
            qkv[g, r, :] = (dot(h1[r, :], wbuf[slot].reshape(D, 768)) + bqkv[g]).astype(bf)

        rows_loop(S, 256, proj)
        for p in range(2):
            if comm and p == 1:
                gather.tick(6 + 2 * g)
            kp = qkv[g, :, 256 + p * 128 : 256 + (p + 1) * 128]
            vp = qkv[g, :, 512 + p * 128 : 512 + (p + 1) * 128]
            q = qkv[g, :, p * 128 : (p + 1) * 128]
            vT = vp.T
            for h in range(2):
                s = dot(lane_half(kp, h), q, NT)
                m = jnp.max(s, axis=0, keepdims=True)
                e = jnp.exp2((s - m) * c)
                l = jnp.sum(e, axis=0, keepdims=True)
                pr = (e * (1.0 / l)).astype(bf)
                o = dot(vT[h * 64 : (h + 1) * 64], pr)
                lse[g, p * 2 + h : p * 2 + h + 1, :] = m * 0.125 + jnp.log(l)
                attnT[pl.ds(pl.multiple_of(g * 256 + (p * 128 + h * 64), 64), 64), :] = o.astype(bf)
        return 0

    lax.fori_loop(0, 4, group, 0)
    if comm:
        for t in (13, 14, 15):
            gather.tick(t)
        gather.finish()


def ka(comm, *a):
    out = (sd((4, S, 768), bf), sd((D, S), bf), sd((4, 4, S), f32), sd((D, S), bf))
    scratch = [pltpu.VMEM((S, D), bf), pltpu.VMEM((2, 4, 2, 2, 2, 32, 768), bf), pltpu.SemaphoreType.DMA((2,))]
    params = dict(vmem_limit_bytes=60 * 2**20)
    specs = [V] * 4
    if comm:
        out += (sd((12, 4, 2, 2, 2, 32, 1024), bf),)
        specs += [A]
        scratch += [pltpu.SemaphoreType.DMA((12,)), pltpu.SemaphoreType.DMA((12, 12)), pltpu.SemaphoreType.DMA((12, 12))]
        params.update(collective_id=3, has_side_effects=True)
    return pl.pallas_call(
        functools.partial(ka_kernel, comm),
        out_shape=out,
        in_specs=[V, V, V, A],
        out_specs=specs,
        scratch_shapes=scratch,
        compiler_params=pltpu.CompilerParams(**params),
        name="attention_forward",
    )(*a)


def kc_kernel(QB, tok, mod, qkv, dat, lse, dx1, h1T, w_h, ig, dw_h, dmod, dbq, dqkv, dk_s, dv_s, dqT_s, dh1, wbuf, dwst, wsem, osem):
    c=LOG2E/8.0
    def cp(g,slot): return pltpu.make_async_copy(w_h.at[g, :, 0:768], wbuf.at[slot], wsem.at[slot])
    def co(g,slot): return pltpu.make_async_copy(dwst.at[slot], dw_h.at[g], osem.at[slot])
    cp(0,0).start()
    dh1[...]=jnp.zeros_like(dh1); dmod[...]=jnp.zeros_like(dmod); dbq[...]=jnp.zeros_like(dbq)
    def group(g,_):
        slot=lax.rem(g,2)
        @pl.when(g<3)
        def _(): cp(g+1,1-slot).start()
        for p in range(2):
            sl=slice(p*128,(p+1)*128); slk=slice(256+p*128,256+(p+1)*128); slv=slice(512+p*128,512+(p+1)*128)
            kp=qkv[g,:,slk]; vp=qkv[g,:,slv]
            ks=[lane_half(kp,h) for h in range(2)]; vs=[lane_half(vp,h) for h in range(2)]
            kT=kp.T
            dk_s[...]=jnp.zeros_like(dk_s); dv_s[...]=jnp.zeros_like(dv_s)
            def qblk(i,_):
                r=pl.ds(pl.multiple_of(i*QB,QB),QB)
                q=qkv[g,r,sl]; da=dat[g,r,sl]
                for h in range(2):
                    s=dot(ks[h],q,NT)
                    pT=jnp.exp2(s*c-lse[g,p*2+h:p*2+h+1,r]*LOG2E)
                    dp=dot(vs[h],da,NT)
                    delta=jnp.sum(pT*dp,axis=0,keepdims=True)
                    ds=(pT*(dp-delta)).astype(bf)
                    dv_s[...]+=dot(pT.astype(bf),lane_half(da,h))
                    dk_s[...]+=dot(ds,lane_half(q,h))
                    dqT_s[h*64:(h+1)*64,r]=dot(kT[h*64:(h+1)*64],ds)
                return 0
            lax.fori_loop(0,S//QB,qblk,0)
            dq=dqT_s[...].T*0.125
            dbq[g,:,sl]=jnp.sum(dq,axis=0,keepdims=True)
            dqkv[:,sl]=dq.astype(bf)
            dqkv[:,slk]=(dk_s[...]*0.125).astype(bf)
            dbq[g,:,slv]=jnp.sum(dv_s[...],axis=0,keepdims=True)
            dqkv[:,slv]=dv_s[...].astype(bf)
        cp(g,slot).wait()
        @pl.when(g>=2)
        def _(): co(g,slot).wait()
        def wrow(r):
            dwst[slot,r,:]=dot(h1T[r,:],dqkv[...])
            dh1[r,:]+=dot(dqkv[r,:],wbuf[slot],NT)
        rows_loop(D,256,wrow)
        co(g,slot).start()
        return 0
    lax.fori_loop(0,4,group,0)
    for s_ in range(2): co(s_,s_).wait()
    scale1=mod[1:2]
    def post(r):
        xh,rstd=nrm(tok[r,:].astype(f32))
        dh=dh1[r,:]
        dmod[0:1]+=jnp.sum(dh,axis=0,keepdims=True)
        dmod[1:2]+=jnp.sum(dh*xh,axis=0,keepdims=True)
        gg=dh*(1.0+scale1)
        ig[r,:]=dx1[r,:]+rstd*(gg-jnp.mean(gg,axis=-1,keepdims=True)-xh*jnp.mean(gg*xh,axis=-1,keepdims=True))
    rows_loop(S,128,post)
def kc(QB,*a):
    return pl.pallas_call(functools.partial(kc_kernel,QB),
      out_shape=(sd((S,D),f32),sd((4,D,768),f32),sd((8,D),f32),sd((4,1,768),f32)),
      in_specs=[V]*7+[A], out_specs=[V,A,V,V],
      scratch_shapes=[pltpu.VMEM((S,768),bf),pltpu.VMEM((S,128),f32),pltpu.VMEM((S,128),f32),pltpu.VMEM((128,S),f32),pltpu.VMEM((S,D),f32),
        pltpu.VMEM((2,D,768),bf),pltpu.VMEM((2,D,768),f32),pltpu.SemaphoreType.DMA((2,)),pltpu.SemaphoreType.DMA((2,))],
      compiler_params=pltpu.CompilerParams(vmem_limit_bytes=60*2**20), name=f"kc{QB}")(*a)
def when(cond, f):
    @pl.when(cond)
    def _():
        f()


class Pair:
    def __init__(self, at, own, theirs, send, recv, credit, count):
        self.at, self.own, self.theirs, self.sems, self.credit, self.count = at, own, theirs, (send, recv), credit, count

    def copy(self, i):
        slot = lax.rem(i, 2)
        return remote(self.own.at[slot], self.theirs.at[slot], self.sems[0].at[slot], self.sems[1].at[slot], self.at.to_c)

    def reuse(self, i):
        when(i >= 2, lambda: self.copy(i).wait_send())

    def start(self, i):
        when(i >= 2, lambda: pl.semaphore_wait(self.credit, 1))
        self.copy(i).start()

    def arrived(self, i):
        self.copy(i).wait_recv()

    def free(self, i):
        when(i + 2 < self.count, lambda: mesh_signal(self.credit, self.at.to_c))

    def finish(self):
        for i in (self.count - 2, self.count - 1):
            self.copy(i).wait_send()


class Scatter:
    shapes = [
        pltpu.VMEM((4, 2, 2, 32, 1024), f32),
        pltpu.VMEM((2, 4, 2, 16, 1024), bf),
        pltpu.VMEM((2, 4, 2, 16, 1024), f32),
        pltpu.VMEM((2, 2, 4, 2, 16, 1024), bf),
        pltpu.VMEM((2, 4, 16, 1024), bf),
        pltpu.VMEM((2, 4, 16, 1024), f32),
        pltpu.VMEM((2, 2, 4, 16, 1024), bf),
        pltpu.VMEM((4, 32, 1024), bf),
        pltpu.VMEM((32, 1024), f32),
        pltpu.VMEM((2, 3, 32, 1024), bf),
        pltpu.SemaphoreType.DMA((7,)),
        pltpu.SemaphoreType.DMA((2, 7)),
        pltpu.SemaphoreType.REGULAR((7,)),
    ]

    def __init__(self, at, refs, out, count):
        self.at, self.out, self.count = at, out, count
        self.acc, self.s2, self.k2, self.r2, self.s3, self.k3, self.r3, self.s4, self.k4, self.r4, self.send, self.recv, self.credit = refs

    def copies(self, stage, i):
        at = self.at
        slot = lax.rem(i, 2)
        if stage == 2:
            todo = [(0, self.s2.at[0], self.r2.at[slot, 0], at.to_y), (1, self.s2.at[1], self.r2.at[slot, 1], at.to_x)]
        elif stage == 3:
            todo = [(2, self.s3.at[0], self.r3.at[slot, 0], at.to_x), (3, self.s3.at[1], self.r3.at[slot, 1], at.to_y)]
        else:
            todo = [(3 + k, self.s4.at[lax.rem(at.z + k, 4)], self.r4.at[slot, k - 1], at.to_z(k)) for k in (1, 2, 3)]
        return [remote(src, dst, self.send.at[q], self.recv.at[slot, q], dev) for q, src, dst, dev in todo]

    def sources(self, stage):
        at = self.at
        if stage == 2:
            return [(0, at.to_y), (1, at.to_x)]
        if stage == 3:
            return [(2, at.to_x), (3, at.to_y)]
        return [(3 + k, at.to_z(4 - k)) for k in (1, 2, 3)]

    def reuse(self, stage, i):
        def go():
            for cp in self.copies(stage, i - 1):
                cp.wait_send()

        when(i >= 1, go)

    def start(self, stage, i):
        def go():
            for q, _ in self.sources(stage):
                pl.semaphore_wait(self.credit.at[q], 1)

        when(i >= 2, go)
        for cp in self.copies(stage, i):
            cp.start()

    def arrived(self, stage, i):
        for cp in self.copies(stage, i):
            cp.wait_recv()

    def free(self, stage, i):
        def go():
            for q, dev in self.sources(stage):
                mesh_signal(self.credit.at[q], dev)

        when(i + 2 < self.count, go)

    def two(self, i):
        y, x = self.at.y, self.at.x
        lo, hi = pl.ds(0, 16), pl.ds(16, 16)
        self.reuse(2, i)
        self.s2[0] = self.acc[:, 1 - y, :, lo, :].astype(bf)
        self.s2[1] = self.acc[:, :, 1 - x, hi, :].astype(bf)
        self.start(2, i)
        self.k2[0] = self.acc[:, y, :, lo, :]
        self.k2[1] = self.acc[:, :, x, hi, :]

    def three(self, i):
        y, x = self.at.y, self.at.x
        slot = lax.rem(i, 2)
        self.arrived(2, i)
        self.reuse(3, i)
        self.s3[0] = (self.k2[0, :, 1 - x] + self.r2[slot, 0, :, 1 - x].astype(f32)).astype(bf)
        self.s3[1] = (self.k2[1, :, 1 - y] + self.r2[slot, 1, :, 1 - y].astype(f32)).astype(bf)
        self.start(3, i)
        self.k3[0] = self.k2[0, :, x] + self.r2[slot, 0, :, x].astype(f32)
        self.k3[1] = self.k2[1, :, y] + self.r2[slot, 1, :, y].astype(f32)
        self.free(2, i)

    def four(self, i):
        z = self.at.z
        slot = lax.rem(i, 2)
        self.arrived(3, i)
        self.reuse(4, i)
        for h in (0, 1):
            rows = slice(16 * h, 16 * h + 16)
            t = self.k3[h] + self.r3[slot, h].astype(f32)
            self.s4[:, rows, :] = t.astype(bf)
            self.k4[rows, :] = self.k3[h, z] + self.r3[slot, h, z].astype(f32)
        self.start(4, i)
        self.free(3, i)

    def five(self, i):
        slot = lax.rem(i, 2)
        self.arrived(4, i)
        t = self.k4[...]
        for k in (0, 1, 2):
            t = t + self.r4[slot, k].astype(f32)
        self.out[i] = t
        self.free(4, i)

    def tick(self, t):
        when((t >= 3) & (t - 3 < self.count), lambda: self.five(t - 3))
        when((t >= 2) & (t - 2 < self.count), lambda: self.four(t - 2))
        when((t >= 1) & (t - 1 < self.count), lambda: self.three(t - 1))

    def finish(self):
        for stage in (2, 3, 4):
            for cp in self.copies(stage, self.count - 1):
                cp.wait_send()


def mlp_kernel(tok, gout, attnT, mod, bias, bup, wall, bo, dx1, dat, dob, gm, dmod_ref, db_ref, dbup_ref,
               h2, hT, dzb, dzT, hS, zS, z, dh2, o_s, wout, wbuf, ad, adS, wsem, wosem, osem, xs, xr, ps, pr, pc, *sc):
    at = Place()
    at.greet()
    pair = Pair(at, ad, adS, ps, pr, pc, NJ)
    scatter = Scatter(at, sc, gm, NJ)

    def fetch(j, slot):
        return pltpu.make_async_copy(wall.at[4 + j], wbuf.at[slot], wsem.at[slot])

    def co(g):
        return pltpu.make_async_copy(wall.at[g, :, 768:1024], wout.at[:, g * 256 : (g + 1) * 256], wosem.at[g])

    for g in range(4):
        co(g).start()
    fetch(0, 0).start()
    gate1, shift2, scale2, gate2 = mod[2:3], mod[3:4], mod[4:5], mod[5:6]
    db_ref[...] = jnp.zeros_like(db_ref)
    dmod_ref[...] = jnp.zeros_like(dmod_ref)
    for g in range(4):
        co(g).wait()

    def pre(r):
        o = dot(attnT[:, r], wout[...], TN) + bias[2:3]
        o_s[r, :] = o
        x1 = tok[r, :].astype(f32) + gate1 * o
        xh, _ = nrm(x1)
        h2[r, :] = (xh * (1.0 + scale2) + shift2).astype(bf)
        dz = gout[r, :].astype(f32) * gate2
        dzb[r, :] = dz.astype(bf)
        db_ref[3:4] += jnp.sum(dz, axis=0, keepdims=True)

    rows_loop(S, 256, pre)
    for i in range(4):
        r = slice(i * 256, (i + 1) * 256)
        hT[:, :, :, r] = h2[r, :].T.reshape(16, 2, 32, 256)
        dzT[:, :, :, r] = dzb[r, :].T.reshape(16, 2, 32, 256)
    halves = [
        remote(hT.at[:, 1 - at.c], hS, xs.at[0], xr.at[0], at.to_c),
        remote(dzT.at[:, 1 - at.c], zS, xs.at[1], xr.at[1], at.to_c),
    ]
    for cp in halves:
        cp.start()
    z[...] = jnp.zeros_like(z)
    dh2[...] = jnp.zeros_like(dh2)

    def chunk(j, _):
        def forward():
            slot = lax.rem(j, 2)
            when(j + 1 < NJ, lambda: fetch(j + 1, 1 - slot).start())
            fetch(j, slot).wait()
            pair.reuse(j)
            dbup_ref[j] = jnp.zeros((1, CH), f32)

            def row(r):
                u = dot(h2[r, :], wbuf[slot, :, :CH]) + bup[j]
                a, sl = gelu_pair(u)
                ab = a.astype(bf)
                ad[slot, r, CH:] = ab
                d = dot(dzb[r, :], wbuf[slot, :, CH:]) * sl
                dbup_ref[j] += jnp.sum(d, axis=0, keepdims=True)
                db_ = d.astype(bf)
                ad[slot, r, :CH] = db_
                z[r, :] += dot(ab, wbuf[slot, :, CH:], NT)
                dh2[r, :] += dot(db_, wbuf[slot, :, :CH], NT)

            rows_loop(S, 512, row)
            pair.start(j)

        when(j < NJ, forward)
        scatter.tick(j - 1)

        def weights():
            i = j - 1
            slot = lax.rem(i, 2)
            when(j == 1, lambda: [cp.wait_recv() for cp in halves])
            pair.arrived(i)
            for q, (lhs, lhs_s) in enumerate(((hT, hS), (dzT, zS))):
                cols = slice(q * CH, (q + 1) * CH)
                t = dot(lhs[:, at.c].reshape(512, S), ad[slot, :, cols]) + dot(lhs_s[...].reshape(512, S), adS[slot, :, cols])
                scatter.acc[:, :, :, :, cols] = t.reshape(4, 2, 2, 32, CH)
            pair.free(i)
            scatter.two(i)

        when(j >= 1, weights)
        return 0

    lax.fori_loop(0, NJ + 1, chunk, 0)
    pair.finish()
    for cp in halves:
        cp.wait_send()

    def post(r):
        g = gout[r, :].astype(f32)
        o = o_s[r, :]
        x1 = tok[r, :].astype(f32) + gate1 * o
        xh, rstd = nrm(x1)
        zz = z[r, :] + bias[3:4]
        h2[r, :] = (x1 + gate2 * zz).astype(bf)
        dmod_ref[5:6] += jnp.sum(g * zz, axis=0, keepdims=True)
        dh = dh2[r, :]
        dmod_ref[3:4] += jnp.sum(dh, axis=0, keepdims=True)
        dmod_ref[4:5] += jnp.sum(dh * xh, axis=0, keepdims=True)
        gg = dh * (1.0 + scale2)
        dx = g + rstd * (gg - jnp.mean(gg, axis=-1, keepdims=True) - xh * jnp.mean(gg * xh, axis=-1, keepdims=True))
        dh2[r, :] = dx
        dmod_ref[2:3] += jnp.sum(dx * o, axis=0, keepdims=True)
        do = dx * gate1
        db_ref[2:3] += jnp.sum(do, axis=0, keepdims=True)
        dob_ = do.astype(bf)
        dzb[r, :] = dob_
        ad[0, r, :] = dot(dob_, wout[...], NT).astype(bf)

    def post_half(h):
        def body(i, _):
            post(pl.ds(pl.multiple_of(h * 512 + i * 128, 128), 128))
            return 0

        lax.fori_loop(0, 4, body, 0)

    post_half(0)
    scatter.tick(NJ)
    post_half(1)
    outs = [pltpu.make_async_copy(h2, bo, osem.at[0]), pltpu.make_async_copy(dh2, dx1, osem.at[1]), pltpu.make_async_copy(dzb, dob, osem.at[2])]
    outs += [pltpu.make_async_copy(ad.at[0, :, g * 256 : (g + 1) * 256], dat.at[g], osem.at[3 + g]) for g in range(4)]
    for cp in outs:
        cp.start()
    scatter.tick(NJ + 1)
    scatter.tick(NJ + 2)
    for cp in outs:
        cp.wait()
    scatter.finish()


def mlp(*a):
    dma = pltpu.SemaphoreType.DMA
    return pl.pallas_call(
        mlp_kernel,
        out_shape=(sd((S, D), bf), sd((S, D), f32), sd((4, S, 256), bf), sd((S, D), bf), sd((NJ, 32, 1024), f32), sd((8, D), f32), sd((8, D), f32), sd((NJ, 1, CH), f32)),
        in_specs=[V] * 6 + [A],
        out_specs=[A] * 4 + [V] * 4,
        scratch_shapes=[pltpu.VMEM((S, D), bf), pltpu.VMEM((16, 2, 32, S), bf)] * 2
        + [pltpu.VMEM((16, 32, S), bf)] * 2
        + [pltpu.VMEM((S, D), f32)] * 3
        + [pltpu.VMEM((D, D), bf), pltpu.VMEM((2, D, 2 * CH), bf), pltpu.VMEM((2, S, 2 * CH), bf), pltpu.VMEM((2, S, 2 * CH), bf)]
        + [dma((2,)), dma((4,)), dma((7,)), dma((2,)), dma((2,)), dma((2,)), dma((2,)), pltpu.SemaphoreType.REGULAR]
        + Scatter.shapes,
        compiler_params=pltpu.CompilerParams(collective_id=4, has_side_effects=True, vmem_limit_bytes=63 * 2**20),
        name="mlp",
    )(*a)


def back_kernel(tok, mod, qkv, dat, lse, dx1, h1T, attnT, dob, wall, ig, gq, dmod, dbq,
                dk_s, dv_s, dqT_s, dh1, wbuf, ex, exS, hS, aS, wsem, xs, xr, ps, pr, pc, *sc):
    c = LOG2E / 8.0
    at = Place()
    at.greet()
    pair = Pair(at, ex, exS, ps, pr, pc, 4)
    scatter = Scatter(at, sc, gq, 4)
    halves = [
        remote(h1T.at[:, 1 - at.c], hS, xs.at[0], xr.at[0], at.to_c),
        remote(attnT.at[:, 1 - at.c], aS, xs.at[1], xr.at[1], at.to_c),
    ]
    for cp in halves:
        cp.start()

    def cp_w(g, slot):
        return pltpu.make_async_copy(wall.at[g, :, 0:768], wbuf.at[slot], wsem.at[slot])

    cp_w(0, 0).start()
    dh1[...] = jnp.zeros_like(dh1)
    dmod[...] = jnp.zeros_like(dmod)
    dbq[...] = jnp.zeros_like(dbq)

    def group(g, _):
        slot = lax.rem(g, 2)
        when(g < 3, lambda: cp_w(g + 1, 1 - slot).start())
        pair.reuse(g)
        ex[slot, :, 768:] = dob[:, pl.ds(pl.multiple_of(g * 256, 256), 256)]
        for p in range(2):
            sl = slice(p * 128, (p + 1) * 128)
            slk = slice(256 + p * 128, 256 + (p + 1) * 128)
            slv = slice(512 + p * 128, 512 + (p + 1) * 128)
            kp, vp, q, da = qkv[g, :, slk], qkv[g, :, slv], qkv[g, :, sl], dat[g, :, sl]
            kT = kp.T
            for h in range(2):
                s = dot(lane_half(kp, h), q, NT)
                pT = jnp.exp2(s * c - lse[g, p * 2 + h : p * 2 + h + 1, :] * LOG2E)
                dp = dot(lane_half(vp, h), da, NT)
                delta = jnp.sum(pT * dp, axis=0, keepdims=True)
                ds = (pT * (dp - delta)).astype(bf)
                dv = dot(pT.astype(bf), lane_half(da, h))
                dk = dot(ds, lane_half(q, h))
                if h == 0:
                    dv_s[...] = dv
                    dk_s[...] = dk
                else:
                    dv_s[...] += dv
                    dk_s[...] += dk
                dqT_s[h * 64 : (h + 1) * 64, :] = dot(kT[h * 64 : (h + 1) * 64], ds)
            dq = dqT_s[...].T * 0.125
            dbq[g, :, sl] = jnp.sum(dq, axis=0, keepdims=True)
            ex[slot, :, sl] = dq.astype(bf)
            ex[slot, :, slk] = (dk_s[...] * 0.125).astype(bf)
            dbq[g, :, slv] = jnp.sum(dv_s[...], axis=0, keepdims=True)
            ex[slot, :, slv] = dv_s[...].astype(bf)
        pair.start(g)
        cp_w(g, slot).wait()

        def wrow(r):
            dh1[r, :] += dot(ex[slot, r, :768], wbuf[slot], NT)

        rows_loop(D, 256, wrow)
        scatter.tick(g)
        when(g == 0, lambda: [cp.wait_recv() for cp in halves])
        pair.arrived(g)
        for lhs, lhs_s, cols in ((h1T, hS, slice(0, 768)), (attnT, aS, slice(768, 1024))):
            t = dot(lhs[:, at.c].reshape(512, S), ex[slot, :, cols]) + dot(lhs_s[...].reshape(512, S), exS[slot, :, cols])
            scatter.acc[:, :, :, :, cols] = t.reshape(4, 2, 2, 32, cols.stop - cols.start)
        pair.free(g)
        scatter.two(g)
        return 0

    lax.fori_loop(0, 4, group, 0)
    pair.finish()
    for cp in halves:
        cp.wait_send()
    scale1 = mod[1:2]

    def post(r):
        xh, rstd = nrm(tok[r, :].astype(f32))
        dh = dh1[r, :]
        dmod[0:1] += jnp.sum(dh, axis=0, keepdims=True)
        dmod[1:2] += jnp.sum(dh * xh, axis=0, keepdims=True)
        gg = dh * (1.0 + scale1)
        ig[r, :] = dx1[r, :] + rstd * (gg - jnp.mean(gg, axis=-1, keepdims=True) - xh * jnp.mean(gg * xh, axis=-1, keepdims=True))

    rows_loop(S, 128, post)
    for t in (4, 5, 6):
        scatter.tick(t)
    scatter.finish()


def back(*a):
    dma = pltpu.SemaphoreType.DMA
    return pl.pallas_call(
        back_kernel,
        out_shape=(sd((S, D), f32), sd((4, 32, 1024), f32), sd((8, D), f32), sd((4, 1, 768), f32)),
        in_specs=[V] * 9 + [A],
        out_specs=[V] * 4,
        scratch_shapes=[pltpu.VMEM((S, 128), f32), pltpu.VMEM((S, 128), f32), pltpu.VMEM((128, S), f32), pltpu.VMEM((S, D), f32), pltpu.VMEM((2, D, 768), bf)]
        + [pltpu.VMEM((2, S, 1024), bf)] * 2
        + [pltpu.VMEM((16, 32, S), bf)] * 2
        + [dma((2,)), dma((2,)), dma((2,)), dma((2,)), dma((2,)), pltpu.SemaphoreType.REGULAR]
        + Scatter.shapes,
        compiler_params=pltpu.CompilerParams(collective_id=5, has_side_effects=True, vmem_limit_bytes=63 * 2**20),
        name="back",
    )(*a)


def adam_step(param, grad, first, second, decay):
    new_first = beta_first * first + (1.0 - beta_first) * grad
    new_second = beta_second * second + (1.0 - beta_second) * grad * grad
    step_size = learn_rate / (1.0 - beta_first**STEP)
    denom = jnp.sqrt(new_second / (1.0 - beta_second**STEP)) + adam_eps
    new_param = param - step_size * new_first / denom - learn_rate * decay * param
    return (new_param, new_first, new_second)


def on_device(n, block_in, condition, out_grad, weights, biases, first_moment, second_moment, bias_first, bias_second):
    me = lax.axis_index("dp")
    rows = D // n
    chips = n == 32
    wb = weights.astype(bf)
    qkvo = wb[:, : 4 * D].reshape(rows, 4, 4, 256).transpose(2, 0, 1, 3).reshape(4, rows, 1024)
    updn = wb[:, 4 * D : 4 * D + 2 * FF].reshape(rows, 2, NJ, CH).transpose(2, 0, 1, 3).reshape(NJ, rows, 1024)
    mine = jnp.concatenate([qkvo, updn], axis=0)
    ada_l = wb[:, 4 * D + 2 * FF :]
    cond_act = jax.nn.silu(condition).astype(bf)
    if chips:
        small = jnp.concatenate([cond_act.astype(f32).reshape(-1), lax.reduce_precision(biases, 8, 7), jnp.zeros((576,), f32)])
        mod, gat = first(n, rows, small.reshape(16, 128), ada_l)
        bias_full = gat[:, 8:12].reshape(n, 512)[:, : biases.shape[0]].reshape(-1)
        cond_all = gat[:, :8].reshape(n, D).astype(bf)
    else:
        bias_full = lax.all_gather(biases.astype(bf), "dp", axis=0, tiled=True).astype(f32)
        cond_all = lax.all_gather(cond_act, "dp", axis=0, tiled=True)
    cond_cols = lax.dynamic_slice_in_dim(cond_all, me * rows, rows, 1)
    if not chips:
        mod = lax.psum_scatter(jnp.dot(cond_cols, ada_l, preferred_element_type=f32), "dp", scatter_dimension=0, tiled=True)
    mod = mod + bias_full[4 * D + FF :]
    mod = jnp.concatenate([mod.reshape(6, D), jnp.zeros((2, D), f32)], axis=0)
    zrow = jnp.zeros((D,), f32)
    bqkv = jnp.stack([bias_full[:D], zrow, bias_full[D : 2 * D]]).reshape(3, 4, 256).transpose(1, 0, 2).reshape(4, 1, 768)
    brows = jnp.stack([zrow, zrow, bias_full[2 * D : 3 * D], bias_full[3 * D + FF : 4 * D + FF], zrow, zrow, zrow, zrow])
    bup = bias_full[3 * D : 3 * D + FF].reshape(NJ, 1, CH)
    tok = block_in[0]
    gout = out_grad[0]
    if chips:
        qkv, attn_t, lse, h1t, wall = ka(True, tok, mod, bqkv, mine)
    else:
        wall = lax.all_gather(mine, "dp", axis=1, tiled=True).reshape(12, 4, 2, 2, 2, 32, 1024)
        qkv, attn_t, lse, h1t = ka(False, tok, mod, bqkv, wall)
    wall = wall.reshape(12, D, 1024)
    if chips:
        bo, dx1, dat, dob, g_mlp, dmod_b, db, db_up = mlp(tok, gout, attn_t, mod, brows, bup, wall)
        parts = (16, 2, 32, S)
        ig, g_qkvo, dmod_a, db_qkv = back(tok, mod, qkv, dat, lse, dx1, h1t.reshape(parts), attn_t.reshape(parts), dob, wall)
        g_mlp = g_mlp.reshape(NJ, rows, 2, CH).transpose(1, 2, 0, 3).reshape(rows, 2 * FF)
        g_qkvo = g_qkvo.reshape(4, rows, 4, 256).transpose(1, 2, 0, 3).reshape(rows, 4 * D)
    else:
        bo, dx1, dat, dw_mlp, dw_out, dmod_b, db, db_up = kb(512, tok, gout, attn_t, mod, brows, bup, wall)
        ig, dw_qkv, dmod_a, db_qkv = kc(1024, tok, mod, qkv, dat, lse, dx1, h1t, wall)
        g_mlp = lax.psum_scatter(dw_mlp, "dp", scatter_dimension=2, tiled=True)
        g_out = lax.psum_scatter(dw_out, "dp", scatter_dimension=0, tiled=True)
        g_qkv = lax.psum_scatter(dw_qkv, "dp", scatter_dimension=1, tiled=True)
        g_qkv = g_qkv.reshape(4, rows, 3, 256).transpose(1, 2, 0, 3).reshape(rows, 3 * D)
        g_qkvo = jnp.concatenate([g_qkv, g_out], axis=1)
        g_mlp = g_mlp.transpose(2, 1, 0, 3).reshape(rows, 2 * FF)
    dmod = (dmod_a + dmod_b)[:6].reshape(1, 6 * D)
    db_qkv = db_qkv.reshape(4, 3, 256).transpose(1, 0, 2).reshape(3, D)
    bias_row = jnp.concatenate([db_qkv[0], db_qkv[2], db[2], db_up.reshape(FF), db[3], dmod[0]])
    dmod_bf = dmod.astype(bf)
    if chips:
        own = biases.shape[0]
        blocks = jnp.pad(bias_row.reshape(n, own), ((0, 0), (0, 1024 - own))).reshape(n, 8, 128)
        bias_grad, dmod_all = last(n, blocks, dmod_bf.reshape(48, 128))
        bias_grad = bias_grad.reshape(-1)[:own]
        dmod_all = dmod_all.reshape(n, 6 * D)
    else:
        bias_grad = lax.psum_scatter(bias_row, "dp", scatter_dimension=0, tiled=True)
        dmod_all = lax.all_gather(dmod_bf, "dp", axis=0, tiled=True)
    g_ada = lax.dot_general(cond_cols, dmod_all, TN, preferred_element_type=f32)
    cond_part = lax.dot_general(dmod_all, ada_l, NT, preferred_element_type=f32)
    if chips:
        cond_grad = swap(n, jnp.pad(cond_part, ((0, 0), (0, 128 - rows))).reshape(n, 1, 128))[:, 0, :rows].reshape(1, D)
    else:
        cond_grad = lax.all_to_all(cond_part, "dp", split_axis=0, concat_axis=1, tiled=True)
    sigma = jax.nn.sigmoid(condition)
    cond_grad = cond_grad * (sigma * (1.0 + condition * (1.0 - sigma)))
    weight_grad = jnp.concatenate([g_qkvo, g_mlp, g_ada], axis=1)
    new_weights, new_first, new_second = adam_step(weights, weight_grad, first_moment, second_moment, weight_decay)
    new_biases, new_bias_first, new_bias_second = adam_step(biases, bias_grad, bias_first, bias_second, 0.0)
    return (bo[None], ig[None], cond_grad, weight_grad, bias_grad, new_weights, new_biases, new_first, new_second, new_bias_first, new_bias_second)


def solution(mesh):
    three, two, one = P("dp", None, None), P("dp", None), P("dp")
    return jax.shard_map(
        functools.partial(on_device, mesh.shape["dp"]),
        mesh=mesh,
        in_specs=(three, two, three, two, one, two, two, one, one),
        out_specs=(three, three, two, two, one, two, one, two, two, one, one),
        check_vma=False,
    )
```

```python
import functools

import jax
import jax.numpy as jnp
from jax import lax
from jax.experimental import pallas as pl
from jax.experimental.pallas import tpu as pltpu
from jax.sharding import PartitionSpec as P

D = 1024
FF = 4096
S = 1024
STEP = 3
CH = 512
NJ = FF // CH
VMEM_BYTES = 63 * 2**20
learn_rate = 0.01
beta_first = 0.9
beta_second = 0.95
adam_eps = 1e-08
weight_decay = 0.05
gc = 0.7978845608028654
LOG2E = 1.4426950408889634
f32 = jnp.float32
bf = jnp.bfloat16
NT = (((1,), (1,)), ((), ()))
TN = (((0,), (0,)), ((), ()))
V = pl.BlockSpec(memory_space=pltpu.VMEM)
A = pl.BlockSpec(memory_space=pl.ANY)
sd = jax.ShapeDtypeStruct
MESH = pl.DeviceIdType.MESH


def mesh_signal(sem, dev):
    pl.semaphore_signal(sem, inc=1, device_id=(dev,), device_id_type=MESH)


def remote(src, dst, send, recv, dev):
    return pltpu.make_async_remote_copy(src_ref=src, dst_ref=dst, send_sem=send, recv_sem=recv, device_id=(dev,), device_id_type=MESH)


def greet_all(n, me):
    barrier = pltpu.get_barrier_semaphore()

    def go(k, _):
        mesh_signal(barrier, lax.rem(me + k, n))
        return 0

    lax.fori_loop(1, n, go, 0)
    pl.semaphore_wait(barrier, n - 1)


def each_peer(n, me, f):
    def go(k, _):
        f(k, lax.rem(me + k, n), lax.rem(me + n - k, n))
        return 0

    lax.fori_loop(1, n, go, 0)


def gather_sems(count):
    return [pltpu.SemaphoreType.DMA((count,)), pltpu.SemaphoreType.DMA((count, 12)), pltpu.SemaphoreType.DMA((count, 12))]


def last_kernel(n, brow, dm, bsum, dall, rec, s0, r0, s1, r1):
    me = lax.axis_index("dp")
    greet_all(n, me)
    each_peer(n, me, lambda k, to, fr: remote(dm, dall.at[me], s0.at[k], r0.at[k], to).start())
    each_peer(n, me, lambda k, to, fr: remote(brow.at[to], rec.at[me], s1.at[k], r1.at[k], to).start())
    dall[pl.ds(me, 1)] = dm[...].reshape(1, 48, 128)
    rec[pl.ds(me, 1)] = brow[pl.ds(me, 1)]
    each_peer(n, me, lambda k, to, fr: remote(dm, dall.at[fr], s0.at[k], r0.at[k], to).wait())
    each_peer(n, me, lambda k, to, fr: remote(brow.at[to], rec.at[fr], s1.at[k], r1.at[k], to).wait())
    bsum[...] = jnp.sum(rec[...], axis=0)


def last(n, brow, dm):
    return pl.pallas_call(
        functools.partial(last_kernel, n),
        out_shape=(sd((8, 128), f32), sd((n, 48, 128), bf)),
        in_specs=[V, V],
        out_specs=[V, V],
        scratch_shapes=[pltpu.VMEM((n, 8, 128), f32)] + [pltpu.SemaphoreType.DMA((n,))] * 4,
        compiler_params=pltpu.CompilerParams(collective_id=1, has_side_effects=True),
        name="last",
    )(brow, dm)


def swap_kernel(n, cp, out, s0, r0):
    me = lax.axis_index("dp")
    greet_all(n, me)
    each_peer(n, me, lambda k, to, fr: remote(cp.at[to], out.at[me], s0.at[k], r0.at[k], to).start())
    out[pl.ds(me, 1)] = cp[pl.ds(me, 1)]
    each_peer(n, me, lambda k, to, fr: remote(cp.at[to], out.at[fr], s0.at[k], r0.at[k], to).wait())


def swap(n, cp):
    return pl.pallas_call(
        functools.partial(swap_kernel, n),
        out_shape=sd(cp.shape, f32),
        in_specs=[V],
        out_specs=V,
        scratch_shapes=[pltpu.SemaphoreType.DMA((n,))] * 2,
        compiler_params=pltpu.CompilerParams(collective_id=2, has_side_effects=True),
        name="swap",
    )(cp)


class Place:
    def __init__(self):
        me = lax.axis_index("dp")
        self.me = me
        self.z = me // 8
        self.y = lax.rem(me // 4, 2)
        self.x = lax.rem(me // 2, 2)
        self.c = lax.rem(me, 2)
        self.to_c = me + 1 - 2 * self.c
        self.to_x = me + 2 - 4 * self.x
        self.to_y = me + 4 - 8 * self.y
        self.a = self.z // 2
        self.b = lax.rem(self.z, 2)
        self.to_b = me + 8 - 16 * self.b
        self.to_a = me + 16 - 32 * self.a

    def to_z(self, k):
        return lax.rem(self.z + k, 4) * 8 + lax.rem(self.me, 8)

    def greet(self):
        barrier = pltpu.get_barrier_semaphore()
        for k in (1, 2, 3):
            mesh_signal(barrier, self.to_z(k))
        for dev in (self.to_c, self.to_x, self.to_y):
            mesh_signal(barrier, dev)
        pl.semaphore_wait(barrier, 6)


class Gather:
    def __init__(self, at, src, buf, local, send, recv, count):
        self.at, self.src, self.buf, self.local, self.send, self.recv, self.count = at, src, buf, local, send, recv, count

    def step_refs(self, i, step, c):
        at, b = self.at, self.buf.at[i]
        y, x = at.y, at.x
        lo, hi = pl.ds(0, 16), pl.ds(16, 16)
        if step == 1:
            return [b.at[:, y, x, c]]
        if step == 2:
            return [b.at[:, y, 1 - x, c, lo], b.at[:, 1 - y, x, c, hi]]
        return [b.at[:, 1 - y, :, c, lo], b.at[:, :, 1 - x, c, hi]]

    def z_copy(self, i, k):
        at = self.at
        return remote(self.src.at[i], self.buf.at[i, at.z, at.y, at.x, at.c], self.send.at[i, k - 1], self.recv.at[i, k - 1], at.to_z(k))

    def z_landed(self, i, k):
        at = self.at
        zz = lax.rem(at.z + 4 - k, 4)
        return remote(self.src.at[i], self.buf.at[i, zz, at.y, at.x, at.c], self.send.at[i, k - 1], self.recv.at[i, k - 1], at.to_z(k))

    def own(self, i):
        at = self.at
        return pltpu.make_async_copy(self.src.at[i], self.buf.at[i, at.z, at.y, at.x, at.c], self.local.at[i])

    def xy_copies(self, i, step):
        at, b = self.at, self.buf.at[i]
        y, x, c = at.y, at.x, at.c
        lo, hi = pl.ds(0, 16), pl.ds(16, 16)
        if step == 2:
            a, d = b.at[:, y, x, c, lo], b.at[:, y, x, c, hi]
            return [
                remote(a, a, self.send.at[i, 3], self.recv.at[i, 3], at.to_x),
                remote(d, d, self.send.at[i, 4], self.recv.at[i, 4], at.to_y),
            ]
        a, d = b.at[:, y, :, c, lo], b.at[:, :, x, c, hi]
        return [
            remote(a, a, self.send.at[i, 5], self.recv.at[i, 5], at.to_y),
            remote(d, d, self.send.at[i, 6], self.recv.at[i, 6], at.to_x),
        ]

    def xy_landed(self, i, step):
        at, b = self.at, self.buf.at[i]
        refs = self.step_refs(i, step, at.c)
        base = 3 if step == 2 else 5
        return [remote(r, r, self.send.at[i, base + q], self.recv.at[i, base + q], at.to_x) for q, r in enumerate(refs)]

    def core_copies(self, i, step):
        at = self.at
        base = {1: 7, 2: 8, 3: 10}[step]
        return [remote(r, r, self.send.at[i, base + q], self.recv.at[i, base + q], at.to_c) for q, r in enumerate(self.step_refs(i, step, at.c))]

    def core_landed(self, i, step):
        at = self.at
        base = {1: 7, 2: 8, 3: 10}[step]
        return [remote(r, r, self.send.at[i, base + q], self.recv.at[i, base + q], at.to_c) for q, r in enumerate(self.step_refs(i, step, 1 - at.c))]

    def start(self):
        def go(i, _):
            self.own(i).start()
            return 0

        lax.fori_loop(0, self.count, go, 0)

    def tick(self, t):
        def at_piece(i, f):
            when((i >= 0) & (i < self.count), f)

        def one():
            for k in (1, 2, 3):
                self.z_copy(t, k).start()

        def two():
            i = t - 1
            for k in (1, 2, 3):
                self.z_landed(i, k).wait_recv()
            self.own(i).wait()
            for cp in self.xy_copies(i, 2) + self.core_copies(i, 1):
                cp.start()

        def three():
            i = t - 2
            for cp in self.xy_landed(i, 2):
                cp.wait_recv()
            for cp in self.xy_copies(i, 3) + self.core_copies(i, 2):
                cp.start()

        def four():
            i = t - 3
            for cp in self.xy_landed(i, 3):
                cp.wait_recv()
            for cp in self.core_copies(i, 3):
                cp.start()

        def five():
            i = t - 4
            for step in (1, 2, 3):
                for cp in self.core_landed(i, step):
                    cp.wait_recv()

        at_piece(t - 4, five)
        at_piece(t - 3, four)
        at_piece(t - 2, three)
        at_piece(t - 1, two)
        at_piece(t, one)

    def finish(self):
        def go(i, _):
            for k in (1, 2, 3):
                self.z_copy(i, k).wait_send()
            for step in (2, 3):
                for cp in self.xy_copies(i, step):
                    cp.wait_send()
            for step in (1, 2, 3):
                for cp in self.core_copies(i, step):
                    cp.wait_send()
            return 0

        lax.fori_loop(0, self.count, go, 0)


def dot(a,b,dn=None):
    if dn is None: return jnp.dot(a,b,preferred_element_type=f32)
    return lax.dot_general(a,b,dn,preferred_element_type=f32)

def lane_half(x, hh):
    lane=lax.broadcasted_iota(jnp.int32, x.shape, 1)
    keep=(lane<64) if hh==0 else (lane>=64)
    return jnp.where(keep, x, jnp.zeros_like(x))

def gelu_pair(u):
    u2=u*u
    t=jnp.tanh(gc*(u+0.044715*u2*u))
    return 0.5*u*(1.0+t), 0.5*(1.0+t)+0.5*u*(1.0-t*t)*gc*(1.0+3.0*0.044715*u2)
def nrm(v):
    c=v-jnp.mean(v,axis=-1,keepdims=True)
    r=lax.rsqrt(jnp.mean(c*c,axis=-1,keepdims=True)+1e-6)
    return c*r,r
def rows_loop(n, R, f):
    def body(i,_):
        f(pl.ds(pl.multiple_of(i*R,R),R)); return 0
    lax.fori_loop(0,n//R,body,0)

def kb_kernel(R, tok, gout, attnT, mod, bias, bup, wall,
      bo_ref, dx1_ref, dat_ref, dw_h, dwout_ref, dmod_ref, db_ref, dbup_ref,
      h2, h2T, dzb, dzT, z, dh2, o_s, wout, wbuf, act, du, dwst, wsem, osem, wosem):
    def co(g): return pltpu.make_async_copy(wall.at[g, :, 768:1024], wout.at[:, g*256:(g+1)*256], wosem.at[g])
    for g in range(4): co(g).start()
    def fetch(j, slot):
        pltpu.make_async_copy(wall.at[4 + j], wbuf.at[slot], wsem.at[slot]).start()
    fetch(0,0)
    shift1=mod[0:1];scale1=mod[1:2];gate1=mod[2:3];shift2=mod[3:4];scale2=mod[4:5];gate2=mod[5:6]
    db_ref[...]=jnp.zeros_like(db_ref); dmod_ref[...]=jnp.zeros_like(dmod_ref)
    for g in range(4): co(g).wait()
    def pre(r):
        o=dot(attnT[:,r],wout[...],TN)+bias[2:3]
        o_s[r,:]=o
        x1=tok[r,:].astype(f32)+gate1*o
        xh,_=nrm(x1)
        h2[r,:]=(xh*(1.0+scale2)+shift2).astype(bf)
        dz=gout[r,:].astype(f32)*gate2
        dzb[r,:]=dz.astype(bf)
        db_ref[3:4]+=jnp.sum(dz,axis=0,keepdims=True)
    rows_loop(S,256,pre)
    for i in range(4):
        r=slice(i*256,(i+1)*256)
        h2T[:,r]=h2[r,:].T
        dzT[:,r]=dzb[r,:].T
    z[...]=jnp.zeros_like(z); dh2[...]=jnp.zeros_like(dh2)
    def chunk(j,_):
        slot=lax.rem(j,2)
        @pl.when(j+1<NJ)
        def _(): fetch(j+1,1-slot)
        pltpu.make_async_copy(wall.at[4 + j], wbuf.at[slot], wsem.at[slot]).wait()
        dbup_ref[j]=jnp.zeros((1,CH),f32)
        def row(r):
            u=dot(h2[r,:],wbuf[slot,:,:CH])+bup[j]
            a,sl=gelu_pair(u)
            ab=a.astype(bf); act[r,:]=ab
            da=dot(dzb[r,:],wbuf[slot,:,CH:])
            d=da*sl
            dbup_ref[j]+=jnp.sum(d,axis=0,keepdims=True)
            db_=d.astype(bf); du[r,:]=db_
            z[r,:]+=dot(ab,wbuf[slot,:,CH:],NT)
            dh2[r,:]+=dot(db_,wbuf[slot,:,:CH],NT)
        rows_loop(S,R,row)
        @pl.when(j>=2)
        def _():
            pltpu.make_async_copy(dwst.at[slot], dw_h.at[j], osem.at[slot]).wait()
        def wrow(r):
            dwst[slot,0,r,:]=dot(h2T[r,:],du[...])
            dwst[slot,1,r,:]=dot(dzT[r,:],act[...])
        rows_loop(D,256,wrow)
        pltpu.make_async_copy(dwst.at[slot], dw_h.at[j], osem.at[slot]).start()
        return 0
    lax.fori_loop(0,NJ,chunk,0)
    for s in range(2): pltpu.make_async_copy(dwst.at[s], dw_h.at[s], osem.at[s]).wait()
    def post(r):
        g=gout[r,:].astype(f32); o=o_s[r,:]
        x1=tok[r,:].astype(f32)+gate1*o
        xh,rstd=nrm(x1)
        zz=z[r,:]+bias[3:4]
        bo_ref[r,:]=(x1+gate2*zz).astype(bf)
        dmod_ref[5:6]+=jnp.sum(g*zz,axis=0,keepdims=True)
        dh=dh2[r,:]
        dmod_ref[3:4]+=jnp.sum(dh,axis=0,keepdims=True)
        dmod_ref[4:5]+=jnp.sum(dh*xh,axis=0,keepdims=True)
        gg=dh*(1.0+scale2)
        dx1=g+rstd*(gg-jnp.mean(gg,axis=-1,keepdims=True)-xh*jnp.mean(gg*xh,axis=-1,keepdims=True))
        dx1_ref[r,:]=dx1
        dmod_ref[2:3]+=jnp.sum(dx1*o,axis=0,keepdims=True)
        do=dx1*gate1
        db_ref[2:3]+=jnp.sum(do,axis=0,keepdims=True)
        dob=do.astype(bf)
        dzb[r,:]=dob
        t=dot(dob,wout[...],NT).astype(bf)
        for g4 in range(4): dat_ref[g4,r,:]=t[:,g4*256:(g4+1)*256]
    rows_loop(S,128,post)
    def wo(r):
        dwout_ref[r,:]=dot(attnT[r,:],dzb[...])
    rows_loop(D,256,wo)

def kb(R,*a):
    V=pl.BlockSpec(memory_space=pltpu.VMEM); A=pl.BlockSpec(memory_space=pl.ANY)
    sd=jax.ShapeDtypeStruct
    return pl.pallas_call(functools.partial(kb_kernel,R),
      out_shape=(sd((S,D),bf),sd((S,D),f32),sd((4,S,256),bf),sd((NJ,2,D,CH),f32),sd((D,D),f32),sd((8,D),f32),sd((8,D),f32),sd((NJ,1,CH),f32)),
      in_specs=[V]*6+[A], out_specs=[V,V,V,A,V,V,V,V],
      scratch_shapes=[pltpu.VMEM((S,D),bf)]*4+[pltpu.VMEM((S,D),f32)]*3+[pltpu.VMEM((D,D),bf),pltpu.VMEM((2,D,2*CH),bf),pltpu.VMEM((S,CH),bf),pltpu.VMEM((S,CH),bf),
         pltpu.VMEM((2,2,D,CH),f32),pltpu.SemaphoreType.DMA((2,)),pltpu.SemaphoreType.DMA((2,)),pltpu.SemaphoreType.DMA((4,))],
      compiler_params=pltpu.CompilerParams(vmem_limit_bytes=62*2**20), name=f"kb{R}")(*a)

def ka_kernel(tok, mod, bqkv, wall, qkv, attnT, lse, h1T, h1, wbuf, wsem):
    c = LOG2E / 8.0

    def cp(g, slot):
        return pltpu.make_async_copy(wall.at[g, :, 0:768], wbuf.at[slot], wsem.at[slot])

    cp(0, 0).start()
    shift1, scale1 = mod[0:1], mod[1:2]

    def ln(r):
        xh, _ = nrm(tok[r, :].astype(f32))
        h1[r, :] = (xh * (1.0 + scale1) + shift1).astype(bf)

    rows_loop(S, 128, ln)
    for i in range(4):
        r = slice(i * 256, (i + 1) * 256)
        h1T[:, r] = h1[r, :].T

    def group(g, _):
        slot = lax.rem(g, 2)
        when(g < 3, lambda: cp(g + 1, 1 - slot).start())
        cp(g, slot).wait()

        def proj(r):
            qkv[g, r, :] = (dot(h1[r, :], wbuf[slot]) + bqkv[g]).astype(bf)

        rows_loop(S, 256, proj)
        for p in range(2):
            kp = qkv[g, :, 256 + p * 128 : 256 + (p + 1) * 128]
            vT = qkv[g, :, 512 + p * 128 : 512 + (p + 1) * 128].T
            q = qkv[g, :, p * 128 : (p + 1) * 128]
            for h in range(2):
                s = dot(lane_half(kp, h), q, NT)
                m = jnp.max(s, axis=0, keepdims=True)
                e = jnp.exp2((s - m) * c)
                l = jnp.sum(e, axis=0, keepdims=True)
                pr = (e * (1.0 / l)).astype(bf)
                o = dot(vT[h * 64 : (h + 1) * 64], pr)
                lse[g, p * 2 + h : p * 2 + h + 1, :] = m * 0.125 + jnp.log(l)
                attnT[pl.ds(pl.multiple_of(g * 256 + (p * 128 + h * 64), 64), 64), :] = o.astype(bf)
        return 0

    lax.fori_loop(0, 4, group, 0)


def ka(*a):
    return pl.pallas_call(
        ka_kernel,
        out_shape=(sd((4, S, 768), bf), sd((D, S), bf), sd((4, 4, S), f32), sd((D, S), bf)),
        in_specs=[V, V, V, A],
        out_specs=[V] * 4,
        scratch_shapes=[pltpu.VMEM((S, D), bf), pltpu.VMEM((2, D, 768), bf), pltpu.SemaphoreType.DMA((2,))],
        compiler_params=pltpu.CompilerParams(vmem_limit_bytes=60 * 2**20),
        name="attention_forward",
    )(*a)


def kc_kernel(QB, tok, mod, qkv, dat, lse, dx1, h1T, w_h, ig, dw_h, dmod, dbq, dqkv, dk_s, dv_s, dqT_s, dh1, wbuf, dwst, wsem, osem):
    c=LOG2E/8.0
    def cp(g,slot): return pltpu.make_async_copy(w_h.at[g, :, 0:768], wbuf.at[slot], wsem.at[slot])
    def co(g,slot): return pltpu.make_async_copy(dwst.at[slot], dw_h.at[g], osem.at[slot])
    cp(0,0).start()
    dh1[...]=jnp.zeros_like(dh1); dmod[...]=jnp.zeros_like(dmod); dbq[...]=jnp.zeros_like(dbq)
    def group(g,_):
        slot=lax.rem(g,2)
        @pl.when(g<3)
        def _(): cp(g+1,1-slot).start()
        for p in range(2):
            sl=slice(p*128,(p+1)*128); slk=slice(256+p*128,256+(p+1)*128); slv=slice(512+p*128,512+(p+1)*128)
            kp=qkv[g,:,slk]; vp=qkv[g,:,slv]
            ks=[lane_half(kp,h) for h in range(2)]; vs=[lane_half(vp,h) for h in range(2)]
            kT=kp.T
            dk_s[...]=jnp.zeros_like(dk_s); dv_s[...]=jnp.zeros_like(dv_s)
            def qblk(i,_):
                r=pl.ds(pl.multiple_of(i*QB,QB),QB)
                q=qkv[g,r,sl]; da=dat[g,r,sl]
                for h in range(2):
                    s=dot(ks[h],q,NT)
                    pT=jnp.exp2(s*c-lse[g,p*2+h:p*2+h+1,r]*LOG2E)
                    dp=dot(vs[h],da,NT)
                    delta=jnp.sum(pT*dp,axis=0,keepdims=True)
                    ds=(pT*(dp-delta)).astype(bf)
                    dv_s[...]+=dot(pT.astype(bf),lane_half(da,h))
                    dk_s[...]+=dot(ds,lane_half(q,h))
                    dqT_s[h*64:(h+1)*64,r]=dot(kT[h*64:(h+1)*64],ds)
                return 0
            lax.fori_loop(0,S//QB,qblk,0)
            dq=dqT_s[...].T*0.125
            dbq[g,:,sl]=jnp.sum(dq,axis=0,keepdims=True)
            dqkv[:,sl]=dq.astype(bf)
            dqkv[:,slk]=(dk_s[...]*0.125).astype(bf)
            dbq[g,:,slv]=jnp.sum(dv_s[...],axis=0,keepdims=True)
            dqkv[:,slv]=dv_s[...].astype(bf)
        cp(g,slot).wait()
        @pl.when(g>=2)
        def _(): co(g,slot).wait()
        def wrow(r):
            dwst[slot,r,:]=dot(h1T[r,:],dqkv[...])
            dh1[r,:]+=dot(dqkv[r,:],wbuf[slot],NT)
        rows_loop(D,256,wrow)
        co(g,slot).start()
        return 0
    lax.fori_loop(0,4,group,0)
    for s_ in range(2): co(s_,s_).wait()
    scale1=mod[1:2]
    def post(r):
        xh,rstd=nrm(tok[r,:].astype(f32))
        dh=dh1[r,:]
        dmod[0:1]+=jnp.sum(dh,axis=0,keepdims=True)
        dmod[1:2]+=jnp.sum(dh*xh,axis=0,keepdims=True)
        gg=dh*(1.0+scale1)
        ig[r,:]=dx1[r,:]+rstd*(gg-jnp.mean(gg,axis=-1,keepdims=True)-xh*jnp.mean(gg*xh,axis=-1,keepdims=True))
    rows_loop(S,128,post)
def kc(QB,*a):
    return pl.pallas_call(functools.partial(kc_kernel,QB),
      out_shape=(sd((S,D),f32),sd((4,D,768),f32),sd((8,D),f32),sd((4,1,768),f32)),
      in_specs=[V]*7+[A], out_specs=[V,A,V,V],
      scratch_shapes=[pltpu.VMEM((S,768),bf),pltpu.VMEM((S,128),f32),pltpu.VMEM((S,128),f32),pltpu.VMEM((128,S),f32),pltpu.VMEM((S,D),f32),
        pltpu.VMEM((2,D,768),bf),pltpu.VMEM((2,D,768),f32),pltpu.SemaphoreType.DMA((2,)),pltpu.SemaphoreType.DMA((2,))],
      compiler_params=pltpu.CompilerParams(vmem_limit_bytes=60*2**20), name=f"kc{QB}")(*a)
def when(cond, f):
    @pl.when(cond)
    def _():
        f()


class Pair:
    def __init__(self, at, own, theirs, send, recv, credit, count):
        self.at, self.own, self.theirs, self.sems, self.credit, self.count = at, own, theirs, (send, recv), credit, count

    def copy(self, i):
        slot = lax.rem(i, 2)
        return remote(self.own.at[slot], self.theirs.at[slot], self.sems[0].at[slot], self.sems[1].at[slot], self.at.to_c)

    def reuse(self, i):
        when(i >= 2, lambda: self.copy(i).wait_send())

    def start(self, i):
        when(i >= 2, lambda: pl.semaphore_wait(self.credit, 1))
        self.copy(i).start()

    def arrived(self, i):
        self.copy(i).wait_recv()

    def free(self, i):
        when(i + 2 < self.count, lambda: mesh_signal(self.credit, self.at.to_c))

    def finish(self):
        for i in (self.count - 2, self.count - 1):
            self.copy(i).wait_send()


class Scatter:
    shapes = [
        pltpu.VMEM((2, 2, 2, 2, 32, 1024), f32),
        pltpu.VMEM((2, 2, 2, 2, 16, 1024), bf),
        pltpu.VMEM((2, 2, 2, 2, 16, 1024), f32),
        pltpu.VMEM((2, 2, 2, 2, 2, 16, 1024), bf),
        pltpu.VMEM((2, 2, 2, 16, 1024), bf),
        pltpu.VMEM((2, 2, 2, 16, 1024), f32),
        pltpu.VMEM((2, 2, 2, 2, 16, 1024), bf),
        pltpu.VMEM((2, 32, 1024), f32),
        pltpu.VMEM((2, 32, 1024), f32),
        pltpu.VMEM((2, 2, 32, 1024), f32),
        pltpu.VMEM((32, 1024), f32),
        pltpu.VMEM((32, 1024), f32),
        pltpu.VMEM((2, 32, 1024), f32),
        pltpu.SemaphoreType.DMA((6,)),
        pltpu.SemaphoreType.DMA((2, 6)),
        pltpu.SemaphoreType.REGULAR((6,)),
    ]

    def __init__(self, at, refs, out, count, gaps=()):
        self.at, self.out, self.count, self.gaps = at, out, count, gaps
        self.acc, self.s2, self.k2, self.r2, self.s3, self.k3, self.r3, self.s4, self.k4, self.r4, self.s5, self.k5, self.r5, self.send, self.recv, self.credit = refs

    def todo(self, stage, slot):
        at = self.at
        if stage == 2:
            return [(0, self.s2.at[0], self.r2.at[slot, 0], at.to_y), (1, self.s2.at[1], self.r2.at[slot, 1], at.to_x)]
        if stage == 3:
            return [(2, self.s3.at[0], self.r3.at[slot, 0], at.to_x), (3, self.s3.at[1], self.r3.at[slot, 1], at.to_y)]
        if stage == 4:
            return [(4, self.s4, self.r4.at[slot], at.to_b)]
        return [(5, self.s5, self.r5.at[slot], at.to_a)]

    def copies(self, stage, i):
        slot = lax.rem(i, 2)
        return [remote(src, dst, self.send.at[q], self.recv.at[slot, q], dev) for q, src, dst, dev in self.todo(stage, slot)]

    def reuse(self, stage, i):
        def go():
            for cp in self.copies(stage, i - 1):
                cp.wait_send()

        when(i >= 1, go)

    def start(self, stage, i):
        def go():
            for q, _, _, _ in self.todo(stage, 0):
                pl.semaphore_wait(self.credit.at[q], 1)

        when(i >= 2, go)
        for cp in self.copies(stage, i):
            cp.start()

    def arrived(self, stage, i):
        for cp in self.copies(stage, i):
            cp.wait_recv()

    def free(self, stage, i):
        def go():
            for q, _, _, dev in self.todo(stage, 0):
                mesh_signal(self.credit.at[q], dev)

        when(i + 2 < self.count, go)

    def two(self, i, acc):
        y, x = self.at.y, self.at.x
        lo, hi = pl.ds(0, 16), pl.ds(16, 16)
        self.reuse(2, i)
        self.s2[0] = acc[:, :, 1 - y, :, lo, :].astype(bf)
        self.s2[1] = acc[:, :, :, 1 - x, hi, :].astype(bf)
        self.start(2, i)
        self.k2[0] = acc[:, :, y, :, lo, :]
        self.k2[1] = acc[:, :, :, x, hi, :]

    def three(self, i):
        y, x = self.at.y, self.at.x
        slot = lax.rem(i, 2)
        self.arrived(2, i)
        self.reuse(3, i)
        self.s3[0] = (self.k2[0, :, :, 1 - x] + self.r2[slot, 0, :, :, 1 - x].astype(f32)).astype(bf)
        self.s3[1] = (self.k2[1, :, :, 1 - y] + self.r2[slot, 1, :, :, 1 - y].astype(f32)).astype(bf)
        self.start(3, i)
        self.k3[0] = self.k2[0, :, :, x] + self.r2[slot, 0, :, :, x].astype(f32)
        self.k3[1] = self.k2[1, :, :, y] + self.r2[slot, 1, :, :, y].astype(f32)
        self.free(2, i)

    def four(self, i):
        b = self.at.b
        slot = lax.rem(i, 2)
        self.arrived(3, i)
        self.reuse(4, i)
        for h in (0, 1):
            rows = slice(16 * h, 16 * h + 16)
            self.s4[:, rows, :] = self.k3[h, :, 1 - b] + self.r3[slot, h, :, 1 - b].astype(f32)
        self.start(4, i)
        for h in (0, 1):
            rows = slice(16 * h, 16 * h + 16)
            self.k4[:, rows, :] = self.k3[h, :, b] + self.r3[slot, h, :, b].astype(f32)
        self.free(3, i)

    def five(self, i):
        a = self.at.a
        slot = lax.rem(i, 2)
        self.arrived(4, i)
        self.reuse(5, i)
        self.s5[...] = self.k4[1 - a] + self.r4[slot, 1 - a]
        self.start(5, i)
        self.k5[...] = self.k4[a] + self.r4[slot, a]
        self.free(4, i)

    def six(self, i):
        slot = lax.rem(i, 2)
        self.arrived(5, i)
        self.out[i] = self.k5[...] + self.r5[slot]
        self.free(5, i)

    def tick(self, t):
        for lag, f in ((4, self.six), (3, self.five), (2, self.four), (1, self.three)):
            u = t - lag
            live = (u >= 0) & (u < self.count + len(self.gaps))
            piece = u
            for gap in self.gaps:
                live = live & (u != gap)
                piece = piece - jnp.where(u > gap, 1, 0)
            when(live, functools.partial(f, piece))

    def finish(self):
        for stage in (2, 3, 4, 5):
            for cp in self.copies(stage, self.count - 1):
                cp.wait_send()


def block_kernel(n, tok, gout, small, bias, ada, mine,
                 bo, ig, gw, dmod, db, dbup, dbq, gat_c, wall, dwh, qkvh, dath,
                 gat_b, part, rec, mod, brow, bqkv, bup, attnT, h1T, lse, dob, dx1, own, theirs, halfS,
                 s0, r0, s1, r1, s2, r2, xs, xr, ps, pr, pc, hc, wsem, qsem, osem, stsem, local, send, recv, *sc):
    c = LOG2E / 8.0
    at = Place()
    me = at.me
    gather = Gather(at, mine, wall, local, send, recv, 12)
    pair = Pair(at, own, theirs, ps, pr, pc, NJ + 4)
    scatter = Scatter(at, sc, gw, 12, gaps=(10, 12))
    gather.start()
    greet_all(n, me)
    gather.tick(0)
    each_peer(n, me, lambda k, to, fr: remote(small, gat_c.at[me], s0.at[k], r0.at[k], to).start())
    each_peer(n, me, lambda k, to, fr: remote(bias, gat_b.at[me], s1.at[k], r1.at[k], to).start())
    gat_c[pl.ds(me, 1)] = small[...].reshape(1, 8, 128)
    gat_b[pl.ds(me, 1)] = bias[...].reshape(1, 7, 1, 128)
    db[...] = jnp.zeros_like(db)
    dmod[...] = jnp.zeros_like(dmod)

    def bias_into(ref, row, start, lead):
        for q in range(lead):
            k = start + q
            ref[row, :, q * 64 : (q + 1) * 64] = gat_b[k // 7, k % 7, :, 0:64]

    def fetch(i, wbuf, slot):
        return pltpu.make_async_copy(wall.at[i], wbuf.at[slot], wsem.at[slot])

    def qkv_out(g, qkv):
        return pltpu.make_async_copy(qkv.at[lax.rem(g, 2)], qkvh.at[g], qsem.at[lax.rem(g, 2)])

    def qkv_in(g, qkv):
        return pltpu.make_async_copy(qkvh.at[g], qkv.at[lax.rem(g, 2)], qsem.at[lax.rem(g, 2)])

    def matrix(wbuf, slot, cols):
        return wbuf[slot, :, :, :, :, :, cols].reshape(D, cols.stop - cols.start)

    lead, tail = pl.ds(0, 2 * D), pl.ds(2 * D, 4 * D)

    def attention(h1, wbuf, qkv):
        def norm_one(r):
            xh, _ = nrm(tok[r, :].astype(f32))
            dx1[r, :] = xh

        rows_loop(S, 128, norm_one)
        each_peer(n, me, lambda k, to, fr: remote(small, gat_c.at[fr], s0.at[k], r0.at[k], to).wait())
        per = 128 // 32
        sel = gat_c[:, pl.ds(me // per, 1), :].reshape(n, 128).astype(bf)
        want = lax.rem(me, per) * 32 + lax.broadcasted_iota(jnp.int32, (128, 32), 1)
        pick = jnp.where(lax.broadcasted_iota(jnp.int32, (128, 32), 0) == want, 1.0, 0.0).astype(bf)
        cond = dot(sel, pick).astype(bf)

        def columns(q):
            cols = slice(q * 512, (q + 1) * 512)
            part[:, :, cols] = dot(cond, ada[:, cols]).reshape(n, 1, 512)

        for q in range(4):
            columns(q)
        each_peer(n, me, lambda k, to, fr: remote(part.at[to, :, lead], rec.at[me, :, lead], s2.at[0, k], r2.at[0, k], to).start())
        gather.tick(1)
        for q in range(4, 12):
            columns(q)
        rec[pl.ds(me, 1)] = part[pl.ds(me, 1)]
        each_peer(n, me, lambda k, to, fr: remote(bias, gat_b.at[fr], s1.at[k], r1.at[k], to).wait())
        for q in range(6):
            bias_into(mod, q, 128 + 16 * q, 16)
        bias_into(brow, 0, 32, 16)
        bias_into(brow, 1, 112, 16)
        for j in range(NJ):
            bias_into(bup, j, 48 + 8 * j, 8)
        for g in range(4):
            bqkv[g] = jnp.zeros((1, 768), f32)
            for q in range(4):
                for first, offset in ((0, 0), (16, 512)):
                    k = first + g * 4 + q
                    bqkv[g, :, offset + q * 64 : offset + (q + 1) * 64] = gat_b[k // 7, k % 7, :, 0:64]
        gather.tick(2)
        each_peer(n, me, lambda k, to, fr: remote(part.at[to, :, lead], rec.at[fr, :, lead], s2.at[0, k], r2.at[0, k], to).wait())
        each_peer(n, me, lambda k, to, fr: remote(part.at[to, :, tail], rec.at[me, :, tail], s2.at[1, k], r2.at[1, k], to).start())
        for q in range(2):
            mod[q] += jnp.sum(rec[:, :, q * D : (q + 1) * D], axis=0)
        shift1, scale1 = mod[0], mod[1]

        def modulate(r):
            h1[r, :] = (dx1[r, :] * (1.0 + scale1) + shift1).astype(bf)

        rows_loop(S, 128, modulate)
        for i in range(4):
            r = slice(i * 256, (i + 1) * 256)
            h1T[:, :, :, r] = h1[r, :].T.reshape(16, 2, 32, 256)
        gather.tick(3)
        gather.tick(4)
        fetch(0, wbuf, 0).start()

        def group(g, _):
            slot = lax.rem(g, 2)
            fetch(g, wbuf, slot).wait()
            when(g >= 2, lambda: qkv_out(g - 2, qkv).wait())
            w = matrix(wbuf, slot, slice(0, 768))

            def proj(r):
                qkv[slot, r, :] = (dot(h1[r, :], w) + bqkv[g]).astype(bf)

            rows_loop(S, 256, proj)
            qkv_out(g, qkv).start()
            for p in range(2):
                kp = qkv[slot, :, 256 + p * 128 : 256 + (p + 1) * 128]
                vT = qkv[slot, :, 512 + p * 128 : 512 + (p + 1) * 128].T
                q = qkv[slot, :, p * 128 : (p + 1) * 128]
                for h in range(2):
                    s = dot(lane_half(kp, h), q, NT)
                    m = jnp.max(s, axis=0, keepdims=True)
                    e = jnp.exp2((s - m) * c)
                    l = jnp.sum(e, axis=0, keepdims=True)
                    pr_ = (e * (1.0 / l)).astype(bf)
                    o = dot(vT[h * 64 : (h + 1) * 64], pr_)
                    lse[g, p * 2 + h : p * 2 + h + 1, :] = m * 0.125 + jnp.log(l)
                    attnT[pl.ds(g * 4 + p * 2 + h, 1)] = o.astype(bf).reshape(1, 2, 32, S)
            gather.tick(5 + g)
            when(g < 3, lambda: fetch(g + 1, wbuf, 1 - slot).start())
            return 0

        lax.fori_loop(0, 4, group, 0)
        for g in (2, 3):
            qkv_out(g, qkv).wait()
        each_peer(n, me, lambda k, to, fr: remote(part.at[to, :, tail], rec.at[fr, :, tail], s2.at[1, k], r2.at[1, k], to).wait())
        for q in range(2, 6):
            mod[q] += jnp.sum(rec[:, :, q * D : (q + 1) * D], axis=0)

    pl.run_scoped(attention, pltpu.VMEM((S, D), bf), pltpu.VMEM((2, 4, 2, 2, 2, 32, 1024), bf), pltpu.VMEM((2, S, 768), bf))

    def unstage(i):
        return pltpu.make_async_copy(dwh.at[i], scatter.acc, stsem.at[1])

    def mlp(h2, hT, dzT, z, wout, wbuf, accw):
        gate1, shift2, scale2, gate2 = mod[2], mod[3], mod[4], mod[5]

        def stage(i):
            return pltpu.make_async_copy(accw, dwh.at[i], stsem.at[0])

        def co(g):
            return pltpu.make_async_copy(wall.at[g, :, :, :, :, :, 768:1024], wout.at[:, :, :, :, :, g * 256 : (g + 1) * 256], osem.at[g])

        for g in range(4):
            co(g).start()
        fetch(4, wbuf, 0).start()
        for g in range(4):
            co(g).wait()

        def branch(r):
            width = r.size
            return dot(attnT[:, :, :, r].reshape(D, width), wout[...].reshape(D, D), TN) + brow[0]

        def pre(r):
            x1 = tok[r, :].astype(f32) + gate1 * branch(r)
            xh, _ = nrm(x1)
            h2[r, :] = (xh * (1.0 + scale2) + shift2).astype(bf)
            dz = gout[r, :].astype(f32) * gate2
            dob[r, :] = dz.astype(bf)
            db[3:4] += jnp.sum(dz, axis=0, keepdims=True)

        rows_loop(S, 256, pre)
        gather.tick(9)
        for i in range(4):
            r = slice(i * 256, (i + 1) * 256)
            hT[:, :, :, r] = h2[r, :].T.reshape(16, 2, 32, 256)
            dzT[:, :, :, r] = dob[r, :].T.reshape(16, 2, 32, 256)
        halves = [
            remote(hT.at[:, 1 - at.c], halfS.at[0], xs.at[0], xr.at[0], at.to_c),
            remote(dzT.at[:, 1 - at.c], halfS.at[1], xs.at[1], xr.at[1], at.to_c),
        ]
        for cp in halves:
            cp.start()
        z[...] = jnp.zeros_like(z)
        dx1[...] = jnp.zeros_like(dx1)

        def chunk(j, _):
            gather.tick(10 + j)

            def forward():
                slot = lax.rem(j, 2)
                when(j + 1 < NJ, lambda: fetch(5 + j, wbuf, 1 - slot).start())
                fetch(4 + j, wbuf, slot).wait()
                pair.reuse(j)
                dbup[j] = jnp.zeros((1, CH), f32)

                def row(r):
                    w_up, w_dn = matrix(wbuf, slot, slice(0, CH)), matrix(wbuf, slot, slice(CH, 2 * CH))
                    u = dot(h2[r, :], w_up) + bup[j]
                    a, sl = gelu_pair(u)
                    ab = a.astype(bf)
                    own[slot, r, CH:] = ab
                    d = dot(dob[r, :], w_dn) * sl
                    dbup[j] += jnp.sum(d, axis=0, keepdims=True)
                    db_ = d.astype(bf)
                    own[slot, r, :CH] = db_
                    z[r, :] += dot(ab, w_dn, NT)
                    dx1[r, :] += dot(db_, w_up, NT)

                rows_loop(S, 512, row)
                pair.start(j)

            when(j < NJ, forward)
            scatter.tick(j - 4)

            def begin():
                unstage(j - 4).wait()
                scatter.two(j - 4, scatter.acc)

            when(j >= 4, begin)
            when(j >= 3, lambda: unstage(j - 3).start())

            def weights():
                i = j - 1
                slot = lax.rem(i, 2)
                when(j == 1, lambda: [cp.wait_recv() for cp in halves])
                pair.arrived(i)
                when(i >= 1, lambda: stage(i - 1).wait())
                for q, lhs in enumerate((hT, dzT)):
                    cols = slice(q * CH, (q + 1) * CH)
                    t = dot(lhs[:, at.c].reshape(512, S), own[slot, :, cols]) + dot(halfS[q].reshape(512, S), theirs[slot, :, cols])
                    accw[:, :, :, :, :, cols] = t.reshape(2, 2, 2, 2, 32, CH)
                pair.free(i)
                stage(i).start()

            when(j >= 1, weights)
            return 0

        lax.fori_loop(0, NJ + 1, chunk, 0)
        mesh_signal(hc, at.to_c)
        stage(NJ - 1).wait()
        for cp in halves:
            cp.wait_send()

        def post(r):
            g = gout[r, :].astype(f32)
            o = branch(r)
            x1 = tok[r, :].astype(f32) + gate1 * o
            xh, rstd = nrm(x1)
            zz = z[r, :] + brow[1]
            h2[r, :] = (x1 + gate2 * zz).astype(bf)
            dmod[5:6] += jnp.sum(g * zz, axis=0, keepdims=True)
            dh = dx1[r, :]
            dmod[3:4] += jnp.sum(dh, axis=0, keepdims=True)
            dmod[4:5] += jnp.sum(dh * xh, axis=0, keepdims=True)
            gg = dh * (1.0 + scale2)
            dx = g + rstd * (gg - jnp.mean(gg, axis=-1, keepdims=True) - xh * jnp.mean(gg * xh, axis=-1, keepdims=True))
            dx1[r, :] = dx
            dmod[2:3] += jnp.sum(dx * o, axis=0, keepdims=True)
            do = dx * gate1
            db[2:3] += jnp.sum(do, axis=0, keepdims=True)
            dob_ = do.astype(bf)
            dob[r, :] = dob_
            own[0, r, :] = dot(dob_, wout[...].reshape(D, D), NT).astype(bf)

        pair.reuse(NJ)

        def post_half(h):
            def body(i, _):
                post(pl.ds(pl.multiple_of(h * 512 + i * 128, 128), 128))
                return 0

            lax.fori_loop(0, 4, body, 0)

        post_half(0)
        post_half(1)
        outs = [pltpu.make_async_copy(h2, bo, osem.at[0])]
        outs += [pltpu.make_async_copy(own.at[0, :, g * 256 : (g + 1) * 256], dath.at[g], osem.at[1 + g]) for g in range(4)]
        for cp in outs:
            cp.start()
        for cp in outs:
            cp.wait()

    pl.run_scoped(
        mlp,
        pltpu.VMEM((S, D), bf),
        pltpu.VMEM((16, 2, 32, S), bf),
        pltpu.VMEM((16, 2, 32, S), bf),
        pltpu.VMEM((S, D), f32),
        pltpu.VMEM((4, 2, 2, 2, 32, 1024), bf),
        pltpu.VMEM((2, 4, 2, 2, 2, 32, 1024), bf),
        pltpu.VMEM((2, 2, 2, 2, 32, 1024), f32),
    )

    def back(dh1, wbuf, qkv, dat, dk_s, dv_s, dqT_s, accw):
        def dat_in(g):
            return pltpu.make_async_copy(dath.at[g], dat.at[lax.rem(g, 2)], osem.at[lax.rem(g, 2)])

        def load(g):
            qkv_in(g, qkv).start()
            dat_in(g).start()
            fetch(g, wbuf, lax.rem(g, 2)).start()

        load(0)
        pl.semaphore_wait(hc, 1)
        halves = [
            remote(h1T.at[:, 1 - at.c], halfS.at[0], xs.at[2], xr.at[2], at.to_c),
            remote(attnT.at[:, 1 - at.c], halfS.at[1], xs.at[3], xr.at[3], at.to_c),
        ]
        for cp in halves:
            cp.start()
        scatter.tick(5)
        unstage(5).wait()
        scatter.two(5, scatter.acc)
        unstage(6).start()
        dh1[...] = jnp.zeros_like(dh1)

        def group(g, _):
            slot = lax.rem(g, 2)
            when(g < 3, lambda: load(g + 1))
            qkv_in(g, qkv).wait()
            dat_in(g).wait()
            when(g >= 1, lambda: pair.reuse(NJ + g))
            own[slot, :, 768:] = dob[:, pl.ds(pl.multiple_of(g * 256, 256), 256)]
            for p in range(2):
                if p == 1:
                    scatter.tick(6 + 2 * g)

                    def staged_six():
                        unstage(6).wait()
                        scatter.two(6, scatter.acc)
                        unstage(7).start()

                    when(g == 0, staged_six)
                    when(g == 1, lambda: scatter.two(8, accw))
                sl = slice(p * 128, (p + 1) * 128)
                slk = slice(256 + p * 128, 256 + (p + 1) * 128)
                slv = slice(512 + p * 128, 512 + (p + 1) * 128)
                kp, vp, q, da = qkv[slot, :, slk], qkv[slot, :, slv], qkv[slot, :, sl], dat[slot, :, sl]
                kT = kp.T
                for h in range(2):
                    s = dot(lane_half(kp, h), q, NT)
                    pT = jnp.exp2(s * c - lse[g, p * 2 + h : p * 2 + h + 1, :] * LOG2E)
                    dp = dot(lane_half(vp, h), da, NT)
                    delta = jnp.sum(pT * dp, axis=0, keepdims=True)
                    ds = (pT * (dp - delta)).astype(bf)
                    dv = dot(pT.astype(bf), lane_half(da, h))
                    dk = dot(ds, lane_half(q, h))
                    if h == 0:
                        dv_s[...] = dv
                        dk_s[...] = dk
                    else:
                        dv_s[...] += dv
                        dk_s[...] += dk
                    dqT_s[h * 64 : (h + 1) * 64, :] = dot(kT[h * 64 : (h + 1) * 64], ds)
                dq = dqT_s[...].T * 0.125
                dbq[g, :, sl] = jnp.sum(dq, axis=0, keepdims=True)
                own[slot, :, sl] = dq.astype(bf)
                own[slot, :, slk] = (dk_s[...] * 0.125).astype(bf)
                dbq[g, :, slk] = jnp.zeros((1, 128), f32)
                dbq[g, :, slv] = jnp.sum(dv_s[...], axis=0, keepdims=True)
                own[slot, :, slv] = dv_s[...].astype(bf)
            pair.start(NJ + g)
            fetch(g, wbuf, slot).wait()
            w = matrix(wbuf, slot, slice(0, 768))

            def wrow(r):
                dh1[r, :] += dot(own[slot, r, :768], w, NT)

            rows_loop(D, 256, wrow)
            scatter.tick(7 + 2 * g)

            def staged_seven():
                unstage(7).wait()
                scatter.two(7, scatter.acc)
                for cp in halves:
                    cp.wait_recv()

            when(g == 0, staged_seven)
            pair.arrived(NJ + g)
            for q, lhs in enumerate((h1T, attnT)):
                cols = slice(0, 768) if q == 0 else slice(768, 1024)
                t = dot(lhs[:, at.c].reshape(512, S), own[slot, :, cols]) + dot(halfS[q].reshape(512, S), theirs[slot, :, cols])
                accw[:, :, :, :, :, cols] = t.reshape(2, 2, 2, 2, 32, cols.stop - cols.start)
            pair.free(NJ + g)
            when(g >= 1, lambda: scatter.two(8 + g, accw))
            return 0

        lax.fori_loop(0, 4, group, 0)
        pair.finish()
        for cp in halves:
            cp.wait_send()
        scale1 = mod[1]

        def post(r):
            xh, rstd = nrm(tok[r, :].astype(f32))
            dh = dh1[r, :]
            dmod[0:1] += jnp.sum(dh, axis=0, keepdims=True)
            dmod[1:2] += jnp.sum(dh * xh, axis=0, keepdims=True)
            gg = dh * (1.0 + scale1)
            dx1[r, :] += rstd * (gg - jnp.mean(gg, axis=-1, keepdims=True) - xh * jnp.mean(gg * xh, axis=-1, keepdims=True))

        rows_loop(S, 128, post)

    pl.run_scoped(
        back,
        pltpu.VMEM((S, D), f32),
        pltpu.VMEM((2, 4, 2, 2, 2, 32, 1024), bf),
        pltpu.VMEM((2, S, 768), bf),
        pltpu.VMEM((2, S, 256), bf),
        pltpu.VMEM((S, 128), f32),
        pltpu.VMEM((S, 128), f32),
        pltpu.VMEM((128, S), f32),
        pltpu.VMEM((2, 2, 2, 2, 32, 1024), f32),
    )
    done = pltpu.make_async_copy(dx1, ig, osem.at[0])
    done.start()
    for t in (14, 15, 16, 17):
        scatter.tick(t)
    done.wait()
    scatter.finish()
    gather.finish()


def block(n, *a):
    dma = pltpu.SemaphoreType.DMA
    vm = pltpu.VMEM
    return pl.pallas_call(
        functools.partial(block_kernel, n),
        out_shape=(sd((S, D), bf), sd((S, D), f32), sd((12, 32, 1024), f32), sd((8, D), f32), sd((8, D), f32), sd((NJ, 1, CH), f32), sd((4, 1, 768), f32), sd((n, 8, 128), f32))
        + (sd((12, 4, 2, 2, 2, 32, 1024), bf), sd((NJ, 2, 2, 2, 2, 32, 1024), f32), sd((4, S, 768), bf), sd((4, S, 256), bf)),
        in_specs=[V] * 6,
        out_specs=[A] * 2 + [V] * 6 + [A] * 4,
        scratch_shapes=[vm((n, 7, 1, 128), f32), vm((n, 1, 6 * D), f32), vm((n, 1, 6 * D), f32), vm((6, 1, D), f32), vm((2, 1, D), f32), vm((4, 1, 768), f32), vm((NJ, 1, CH), f32)]
        + [vm((16, 2, 32, S), bf), vm((16, 2, 32, S), bf), vm((4, 4, S), f32), vm((S, D), bf), vm((S, D), f32)]
        + [vm((2, S, 1024), bf), vm((2, S, 1024), bf), vm((2, 16, 32, S), bf)]
        + [dma((n,))] * 4
        + [dma((2, n))] * 2
        + [dma((4,)), dma((4,)), dma((2,)), dma((2,)), pltpu.SemaphoreType.REGULAR, pltpu.SemaphoreType.REGULAR]
        + [dma((2,)), dma((2,)), dma((5,)), dma((2,))]
        + gather_sems(12)
        + Scatter.shapes,
        compiler_params=pltpu.CompilerParams(collective_id=0, has_side_effects=True, vmem_limit_bytes=VMEM_BYTES),
        name="block",
    )(*a)


def adam_step(param, grad, first, second, decay):
    new_first = beta_first * first + (1.0 - beta_first) * grad
    new_second = beta_second * second + (1.0 - beta_second) * grad * grad
    step_size = learn_rate / (1.0 - beta_first**STEP)
    denom = jnp.sqrt(new_second / (1.0 - beta_second**STEP)) + adam_eps
    new_param = param - step_size * new_first / denom - learn_rate * decay * param
    return (new_param, new_first, new_second)


def on_device(n, block_in, condition, out_grad, weights, biases, first_moment, second_moment, bias_first, bias_second):
    me = lax.axis_index("dp")
    rows = D // n
    chips = n == 32
    wb = weights.astype(bf)
    qkvo = wb[:, : 4 * D].reshape(rows, 4, 4, 256).transpose(2, 0, 1, 3).reshape(4, rows, 1024)
    updn = wb[:, 4 * D : 4 * D + 2 * FF].reshape(rows, 2, NJ, CH).transpose(2, 0, 1, 3).reshape(NJ, rows, 1024)
    mine = jnp.concatenate([qkvo, updn], axis=0)
    ada_l = wb[:, 4 * D + 2 * FF :]
    cond_act = jax.nn.silu(condition).astype(bf)
    tok = block_in[0]
    gout = out_grad[0]
    if chips:
        small = cond_act.astype(f32).reshape(8, 128)
        own_bias = jnp.pad(lax.reduce_precision(biases, 8, 7).reshape(7, 1, 64), ((0, 0), (0, 0), (0, 64)))
        bo, ig, gw, dmod, db, db_up, db_qkv, gat = block(n, tok, gout, small, own_bias, ada_l, mine)[:8]
        cond_all = gat.reshape(n, D).astype(bf)
        cond_cols = lax.dynamic_slice_in_dim(cond_all, me * rows, rows, 1)
        g_mlp = gw[:NJ].reshape(NJ, rows, 2, CH).transpose(1, 2, 0, 3).reshape(rows, 2 * FF)
        g_qkvo = gw[NJ:].reshape(4, rows, 4, 256).transpose(1, 2, 0, 3).reshape(rows, 4 * D)
        dmod = dmod[:6].reshape(1, 6 * D)
    else:
        bias_full = lax.all_gather(biases.astype(bf), "dp", axis=0, tiled=True).astype(f32)
        cond_all = lax.all_gather(cond_act, "dp", axis=0, tiled=True)
        cond_cols = lax.dynamic_slice_in_dim(cond_all, me * rows, rows, 1)
        mod = lax.psum_scatter(jnp.dot(cond_cols, ada_l, preferred_element_type=f32), "dp", scatter_dimension=0, tiled=True)
        mod = jnp.concatenate([(mod[0] + bias_full[4 * D + FF :]).reshape(6, D), jnp.zeros((2, D), f32)], axis=0)
        zrow = jnp.zeros((D,), f32)
        bqkv = jnp.stack([bias_full[:D], zrow, bias_full[D : 2 * D]]).reshape(3, 4, 256).transpose(1, 0, 2).reshape(4, 1, 768)
        brows = jnp.stack([zrow, zrow, bias_full[2 * D : 3 * D], bias_full[3 * D + FF : 4 * D + FF], zrow, zrow, zrow, zrow])
        bup = bias_full[3 * D : 3 * D + FF].reshape(NJ, 1, CH)
        wall = lax.all_gather(mine, "dp", axis=1, tiled=True)
        qkv, attn_t, lse, h1t = ka(tok, mod, bqkv, wall)
        bo, dx1, dat, dw_mlp, dw_out, dmod_b, db, db_up = kb(512, tok, gout, attn_t, mod, brows, bup, wall)
        ig, dw_qkv, dmod_a, db_qkv = kc(1024, tok, mod, qkv, dat, lse, dx1, h1t, wall)
        g_mlp = lax.psum_scatter(dw_mlp, "dp", scatter_dimension=2, tiled=True)
        g_out = lax.psum_scatter(dw_out, "dp", scatter_dimension=0, tiled=True)
        g_qkv = lax.psum_scatter(dw_qkv, "dp", scatter_dimension=1, tiled=True)
        g_qkv = g_qkv.reshape(4, rows, 3, 256).transpose(1, 2, 0, 3).reshape(rows, 3 * D)
        g_qkvo = jnp.concatenate([g_qkv, g_out], axis=1)
        g_mlp = g_mlp.transpose(2, 1, 0, 3).reshape(rows, 2 * FF)
        dmod = (dmod_a + dmod_b)[:6].reshape(1, 6 * D)
    db_qkv = db_qkv.reshape(4, 3, 256).transpose(1, 0, 2).reshape(3, D)
    bias_row = jnp.concatenate([db_qkv[0], db_qkv[2], db[2], db_up.reshape(FF), db[3], dmod[0]])
    dmod_bf = dmod.astype(bf)
    if chips:
        own = biases.shape[0]
        blocks = jnp.pad(bias_row.reshape(n, own), ((0, 0), (0, 1024 - own))).reshape(n, 8, 128)
        bias_grad, dmod_all = last(n, blocks, dmod_bf.reshape(48, 128))
        bias_grad = bias_grad.reshape(-1)[:own]
        dmod_all = dmod_all.reshape(n, 6 * D)
    else:
        bias_grad = lax.psum_scatter(bias_row, "dp", scatter_dimension=0, tiled=True)
        dmod_all = lax.all_gather(dmod_bf, "dp", axis=0, tiled=True)
    g_ada = lax.dot_general(cond_cols, dmod_all, TN, preferred_element_type=f32)
    cond_part = lax.dot_general(dmod_all, ada_l, NT, preferred_element_type=f32)
    if chips:
        cond_grad = swap(n, jnp.pad(cond_part, ((0, 0), (0, 128 - rows))).reshape(n, 1, 128))[:, 0, :rows].reshape(1, D)
    else:
        cond_grad = lax.all_to_all(cond_part, "dp", split_axis=0, concat_axis=1, tiled=True)
    sigma = jax.nn.sigmoid(condition)
    cond_grad = cond_grad * (sigma * (1.0 + condition * (1.0 - sigma)))
    weight_grad = jnp.concatenate([g_qkvo, g_mlp, g_ada], axis=1)
    new_weights, new_first, new_second = adam_step(weights, weight_grad, first_moment, second_moment, weight_decay)
    new_biases, new_bias_first, new_bias_second = adam_step(biases, bias_grad, bias_first, bias_second, 0.0)
    return (bo[None], ig[None], cond_grad, weight_grad, bias_grad, new_weights, new_biases, new_first, new_second, new_bias_first, new_bias_second)


def solution(mesh):
    three, two, one = P("dp", None, None), P("dp", None), P("dp")
    return jax.shard_map(
        functools.partial(on_device, mesh.shape["dp"]),
        mesh=mesh,
        in_specs=(three, two, three, two, one, two, two, one, one),
        out_specs=(three, three, two, two, one, two, one, two, two, one, one),
        check_vma=False,
    )
```

```python
import functools

import jax
import jax.numpy as jnp
from jax import lax
from jax.experimental import pallas as pl
from jax.experimental.pallas import tpu as pltpu
from jax.sharding import PartitionSpec as P

D = 1024
FF = 4096
S = 1024
STEP = 3
CH = 512
NJ = FF // CH
VMEM_BYTES = 63 * 2**20
learn_rate = 0.01
beta_first = 0.9
beta_second = 0.95
adam_eps = 1e-08
weight_decay = 0.05
gc = 0.7978845608028654
LOG2E = 1.4426950408889634
f32 = jnp.float32
bf = jnp.bfloat16
NT = (((1,), (1,)), ((), ()))
TN = (((0,), (0,)), ((), ()))
V = pl.BlockSpec(memory_space=pltpu.VMEM)
A = pl.BlockSpec(memory_space=pl.ANY)
sd = jax.ShapeDtypeStruct
MESH = pl.DeviceIdType.MESH


def mesh_signal(sem, dev):
    pl.semaphore_signal(sem, inc=1, device_id=(dev,), device_id_type=MESH)


def remote(src, dst, send, recv, dev):
    return pltpu.make_async_remote_copy(src_ref=src, dst_ref=dst, send_sem=send, recv_sem=recv, device_id=(dev,), device_id_type=MESH)


def greet_all(n, me, between):
    barrier = pltpu.get_barrier_semaphore()

    def go(k, _):
        mesh_signal(barrier, lax.rem(me + k, n))
        return 0

    lax.fori_loop(1, n, go, 0)
    between()
    pl.semaphore_wait(barrier, n - 1)


def each_peer(n, me, f):
    def go(k, _):
        f(k, lax.rem(me + k, n), lax.rem(me + n - k, n))
        return 0

    lax.fori_loop(1, n, go, 0)


def gather_sems(count):
    return [pltpu.SemaphoreType.DMA((count,)), pltpu.SemaphoreType.DMA((count, 12)), pltpu.SemaphoreType.DMA((count, 12))]


class Place:
    def __init__(self):
        me = lax.axis_index("dp")
        self.me = me
        self.z = me // 8
        self.y = lax.rem(me // 4, 2)
        self.x = lax.rem(me // 2, 2)
        self.c = lax.rem(me, 2)
        self.to_c = me + 1 - 2 * self.c
        self.to_x = me + 2 - 4 * self.x
        self.to_y = me + 4 - 8 * self.y
        self.a = self.z // 2
        self.b = lax.rem(self.z, 2)
        self.to_b = me + 8 - 16 * self.b
        self.to_a = me + 16 - 32 * self.a

    def to_z(self, k):
        return lax.rem(self.z + k, 4) * 8 + lax.rem(self.me, 8)


class Gather:
    def __init__(self, at, src, buf, local, send, recv, count):
        self.at, self.src, self.buf, self.local, self.send, self.recv, self.count = at, src, buf, local, send, recv, count

    def step_refs(self, i, step, c):
        at, b = self.at, self.buf.at[i]
        y, x = at.y, at.x
        lo, hi = pl.ds(0, 16), pl.ds(16, 16)
        if step == 1:
            return [b.at[:, y, x, c]]
        if step == 2:
            return [b.at[:, y, 1 - x, c, lo], b.at[:, 1 - y, x, c, hi]]
        return [b.at[:, 1 - y, :, c, lo], b.at[:, :, 1 - x, c, hi]]

    def z_copy(self, i, k):
        at = self.at
        return remote(self.src.at[i], self.buf.at[i, at.z, at.y, at.x, at.c], self.send.at[i, k - 1], self.recv.at[i, k - 1], at.to_z(k))

    def z_landed(self, i, k):
        at = self.at
        zz = lax.rem(at.z + 4 - k, 4)
        return remote(self.src.at[i], self.buf.at[i, zz, at.y, at.x, at.c], self.send.at[i, k - 1], self.recv.at[i, k - 1], at.to_z(k))

    def own(self, i):
        at = self.at
        return pltpu.make_async_copy(self.src.at[i], self.buf.at[i, at.z, at.y, at.x, at.c], self.local.at[i])

    def xy_copies(self, i, step):
        at, b = self.at, self.buf.at[i]
        y, x, c = at.y, at.x, at.c
        lo, hi = pl.ds(0, 16), pl.ds(16, 16)
        if step == 2:
            a, d = b.at[:, y, x, c, lo], b.at[:, y, x, c, hi]
            return [
                remote(a, a, self.send.at[i, 3], self.recv.at[i, 3], at.to_x),
                remote(d, d, self.send.at[i, 4], self.recv.at[i, 4], at.to_y),
            ]
        a, d = b.at[:, y, :, c, lo], b.at[:, :, x, c, hi]
        return [
            remote(a, a, self.send.at[i, 5], self.recv.at[i, 5], at.to_y),
            remote(d, d, self.send.at[i, 6], self.recv.at[i, 6], at.to_x),
        ]

    def xy_landed(self, i, step):
        at, b = self.at, self.buf.at[i]
        refs = self.step_refs(i, step, at.c)
        base = 3 if step == 2 else 5
        return [remote(r, r, self.send.at[i, base + q], self.recv.at[i, base + q], at.to_x) for q, r in enumerate(refs)]

    def core_copies(self, i, step):
        at = self.at
        base = {1: 7, 2: 8, 3: 10}[step]
        return [remote(r, r, self.send.at[i, base + q], self.recv.at[i, base + q], at.to_c) for q, r in enumerate(self.step_refs(i, step, at.c))]

    def core_landed(self, i, step):
        at = self.at
        base = {1: 7, 2: 8, 3: 10}[step]
        return [remote(r, r, self.send.at[i, base + q], self.recv.at[i, base + q], at.to_c) for q, r in enumerate(self.step_refs(i, step, 1 - at.c))]

    def start(self, first, last):
        def go(i, _):
            self.own(i).start()
            return 0

        lax.fori_loop(first, last, go, 0)

    def tick(self, t):
        def at_piece(i, f):
            when((i >= 0) & (i < self.count), f)

        def one():
            for k in (1, 2, 3):
                self.z_copy(t, k).start()

        def two():
            i = t - 1
            for k in (1, 2, 3):
                self.z_landed(i, k).wait_recv()
            self.own(i).wait()
            for cp in self.xy_copies(i, 2) + self.core_copies(i, 1):
                cp.start()

        def three():
            i = t - 2
            for cp in self.xy_landed(i, 2):
                cp.wait_recv()
            for cp in self.xy_copies(i, 3) + self.core_copies(i, 2):
                cp.start()

        def four():
            i = t - 3
            for cp in self.xy_landed(i, 3):
                cp.wait_recv()
            for cp in self.core_copies(i, 3):
                cp.start()

        def five():
            i = t - 4
            for step in (1, 2, 3):
                for cp in self.core_landed(i, step):
                    cp.wait_recv()

        at_piece(t - 4, five)
        at_piece(t - 3, four)
        at_piece(t - 2, three)
        at_piece(t - 1, two)
        at_piece(t, one)

    def finish(self):
        def go(i, _):
            for k in (1, 2, 3):
                self.z_copy(i, k).wait_send()
            for step in (2, 3):
                for cp in self.xy_copies(i, step):
                    cp.wait_send()
            for step in (1, 2, 3):
                for cp in self.core_copies(i, step):
                    cp.wait_send()
            return 0

        lax.fori_loop(0, self.count, go, 0)


def dot(a,b,dn=None):
    if dn is None: return jnp.dot(a,b,preferred_element_type=f32)
    return lax.dot_general(a,b,dn,preferred_element_type=f32)

def lane_half(x, hh):
    lane=lax.broadcasted_iota(jnp.int32, x.shape, 1)
    keep=(lane<64) if hh==0 else (lane>=64)
    return jnp.where(keep, x, jnp.zeros_like(x))

def gelu_pair(u):
    u2=u*u
    t=jnp.tanh(gc*(u+0.044715*u2*u))
    return 0.5*u*(1.0+t), 0.5*(1.0+t)+0.5*u*(1.0-t*t)*gc*(1.0+3.0*0.044715*u2)
def nrm(v):
    c=v-jnp.mean(v,axis=-1,keepdims=True)
    r=lax.rsqrt(jnp.mean(c*c,axis=-1,keepdims=True)+1e-6)
    return c*r,r
def rows_loop(n, R, f):
    def body(i,_):
        f(pl.ds(pl.multiple_of(i*R,R),R)); return 0
    lax.fori_loop(0,n//R,body,0)

def kb_kernel(R, tok, gout, attnT, mod, bias, bup, wall,
      bo_ref, dx1_ref, dat_ref, dw_h, dwout_ref, dmod_ref, db_ref, dbup_ref,
      h2, h2T, dzb, dzT, z, dh2, o_s, wout, wbuf, act, du, dwst, wsem, osem, wosem):
    def co(g): return pltpu.make_async_copy(wall.at[g, :, 768:1024], wout.at[:, g*256:(g+1)*256], wosem.at[g])
    for g in range(4): co(g).start()
    def fetch(j, slot):
        pltpu.make_async_copy(wall.at[4 + j], wbuf.at[slot], wsem.at[slot]).start()
    fetch(0,0)
    shift1=mod[0:1];scale1=mod[1:2];gate1=mod[2:3];shift2=mod[3:4];scale2=mod[4:5];gate2=mod[5:6]
    db_ref[...]=jnp.zeros_like(db_ref); dmod_ref[...]=jnp.zeros_like(dmod_ref)
    for g in range(4): co(g).wait()
    def pre(r):
        o=dot(attnT[:,r],wout[...],TN)+bias[2:3]
        o_s[r,:]=o
        x1=tok[r,:].astype(f32)+gate1*o
        xh,_=nrm(x1)
        h2[r,:]=(xh*(1.0+scale2)+shift2).astype(bf)
        dz=gout[r,:].astype(f32)*gate2
        dzb[r,:]=dz.astype(bf)
        db_ref[3:4]+=jnp.sum(dz,axis=0,keepdims=True)
    rows_loop(S,256,pre)
    for i in range(4):
        r=slice(i*256,(i+1)*256)
        h2T[:,r]=h2[r,:].T
        dzT[:,r]=dzb[r,:].T
    z[...]=jnp.zeros_like(z); dh2[...]=jnp.zeros_like(dh2)
    def chunk(j,_):
        slot=lax.rem(j,2)
        @pl.when(j+1<NJ)
        def _(): fetch(j+1,1-slot)
        pltpu.make_async_copy(wall.at[4 + j], wbuf.at[slot], wsem.at[slot]).wait()
        dbup_ref[j]=jnp.zeros((1,CH),f32)
        def row(r):
            u=dot(h2[r,:],wbuf[slot,:,:CH])+bup[j]
            a,sl=gelu_pair(u)
            ab=a.astype(bf); act[r,:]=ab
            da=dot(dzb[r,:],wbuf[slot,:,CH:])
            d=da*sl
            dbup_ref[j]+=jnp.sum(d,axis=0,keepdims=True)
            db_=d.astype(bf); du[r,:]=db_
            z[r,:]+=dot(ab,wbuf[slot,:,CH:],NT)
            dh2[r,:]+=dot(db_,wbuf[slot,:,:CH],NT)
        rows_loop(S,R,row)
        @pl.when(j>=2)
        def _():
            pltpu.make_async_copy(dwst.at[slot], dw_h.at[j], osem.at[slot]).wait()
        def wrow(r):
            dwst[slot,0,r,:]=dot(h2T[r,:],du[...])
            dwst[slot,1,r,:]=dot(dzT[r,:],act[...])
        rows_loop(D,256,wrow)
        pltpu.make_async_copy(dwst.at[slot], dw_h.at[j], osem.at[slot]).start()
        return 0
    lax.fori_loop(0,NJ,chunk,0)
    for s in range(2): pltpu.make_async_copy(dwst.at[s], dw_h.at[s], osem.at[s]).wait()
    def post(r):
        g=gout[r,:].astype(f32); o=o_s[r,:]
        x1=tok[r,:].astype(f32)+gate1*o
        xh,rstd=nrm(x1)
        zz=z[r,:]+bias[3:4]
        bo_ref[r,:]=(x1+gate2*zz).astype(bf)
        dmod_ref[5:6]+=jnp.sum(g*zz,axis=0,keepdims=True)
        dh=dh2[r,:]
        dmod_ref[3:4]+=jnp.sum(dh,axis=0,keepdims=True)
        dmod_ref[4:5]+=jnp.sum(dh*xh,axis=0,keepdims=True)
        gg=dh*(1.0+scale2)
        dx1=g+rstd*(gg-jnp.mean(gg,axis=-1,keepdims=True)-xh*jnp.mean(gg*xh,axis=-1,keepdims=True))
        dx1_ref[r,:]=dx1
        dmod_ref[2:3]+=jnp.sum(dx1*o,axis=0,keepdims=True)
        do=dx1*gate1
        db_ref[2:3]+=jnp.sum(do,axis=0,keepdims=True)
        dob=do.astype(bf)
        dzb[r,:]=dob
        t=dot(dob,wout[...],NT).astype(bf)
        for g4 in range(4): dat_ref[g4,r,:]=t[:,g4*256:(g4+1)*256]
    rows_loop(S,128,post)
    def wo(r):
        dwout_ref[r,:]=dot(attnT[r,:],dzb[...])
    rows_loop(D,256,wo)

def kb(R,*a):
    V=pl.BlockSpec(memory_space=pltpu.VMEM); A=pl.BlockSpec(memory_space=pl.ANY)
    sd=jax.ShapeDtypeStruct
    return pl.pallas_call(functools.partial(kb_kernel,R),
      out_shape=(sd((S,D),bf),sd((S,D),f32),sd((4,S,256),bf),sd((NJ,2,D,CH),f32),sd((D,D),f32),sd((8,D),f32),sd((8,D),f32),sd((NJ,1,CH),f32)),
      in_specs=[V]*6+[A], out_specs=[V,V,V,A,V,V,V,V],
      scratch_shapes=[pltpu.VMEM((S,D),bf)]*4+[pltpu.VMEM((S,D),f32)]*3+[pltpu.VMEM((D,D),bf),pltpu.VMEM((2,D,2*CH),bf),pltpu.VMEM((S,CH),bf),pltpu.VMEM((S,CH),bf),
         pltpu.VMEM((2,2,D,CH),f32),pltpu.SemaphoreType.DMA((2,)),pltpu.SemaphoreType.DMA((2,)),pltpu.SemaphoreType.DMA((4,))],
      compiler_params=pltpu.CompilerParams(vmem_limit_bytes=62*2**20), name=f"kb{R}")(*a)

def ka_kernel(tok, mod, bqkv, wall, qkv, attnT, lse, h1T, h1, wbuf, wsem):
    c = LOG2E / 8.0

    def cp(g, slot):
        return pltpu.make_async_copy(wall.at[g, :, 0:768], wbuf.at[slot], wsem.at[slot])

    cp(0, 0).start()
    shift1, scale1 = mod[0:1], mod[1:2]

    def ln(r):
        xh, _ = nrm(tok[r, :].astype(f32))
        h1[r, :] = (xh * (1.0 + scale1) + shift1).astype(bf)

    rows_loop(S, 128, ln)
    for i in range(4):
        r = slice(i * 256, (i + 1) * 256)
        h1T[:, r] = h1[r, :].T

    def group(g, _):
        slot = lax.rem(g, 2)
        when(g < 3, lambda: cp(g + 1, 1 - slot).start())
        cp(g, slot).wait()

        def proj(r):
            qkv[g, r, :] = (dot(h1[r, :], wbuf[slot]) + bqkv[g]).astype(bf)

        rows_loop(S, 256, proj)
        for p in range(2):
            kp = qkv[g, :, 256 + p * 128 : 256 + (p + 1) * 128]
            vT = qkv[g, :, 512 + p * 128 : 512 + (p + 1) * 128].T
            q = qkv[g, :, p * 128 : (p + 1) * 128]
            for h in range(2):
                s = dot(lane_half(kp, h), q, NT)
                m = jnp.max(s, axis=0, keepdims=True)
                e = jnp.exp2((s - m) * c)
                l = jnp.sum(e, axis=0, keepdims=True)
                pr = (e * (1.0 / l)).astype(bf)
                o = dot(vT[h * 64 : (h + 1) * 64], pr)
                lse[g, p * 2 + h : p * 2 + h + 1, :] = m * 0.125 + jnp.log(l)
                attnT[pl.ds(pl.multiple_of(g * 256 + (p * 128 + h * 64), 64), 64), :] = o.astype(bf)
        return 0

    lax.fori_loop(0, 4, group, 0)


def ka(*a):
    return pl.pallas_call(
        ka_kernel,
        out_shape=(sd((4, S, 768), bf), sd((D, S), bf), sd((4, 4, S), f32), sd((D, S), bf)),
        in_specs=[V, V, V, A],
        out_specs=[V] * 4,
        scratch_shapes=[pltpu.VMEM((S, D), bf), pltpu.VMEM((2, D, 768), bf), pltpu.SemaphoreType.DMA((2,))],
        compiler_params=pltpu.CompilerParams(vmem_limit_bytes=60 * 2**20),
        name="attention_forward",
    )(*a)


def kc_kernel(QB, tok, mod, qkv, dat, lse, dx1, h1T, w_h, ig, dw_h, dmod, dbq, dqkv, dk_s, dv_s, dqT_s, dh1, wbuf, dwst, wsem, osem):
    c=LOG2E/8.0
    def cp(g,slot): return pltpu.make_async_copy(w_h.at[g, :, 0:768], wbuf.at[slot], wsem.at[slot])
    def co(g,slot): return pltpu.make_async_copy(dwst.at[slot], dw_h.at[g], osem.at[slot])
    cp(0,0).start()
    dh1[...]=jnp.zeros_like(dh1); dmod[...]=jnp.zeros_like(dmod); dbq[...]=jnp.zeros_like(dbq)
    def group(g,_):
        slot=lax.rem(g,2)
        @pl.when(g<3)
        def _(): cp(g+1,1-slot).start()
        for p in range(2):
            sl=slice(p*128,(p+1)*128); slk=slice(256+p*128,256+(p+1)*128); slv=slice(512+p*128,512+(p+1)*128)
            kp=qkv[g,:,slk]; vp=qkv[g,:,slv]
            ks=[lane_half(kp,h) for h in range(2)]; vs=[lane_half(vp,h) for h in range(2)]
            kT=kp.T
            dk_s[...]=jnp.zeros_like(dk_s); dv_s[...]=jnp.zeros_like(dv_s)
            def qblk(i,_):
                r=pl.ds(pl.multiple_of(i*QB,QB),QB)
                q=qkv[g,r,sl]; da=dat[g,r,sl]
                for h in range(2):
                    s=dot(ks[h],q,NT)
                    pT=jnp.exp2(s*c-lse[g,p*2+h:p*2+h+1,r]*LOG2E)
                    dp=dot(vs[h],da,NT)
                    delta=jnp.sum(pT*dp,axis=0,keepdims=True)
                    ds=(pT*(dp-delta)).astype(bf)
                    dv_s[...]+=dot(pT.astype(bf),lane_half(da,h))
                    dk_s[...]+=dot(ds,lane_half(q,h))
                    dqT_s[h*64:(h+1)*64,r]=dot(kT[h*64:(h+1)*64],ds)
                return 0
            lax.fori_loop(0,S//QB,qblk,0)
            dq=dqT_s[...].T*0.125
            dbq[g,:,sl]=jnp.sum(dq,axis=0,keepdims=True)
            dqkv[:,sl]=dq.astype(bf)
            dqkv[:,slk]=(dk_s[...]*0.125).astype(bf)
            dbq[g,:,slv]=jnp.sum(dv_s[...],axis=0,keepdims=True)
            dqkv[:,slv]=dv_s[...].astype(bf)
        cp(g,slot).wait()
        @pl.when(g>=2)
        def _(): co(g,slot).wait()
        def wrow(r):
            dwst[slot,r,:]=dot(h1T[r,:],dqkv[...])
            dh1[r,:]+=dot(dqkv[r,:],wbuf[slot],NT)
        rows_loop(D,256,wrow)
        co(g,slot).start()
        return 0
    lax.fori_loop(0,4,group,0)
    for s_ in range(2): co(s_,s_).wait()
    scale1=mod[1:2]
    def post(r):
        xh,rstd=nrm(tok[r,:].astype(f32))
        dh=dh1[r,:]
        dmod[0:1]+=jnp.sum(dh,axis=0,keepdims=True)
        dmod[1:2]+=jnp.sum(dh*xh,axis=0,keepdims=True)
        gg=dh*(1.0+scale1)
        ig[r,:]=dx1[r,:]+rstd*(gg-jnp.mean(gg,axis=-1,keepdims=True)-xh*jnp.mean(gg*xh,axis=-1,keepdims=True))
    rows_loop(S,128,post)
def kc(QB,*a):
    return pl.pallas_call(functools.partial(kc_kernel,QB),
      out_shape=(sd((S,D),f32),sd((4,D,768),f32),sd((8,D),f32),sd((4,1,768),f32)),
      in_specs=[V]*7+[A], out_specs=[V,A,V,V],
      scratch_shapes=[pltpu.VMEM((S,768),bf),pltpu.VMEM((S,128),f32),pltpu.VMEM((S,128),f32),pltpu.VMEM((128,S),f32),pltpu.VMEM((S,D),f32),
        pltpu.VMEM((2,D,768),bf),pltpu.VMEM((2,D,768),f32),pltpu.SemaphoreType.DMA((2,)),pltpu.SemaphoreType.DMA((2,))],
      compiler_params=pltpu.CompilerParams(vmem_limit_bytes=60*2**20), name=f"kc{QB}")(*a)
def when(cond, f):
    @pl.when(cond)
    def _():
        f()


class Pair:
    def __init__(self, at, own, theirs, send, recv, credit, count):
        self.at, self.own, self.theirs, self.sems, self.credit, self.count = at, own, theirs, (send, recv), credit, count

    def copy(self, i, part, cols):
        slot = lax.rem(i, 2)
        return remote(self.own.at[slot, :, cols], self.theirs.at[slot, :, cols], self.sems[0].at[slot, part], self.sems[1].at[slot, part], self.at.to_c)

    def start(self, i, part, cols):
        if part == 0:
            when(i >= 2, lambda: pl.semaphore_wait(self.credit, 1))
        self.copy(i, part, cols).start()

    def sent(self, i, parts):
        for part, cols in enumerate(parts):
            self.copy(i, part, cols).wait_send()

    def arrived(self, i, parts):
        for part, cols in enumerate(parts):
            self.copy(i, part, cols).wait_recv()

    def free(self, i):
        when(i + 2 < self.count, lambda: mesh_signal(self.credit, self.at.to_c))


WHOLE = (slice(0, 1024),)
PARTS = (slice(768, 1024), slice(0, 384), slice(384, 768))


class Scatter:
    shapes = [
        pltpu.VMEM((2, 2, 2, 2, 32, 1024), f32),
        pltpu.VMEM((2, 2, 2, 2, 16, 1024), bf),
        pltpu.VMEM((2, 2, 2, 2, 16, 1024), f32),
        pltpu.VMEM((2, 2, 2, 2, 2, 16, 1024), bf),
        pltpu.VMEM((2, 2, 2, 16, 1024), bf),
        pltpu.VMEM((2, 2, 2, 16, 1024), f32),
        pltpu.VMEM((2, 2, 2, 2, 16, 1024), bf),
        pltpu.VMEM((2, 32, 1024), f32),
        pltpu.VMEM((2, 32, 1024), f32),
        pltpu.VMEM((2, 2, 32, 1024), f32),
        pltpu.VMEM((32, 1024), f32),
        pltpu.VMEM((32, 1024), f32),
        pltpu.VMEM((2, 32, 1024), f32),
        pltpu.SemaphoreType.DMA((6,)),
        pltpu.SemaphoreType.DMA((2, 6)),
        pltpu.SemaphoreType.REGULAR((6,)),
    ]

    def __init__(self, at, refs, out, count, gaps=()):
        self.at, self.out, self.count, self.gaps = at, out, count, gaps
        self.acc, self.s2, self.k2, self.r2, self.s3, self.k3, self.r3, self.s4, self.k4, self.r4, self.s5, self.k5, self.r5, self.send, self.recv, self.credit = refs

    def todo(self, stage, slot):
        at = self.at
        if stage == 2:
            return [(0, self.s2.at[0], self.r2.at[slot, 0], at.to_y), (1, self.s2.at[1], self.r2.at[slot, 1], at.to_x)]
        if stage == 3:
            return [(2, self.s3.at[0], self.r3.at[slot, 0], at.to_x), (3, self.s3.at[1], self.r3.at[slot, 1], at.to_y)]
        if stage == 4:
            return [(4, self.s4, self.r4.at[slot], at.to_b)]
        return [(5, self.s5, self.r5.at[slot], at.to_a)]

    def copies(self, stage, i):
        slot = lax.rem(i, 2)
        return [remote(src, dst, self.send.at[q], self.recv.at[slot, q], dev) for q, src, dst, dev in self.todo(stage, slot)]

    def reuse(self, stage, i):
        def go():
            for cp in self.copies(stage, i - 1):
                cp.wait_send()

        when(i >= 1, go)

    def start(self, stage, i):
        def go():
            for q, _, _, _ in self.todo(stage, 0):
                pl.semaphore_wait(self.credit.at[q], 1)

        when(i >= 2, go)
        for cp in self.copies(stage, i):
            cp.start()

    def arrived(self, stage, i):
        for cp in self.copies(stage, i):
            cp.wait_recv()

    def free(self, stage, i):
        def go():
            for q, _, _, dev in self.todo(stage, 0):
                mesh_signal(self.credit.at[q], dev)

        when(i + 2 < self.count, go)

    def two(self, i, acc):
        y, x = self.at.y, self.at.x
        lo, hi = pl.ds(0, 16), pl.ds(16, 16)
        self.reuse(2, i)
        self.s2[0] = acc[:, :, 1 - y, :, lo, :].astype(bf)
        self.s2[1] = acc[:, :, :, 1 - x, hi, :].astype(bf)
        self.start(2, i)
        self.k2[0] = acc[:, :, y, :, lo, :]
        self.k2[1] = acc[:, :, :, x, hi, :]

    def three(self, i):
        y, x = self.at.y, self.at.x
        slot = lax.rem(i, 2)
        self.arrived(2, i)
        self.reuse(3, i)
        self.s3[0] = (self.k2[0, :, :, 1 - x] + self.r2[slot, 0, :, :, 1 - x].astype(f32)).astype(bf)
        self.s3[1] = (self.k2[1, :, :, 1 - y] + self.r2[slot, 1, :, :, 1 - y].astype(f32)).astype(bf)
        self.start(3, i)
        self.k3[0] = self.k2[0, :, :, x] + self.r2[slot, 0, :, :, x].astype(f32)
        self.k3[1] = self.k2[1, :, :, y] + self.r2[slot, 1, :, :, y].astype(f32)
        self.free(2, i)

    def four(self, i):
        b = self.at.b
        slot = lax.rem(i, 2)
        self.arrived(3, i)
        self.reuse(4, i)
        for h in (0, 1):
            rows = slice(16 * h, 16 * h + 16)
            self.s4[:, rows, :] = self.k3[h, :, 1 - b] + self.r3[slot, h, :, 1 - b].astype(f32)
        self.start(4, i)
        for h in (0, 1):
            rows = slice(16 * h, 16 * h + 16)
            self.k4[:, rows, :] = self.k3[h, :, b] + self.r3[slot, h, :, b].astype(f32)
        self.free(3, i)

    def five(self, i):
        a = self.at.a
        slot = lax.rem(i, 2)
        self.arrived(4, i)
        self.reuse(5, i)
        self.s5[...] = self.k4[1 - a] + self.r4[slot, 1 - a]
        self.start(5, i)
        self.k5[...] = self.k4[a] + self.r4[slot, a]
        self.free(4, i)

    def six(self, i):
        slot = lax.rem(i, 2)
        self.arrived(5, i)
        t = self.k5[...] + self.r5[slot]

        def spread(start, src, width):
            self.out[:, pl.ds(pl.multiple_of(start, 128), width)] = t[:, src : src + width]

        def feed_forward():
            spread(4 * D + i * CH, 0, CH)
            spread(4 * D + FF + i * CH, CH, CH)

        def attention():
            g = i - NJ
            for p in range(2):
                for q in range(3):
                    spread(q * D + g * 256 + p * 128, p * 384 + q * 128, 128)
            spread(3 * D + g * 256, 768, 256)

        when(i < NJ, feed_forward)
        when(i >= NJ, attention)
        self.free(5, i)

    def tick(self, t):
        for lag, f in ((4, self.six), (3, self.five), (2, self.four), (1, self.three)):
            u = t - lag
            live = (u >= 0) & (u < self.count + len(self.gaps))
            piece = u
            for gap in self.gaps:
                live = live & (u != gap)
                piece = piece - jnp.where(u > gap, 1, 0)
            when(live, functools.partial(f, piece))

    def finish(self):
        for stage in (2, 3, 4, 5):
            for cp in self.copies(stage, self.count - 1):
                cp.wait_send()


def block_kernel(n, tok, gout, small, weights,
                 bo, ig, gw, bsum, crec, wall, dwh, qkvh, dath,
                 mine, ada, gat, condc, part, rec, dsrc, dall, esrc, erec, csrc, mod, brow, bqkv, bup, dmod, db, dbup, dbq,
                 attnT, h1T, lse, dob, dx1, own, theirs, halfS,
                 s0, r0, s2, r2, s3, r3, s4, r4, s5, r5, xs, xr, ps, pr, pc, hc, wsem, qsem, osem, stsem, local, send, recv, *sc):
    c = LOG2E / 8.0
    at = Place()
    me = at.me
    gather = Gather(at, mine, wall, local, send, recv, 12)
    pair = Pair(at, own, theirs, ps, pr, pc, NJ + 4)
    scatter = Scatter(at, sc, gw, 12, gaps=(11,))

    def cut(shard):
        load = pltpu.make_async_copy(weights, shard, osem.at[0])
        load.start()
        load.wait()
        for g in range(4):
            for p in range(2):
                for q in range(3):
                    a = q * D + g * 256 + p * 128
                    b = p * 384 + q * 128
                    mine[g, :, b : b + 128] = shard[:, a : a + 128].astype(bf)
            mine[g, :, 768:] = shard[:, 3 * D + g * 256 : 3 * D + (g + 1) * 256].astype(bf)
        gather.start(0, 4)
        for j in range(NJ):
            for q in range(2):
                a = 4 * D + q * FF + j * CH
                mine[4 + j, :, q * CH : (q + 1) * CH] = shard[:, a : a + CH].astype(bf)
        gather.start(4, 12)
        for q in range(6):
            a = 4 * D + 2 * FF + q * D
            ada[:, q * D : (q + 1) * D] = shard[:, a : a + D].astype(bf)

    greet_all(n, me, lambda: pl.run_scoped(cut, pltpu.VMEM((32, 18 * D), f32)))
    gather.tick(0)
    each_peer(n, me, lambda k, to, fr: remote(small, gat.at[me], s0.at[k], r0.at[k], to).start())
    gat[pl.ds(me, 1)] = small[...].reshape(1, 16, 128)
    db[...] = jnp.zeros_like(db)
    dmod[...] = jnp.zeros_like(dmod)

    def bias_into(ref, row, start, lead):
        for q in range(lead):
            k = start + q
            ref[row, :, q * 64 : (q + 1) * 64] = gat[k // 7, 8 + k % 7 : 9 + k % 7, 0:64]

    def fetch(i, wbuf, slot):
        return pltpu.make_async_copy(wall.at[i], wbuf.at[slot], wsem.at[slot])

    def bias_from(k, piece):
        esrc[k // 7, :, 2 * D + (k % 7) * 64 : 2 * D + (k % 7 + 1) * 64] = piece

    def ada_columns(x, q):
        cols = slice(q * 512, (q + 1) * 512)
        gw[:, 4 * D + 2 * FF + q * 512 : 4 * D + 2 * FF + (q + 1) * 512] = dot(condc[...], x, TN)
        return dot(x, ada[:, cols], NT)

    def qkv_out(g, qkv):
        return pltpu.make_async_copy(qkv.at[lax.rem(g, 2)], qkvh.at[g], qsem.at[lax.rem(g, 2)])

    def qkv_in(g, qkv):
        return pltpu.make_async_copy(qkvh.at[g], qkv.at[lax.rem(g, 2)], qsem.at[lax.rem(g, 2)])

    def matrix(wbuf, slot, cols):
        return wbuf[slot, :, :, :, :, :, cols].reshape(D, cols.stop - cols.start)

    lead, tail = pl.ds(0, 2 * D), pl.ds(2 * D, 4 * D)

    def attention(h1, wbuf, qkv):
        def norm_one(r):
            xh, _ = nrm(tok[r, :].astype(f32))
            dx1[r, :] = xh

        rows_loop(S, 128, norm_one)
        each_peer(n, me, lambda k, to, fr: remote(small, gat.at[fr], s0.at[k], r0.at[k], to).wait())
        per = 128 // 32
        sel = gat[:, pl.ds(me // per, 1), :].reshape(n, 128).astype(bf)
        want = lax.rem(me, per) * 32 + lax.broadcasted_iota(jnp.int32, (128, 32), 1)
        pick = jnp.where(lax.broadcasted_iota(jnp.int32, (128, 32), 0) == want, 1.0, 0.0).astype(bf)
        cond = dot(sel, pick).astype(bf)
        condc[...] = cond

        def columns(q):
            cols = slice(q * 512, (q + 1) * 512)
            part[:, :, cols] = dot(cond, ada[:, cols]).reshape(n, 1, 512)

        for q in range(4):
            columns(q)
        each_peer(n, me, lambda k, to, fr: remote(part.at[to, :, lead], rec.at[me, :, lead], s2.at[0, k], r2.at[0, k], to).start())
        gather.tick(1)
        for q in range(4, 12):
            columns(q)
        rec[pl.ds(me, 1)] = part[pl.ds(me, 1)]
        for q in range(6):
            bias_into(mod, q, 128 + 16 * q, 16)
        bias_into(brow, 0, 32, 16)
        bias_into(brow, 1, 112, 16)
        for j in range(NJ):
            bias_into(bup, j, 48 + 8 * j, 8)
        for g in range(4):
            bqkv[g] = jnp.zeros((1, 768), f32)
            for q in range(4):
                for first, offset in ((0, 0), (16, 256)):
                    k = first + g * 4 + q
                    to = (q // 2) * 384 + offset + (q % 2) * 64
                    bqkv[g, :, to : to + 64] = gat[k // 7, 8 + k % 7 : 9 + k % 7, 0:64]
        gather.tick(2)
        each_peer(n, me, lambda k, to, fr: remote(part.at[to, :, lead], rec.at[fr, :, lead], s2.at[0, k], r2.at[0, k], to).wait())
        each_peer(n, me, lambda k, to, fr: remote(part.at[to, :, tail], rec.at[me, :, tail], s2.at[1, k], r2.at[1, k], to).start())
        for q in range(2):
            mod[q] += jnp.sum(rec[:, :, q * D : (q + 1) * D], axis=0)
        shift1, scale1 = mod[0], mod[1]

        def modulate(r):
            h1[r, :] = (dx1[r, :] * (1.0 + scale1) + shift1).astype(bf)

        rows_loop(S, 128, modulate)
        for i in range(4):
            r = slice(i * 256, (i + 1) * 256)
            h1T[:, :, :, r] = h1[r, :].T.reshape(16, 2, 32, 256)
        gather.tick(3)
        gather.tick(4)
        fetch(0, wbuf, 0).start()

        def group(g, _):
            slot = lax.rem(g, 2)
            fetch(g, wbuf, slot).wait()
            when(g >= 2, lambda: qkv_out(g - 2, qkv).wait())
            w = matrix(wbuf, slot, slice(0, 768))

            def proj(r):
                qkv[slot, r, :] = (dot(h1[r, :], w) + bqkv[g]).astype(bf)

            rows_loop(S, 256, proj)
            qkv_out(g, qkv).start()
            for p in range(2):
                kp = qkv[slot, :, p * 384 + 128 : p * 384 + 256]
                vT = qkv[slot, :, p * 384 + 256 : p * 384 + 384].T
                q = qkv[slot, :, p * 384 : p * 384 + 128]
                for h in range(2):
                    s = dot(lane_half(kp, h), q, NT)
                    m = jnp.max(s, axis=0, keepdims=True)
                    e = jnp.exp2((s - m) * c)
                    l = jnp.sum(e, axis=0, keepdims=True)
                    pr_ = (e * (1.0 / l)).astype(bf)
                    o = dot(vT[h * 64 : (h + 1) * 64], pr_)
                    lse[g, p * 2 + h : p * 2 + h + 1, :] = m * 0.125 + jnp.log(l)
                    attnT[pl.ds(g * 4 + p * 2 + h, 1)] = o.astype(bf).reshape(1, 2, 32, S)
            gather.tick(5 + g)
            when(g < 3, lambda: fetch(g + 1, wbuf, 1 - slot).start())
            return 0

        lax.fori_loop(0, 4, group, 0)
        for g in (2, 3):
            qkv_out(g, qkv).wait()
        each_peer(n, me, lambda k, to, fr: remote(part.at[to, :, tail], rec.at[fr, :, tail], s2.at[1, k], r2.at[1, k], to).wait())
        for q in range(2, 6):
            mod[q] += jnp.sum(rec[:, :, q * D : (q + 1) * D], axis=0)

    pl.run_scoped(attention, pltpu.VMEM((S, D), bf), pltpu.VMEM((2, 4, 2, 2, 2, 32, 1024), bf), pltpu.VMEM((2, S, 768), bf))

    def unstage(i):
        return pltpu.make_async_copy(dwh.at[i], scatter.acc, stsem.at[1])

    def staged(i):
        unstage(i).wait()
        scatter.two(i, scatter.acc)
        when(i + 1 < NJ, lambda: unstage(i + 1).start())

    def mlp(h2, hT, dzT, z, wout, wbuf, accw):
        gate1, shift2, scale2, gate2 = mod[2], mod[3], mod[4], mod[5]

        def stage(i):
            return pltpu.make_async_copy(accw, dwh.at[i], stsem.at[0])

        def co(g):
            return pltpu.make_async_copy(wall.at[g, :, :, :, :, :, 768:1024], wout.at[:, :, :, :, :, g * 256 : (g + 1) * 256], osem.at[g])

        for g in range(4):
            co(g).start()
        fetch(4, wbuf, 0).start()
        for g in range(4):
            co(g).wait()

        def branch(r):
            width = r.size
            return dot(attnT[:, :, :, r].reshape(D, width), wout[...].reshape(D, D), TN) + brow[0]

        def pre(r):
            x1 = tok[r, :].astype(f32) + gate1 * branch(r)
            xh, _ = nrm(x1)
            h2[r, :] = (xh * (1.0 + scale2) + shift2).astype(bf)
            dz = gout[r, :].astype(f32) * gate2
            dob[r, :] = dz.astype(bf)
            db[1] += jnp.sum(dz, axis=0, keepdims=True)

        rows_loop(S, 256, pre)
        gather.tick(9)
        for i in range(4):
            r = slice(i * 256, (i + 1) * 256)
            hT[:, :, :, r] = h2[r, :].T.reshape(16, 2, 32, 256)
            dzT[:, :, :, r] = dob[r, :].T.reshape(16, 2, 32, 256)
        halves = [
            remote(hT.at[:, 1 - at.c], halfS.at[0], xs.at[0], xr.at[0], at.to_c),
            remote(dzT.at[:, 1 - at.c], halfS.at[1], xs.at[1], xr.at[1], at.to_c),
        ]
        for cp in halves:
            cp.start()
        z[...] = jnp.zeros_like(z)
        dx1[...] = jnp.zeros_like(dx1)

        def chunk(j, _):
            gather.tick(10 + j)

            def forward():
                slot = lax.rem(j, 2)
                when(j + 1 < NJ, lambda: fetch(5 + j, wbuf, 1 - slot).start())
                fetch(4 + j, wbuf, slot).wait()
                when(j >= 2, lambda: pair.sent(j - 2, WHOLE))
                dbup[j] = jnp.zeros((1, CH), f32)

                def row(r):
                    w_up, w_dn = matrix(wbuf, slot, slice(0, CH)), matrix(wbuf, slot, slice(CH, 2 * CH))
                    u = dot(h2[r, :], w_up) + bup[j]
                    a, sl = gelu_pair(u)
                    ab = a.astype(bf)
                    own[slot, r, CH:] = ab
                    d = dot(dob[r, :], w_dn) * sl
                    dbup[j] += jnp.sum(d, axis=0, keepdims=True)
                    db_ = d.astype(bf)
                    own[slot, r, :CH] = db_
                    z[r, :] += dot(ab, w_dn, NT)
                    dx1[r, :] += dot(db_, w_up, NT)

                rows_loop(S, 512, row)
                pair.start(j, 0, WHOLE[0])

            when(j < NJ, forward)
            scatter.tick(j - 6)
            when(j >= 6, lambda: staged(j - 6))
            when(j == 5, lambda: unstage(0).start())

            def weights():
                i = j - 1
                slot = lax.rem(i, 2)
                when(j == 1, lambda: [cp.wait_recv() for cp in halves])
                pair.arrived(i, WHOLE)
                when(i >= 1, lambda: stage(i - 1).wait())
                for q, lhs in enumerate((hT, dzT)):
                    cols = slice(q * CH, (q + 1) * CH)
                    t = dot(lhs[:, at.c].reshape(512, S), own[slot, :, cols]) + dot(halfS[q].reshape(512, S), theirs[slot, :, cols])
                    accw[:, :, :, :, :, cols] = t.reshape(2, 2, 2, 2, 32, CH)
                pair.free(i)
                stage(i).start()

            when(j >= 1, weights)
            return 0

        lax.fori_loop(0, NJ + 1, chunk, 0)
        mesh_signal(hc, at.to_c)
        stage(NJ - 1).wait()
        for cp in halves:
            cp.wait_send()

        def post(r):
            g = gout[r, :].astype(f32)
            o = branch(r)
            x1 = tok[r, :].astype(f32) + gate1 * o
            xh, rstd = nrm(x1)
            zz = z[r, :] + brow[1]
            h2[r, :] = (x1 + gate2 * zz).astype(bf)
            dmod[5] += jnp.sum(g * zz, axis=0, keepdims=True)
            dh = dx1[r, :]
            dmod[3] += jnp.sum(dh, axis=0, keepdims=True)
            dmod[4] += jnp.sum(dh * xh, axis=0, keepdims=True)
            gg = dh * (1.0 + scale2)
            dx = g + rstd * (gg - jnp.mean(gg, axis=-1, keepdims=True) - xh * jnp.mean(gg * xh, axis=-1, keepdims=True))
            dx1[r, :] = dx
            dmod[2] += jnp.sum(dx * o, axis=0, keepdims=True)
            do = dx * gate1
            db[0] += jnp.sum(do, axis=0, keepdims=True)
            dob_ = do.astype(bf)
            dob[r, :] = dob_
            own[0, r, :] = dot(dob_, wout[...].reshape(D, D), NT).astype(bf)

        pair.sent(NJ - 2, WHOLE)

        def post_half(h):
            def body(i, _):
                post(pl.ds(pl.multiple_of(h * 512 + i * 128, 128), 128))
                return 0

            lax.fori_loop(0, 4, body, 0)

        post_half(0)
        scatter.tick(3)
        staged(3)
        post_half(1)
        outs = [pltpu.make_async_copy(h2, bo, osem.at[0])]
        outs += [pltpu.make_async_copy(own.at[0, :, g * 256 : (g + 1) * 256], dath.at[g], osem.at[1 + g]) for g in range(4)]
        for cp in outs:
            cp.start()
        for cp in outs:
            cp.wait()

    pl.run_scoped(
        mlp,
        pltpu.VMEM((S, D), bf),
        pltpu.VMEM((16, 2, 32, S), bf),
        pltpu.VMEM((16, 2, 32, S), bf),
        pltpu.VMEM((S, D), f32),
        pltpu.VMEM((4, 2, 2, 2, 32, 1024), bf),
        pltpu.VMEM((2, 4, 2, 2, 2, 32, 1024), bf),
        pltpu.VMEM((2, 2, 2, 2, 32, 1024), f32),
    )

    def back(dh1, wbuf, qkv, dat, dk_s, dv_s, dqT_s, accw):
        def dat_in(g):
            return pltpu.make_async_copy(dath.at[g], dat.at[lax.rem(g, 2)], osem.at[lax.rem(g, 2)])

        def load(g):
            qkv_in(g, qkv).start()
            dat_in(g).start()
            fetch(g, wbuf, lax.rem(g, 2)).start()

        load(0)
        pl.semaphore_wait(hc, 1)
        halves = [
            remote(h1T.at[:, 1 - at.c], halfS.at[0], xs.at[2], xr.at[2], at.to_c),
            remote(attnT.at[:, 1 - at.c], halfS.at[1], xs.at[3], xr.at[3], at.to_c),
        ]
        for cp in halves:
            cp.start()
        scatter.tick(4)
        staged(4)
        for q in range(4):
            dsrc[:, q * D : (q + 1) * D] = dmod[2 + q]
        each_peer(n, me, lambda k, to, fr: remote(dsrc, dall.at[me, :, tail], s3.at[k], r3.at[k], to).start())
        dall[pl.ds(me, 1), :, 2 * D : 6 * D] = dsrc[...].reshape(1, 1, 4 * D)
        for q in range(16):
            bias_from(32 + q, db[0, :, q * 64 : (q + 1) * 64])
            bias_from(112 + q, db[1, :, q * 64 : (q + 1) * 64])
        for j in range(NJ):
            for q in range(8):
                bias_from(48 + 8 * j + q, dbup[j, :, q * 64 : (q + 1) * 64])
        for k in range(2, 6):
            for q in range(16):
                bias_from(128 + 16 * k + q, dmod[k, :, q * 64 : (q + 1) * 64])
        dh1[...] = jnp.zeros_like(dh1)

        def group(g, _):
            slot = lax.rem(g, 2)
            when(g < 3, lambda: load(g + 1))
            qkv_in(g, qkv).wait()
            dat_in(g).wait()
            when(g == 1, lambda: pair.sent(NJ - 1, WHOLE))
            when(g >= 2, lambda: pair.sent(NJ + g - 2, PARTS))
            own[slot, :, 768:] = dob[:, pl.ds(pl.multiple_of(g * 256, 256), 256)]
            pair.start(NJ + g, 0, PARTS[0])
            for p in range(2):
                if p == 1:
                    scatter.tick(5 + 2 * g)
                    when(g < 2, lambda: staged(5 + 2 * g))
                    when(g == 2, lambda: scatter.two(9, accw))
                sl = slice(p * 128, (p + 1) * 128)
                slq, slk, slv = (slice(p * 384 + q * 128, p * 384 + (q + 1) * 128) for q in range(3))
                kp, vp, q, da = qkv[slot, :, slk], qkv[slot, :, slv], qkv[slot, :, slq], dat[slot, :, sl]
                kT = kp.T
                for h in range(2):
                    s = dot(lane_half(kp, h), q, NT)
                    pT = jnp.exp2(s * c - lse[g, p * 2 + h : p * 2 + h + 1, :] * LOG2E)
                    dp = dot(lane_half(vp, h), da, NT)
                    delta = jnp.sum(pT * dp, axis=0, keepdims=True)
                    ds = (pT * (dp - delta)).astype(bf)
                    dv = dot(pT.astype(bf), lane_half(da, h))
                    dk = dot(ds, lane_half(q, h))
                    if h == 0:
                        dv_s[...] = dv
                        dk_s[...] = dk
                    else:
                        dv_s[...] += dv
                        dk_s[...] += dk
                    dqT_s[h * 64 : (h + 1) * 64, :] = dot(kT[h * 64 : (h + 1) * 64], ds)
                dq = dqT_s[...].T * 0.125
                dbq[g, :, sl] = jnp.sum(dq, axis=0, keepdims=True)
                own[slot, :, slq] = dq.astype(bf)
                own[slot, :, slk] = (dk_s[...] * 0.125).astype(bf)
                dbq[g, :, 256 + p * 128 : 256 + (p + 1) * 128] = jnp.sum(dv_s[...], axis=0, keepdims=True)
                own[slot, :, slv] = dv_s[...].astype(bf)
                pair.start(NJ + g, 1 + p, PARTS[1 + p])
            fetch(g, wbuf, slot).wait()
            w = matrix(wbuf, slot, slice(0, 768))

            def wrow(r):
                dh1[r, :] += dot(own[slot, r, :768], w, NT)

            rows_loop(D, 256, wrow)
            scatter.tick(6 + 2 * g)

            def at_first():
                staged(6)
                for cp in halves:
                    cp.wait_recv()

            when(g == 0, at_first)
            when(g == 1, lambda: scatter.two(8, accw))
            pair.arrived(NJ + g, PARTS)
            for q, lhs in enumerate((h1T, attnT)):
                cols = slice(0, 768) if q == 0 else slice(768, 1024)
                t = dot(lhs[:, at.c].reshape(512, S), own[slot, :, cols]) + dot(halfS[q].reshape(512, S), theirs[slot, :, cols])
                accw[:, :, :, :, :, cols] = t.reshape(2, 2, 2, 2, 32, cols.stop - cols.start)
            pair.free(NJ + g)
            when(g >= 2, lambda: scatter.two(8 + g, accw))
            return 0

        lax.fori_loop(0, 4, group, 0)
        for i in (2, 3):
            pair.sent(NJ + i, PARTS)
        for cp in halves:
            cp.wait_send()
        scale1 = mod[1]

        def post(r):
            xh, rstd = nrm(tok[r, :].astype(f32))
            dh = dh1[r, :]
            dmod[0] += jnp.sum(dh, axis=0, keepdims=True)
            dmod[1] += jnp.sum(dh * xh, axis=0, keepdims=True)
            gg = dh * (1.0 + scale1)
            dx1[r, :] += rstd * (gg - jnp.mean(gg, axis=-1, keepdims=True) - xh * jnp.mean(gg * xh, axis=-1, keepdims=True))

        rows_loop(S, 128, post)

    pl.run_scoped(
        back,
        pltpu.VMEM((S, D), f32),
        pltpu.VMEM((2, 4, 2, 2, 2, 32, 1024), bf),
        pltpu.VMEM((2, S, 768), bf),
        pltpu.VMEM((2, S, 256), bf),
        pltpu.VMEM((S, 128), f32),
        pltpu.VMEM((S, 128), f32),
        pltpu.VMEM((128, S), f32),
        pltpu.VMEM((2, 2, 2, 2, 32, 1024), f32),
    )
    done = pltpu.make_async_copy(dx1, ig, osem.at[0])
    done.start()
    for k in range(2):
        for q in range(16):
            bias_from(128 + 16 * k + q, dmod[k, :, q * 64 : (q + 1) * 64])
    for g in range(4):
        for q in range(4):
            bias_from(g * 4 + q, dbq[g, :, q * 64 : (q + 1) * 64])
            bias_from(16 + g * 4 + q, dbq[g, :, 256 + q * 64 : 256 + (q + 1) * 64])
    for k in range(2):
        esrc[:, :, k * D : (k + 1) * D] = jnp.broadcast_to(dmod[k].reshape(1, 1, D), (n, 1, D))
    each_peer(n, me, lambda k, to, fr: remote(esrc.at[to], erec.at[me], s4.at[k], r4.at[k], to).start())
    erec[pl.ds(me, 1)] = esrc[pl.ds(me, 1)]
    scatter.tick(13)
    each_peer(n, me, lambda k, to, fr: remote(dsrc, dall.at[fr, :, tail], s3.at[k], r3.at[k], to).wait())
    total = jnp.zeros((n, 32), f32)
    for q in range(4, 12):
        total += ada_columns(dall[:, :, q * 512 : (q + 1) * 512].reshape(n, 512).astype(bf), q)
    scatter.tick(14)
    each_peer(n, me, lambda k, to, fr: remote(esrc.at[to], erec.at[fr], s4.at[k], r4.at[k], to).wait())
    for q in range(4):
        total += ada_columns(erec[:, :, q * 512 : (q + 1) * 512].reshape(n, 512).astype(bf), q)
    csrc[:, :, 0:32] = total.reshape(n, 1, 32)
    each_peer(n, me, lambda k, to, fr: remote(csrc.at[to], crec.at[me], s5.at[k], r5.at[k], to).start())
    crec[pl.ds(me, 1)] = csrc[pl.ds(me, 1)]
    bsum[...] = jnp.sum(erec[:, :, 2 * D :], axis=0)
    scatter.tick(15)
    each_peer(n, me, lambda k, to, fr: remote(csrc.at[to], crec.at[fr], s5.at[k], r5.at[k], to).wait())
    scatter.tick(16)
    done.wait()
    scatter.finish()
    gather.finish()


def block(n, *a):
    dma = pltpu.SemaphoreType.DMA
    regular = pltpu.SemaphoreType.REGULAR
    vm = pltpu.VMEM
    return pl.pallas_call(
        functools.partial(block_kernel, n),
        out_shape=(sd((S, D), bf), sd((S, D), f32), sd((32, 18 * D), f32), sd((1, 512), f32), sd((n, 1, 128), f32))
        + (sd((12, 4, 2, 2, 2, 32, 1024), bf), sd((NJ, 2, 2, 2, 2, 32, 1024), f32), sd((4, S, 768), bf), sd((4, S, 256), bf)),
        in_specs=[V] * 3 + [A],
        out_specs=[A] * 2 + [V] * 3 + [A] * 4,
        scratch_shapes=[vm((12, 32, 1024), bf), vm((32, 6 * D), bf), vm((n, 16, 128), f32), vm((n, 32), bf)]
        + [vm((n, 1, 6 * D), f32), vm((n, 1, 6 * D), f32), vm((1, 4 * D), f32), vm((n, 1, 6 * D), f32), vm((n, 1, 2560), f32), vm((n, 1, 2560), f32), vm((n, 1, 128), f32)]
        + [vm((6, 1, D), f32), vm((2, 1, D), f32), vm((4, 1, 768), f32), vm((NJ, 1, CH), f32), vm((6, 1, D), f32), vm((2, 1, D), f32), vm((NJ, 1, CH), f32), vm((4, 1, 512), f32)]
        + [vm((16, 2, 32, S), bf), vm((16, 2, 32, S), bf), vm((4, 4, S), f32), vm((S, D), bf), vm((S, D), f32)]
        + [vm((2, S, 1024), bf), vm((2, S, 1024), bf), vm((2, 16, 32, S), bf)]
        + [dma((n,))] * 2
        + [dma((2, n))] * 2
        + [dma((n,))] * 6
        + [dma((4,)), dma((4,)), dma((2, 3)), dma((2, 3)), regular, regular]
        + [dma((2,)), dma((2,)), dma((5,)), dma((2,))]
        + gather_sems(12)
        + Scatter.shapes,
        compiler_params=pltpu.CompilerParams(collective_id=0, has_side_effects=True, vmem_limit_bytes=VMEM_BYTES),
        name="block",
    )(*a)


def adam_step(param, grad, first, second, decay):
    new_first = beta_first * first + (1.0 - beta_first) * grad
    new_second = beta_second * second + (1.0 - beta_second) * grad * grad
    step_size = learn_rate / (1.0 - beta_first**STEP)
    denom = jnp.sqrt(new_second / (1.0 - beta_second**STEP)) + adam_eps
    new_param = param - step_size * new_first / denom - learn_rate * decay * param
    return (new_param, new_first, new_second)


def plain(n, tok, gout, condition, weights, biases):
    me = lax.axis_index("dp")
    rows = D // n
    wb = weights.astype(bf)
    qkvo = wb[:, : 4 * D].reshape(rows, 4, 4, 256).transpose(2, 0, 1, 3).reshape(4, rows, 1024)
    updn = wb[:, 4 * D : 4 * D + 2 * FF].reshape(rows, 2, NJ, CH).transpose(2, 0, 1, 3).reshape(NJ, rows, 1024)
    mine = jnp.concatenate([qkvo, updn], axis=0)
    ada_l = wb[:, 4 * D + 2 * FF :]
    cond_act = jax.nn.silu(condition).astype(bf)
    bias_full = lax.all_gather(biases.astype(bf), "dp", axis=0, tiled=True).astype(f32)
    cond_all = lax.all_gather(cond_act, "dp", axis=0, tiled=True)
    cond_cols = lax.dynamic_slice_in_dim(cond_all, me * rows, rows, 1)
    mod = lax.psum_scatter(jnp.dot(cond_cols, ada_l, preferred_element_type=f32), "dp", scatter_dimension=0, tiled=True)
    mod = jnp.concatenate([(mod[0] + bias_full[4 * D + FF :]).reshape(6, D), jnp.zeros((2, D), f32)], axis=0)
    zrow = jnp.zeros((D,), f32)
    bqkv = jnp.stack([bias_full[:D], zrow, bias_full[D : 2 * D]]).reshape(3, 4, 256).transpose(1, 0, 2).reshape(4, 1, 768)
    brows = jnp.stack([zrow, zrow, bias_full[2 * D : 3 * D], bias_full[3 * D + FF : 4 * D + FF], zrow, zrow, zrow, zrow])
    bup = bias_full[3 * D : 3 * D + FF].reshape(NJ, 1, CH)
    wall = lax.all_gather(mine, "dp", axis=1, tiled=True)
    qkv, attn_t, lse, h1t = ka(tok, mod, bqkv, wall)
    bo, dx1, dat, dw_mlp, dw_out, dmod_b, db, db_up = kb(512, tok, gout, attn_t, mod, brows, bup, wall)
    ig, dw_qkv, dmod_a, db_qkv = kc(1024, tok, mod, qkv, dat, lse, dx1, h1t, wall)
    g_mlp = lax.psum_scatter(dw_mlp, "dp", scatter_dimension=2, tiled=True)
    g_out = lax.psum_scatter(dw_out, "dp", scatter_dimension=0, tiled=True)
    g_qkv = lax.psum_scatter(dw_qkv, "dp", scatter_dimension=1, tiled=True)
    g_qkv = g_qkv.reshape(4, rows, 3, 256).transpose(1, 2, 0, 3).reshape(rows, 3 * D)
    g_mlp = g_mlp.transpose(2, 1, 0, 3).reshape(rows, 2 * FF)
    dmod = (dmod_a + dmod_b)[:6].reshape(1, 6 * D)
    db_qkv = db_qkv.reshape(4, 3, 256).transpose(1, 0, 2).reshape(3, D)
    bias_row = jnp.concatenate([db_qkv[0], db_qkv[2], db[2], db_up.reshape(FF), db[3], dmod[0]])
    bias_grad = lax.psum_scatter(bias_row, "dp", scatter_dimension=0, tiled=True)
    dmod_all = lax.all_gather(dmod.astype(bf), "dp", axis=0, tiled=True)
    g_ada = lax.dot_general(cond_cols, dmod_all, TN, preferred_element_type=f32)
    cond_part = lax.dot_general(dmod_all, ada_l, NT, preferred_element_type=f32)
    cond_grad = lax.all_to_all(cond_part, "dp", split_axis=0, concat_axis=1, tiled=True)
    return bo, ig, cond_grad, jnp.concatenate([g_qkv, g_out, g_mlp, g_ada], axis=1), bias_grad


def on_chips(n, tok, gout, condition, weights, biases):
    cond_act = jax.nn.silu(condition).reshape(8, 128)
    rounded = jnp.pad(lax.reduce_precision(biases, 8, 7).reshape(7, 64), ((0, 1), (0, 64)))
    bo, ig, weight_grad, bsum, crec = block(n, tok, gout, jnp.concatenate([cond_act, rounded]), weights)[:5]
    return bo, ig, crec[:, 0, :32].reshape(1, D), weight_grad, bsum[0, : biases.shape[0]]


def on_device(n, block_in, condition, out_grad, weights, biases, first_moment, second_moment, bias_first, bias_second):
    run = on_chips if n == 32 else plain
    bo, ig, cond_grad, weight_grad, bias_grad = run(n, block_in[0], out_grad[0], condition, weights, biases)
    sigma = jax.nn.sigmoid(condition)
    cond_grad = cond_grad * (sigma * (1.0 + condition * (1.0 - sigma)))
    new_weights, new_first, new_second = adam_step(weights, weight_grad, first_moment, second_moment, weight_decay)
    new_biases, new_bias_first, new_bias_second = adam_step(biases, bias_grad, bias_first, bias_second, 0.0)
    return (bo[None], ig[None], cond_grad, weight_grad, bias_grad, new_weights, new_biases, new_first, new_second, new_bias_first, new_bias_second)


def solution(mesh):
    three, two, one = P("dp", None, None), P("dp", None), P("dp")
    return jax.shard_map(
        functools.partial(on_device, mesh.shape["dp"]),
        mesh=mesh,
        in_specs=(three, two, three, two, one, two, two, one, one),
        out_specs=(three, three, two, two, one, two, one, two, two, one, one),
        check_vma=False,
    )
```

```python
import functools

import jax
import jax.numpy as jnp
from jax import lax
from jax.experimental import pallas as pl
from jax.experimental.pallas import tpu as pltpu
from jax.sharding import PartitionSpec as P

D = 1024
FF = 4096
S = 1024
STEP = 3
CH = 512
NJ = FF // CH
VMEM_BYTES = 63 * 2**20
learn_rate = 0.01
beta_first = 0.9
beta_second = 0.95
adam_eps = 1e-08
weight_decay = 0.05
gc = 0.7978845608028654
LOG2E = 1.4426950408889634
f32 = jnp.float32
bf = jnp.bfloat16
NT = (((1,), (1,)), ((), ()))
TN = (((0,), (0,)), ((), ()))
V = pl.BlockSpec(memory_space=pltpu.VMEM)
A = pl.BlockSpec(memory_space=pl.ANY)
sd = jax.ShapeDtypeStruct
MESH = pl.DeviceIdType.MESH


def mesh_signal(sem, dev):
    pl.semaphore_signal(sem, inc=1, device_id=(dev,), device_id_type=MESH)


def remote(src, dst, send, recv, dev):
    return pltpu.make_async_remote_copy(src_ref=src, dst_ref=dst, send_sem=send, recv_sem=recv, device_id=(dev,), device_id_type=MESH)


def greet_all(n, me, between):
    barrier = pltpu.get_barrier_semaphore()

    def go(k, _):
        mesh_signal(barrier, lax.rem(me + k, n))
        return 0

    lax.fori_loop(1, n, go, 0)
    between()
    pl.semaphore_wait(barrier, n - 1)


def each_peer(n, me, f):
    def go(k, _):
        f(k, lax.rem(me + k, n), lax.rem(me + n - k, n))
        return 0

    lax.fori_loop(1, n, go, 0)


def gather_sems(count):
    return [pltpu.SemaphoreType.DMA((count,)), pltpu.SemaphoreType.DMA((count, 12)), pltpu.SemaphoreType.DMA((count, 12))]


def each_mate(n, me, f):
    def go(k, _):
        f(k, lax.rem(me + 2 * k, n), lax.rem(me + n - 2 * k, n))
        return 0

    lax.fori_loop(1, n // 2, go, 0)


class Place:
    def __init__(self):
        me = lax.axis_index("dp")
        self.me = me
        self.z = me // 8
        self.y = lax.rem(me // 4, 2)
        self.x = lax.rem(me // 2, 2)
        self.c = lax.rem(me, 2)
        self.to_c = me + 1 - 2 * self.c
        self.to_x = me + 2 - 4 * self.x
        self.to_y = me + 4 - 8 * self.y
        self.a = self.z // 2
        self.b = lax.rem(self.z, 2)
        self.to_b = me + 8 - 16 * self.b
        self.to_a = me + 16 - 32 * self.a

    def to_z(self, k):
        return lax.rem(self.z + k, 4) * 8 + lax.rem(self.me, 8)


class Gather:
    def __init__(self, at, src, buf, local, send, recv, count):
        self.at, self.src, self.buf, self.local, self.send, self.recv, self.count = at, src, buf, local, send, recv, count

    def step_refs(self, i, step, c):
        at, b = self.at, self.buf.at[i]
        y, x = at.y, at.x
        lo, hi = pl.ds(0, 16), pl.ds(16, 16)
        if step == 1:
            return [b.at[:, y, x, c]]
        if step == 2:
            return [b.at[:, y, 1 - x, c, lo], b.at[:, 1 - y, x, c, hi]]
        return [b.at[:, 1 - y, :, c, lo], b.at[:, :, 1 - x, c, hi]]

    def z_copy(self, i, k):
        at = self.at
        return remote(self.src.at[i], self.buf.at[i, at.z, at.y, at.x, at.c], self.send.at[i, k - 1], self.recv.at[i, k - 1], at.to_z(k))

    def z_landed(self, i, k):
        at = self.at
        zz = lax.rem(at.z + 4 - k, 4)
        return remote(self.src.at[i], self.buf.at[i, zz, at.y, at.x, at.c], self.send.at[i, k - 1], self.recv.at[i, k - 1], at.to_z(k))

    def own(self, i):
        at = self.at
        return pltpu.make_async_copy(self.src.at[i], self.buf.at[i, at.z, at.y, at.x, at.c], self.local.at[i])

    def xy_copies(self, i, step):
        at, b = self.at, self.buf.at[i]
        y, x, c = at.y, at.x, at.c
        lo, hi = pl.ds(0, 16), pl.ds(16, 16)
        if step == 2:
            a, d = b.at[:, y, x, c, lo], b.at[:, y, x, c, hi]
            return [
                remote(a, a, self.send.at[i, 3], self.recv.at[i, 3], at.to_x),
                remote(d, d, self.send.at[i, 4], self.recv.at[i, 4], at.to_y),
            ]
        a, d = b.at[:, y, :, c, lo], b.at[:, :, x, c, hi]
        return [
            remote(a, a, self.send.at[i, 5], self.recv.at[i, 5], at.to_y),
            remote(d, d, self.send.at[i, 6], self.recv.at[i, 6], at.to_x),
        ]

    def xy_landed(self, i, step):
        at, b = self.at, self.buf.at[i]
        refs = self.step_refs(i, step, at.c)
        base = 3 if step == 2 else 5
        return [remote(r, r, self.send.at[i, base + q], self.recv.at[i, base + q], at.to_x) for q, r in enumerate(refs)]

    def core_copies(self, i, step):
        at = self.at
        base = {1: 7, 2: 8, 3: 10}[step]
        return [remote(r, r, self.send.at[i, base + q], self.recv.at[i, base + q], at.to_c) for q, r in enumerate(self.step_refs(i, step, at.c))]

    def core_landed(self, i, step):
        at = self.at
        base = {1: 7, 2: 8, 3: 10}[step]
        return [remote(r, r, self.send.at[i, base + q], self.recv.at[i, base + q], at.to_c) for q, r in enumerate(self.step_refs(i, step, 1 - at.c))]

    def start(self, first, last):
        def go(i, _):
            self.own(i).start()
            return 0

        lax.fori_loop(first, last, go, 0)

    def tick(self, t, parts=(5, 4, 3, 2, 1)):
        def one():
            for k in (1, 2, 3):
                self.z_copy(t, k).start()

        def two():
            i = t - 1
            for k in (1, 2, 3):
                self.z_landed(i, k).wait_recv()
            self.own(i).wait()
            for cp in self.xy_copies(i, 2) + self.core_copies(i, 1):
                cp.start()

        def three():
            i = t - 2
            for cp in self.xy_landed(i, 2):
                cp.wait_recv()
            for cp in self.xy_copies(i, 3) + self.core_copies(i, 2):
                cp.start()

        def four():
            i = t - 3
            for cp in self.xy_landed(i, 3):
                cp.wait_recv()
            for cp in self.core_copies(i, 3):
                cp.start()

        def five():
            i = t - 4
            for step in (1, 2, 3):
                for cp in self.core_landed(i, step):
                    cp.wait_recv()

        for part in parts:
            i = t - part + 1
            when((i >= 0) & (i < self.count), (one, two, three, four, five)[part - 1])

    def finish(self):
        def go(i, _):
            for k in (1, 2, 3):
                self.z_copy(i, k).wait_send()
            for step in (2, 3):
                for cp in self.xy_copies(i, step):
                    cp.wait_send()
            for step in (1, 2, 3):
                for cp in self.core_copies(i, step):
                    cp.wait_send()
            return 0

        lax.fori_loop(0, self.count, go, 0)


def dot(a,b,dn=None):
    if dn is None: return jnp.dot(a,b,preferred_element_type=f32)
    return lax.dot_general(a,b,dn,preferred_element_type=f32)

def lane_half(x, hh):
    lane=lax.broadcasted_iota(jnp.int32, x.shape, 1)
    keep=(lane<64) if hh==0 else (lane>=64)
    return jnp.where(keep, x, jnp.zeros_like(x))

def gelu_pair(u):
    u2=u*u
    t=jnp.tanh(gc*(u+0.044715*u2*u))
    return 0.5*u*(1.0+t), 0.5*(1.0+t)+0.5*u*(1.0-t*t)*gc*(1.0+3.0*0.044715*u2)
def nrm(v):
    c=v-jnp.mean(v,axis=-1,keepdims=True)
    r=lax.rsqrt(jnp.mean(c*c,axis=-1,keepdims=True)+1e-6)
    return c*r,r
def rows_loop(n, R, f):
    def body(i,_):
        f(pl.ds(pl.multiple_of(i*R,R),R)); return 0
    lax.fori_loop(0,n//R,body,0)

def kb_kernel(R, tok, gout, attnT, mod, bias, bup, wall,
      bo_ref, dx1_ref, dat_ref, dw_h, dwout_ref, dmod_ref, db_ref, dbup_ref,
      h2, h2T, dzb, dzT, z, dh2, o_s, wout, wbuf, act, du, dwst, wsem, osem, wosem):
    def co(g): return pltpu.make_async_copy(wall.at[g, :, 768:1024], wout.at[:, g*256:(g+1)*256], wosem.at[g])
    for g in range(4): co(g).start()
    def fetch(j, slot):
        pltpu.make_async_copy(wall.at[4 + j], wbuf.at[slot], wsem.at[slot]).start()
    fetch(0,0)
    shift1=mod[0:1];scale1=mod[1:2];gate1=mod[2:3];shift2=mod[3:4];scale2=mod[4:5];gate2=mod[5:6]
    db_ref[...]=jnp.zeros_like(db_ref); dmod_ref[...]=jnp.zeros_like(dmod_ref)
    for g in range(4): co(g).wait()
    def pre(r):
        o=dot(attnT[:,r],wout[...],TN)+bias[2:3]
        o_s[r,:]=o
        x1=tok[r,:].astype(f32)+gate1*o
        xh,_=nrm(x1)
        h2[r,:]=(xh*(1.0+scale2)+shift2).astype(bf)
        dz=gout[r,:].astype(f32)*gate2
        dzb[r,:]=dz.astype(bf)
        db_ref[3:4]+=jnp.sum(dz,axis=0,keepdims=True)
    rows_loop(S,256,pre)
    for i in range(4):
        r=slice(i*256,(i+1)*256)
        h2T[:,r]=h2[r,:].T
        dzT[:,r]=dzb[r,:].T
    z[...]=jnp.zeros_like(z); dh2[...]=jnp.zeros_like(dh2)
    def chunk(j,_):
        slot=lax.rem(j,2)
        @pl.when(j+1<NJ)
        def _(): fetch(j+1,1-slot)
        pltpu.make_async_copy(wall.at[4 + j], wbuf.at[slot], wsem.at[slot]).wait()
        dbup_ref[j]=jnp.zeros((1,CH),f32)
        def row(r):
            u=dot(h2[r,:],wbuf[slot,:,:CH])+bup[j]
            a,sl=gelu_pair(u)
            ab=a.astype(bf); act[r,:]=ab
            da=dot(dzb[r,:],wbuf[slot,:,CH:])
            d=da*sl
            dbup_ref[j]+=jnp.sum(d,axis=0,keepdims=True)
            db_=d.astype(bf); du[r,:]=db_
            z[r,:]+=dot(ab,wbuf[slot,:,CH:],NT)
            dh2[r,:]+=dot(db_,wbuf[slot,:,:CH],NT)
        rows_loop(S,R,row)
        @pl.when(j>=2)
        def _():
            pltpu.make_async_copy(dwst.at[slot], dw_h.at[j], osem.at[slot]).wait()
        def wrow(r):
            dwst[slot,0,r,:]=dot(h2T[r,:],du[...])
            dwst[slot,1,r,:]=dot(dzT[r,:],act[...])
        rows_loop(D,256,wrow)
        pltpu.make_async_copy(dwst.at[slot], dw_h.at[j], osem.at[slot]).start()
        return 0
    lax.fori_loop(0,NJ,chunk,0)
    for s in range(2): pltpu.make_async_copy(dwst.at[s], dw_h.at[s], osem.at[s]).wait()
    def post(r):
        g=gout[r,:].astype(f32); o=o_s[r,:]
        x1=tok[r,:].astype(f32)+gate1*o
        xh,rstd=nrm(x1)
        zz=z[r,:]+bias[3:4]
        bo_ref[r,:]=(x1+gate2*zz).astype(bf)
        dmod_ref[5:6]+=jnp.sum(g*zz,axis=0,keepdims=True)
        dh=dh2[r,:]
        dmod_ref[3:4]+=jnp.sum(dh,axis=0,keepdims=True)
        dmod_ref[4:5]+=jnp.sum(dh*xh,axis=0,keepdims=True)
        gg=dh*(1.0+scale2)
        dx1=g+rstd*(gg-jnp.mean(gg,axis=-1,keepdims=True)-xh*jnp.mean(gg*xh,axis=-1,keepdims=True))
        dx1_ref[r,:]=dx1
        dmod_ref[2:3]+=jnp.sum(dx1*o,axis=0,keepdims=True)
        do=dx1*gate1
        db_ref[2:3]+=jnp.sum(do,axis=0,keepdims=True)
        dob=do.astype(bf)
        dzb[r,:]=dob
        t=dot(dob,wout[...],NT).astype(bf)
        for g4 in range(4): dat_ref[g4,r,:]=t[:,g4*256:(g4+1)*256]
    rows_loop(S,128,post)
    def wo(r):
        dwout_ref[r,:]=dot(attnT[r,:],dzb[...])
    rows_loop(D,256,wo)

def kb(R,*a):
    V=pl.BlockSpec(memory_space=pltpu.VMEM); A=pl.BlockSpec(memory_space=pl.ANY)
    sd=jax.ShapeDtypeStruct
    return pl.pallas_call(functools.partial(kb_kernel,R),
      out_shape=(sd((S,D),bf),sd((S,D),f32),sd((4,S,256),bf),sd((NJ,2,D,CH),f32),sd((D,D),f32),sd((8,D),f32),sd((8,D),f32),sd((NJ,1,CH),f32)),
      in_specs=[V]*6+[A], out_specs=[V,V,V,A,V,V,V,V],
      scratch_shapes=[pltpu.VMEM((S,D),bf)]*4+[pltpu.VMEM((S,D),f32)]*3+[pltpu.VMEM((D,D),bf),pltpu.VMEM((2,D,2*CH),bf),pltpu.VMEM((S,CH),bf),pltpu.VMEM((S,CH),bf),
         pltpu.VMEM((2,2,D,CH),f32),pltpu.SemaphoreType.DMA((2,)),pltpu.SemaphoreType.DMA((2,)),pltpu.SemaphoreType.DMA((4,))],
      compiler_params=pltpu.CompilerParams(vmem_limit_bytes=62*2**20), name=f"kb{R}")(*a)

def ka_kernel(tok, mod, bqkv, wall, qkv, attnT, lse, h1T, h1, wbuf, wsem):
    c = LOG2E / 8.0

    def cp(g, slot):
        return pltpu.make_async_copy(wall.at[g, :, 0:768], wbuf.at[slot], wsem.at[slot])

    cp(0, 0).start()
    shift1, scale1 = mod[0:1], mod[1:2]

    def ln(r):
        xh, _ = nrm(tok[r, :].astype(f32))
        h1[r, :] = (xh * (1.0 + scale1) + shift1).astype(bf)

    rows_loop(S, 128, ln)
    for i in range(4):
        r = slice(i * 256, (i + 1) * 256)
        h1T[:, r] = h1[r, :].T

    def group(g, _):
        slot = lax.rem(g, 2)
        when(g < 3, lambda: cp(g + 1, 1 - slot).start())
        cp(g, slot).wait()

        def proj(r):
            qkv[g, r, :] = (dot(h1[r, :], wbuf[slot]) + bqkv[g]).astype(bf)

        rows_loop(S, 256, proj)
        for p in range(2):
            kp = qkv[g, :, 256 + p * 128 : 256 + (p + 1) * 128]
            vT = qkv[g, :, 512 + p * 128 : 512 + (p + 1) * 128].T
            q = qkv[g, :, p * 128 : (p + 1) * 128]
            for h in range(2):
                s = dot(lane_half(kp, h), q, NT)
                m = jnp.max(s, axis=0, keepdims=True)
                e = jnp.exp2((s - m) * c)
                l = jnp.sum(e, axis=0, keepdims=True)
                pr = (e * (1.0 / l)).astype(bf)
                o = dot(vT[h * 64 : (h + 1) * 64], pr)
                lse[g, p * 2 + h : p * 2 + h + 1, :] = m * 0.125 + jnp.log(l)
                attnT[pl.ds(pl.multiple_of(g * 256 + (p * 128 + h * 64), 64), 64), :] = o.astype(bf)
        return 0

    lax.fori_loop(0, 4, group, 0)


def ka(*a):
    return pl.pallas_call(
        ka_kernel,
        out_shape=(sd((4, S, 768), bf), sd((D, S), bf), sd((4, 4, S), f32), sd((D, S), bf)),
        in_specs=[V, V, V, A],
        out_specs=[V] * 4,
        scratch_shapes=[pltpu.VMEM((S, D), bf), pltpu.VMEM((2, D, 768), bf), pltpu.SemaphoreType.DMA((2,))],
        compiler_params=pltpu.CompilerParams(vmem_limit_bytes=60 * 2**20),
        name="attention_forward",
    )(*a)


def kc_kernel(QB, tok, mod, qkv, dat, lse, dx1, h1T, w_h, ig, dw_h, dmod, dbq, dqkv, dk_s, dv_s, dqT_s, dh1, wbuf, dwst, wsem, osem):
    c=LOG2E/8.0
    def cp(g,slot): return pltpu.make_async_copy(w_h.at[g, :, 0:768], wbuf.at[slot], wsem.at[slot])
    def co(g,slot): return pltpu.make_async_copy(dwst.at[slot], dw_h.at[g], osem.at[slot])
    cp(0,0).start()
    dh1[...]=jnp.zeros_like(dh1); dmod[...]=jnp.zeros_like(dmod); dbq[...]=jnp.zeros_like(dbq)
    def group(g,_):
        slot=lax.rem(g,2)
        @pl.when(g<3)
        def _(): cp(g+1,1-slot).start()
        for p in range(2):
            sl=slice(p*128,(p+1)*128); slk=slice(256+p*128,256+(p+1)*128); slv=slice(512+p*128,512+(p+1)*128)
            kp=qkv[g,:,slk]; vp=qkv[g,:,slv]
            ks=[lane_half(kp,h) for h in range(2)]; vs=[lane_half(vp,h) for h in range(2)]
            kT=kp.T
            dk_s[...]=jnp.zeros_like(dk_s); dv_s[...]=jnp.zeros_like(dv_s)
            def qblk(i,_):
                r=pl.ds(pl.multiple_of(i*QB,QB),QB)
                q=qkv[g,r,sl]; da=dat[g,r,sl]
                for h in range(2):
                    s=dot(ks[h],q,NT)
                    pT=jnp.exp2(s*c-lse[g,p*2+h:p*2+h+1,r]*LOG2E)
                    dp=dot(vs[h],da,NT)
                    delta=jnp.sum(pT*dp,axis=0,keepdims=True)
                    ds=(pT*(dp-delta)).astype(bf)
                    dv_s[...]+=dot(pT.astype(bf),lane_half(da,h))
                    dk_s[...]+=dot(ds,lane_half(q,h))
                    dqT_s[h*64:(h+1)*64,r]=dot(kT[h*64:(h+1)*64],ds)
                return 0
            lax.fori_loop(0,S//QB,qblk,0)
            dq=dqT_s[...].T*0.125
            dbq[g,:,sl]=jnp.sum(dq,axis=0,keepdims=True)
            dqkv[:,sl]=dq.astype(bf)
            dqkv[:,slk]=(dk_s[...]*0.125).astype(bf)
            dbq[g,:,slv]=jnp.sum(dv_s[...],axis=0,keepdims=True)
            dqkv[:,slv]=dv_s[...].astype(bf)
        cp(g,slot).wait()
        @pl.when(g>=2)
        def _(): co(g,slot).wait()
        def wrow(r):
            dwst[slot,r,:]=dot(h1T[r,:],dqkv[...])
            dh1[r,:]+=dot(dqkv[r,:],wbuf[slot],NT)
        rows_loop(D,256,wrow)
        co(g,slot).start()
        return 0
    lax.fori_loop(0,4,group,0)
    for s_ in range(2): co(s_,s_).wait()
    scale1=mod[1:2]
    def post(r):
        xh,rstd=nrm(tok[r,:].astype(f32))
        dh=dh1[r,:]
        dmod[0:1]+=jnp.sum(dh,axis=0,keepdims=True)
        dmod[1:2]+=jnp.sum(dh*xh,axis=0,keepdims=True)
        gg=dh*(1.0+scale1)
        ig[r,:]=dx1[r,:]+rstd*(gg-jnp.mean(gg,axis=-1,keepdims=True)-xh*jnp.mean(gg*xh,axis=-1,keepdims=True))
    rows_loop(S,128,post)
def kc(QB,*a):
    return pl.pallas_call(functools.partial(kc_kernel,QB),
      out_shape=(sd((S,D),f32),sd((4,D,768),f32),sd((8,D),f32),sd((4,1,768),f32)),
      in_specs=[V]*7+[A], out_specs=[V,A,V,V],
      scratch_shapes=[pltpu.VMEM((S,768),bf),pltpu.VMEM((S,128),f32),pltpu.VMEM((S,128),f32),pltpu.VMEM((128,S),f32),pltpu.VMEM((S,D),f32),
        pltpu.VMEM((2,D,768),bf),pltpu.VMEM((2,D,768),f32),pltpu.SemaphoreType.DMA((2,)),pltpu.SemaphoreType.DMA((2,))],
      compiler_params=pltpu.CompilerParams(vmem_limit_bytes=60*2**20), name=f"kc{QB}")(*a)
def when(cond, f):
    @pl.when(cond)
    def _():
        f()


class Pair:
    def __init__(self, at, own, theirs, send, recv, credit, count):
        self.at, self.own, self.theirs, self.sems, self.credit, self.count = at, own, theirs, (send, recv), credit, count

    def copy(self, i, part, cols):
        slot = lax.rem(i, 2)
        return remote(self.own.at[slot, :, cols], self.theirs.at[slot, :, cols], self.sems[0].at[slot, part], self.sems[1].at[slot, part], self.at.to_c)

    def start(self, i, part, cols):
        if part == 0:
            when(i >= 2, lambda: pl.semaphore_wait(self.credit, 1))
        self.copy(i, part, cols).start()

    def sent(self, i, parts):
        for part, cols in enumerate(parts):
            self.copy(i, part, cols).wait_send()

    def arrived(self, i, parts):
        for part, cols in enumerate(parts):
            self.copy(i, part, cols).wait_recv()

    def free(self, i):
        when(i + 2 < self.count, lambda: mesh_signal(self.credit, self.at.to_c))


WHOLE = (slice(0, 1024),)
PARTS = (slice(768, 1024), slice(0, 384), slice(384, 768))


class Scatter:
    shapes = [
        pltpu.VMEM((2, 2, 2, 2, 32, 1024), f32),
        pltpu.VMEM((2, 2, 2, 2, 16, 1024), bf),
        pltpu.VMEM((2, 2, 2, 2, 16, 1024), f32),
        pltpu.VMEM((2, 2, 2, 2, 2, 16, 1024), bf),
        pltpu.VMEM((2, 2, 2, 16, 1024), bf),
        pltpu.VMEM((2, 2, 2, 16, 1024), f32),
        pltpu.VMEM((2, 2, 2, 2, 16, 1024), bf),
        pltpu.VMEM((2, 32, 1024), f32),
        pltpu.VMEM((2, 32, 1024), f32),
        pltpu.VMEM((2, 2, 32, 1024), f32),
        pltpu.VMEM((32, 1024), f32),
        pltpu.VMEM((32, 1024), f32),
        pltpu.VMEM((2, 32, 1024), f32),
        pltpu.SemaphoreType.DMA((6,)),
        pltpu.SemaphoreType.DMA((2, 6)),
        pltpu.SemaphoreType.REGULAR((6,)),
    ]

    def __init__(self, at, refs, out, count, gaps=()):
        self.at, self.out, self.count, self.gaps = at, out, count, gaps
        self.acc, self.s2, self.k2, self.r2, self.s3, self.k3, self.r3, self.s4, self.k4, self.r4, self.s5, self.k5, self.r5, self.send, self.recv, self.credit = refs

    def todo(self, stage, slot):
        at = self.at
        if stage == 2:
            return [(0, self.s2.at[0], self.r2.at[slot, 0], at.to_y), (1, self.s2.at[1], self.r2.at[slot, 1], at.to_x)]
        if stage == 3:
            return [(2, self.s3.at[0], self.r3.at[slot, 0], at.to_x), (3, self.s3.at[1], self.r3.at[slot, 1], at.to_y)]
        if stage == 4:
            return [(4, self.s4, self.r4.at[slot], at.to_b)]
        return [(5, self.s5, self.r5.at[slot], at.to_a)]

    def copies(self, stage, i):
        slot = lax.rem(i, 2)
        return [remote(src, dst, self.send.at[q], self.recv.at[slot, q], dev) for q, src, dst, dev in self.todo(stage, slot)]

    def reuse(self, stage, i):
        def go():
            for cp in self.copies(stage, i - 1):
                cp.wait_send()

        when(i >= 1, go)

    def start(self, stage, i):
        def go():
            for q, _, _, _ in self.todo(stage, 0):
                pl.semaphore_wait(self.credit.at[q], 1)

        when(i >= 2, go)
        for cp in self.copies(stage, i):
            cp.start()

    def arrived(self, stage, i):
        for cp in self.copies(stage, i):
            cp.wait_recv()

    def free(self, stage, i):
        def go():
            for q, _, _, dev in self.todo(stage, 0):
                mesh_signal(self.credit.at[q], dev)

        when(i + 2 < self.count, go)

    def two(self, i, acc):
        y, x = self.at.y, self.at.x
        lo, hi = pl.ds(0, 16), pl.ds(16, 16)
        self.reuse(2, i)
        self.s2[0] = acc[:, :, 1 - y, :, lo, :].astype(bf)
        self.s2[1] = acc[:, :, :, 1 - x, hi, :].astype(bf)
        self.start(2, i)
        self.k2[0] = acc[:, :, y, :, lo, :]
        self.k2[1] = acc[:, :, :, x, hi, :]

    def three(self, i):
        y, x = self.at.y, self.at.x
        slot = lax.rem(i, 2)
        self.arrived(2, i)
        self.reuse(3, i)
        self.s3[0] = (self.k2[0, :, :, 1 - x] + self.r2[slot, 0, :, :, 1 - x].astype(f32)).astype(bf)
        self.s3[1] = (self.k2[1, :, :, 1 - y] + self.r2[slot, 1, :, :, 1 - y].astype(f32)).astype(bf)
        self.start(3, i)
        self.k3[0] = self.k2[0, :, :, x] + self.r2[slot, 0, :, :, x].astype(f32)
        self.k3[1] = self.k2[1, :, :, y] + self.r2[slot, 1, :, :, y].astype(f32)
        self.free(2, i)

    def four(self, i):
        b = self.at.b
        slot = lax.rem(i, 2)
        self.arrived(3, i)
        self.reuse(4, i)
        for h in (0, 1):
            rows = slice(16 * h, 16 * h + 16)
            self.s4[:, rows, :] = self.k3[h, :, 1 - b] + self.r3[slot, h, :, 1 - b].astype(f32)
        self.start(4, i)
        for h in (0, 1):
            rows = slice(16 * h, 16 * h + 16)
            self.k4[:, rows, :] = self.k3[h, :, b] + self.r3[slot, h, :, b].astype(f32)
        self.free(3, i)

    def five(self, i):
        a = self.at.a
        slot = lax.rem(i, 2)
        self.arrived(4, i)
        self.reuse(5, i)
        self.s5[...] = self.k4[1 - a] + self.r4[slot, 1 - a]
        self.start(5, i)
        self.k5[...] = self.k4[a] + self.r4[slot, a]
        self.free(4, i)

    def six(self, i):
        slot = lax.rem(i, 2)
        self.arrived(5, i)
        t = self.k5[...] + self.r5[slot]

        def spread(start, src, width):
            self.out[:, pl.ds(pl.multiple_of(start, 128), width)] = t[:, src : src + width]

        def feed_forward():
            spread(4 * D + i * CH, 0, CH)
            spread(4 * D + FF + i * CH, CH, CH)

        def attention():
            g = i - NJ
            for p in range(2):
                for q in range(3):
                    spread(q * D + g * 256 + p * 128, p * 384 + q * 128, 128)
            spread(3 * D + g * 256, 768, 256)

        when(i < NJ, feed_forward)
        when(i >= NJ, attention)
        self.free(5, i)

    def tick(self, t):
        for lag, f in ((4, self.six), (3, self.five), (2, self.four), (1, self.three)):
            u = t - lag
            live = (u >= 0) & (u < self.count + len(self.gaps))
            piece = u
            for gap in self.gaps:
                live = live & (u != gap)
                piece = piece - jnp.where(u > gap, 1, 0)
            when(live, functools.partial(f, piece))

    def finish(self):
        for stage in (2, 3, 4, 5):
            for cp in self.copies(stage, self.count - 1):
                cp.wait_send()


def block_kernel(n, tok, gout, small, weights,
                 bo, ig, gw, bsum, crec, wall, dwh, qkvh, dath,
                 mine, ada, gat, biases, conds, condc, part, rec, dsrc, dall, esrc, erec, csrc, mod, brow, bqkv, bup, dmod, db, dbup, dbq,
                 attnT, h1T, lse, dob, dx1, own, theirs, halfS,
                 s0, r0, s2, r2, s3, r3, s4, r4, s5, r5, xs, xr, ps, pr, pc, hc, wsem, qsem, osem, stsem, local, send, recv, *sc):
    c = LOG2E / 8.0
    at = Place()
    me = at.me
    gather = Gather(at, mine, wall, local, send, recv, 12)
    pair = Pair(at, own, theirs, ps, pr, pc, NJ + 4)
    scatter = Scatter(at, sc, gw, 12, gaps=(11,))

    def cut(shard):
        load = pltpu.make_async_copy(weights, shard, osem.at[0])
        load.start()
        load.wait()
        for g in range(4):
            for p in range(2):
                for q in range(3):
                    a = q * D + g * 256 + p * 128
                    b = p * 384 + q * 128
                    mine[g, :, b : b + 128] = shard[:, a : a + 128].astype(bf)
            mine[g, :, 768:] = shard[:, 3 * D + g * 256 : 3 * D + (g + 1) * 256].astype(bf)
        gather.start(0, 4)
        for j in range(NJ):
            for q in range(2):
                a = 4 * D + q * FF + j * CH
                mine[4 + j, :, q * CH : (q + 1) * CH] = shard[:, a : a + CH].astype(bf)
        gather.start(4, 12)
        for q in range(6):
            a = 4 * D + 2 * FF + q * D
            ada[at.c, :, q * D : (q + 1) * D] = shard[:, a : a + D].astype(bf)

    greet_all(n, me, lambda: pl.run_scoped(cut, pltpu.VMEM((32, 18 * D), f32)))
    gather.tick(0)
    trade_ada = remote(ada.at[at.c], ada.at[at.c], xs.at[4], xr.at[4], at.to_c)
    trade_ada.start()
    each_peer(n, me, lambda k, to, fr: remote(small, gat.at[me // 2, at.c], s0.at[k], r0.at[k], to).start())
    gat[pl.ds(me // 2, 1), pl.ds(at.c, 1)] = small[...].reshape(1, 1, 16, 128)
    db[...] = jnp.zeros_like(db)
    dmod[...] = jnp.zeros_like(dmod)

    def bias_into(ref, row, start, lead):
        for q in range(lead):
            k = start + q
            ref[row, :, q * 64 : (q + 1) * 64] = biases[k // 7, k % 7 : k % 7 + 1, 0:64]

    def fetch(i, wbuf, slot):
        return pltpu.make_async_copy(wall.at[i], wbuf.at[slot], wsem.at[slot])

    def bias_from(k, piece):
        esrc[k // 7, :, 2 * D + (k % 7) * 64 : 2 * D + (k % 7 + 1) * 64] = piece

    def ada_columns(x, q):
        cols = slice(q * 512, (q + 1) * 512)
        gw[:, 4 * D + 2 * FF + q * 512 : 4 * D + 2 * FF + (q + 1) * 512] = dot(condc[...], x, TN)
        return dot(x, ada[pl.ds(at.c, 1), :, cols].reshape(32, 512), NT)

    def qkv_out(g, qkv):
        return pltpu.make_async_copy(qkv.at[lax.rem(g, 2)], qkvh.at[g], qsem.at[lax.rem(g, 2)])

    def qkv_in(g, qkv):
        return pltpu.make_async_copy(qkvh.at[g], qkv.at[lax.rem(g, 2)], qsem.at[lax.rem(g, 2)])

    def matrix(wbuf, slot, cols):
        return wbuf[slot, :, :, :, :, :, cols].reshape(D, cols.stop - cols.start)

    lead, tail = pl.ds(0, 2 * D), pl.ds(2 * D, 4 * D)

    def attention(h1, wbuf, qkv):
        def norm_one(r):
            xh, _ = nrm(tok[r, :].astype(f32))
            dx1[r, :] = xh

        rows_loop(S, 128, norm_one)
        each_peer(n, me, lambda k, to, fr: remote(small, gat.at[fr // 2, lax.rem(fr, 2)], s0.at[k], r0.at[k], to).wait())
        biases[...] = gat[...].astype(f32).reshape(n, 16, 128)[:, 8:16]
        conds[...] = gat[...].astype(f32).reshape(n // 2, 2, 16, 128)[:, :, 0:8]
        lane = lax.broadcasted_iota(jnp.int32, (128, 64), 0)
        want = lax.rem(me // 2, 2) * 64 + lax.broadcasted_iota(jnp.int32, (128, 64), 1)
        pick = jnp.where(lane == want, 1.0, 0.0).astype(bf)
        wanted = conds[:, :, pl.ds(me // 4, 1), :].reshape(n, 128).astype(bf)
        both = dot(wanted, pick)
        condc[...] = jnp.where(at.c == 0, both[:, 0:32], both[:, 32:64]).astype(bf)
        mates = dot(conds[:, pl.ds(at.c, 1), pl.ds(me // 4, 1), :].reshape(n // 2, 128).astype(bf), pick).astype(bf)
        trade_ada.wait_send()
        remote(ada.at[at.c], ada.at[1 - at.c], xs.at[4], xr.at[4], at.to_c).wait_recv()

        def columns(q):
            cols = slice(q * 512, (q + 1) * 512)
            part[:, :, cols] = dot(mates, ada[:, :, cols].reshape(64, 512)).reshape(n // 2, 1, 512)

        for q in range(4):
            columns(q)
        each_mate(n, me, lambda k, to, fr: remote(part.at[to // 2, :, lead], rec.at[me // 2, :, lead], s2.at[0, k], r2.at[0, k], to).start())
        gather.tick(1)
        for q in range(4, 12):
            columns(q)
        rec[pl.ds(me // 2, 1)] = part[pl.ds(me // 2, 1)]
        for q in range(6):
            bias_into(mod, q, 128 + 16 * q, 16)
        bias_into(brow, 0, 32, 16)
        bias_into(brow, 1, 112, 16)
        for j in range(NJ):
            bias_into(bup, j, 48 + 8 * j, 8)
        for g in range(4):
            bqkv[g] = jnp.zeros((1, 768), f32)
            for q in range(4):
                for first, offset in ((0, 0), (16, 256)):
                    k = first + g * 4 + q
                    to = (q // 2) * 384 + offset + (q % 2) * 64
                    bqkv[g, :, to : to + 64] = biases[k // 7, k % 7 : k % 7 + 1, 0:64]
        gather.tick(2)
        each_mate(n, me, lambda k, to, fr: remote(part.at[to // 2, :, lead], rec.at[fr // 2, :, lead], s2.at[0, k], r2.at[0, k], to).wait())
        each_mate(n, me, lambda k, to, fr: remote(part.at[to // 2, :, tail], rec.at[me // 2, :, tail], s2.at[1, k], r2.at[1, k], to).start())
        for q in range(2):
            mod[q] += jnp.sum(rec[:, :, q * D : (q + 1) * D], axis=0)
        shift1, scale1 = mod[0], mod[1]

        def modulate(r):
            h1[r, :] = (dx1[r, :] * (1.0 + scale1) + shift1).astype(bf)

        rows_loop(S, 128, modulate)
        for i in range(4):
            r = slice(i * 256, (i + 1) * 256)
            h1T[:, :, :, r] = h1[r, :].T.reshape(16, 2, 32, 256)
        gather.tick(3, (4,))
        gather.tick(4, (5,))
        fetch(0, wbuf, 0).start()
        gather.tick(3, (3, 2, 1))

        def group(g, _):
            slot = lax.rem(g, 2)
            fetch(g, wbuf, slot).wait()
            when(g >= 2, lambda: qkv_out(g - 2, qkv).wait())
            w = matrix(wbuf, slot, slice(0, 768))

            def proj(r):
                qkv[slot, r, :] = (dot(h1[r, :], w) + bqkv[g]).astype(bf)

            rows_loop(S, 256, proj)
            qkv_out(g, qkv).start()
            when(g == 0, lambda: gather.tick(4, (4, 3, 2, 1)))
            for p in range(2):
                kp = qkv[slot, :, p * 384 + 128 : p * 384 + 256]
                vT = qkv[slot, :, p * 384 + 256 : p * 384 + 384].T
                q = qkv[slot, :, p * 384 : p * 384 + 128]
                for h in range(2):
                    s = dot(lane_half(kp, h), q, NT)
                    m = jnp.max(s, axis=0, keepdims=True)
                    e = jnp.exp2((s - m) * c)
                    l = jnp.sum(e, axis=0, keepdims=True)
                    pr_ = (e * (1.0 / l)).astype(bf)
                    o = dot(vT[h * 64 : (h + 1) * 64], pr_)
                    lse[g, p * 2 + h : p * 2 + h + 1, :] = m * 0.125 + jnp.log(l)
                    attnT[pl.ds(g * 4 + p * 2 + h, 1)] = o.astype(bf).reshape(1, 2, 32, S)
            gather.tick(5 + g)
            when(g < 3, lambda: fetch(g + 1, wbuf, 1 - slot).start())
            return 0

        lax.fori_loop(0, 4, group, 0)
        for g in (2, 3):
            qkv_out(g, qkv).wait()
        each_mate(n, me, lambda k, to, fr: remote(part.at[to // 2, :, tail], rec.at[fr // 2, :, tail], s2.at[1, k], r2.at[1, k], to).wait())
        for q in range(2, 6):
            mod[q] += jnp.sum(rec[:, :, q * D : (q + 1) * D], axis=0)

    pl.run_scoped(attention, pltpu.VMEM((S, D), bf), pltpu.VMEM((2, 4, 2, 2, 2, 32, 1024), bf), pltpu.VMEM((2, S, 768), bf))

    def unstage(i):
        return pltpu.make_async_copy(dwh.at[i], scatter.acc, stsem.at[1])

    def staged(i):
        unstage(i).wait()
        scatter.two(i, scatter.acc)
        when(i + 1 < NJ, lambda: unstage(i + 1).start())

    def mlp(h2, hT, dzT, z, wout, wbuf, accw):
        gate1, shift2, scale2, gate2 = mod[2], mod[3], mod[4], mod[5]

        def stage(i):
            return pltpu.make_async_copy(accw, dwh.at[i], stsem.at[0])

        def co(g):
            return pltpu.make_async_copy(wall.at[g, :, :, :, :, :, 768:1024], wout.at[:, :, :, :, :, g * 256 : (g + 1) * 256], osem.at[g])

        for g in range(4):
            co(g).start()
        fetch(4, wbuf, 0).start()
        for g in range(4):
            co(g).wait()

        def branch(r):
            width = r.size
            return dot(attnT[:, :, :, r].reshape(D, width), wout[...].reshape(D, D), TN) + brow[0]

        def pre(r):
            x1 = tok[r, :].astype(f32) + gate1 * branch(r)
            xh, _ = nrm(x1)
            h2[r, :] = (xh * (1.0 + scale2) + shift2).astype(bf)
            dz = gout[r, :].astype(f32) * gate2
            dob[r, :] = dz.astype(bf)
            db[1] += jnp.sum(dz, axis=0, keepdims=True)

        def pre_block(i, _):
            pre(pl.ds(pl.multiple_of(i * 256, 256), 256))
            when(i == 2, lambda: gather.tick(9))
            return 0

        lax.fori_loop(0, 4, pre_block, 0)
        for i in range(4):
            r = slice(i * 256, (i + 1) * 256)
            hT[:, :, :, r] = h2[r, :].T.reshape(16, 2, 32, 256)
            dzT[:, :, :, r] = dob[r, :].T.reshape(16, 2, 32, 256)
        halves = [
            remote(hT.at[:, 1 - at.c], halfS.at[0], xs.at[0], xr.at[0], at.to_c),
            remote(dzT.at[:, 1 - at.c], halfS.at[1], xs.at[1], xr.at[1], at.to_c),
        ]
        for cp in halves:
            cp.start()
        z[...] = jnp.zeros_like(z)
        dx1[...] = jnp.zeros_like(dx1)

        def chunk(j, _):
            when(j >= 1, lambda: gather.tick(9 + j))

            def forward():
                slot = lax.rem(j, 2)
                when(j + 1 < NJ, lambda: fetch(5 + j, wbuf, 1 - slot).start())
                fetch(4 + j, wbuf, slot).wait()
                when(j >= 2, lambda: pair.sent(j - 2, WHOLE))
                dbup[j] = jnp.zeros((1, CH), f32)

                def row(r):
                    w_up, w_dn = matrix(wbuf, slot, slice(0, CH)), matrix(wbuf, slot, slice(CH, 2 * CH))
                    u = dot(h2[r, :], w_up) + bup[j]
                    a, sl = gelu_pair(u)
                    ab = a.astype(bf)
                    own[slot, r, CH:] = ab
                    d = dot(dob[r, :], w_dn) * sl
                    dbup[j] += jnp.sum(d, axis=0, keepdims=True)
                    db_ = d.astype(bf)
                    own[slot, r, :CH] = db_
                    z[r, :] += dot(ab, w_dn, NT)
                    dx1[r, :] += dot(db_, w_up, NT)

                rows_loop(S, 512, row)
                pair.start(j, 0, WHOLE[0])

            when(j < NJ, forward)
            scatter.tick(j - 5)
            when(j >= 5, lambda: staged(j - 5))
            when(j == 4, lambda: unstage(0).start())

            def weights():
                i = j - 1
                slot = lax.rem(i, 2)
                when(j == 1, lambda: [cp.wait_recv() for cp in halves])
                pair.arrived(i, WHOLE)
                when(i >= 1, lambda: stage(i - 1).wait())
                for q, lhs in enumerate((hT, dzT)):
                    cols = slice(q * CH, (q + 1) * CH)
                    t = dot(lhs[:, at.c].reshape(512, S), own[slot, :, cols]) + dot(halfS[q].reshape(512, S), theirs[slot, :, cols])
                    accw[:, :, :, :, :, cols] = t.reshape(2, 2, 2, 2, 32, CH)
                pair.free(i)
                stage(i).start()

            when(j >= 1, weights)
            return 0

        lax.fori_loop(0, NJ + 1, chunk, 0)
        mesh_signal(hc, at.to_c)
        stage(NJ - 1).wait()
        for cp in halves:
            cp.wait_send()

        def post(r):
            g = gout[r, :].astype(f32)
            o = branch(r)
            x1 = tok[r, :].astype(f32) + gate1 * o
            xh, rstd = nrm(x1)
            zz = z[r, :] + brow[1]
            h2[r, :] = (x1 + gate2 * zz).astype(bf)
            dmod[5] += jnp.sum(g * zz, axis=0, keepdims=True)
            dh = dx1[r, :]
            dmod[3] += jnp.sum(dh, axis=0, keepdims=True)
            dmod[4] += jnp.sum(dh * xh, axis=0, keepdims=True)
            gg = dh * (1.0 + scale2)
            dx = g + rstd * (gg - jnp.mean(gg, axis=-1, keepdims=True) - xh * jnp.mean(gg * xh, axis=-1, keepdims=True))
            dx1[r, :] = dx
            dmod[2] += jnp.sum(dx * o, axis=0, keepdims=True)
            do = dx * gate1
            db[0] += jnp.sum(do, axis=0, keepdims=True)
            dob_ = do.astype(bf)
            dob[r, :] = dob_
            own[0, r, :] = dot(dob_, wout[...].reshape(D, D), NT).astype(bf)

        pair.sent(NJ - 2, WHOLE)

        def post_half(h):
            def body(i, _):
                post(pl.ds(pl.multiple_of(h * 512 + i * 128, 128), 128))
                return 0

            lax.fori_loop(0, 4, body, 0)

        post_half(0)
        post_half(1)
        outs = [pltpu.make_async_copy(h2, bo, osem.at[0])]
        outs += [pltpu.make_async_copy(own.at[0, :, g * 256 : (g + 1) * 256], dath.at[g], osem.at[1 + g]) for g in range(4)]
        for cp in outs:
            cp.start()
        for cp in outs:
            cp.wait()

    pl.run_scoped(
        mlp,
        pltpu.VMEM((S, D), bf),
        pltpu.VMEM((16, 2, 32, S), bf),
        pltpu.VMEM((16, 2, 32, S), bf),
        pltpu.VMEM((S, D), f32),
        pltpu.VMEM((4, 2, 2, 2, 32, 1024), bf),
        pltpu.VMEM((2, 4, 2, 2, 2, 32, 1024), bf),
        pltpu.VMEM((2, 2, 2, 2, 32, 1024), f32),
    )

    def back(dh1, wbuf, qkv, dat, dk_s, dv_s, dqT_s, accw):
        def dat_in(g):
            return pltpu.make_async_copy(dath.at[g], dat.at[lax.rem(g, 2)], osem.at[lax.rem(g, 2)])

        def load(g):
            qkv_in(g, qkv).start()
            dat_in(g).start()
            fetch(g, wbuf, lax.rem(g, 2)).start()

        load(0)
        pl.semaphore_wait(hc, 1)
        halves = [
            remote(h1T.at[:, 1 - at.c], halfS.at[0], xs.at[2], xr.at[2], at.to_c),
            remote(attnT.at[:, 1 - at.c], halfS.at[1], xs.at[3], xr.at[3], at.to_c),
        ]
        for cp in halves:
            cp.start()
        scatter.tick(4)
        staged(4)
        for q in range(4):
            dsrc[:, q * D : (q + 1) * D] = dmod[2 + q]
        each_mate(n, me, lambda k, to, fr: remote(dsrc, dall.at[at.c, me // 2], s3.at[k], r3.at[k], to).start())
        dall[pl.ds(at.c, 1), pl.ds(me // 2, 1)] = dsrc[...].reshape(1, 1, 1, 4 * D)
        for q in range(16):
            bias_from(32 + q, db[0, :, q * 64 : (q + 1) * 64])
            bias_from(112 + q, db[1, :, q * 64 : (q + 1) * 64])
        for j in range(NJ):
            for q in range(8):
                bias_from(48 + 8 * j + q, dbup[j, :, q * 64 : (q + 1) * 64])
        for k in range(2, 6):
            for q in range(16):
                bias_from(128 + 16 * k + q, dmod[k, :, q * 64 : (q + 1) * 64])
        dh1[...] = jnp.zeros_like(dh1)

        def group(g, _):
            slot = lax.rem(g, 2)
            when(g < 3, lambda: load(g + 1))
            qkv_in(g, qkv).wait()
            dat_in(g).wait()
            when(g == 1, lambda: pair.sent(NJ - 1, WHOLE))
            when(g >= 2, lambda: pair.sent(NJ + g - 2, PARTS))
            own[slot, :, 768:] = dob[:, pl.ds(pl.multiple_of(g * 256, 256), 256)]
            pair.start(NJ + g, 0, PARTS[0])
            for p in range(2):
                if p == 1:
                    scatter.tick(5 + 2 * g)
                    when(g < 2, lambda: staged(5 + 2 * g))
                    when(g == 2, lambda: scatter.two(9, accw))
                sl = slice(p * 128, (p + 1) * 128)
                slq, slk, slv = (slice(p * 384 + q * 128, p * 384 + (q + 1) * 128) for q in range(3))
                kp, vp, q, da = qkv[slot, :, slk], qkv[slot, :, slv], qkv[slot, :, slq], dat[slot, :, sl]
                kT = kp.T
                for h in range(2):
                    s = dot(lane_half(kp, h), q, NT)
                    pT = jnp.exp2(s * c - lse[g, p * 2 + h : p * 2 + h + 1, :] * LOG2E)
                    dp = dot(lane_half(vp, h), da, NT)
                    delta = jnp.sum(pT * dp, axis=0, keepdims=True)
                    ds = (pT * (dp - delta)).astype(bf)
                    dv = dot(pT.astype(bf), lane_half(da, h))
                    dk = dot(ds, lane_half(q, h))
                    if h == 0:
                        dv_s[...] = dv
                        dk_s[...] = dk
                    else:
                        dv_s[...] += dv
                        dk_s[...] += dk
                    dqT_s[h * 64 : (h + 1) * 64, :] = dot(kT[h * 64 : (h + 1) * 64], ds)
                dq = dqT_s[...].T * 0.125
                dbq[g, :, sl] = jnp.sum(dq, axis=0, keepdims=True)
                own[slot, :, slq] = dq.astype(bf)
                own[slot, :, slk] = (dk_s[...] * 0.125).astype(bf)
                dbq[g, :, 256 + p * 128 : 256 + (p + 1) * 128] = jnp.sum(dv_s[...], axis=0, keepdims=True)
                own[slot, :, slv] = dv_s[...].astype(bf)
                pair.start(NJ + g, 1 + p, PARTS[1 + p])
            fetch(g, wbuf, slot).wait()
            w = matrix(wbuf, slot, slice(0, 768))

            def wrow(r):
                dh1[r, :] += dot(own[slot, r, :768], w, NT)

            rows_loop(D, 256, wrow)
            scatter.tick(6 + 2 * g)

            def at_first():
                staged(6)
                for cp in halves:
                    cp.wait_recv()

            when(g == 0, at_first)
            when(g == 1, lambda: scatter.two(8, accw))

            def pass_on():
                each_mate(n, me, lambda k, to, fr: remote(dsrc, dall.at[at.c, fr // 2], s3.at[k], r3.at[k], to).wait())
                remote(dall.at[at.c], dall.at[at.c], xs.at[5], xr.at[5], at.to_c).start()

            when(g == 1, pass_on)
            pair.arrived(NJ + g, PARTS)
            for q, lhs in enumerate((h1T, attnT)):
                cols = slice(0, 768) if q == 0 else slice(768, 1024)
                t = dot(lhs[:, at.c].reshape(512, S), own[slot, :, cols]) + dot(halfS[q].reshape(512, S), theirs[slot, :, cols])
                accw[:, :, :, :, :, cols] = t.reshape(2, 2, 2, 2, 32, cols.stop - cols.start)
            pair.free(NJ + g)
            when(g >= 2, lambda: scatter.two(8 + g, accw))
            return 0

        lax.fori_loop(0, 4, group, 0)
        for i in (2, 3):
            pair.sent(NJ + i, PARTS)
        for cp in halves:
            cp.wait_send()
        scale1 = mod[1]

        def post(r):
            xh, rstd = nrm(tok[r, :].astype(f32))
            dh = dh1[r, :]
            dmod[0] += jnp.sum(dh, axis=0, keepdims=True)
            dmod[1] += jnp.sum(dh * xh, axis=0, keepdims=True)
            gg = dh * (1.0 + scale1)
            dx1[r, :] += rstd * (gg - jnp.mean(gg, axis=-1, keepdims=True) - xh * jnp.mean(gg * xh, axis=-1, keepdims=True))

        rows_loop(S, 128, post)

    pl.run_scoped(
        back,
        pltpu.VMEM((S, D), f32),
        pltpu.VMEM((2, 4, 2, 2, 2, 32, 1024), bf),
        pltpu.VMEM((2, S, 768), bf),
        pltpu.VMEM((2, S, 256), bf),
        pltpu.VMEM((S, 128), f32),
        pltpu.VMEM((S, 128), f32),
        pltpu.VMEM((128, S), f32),
        pltpu.VMEM((2, 2, 2, 2, 32, 1024), f32),
    )
    done = pltpu.make_async_copy(dx1, ig, osem.at[0])
    done.start()
    for k in range(2):
        for q in range(16):
            bias_from(128 + 16 * k + q, dmod[k, :, q * 64 : (q + 1) * 64])
    for g in range(4):
        for q in range(4):
            bias_from(g * 4 + q, dbq[g, :, q * 64 : (q + 1) * 64])
            bias_from(16 + g * 4 + q, dbq[g, :, 256 + q * 64 : 256 + (q + 1) * 64])
    for k in range(2):
        esrc[:, :, k * D : (k + 1) * D] = jnp.broadcast_to(dmod[k].reshape(1, 1, D), (n, 1, D))
    each_peer(n, me, lambda k, to, fr: remote(esrc.at[to], erec.at[me], s4.at[k], r4.at[k], to).start())
    erec[pl.ds(me, 1)] = esrc[pl.ds(me, 1)]
    scatter.tick(13)
    remote(dall.at[at.c], dall.at[at.c], xs.at[5], xr.at[5], at.to_c).wait_send()
    remote(dall.at[1 - at.c], dall.at[1 - at.c], xs.at[5], xr.at[5], at.to_c).wait_recv()
    total = jnp.zeros((n, 32), f32)
    for q in range(4, 12):
        cols = slice((q - 4) * 512, (q - 3) * 512)
        halves_ = [dall[k, :, :, cols].reshape(n // 2, 1, 512) for k in range(2)]
        total += ada_columns(jnp.concatenate(halves_, axis=1).reshape(n, 512).astype(bf), q)
    scatter.tick(14)
    each_peer(n, me, lambda k, to, fr: remote(esrc.at[to], erec.at[fr], s4.at[k], r4.at[k], to).wait())
    for q in range(4):
        total += ada_columns(erec[:, :, q * 512 : (q + 1) * 512].reshape(n, 512).astype(bf), q)
    csrc[:, :, 0:32] = total.reshape(n, 1, 32)
    each_peer(n, me, lambda k, to, fr: remote(csrc.at[to], crec.at[me], s5.at[k], r5.at[k], to).start())
    crec[pl.ds(me, 1)] = csrc[pl.ds(me, 1)]
    bsum[...] = jnp.sum(erec[:, :, 2 * D :], axis=0)
    scatter.tick(15)
    each_peer(n, me, lambda k, to, fr: remote(csrc.at[to], crec.at[fr], s5.at[k], r5.at[k], to).wait())
    scatter.tick(16)
    done.wait()
    scatter.finish()
    gather.finish()


def block(n, *a):
    dma = pltpu.SemaphoreType.DMA
    regular = pltpu.SemaphoreType.REGULAR
    vm = pltpu.VMEM
    return pl.pallas_call(
        functools.partial(block_kernel, n),
        out_shape=(sd((S, D), bf), sd((S, D), f32), sd((32, 18 * D), f32), sd((1, 512), f32), sd((n, 1, 128), f32))
        + (sd((12, 4, 2, 2, 2, 32, 1024), bf), sd((NJ, 2, 2, 2, 2, 32, 1024), f32), sd((4, S, 768), bf), sd((4, S, 256), bf)),
        in_specs=[V] * 3 + [A],
        out_specs=[A] * 2 + [V] * 3 + [A] * 4,
        scratch_shapes=[vm((12, 32, 1024), bf), vm((2, 32, 6 * D), bf), vm((n // 2, 2, 16, 128), bf), vm((n, 8, 128), f32), vm((n // 2, 2, 8, 128), f32), vm((n, 32), bf)]
        + [vm((n // 2, 1, 6 * D), f32), vm((n // 2, 1, 6 * D), f32), vm((1, 4 * D), f32), vm((2, n // 2, 1, 4 * D), f32), vm((n, 1, 2560), f32), vm((n, 1, 2560), f32), vm((n, 1, 128), f32)]
        + [vm((6, 1, D), f32), vm((2, 1, D), f32), vm((4, 1, 768), f32), vm((NJ, 1, CH), f32), vm((6, 1, D), f32), vm((2, 1, D), f32), vm((NJ, 1, CH), f32), vm((4, 1, 512), f32)]
        + [vm((16, 2, 32, S), bf), vm((16, 2, 32, S), bf), vm((4, 4, S), f32), vm((S, D), bf), vm((S, D), f32)]
        + [vm((2, S, 1024), bf), vm((2, S, 1024), bf), vm((2, 16, 32, S), bf)]
        + [dma((n,))] * 2
        + [dma((2, n))] * 2
        + [dma((n,))] * 6
        + [dma((6,)), dma((6,)), dma((2, 3)), dma((2, 3)), regular, regular]
        + [dma((2,)), dma((2,)), dma((5,)), dma((2,))]
        + gather_sems(12)
        + Scatter.shapes,
        compiler_params=pltpu.CompilerParams(collective_id=0, has_side_effects=True, vmem_limit_bytes=VMEM_BYTES),
        name="block",
    )(*a)


def adam_step(param, grad, first, second, decay):
    new_first = beta_first * first + (1.0 - beta_first) * grad
    new_second = beta_second * second + (1.0 - beta_second) * grad * grad
    step_size = learn_rate / (1.0 - beta_first**STEP)
    denom = jnp.sqrt(new_second / (1.0 - beta_second**STEP)) + adam_eps
    new_param = param - step_size * new_first / denom - learn_rate * decay * param
    return (new_param, new_first, new_second)


def plain(n, tok, gout, condition, weights, biases):
    me = lax.axis_index("dp")
    rows = D // n
    wb = weights.astype(bf)
    qkvo = wb[:, : 4 * D].reshape(rows, 4, 4, 256).transpose(2, 0, 1, 3).reshape(4, rows, 1024)
    updn = wb[:, 4 * D : 4 * D + 2 * FF].reshape(rows, 2, NJ, CH).transpose(2, 0, 1, 3).reshape(NJ, rows, 1024)
    mine = jnp.concatenate([qkvo, updn], axis=0)
    ada_l = wb[:, 4 * D + 2 * FF :]
    cond_act = jax.nn.silu(condition).astype(bf)
    bias_full = lax.all_gather(biases.astype(bf), "dp", axis=0, tiled=True).astype(f32)
    cond_all = lax.all_gather(cond_act, "dp", axis=0, tiled=True)
    cond_cols = lax.dynamic_slice_in_dim(cond_all, me * rows, rows, 1)
    mod = lax.psum_scatter(jnp.dot(cond_cols, ada_l, preferred_element_type=f32), "dp", scatter_dimension=0, tiled=True)
    mod = jnp.concatenate([(mod[0] + bias_full[4 * D + FF :]).reshape(6, D), jnp.zeros((2, D), f32)], axis=0)
    zrow = jnp.zeros((D,), f32)
    bqkv = jnp.stack([bias_full[:D], zrow, bias_full[D : 2 * D]]).reshape(3, 4, 256).transpose(1, 0, 2).reshape(4, 1, 768)
    brows = jnp.stack([zrow, zrow, bias_full[2 * D : 3 * D], bias_full[3 * D + FF : 4 * D + FF], zrow, zrow, zrow, zrow])
    bup = bias_full[3 * D : 3 * D + FF].reshape(NJ, 1, CH)
    wall = lax.all_gather(mine, "dp", axis=1, tiled=True)
    qkv, attn_t, lse, h1t = ka(tok, mod, bqkv, wall)
    bo, dx1, dat, dw_mlp, dw_out, dmod_b, db, db_up = kb(512, tok, gout, attn_t, mod, brows, bup, wall)
    ig, dw_qkv, dmod_a, db_qkv = kc(1024, tok, mod, qkv, dat, lse, dx1, h1t, wall)
    g_mlp = lax.psum_scatter(dw_mlp, "dp", scatter_dimension=2, tiled=True)
    g_out = lax.psum_scatter(dw_out, "dp", scatter_dimension=0, tiled=True)
    g_qkv = lax.psum_scatter(dw_qkv, "dp", scatter_dimension=1, tiled=True)
    g_qkv = g_qkv.reshape(4, rows, 3, 256).transpose(1, 2, 0, 3).reshape(rows, 3 * D)
    g_mlp = g_mlp.transpose(2, 1, 0, 3).reshape(rows, 2 * FF)
    dmod = (dmod_a + dmod_b)[:6].reshape(1, 6 * D)
    db_qkv = db_qkv.reshape(4, 3, 256).transpose(1, 0, 2).reshape(3, D)
    bias_row = jnp.concatenate([db_qkv[0], db_qkv[2], db[2], db_up.reshape(FF), db[3], dmod[0]])
    bias_grad = lax.psum_scatter(bias_row, "dp", scatter_dimension=0, tiled=True)
    dmod_all = lax.all_gather(dmod.astype(bf), "dp", axis=0, tiled=True)
    g_ada = lax.dot_general(cond_cols, dmod_all, TN, preferred_element_type=f32)
    cond_part = lax.dot_general(dmod_all, ada_l, NT, preferred_element_type=f32)
    cond_grad = lax.all_to_all(cond_part, "dp", split_axis=0, concat_axis=1, tiled=True)
    return bo, ig, cond_grad, jnp.concatenate([g_qkv, g_out, g_mlp, g_ada], axis=1), bias_grad


def on_chips(n, tok, gout, condition, weights, biases):
    cond_act = jax.nn.silu(condition).reshape(8, 128)
    padded = jnp.pad(biases.reshape(7, 64), ((0, 1), (0, 64)))
    bo, ig, weight_grad, bsum, crec = block(n, tok, gout, jnp.concatenate([cond_act, padded]).astype(bf), weights)[:5]
    return bo, ig, crec[:, 0, :32].reshape(1, D), weight_grad, bsum[0, : biases.shape[0]]


def on_device(n, block_in, condition, out_grad, weights, biases, first_moment, second_moment, bias_first, bias_second):
    run = on_chips if n == 32 else plain
    bo, ig, cond_grad, weight_grad, bias_grad = run(n, block_in[0], out_grad[0], condition, weights, biases)
    sigma = jax.nn.sigmoid(condition)
    cond_grad = cond_grad * (sigma * (1.0 + condition * (1.0 - sigma)))
    new_weights, new_first, new_second = adam_step(weights, weight_grad, first_moment, second_moment, weight_decay)
    new_biases, new_bias_first, new_bias_second = adam_step(biases, bias_grad, bias_first, bias_second, 0.0)
    return (bo[None], ig[None], cond_grad, weight_grad, bias_grad, new_weights, new_biases, new_first, new_second, new_bias_first, new_bias_second)


def solution(mesh):
    three, two, one = P("dp", None, None), P("dp", None), P("dp")
    return jax.shard_map(
        functools.partial(on_device, mesh.shape["dp"]),
        mesh=mesh,
        in_specs=(three, two, three, two, one, two, two, one, one),
        out_specs=(three, three, two, two, one, two, one, two, two, one, one),
        check_vma=False,
    )
```

```python
import functools

import jax
import jax.numpy as jnp
from jax import lax
from jax.experimental import pallas as pl
from jax.experimental.pallas import tpu as pltpu
from jax.sharding import PartitionSpec as P

D = 1024
FF = 4096
S = 1024
STEP = 3
CH = 512
NJ = FF // CH
VMEM_BYTES = 64 * 2**20
learn_rate = 0.01
beta_first = 0.9
beta_second = 0.95
adam_eps = 1e-08
weight_decay = 0.05
gc = 0.7978845608028654
LOG2E = 1.4426950408889634
f32 = jnp.float32
bf = jnp.bfloat16
NT = (((1,), (1,)), ((), ()))
TN = (((0,), (0,)), ((), ()))
V = pl.BlockSpec(memory_space=pltpu.VMEM)
A = pl.BlockSpec(memory_space=pl.ANY)
sd = jax.ShapeDtypeStruct
MESH = pl.DeviceIdType.MESH


def mesh_signal(sem, dev):
    pl.semaphore_signal(sem, inc=1, device_id=(dev,), device_id_type=MESH)


def remote(src, dst, send, recv, dev):
    return pltpu.make_async_remote_copy(src_ref=src, dst_ref=dst, send_sem=send, recv_sem=recv, device_id=(dev,), device_id_type=MESH)


def greet_all(n, me, between):
    barrier = pltpu.get_barrier_semaphore()

    def go(k, _):
        mesh_signal(barrier, lax.rem(me + k, n))
        return 0

    lax.fori_loop(1, n, go, 0)
    between()
    pl.semaphore_wait(barrier, n - 1)


def each_peer(n, me, f):
    def go(k, _):
        f(k, lax.rem(me + k, n), lax.rem(me + n - k, n))
        return 0

    lax.fori_loop(1, n, go, 0)


def gather_sems(count):
    return [pltpu.SemaphoreType.DMA((count,)), pltpu.SemaphoreType.DMA((count, 12)), pltpu.SemaphoreType.DMA((count, 12))]


def each_mate(n, me, f):
    def go(k, _):
        f(k, lax.rem(me + 2 * k, n), lax.rem(me + n - 2 * k, n))
        return 0

    lax.fori_loop(1, n // 2, go, 0)


class Place:
    def __init__(self):
        me = lax.axis_index("dp")
        self.me = me
        self.z = me // 8
        self.y = lax.rem(me // 4, 2)
        self.x = lax.rem(me // 2, 2)
        self.c = lax.rem(me, 2)
        self.to_c = me + 1 - 2 * self.c
        self.to_x = me + 2 - 4 * self.x
        self.to_y = me + 4 - 8 * self.y
        self.a = self.z // 2
        self.b = lax.rem(self.z, 2)
        self.to_b = me + 8 - 16 * self.b
        self.to_a = me + 16 - 32 * self.a

    def to_z(self, k):
        return lax.rem(self.z + k, 4) * 8 + lax.rem(self.me, 8)


class Gather:
    def __init__(self, at, src, buf, local, send, recv, count):
        self.at, self.src, self.buf, self.local, self.send, self.recv, self.count = at, src, buf, local, send, recv, count

    def step_refs(self, i, step, c):
        at, b = self.at, self.buf.at[i]
        y, x = at.y, at.x
        lo, hi = pl.ds(0, 16), pl.ds(16, 16)
        if step == 1:
            return [b.at[:, y, x, c]]
        if step == 2:
            return [b.at[:, y, 1 - x, c, lo], b.at[:, 1 - y, x, c, hi]]
        return [b.at[:, 1 - y, :, c, lo], b.at[:, :, 1 - x, c, hi]]

    def z_copy(self, i, k):
        at = self.at
        return remote(self.src.at[i], self.buf.at[i, at.z, at.y, at.x, at.c], self.send.at[i, k - 1], self.recv.at[i, k - 1], at.to_z(k))

    def z_landed(self, i, k):
        at = self.at
        zz = lax.rem(at.z + 4 - k, 4)
        return remote(self.src.at[i], self.buf.at[i, zz, at.y, at.x, at.c], self.send.at[i, k - 1], self.recv.at[i, k - 1], at.to_z(k))

    def own(self, i):
        at = self.at
        return pltpu.make_async_copy(self.src.at[i], self.buf.at[i, at.z, at.y, at.x, at.c], self.local.at[i])

    def xy_copies(self, i, step):
        at, b = self.at, self.buf.at[i]
        y, x, c = at.y, at.x, at.c
        lo, hi = pl.ds(0, 16), pl.ds(16, 16)
        if step == 2:
            a, d = b.at[:, y, x, c, lo], b.at[:, y, x, c, hi]
            return [
                remote(a, a, self.send.at[i, 3], self.recv.at[i, 3], at.to_x),
                remote(d, d, self.send.at[i, 4], self.recv.at[i, 4], at.to_y),
            ]
        a, d = b.at[:, y, :, c, lo], b.at[:, :, x, c, hi]
        return [
            remote(a, a, self.send.at[i, 5], self.recv.at[i, 5], at.to_y),
            remote(d, d, self.send.at[i, 6], self.recv.at[i, 6], at.to_x),
        ]

    def xy_landed(self, i, step):
        at, b = self.at, self.buf.at[i]
        refs = self.step_refs(i, step, at.c)
        base = 3 if step == 2 else 5
        return [remote(r, r, self.send.at[i, base + q], self.recv.at[i, base + q], at.to_x) for q, r in enumerate(refs)]

    def core_copies(self, i, step):
        at = self.at
        base = {1: 7, 2: 8, 3: 10}[step]
        return [remote(r, r, self.send.at[i, base + q], self.recv.at[i, base + q], at.to_c) for q, r in enumerate(self.step_refs(i, step, at.c))]

    def core_landed(self, i, step):
        at = self.at
        base = {1: 7, 2: 8, 3: 10}[step]
        return [remote(r, r, self.send.at[i, base + q], self.recv.at[i, base + q], at.to_c) for q, r in enumerate(self.step_refs(i, step, 1 - at.c))]

    def start(self, first, last):
        def go(i, _):
            self.own(i).start()
            return 0

        lax.fori_loop(first, last, go, 0)

    def tick(self, t, parts=(5, 4, 3, 2, 1)):
        def one():
            for k in (1, 2, 3):
                self.z_copy(t, k).start()

        def two():
            i = t - 1
            for k in (1, 2, 3):
                self.z_landed(i, k).wait_recv()
            self.own(i).wait()
            for cp in self.xy_copies(i, 2) + self.core_copies(i, 1):
                cp.start()

        def three():
            i = t - 2
            for cp in self.xy_landed(i, 2):
                cp.wait_recv()
            for cp in self.xy_copies(i, 3) + self.core_copies(i, 2):
                cp.start()

        def four():
            i = t - 3
            for cp in self.xy_landed(i, 3):
                cp.wait_recv()
            for cp in self.core_copies(i, 3):
                cp.start()

        def five():
            i = t - 4
            for step in (1, 2, 3):
                for cp in self.core_landed(i, step):
                    cp.wait_recv()

        for part in parts:
            i = t - part + 1
            when((i >= 0) & (i < self.count), (one, two, three, four, five)[part - 1])

    def finish(self):
        def go(i, _):
            for k in (1, 2, 3):
                self.z_copy(i, k).wait_send()
            for step in (2, 3):
                for cp in self.xy_copies(i, step):
                    cp.wait_send()
            for step in (1, 2, 3):
                for cp in self.core_copies(i, step):
                    cp.wait_send()
            return 0

        lax.fori_loop(0, self.count, go, 0)


def dot(a,b,dn=None):
    if dn is None: return jnp.dot(a,b,preferred_element_type=f32)
    return lax.dot_general(a,b,dn,preferred_element_type=f32)

def lane_half(x, hh):
    lane=lax.broadcasted_iota(jnp.int32, x.shape, 1)
    keep=(lane<64) if hh==0 else (lane>=64)
    return jnp.where(keep, x, jnp.zeros_like(x))

def gelu_pair(u):
    u2=u*u
    t=jnp.tanh(gc*(u+0.044715*u2*u))
    return 0.5*u*(1.0+t), 0.5*(1.0+t)+0.5*u*(1.0-t*t)*gc*(1.0+3.0*0.044715*u2)
def nrm(v):
    c=v-jnp.mean(v,axis=-1,keepdims=True)
    r=lax.rsqrt(jnp.mean(c*c,axis=-1,keepdims=True)+1e-6)
    return c*r,r
def rows_loop(n, R, f):
    def body(i,_):
        f(pl.ds(pl.multiple_of(i*R,R),R)); return 0
    lax.fori_loop(0,n//R,body,0)

def kb_kernel(R, tok, gout, attnT, mod, bias, bup, wall,
      bo_ref, dx1_ref, dat_ref, dw_h, dwout_ref, dmod_ref, db_ref, dbup_ref,
      h2, h2T, dzb, dzT, z, dh2, o_s, wout, wbuf, act, du, dwst, wsem, osem, wosem):
    def co(g): return pltpu.make_async_copy(wall.at[g, :, 768:1024], wout.at[:, g*256:(g+1)*256], wosem.at[g])
    for g in range(4): co(g).start()
    def fetch(j, slot):
        pltpu.make_async_copy(wall.at[4 + j], wbuf.at[slot], wsem.at[slot]).start()
    fetch(0,0)
    shift1=mod[0:1];scale1=mod[1:2];gate1=mod[2:3];shift2=mod[3:4];scale2=mod[4:5];gate2=mod[5:6]
    db_ref[...]=jnp.zeros_like(db_ref); dmod_ref[...]=jnp.zeros_like(dmod_ref)
    for g in range(4): co(g).wait()
    def pre(r):
        o=dot(attnT[:,r],wout[...],TN)+bias[2:3]
        o_s[r,:]=o
        x1=tok[r,:].astype(f32)+gate1*o
        xh,_=nrm(x1)
        h2[r,:]=(xh*(1.0+scale2)+shift2).astype(bf)
        dz=gout[r,:].astype(f32)*gate2
        dzb[r,:]=dz.astype(bf)
        db_ref[3:4]+=jnp.sum(dz,axis=0,keepdims=True)
    rows_loop(S,256,pre)
    for i in range(4):
        r=slice(i*256,(i+1)*256)
        h2T[:,r]=h2[r,:].T
        dzT[:,r]=dzb[r,:].T
    z[...]=jnp.zeros_like(z); dh2[...]=jnp.zeros_like(dh2)
    def chunk(j,_):
        slot=lax.rem(j,2)
        @pl.when(j+1<NJ)
        def _(): fetch(j+1,1-slot)
        pltpu.make_async_copy(wall.at[4 + j], wbuf.at[slot], wsem.at[slot]).wait()
        dbup_ref[j]=jnp.zeros((1,CH),f32)
        def row(r):
            u=dot(h2[r,:],wbuf[slot,:,:CH])+bup[j]
            a,sl=gelu_pair(u)
            ab=a.astype(bf); act[r,:]=ab
            da=dot(dzb[r,:],wbuf[slot,:,CH:])
            d=da*sl
            dbup_ref[j]+=jnp.sum(d,axis=0,keepdims=True)
            db_=d.astype(bf); du[r,:]=db_
            z[r,:]+=dot(ab,wbuf[slot,:,CH:],NT)
            dh2[r,:]+=dot(db_,wbuf[slot,:,:CH],NT)
        rows_loop(S,R,row)
        @pl.when(j>=2)
        def _():
            pltpu.make_async_copy(dwst.at[slot], dw_h.at[j], osem.at[slot]).wait()
        def wrow(r):
            dwst[slot,0,r,:]=dot(h2T[r,:],du[...])
            dwst[slot,1,r,:]=dot(dzT[r,:],act[...])
        rows_loop(D,256,wrow)
        pltpu.make_async_copy(dwst.at[slot], dw_h.at[j], osem.at[slot]).start()
        return 0
    lax.fori_loop(0,NJ,chunk,0)
    for s in range(2): pltpu.make_async_copy(dwst.at[s], dw_h.at[s], osem.at[s]).wait()
    def post(r):
        g=gout[r,:].astype(f32); o=o_s[r,:]
        x1=tok[r,:].astype(f32)+gate1*o
        xh,rstd=nrm(x1)
        zz=z[r,:]+bias[3:4]
        bo_ref[r,:]=(x1+gate2*zz).astype(bf)
        dmod_ref[5:6]+=jnp.sum(g*zz,axis=0,keepdims=True)
        dh=dh2[r,:]
        dmod_ref[3:4]+=jnp.sum(dh,axis=0,keepdims=True)
        dmod_ref[4:5]+=jnp.sum(dh*xh,axis=0,keepdims=True)
        gg=dh*(1.0+scale2)
        dx1=g+rstd*(gg-jnp.mean(gg,axis=-1,keepdims=True)-xh*jnp.mean(gg*xh,axis=-1,keepdims=True))
        dx1_ref[r,:]=dx1
        dmod_ref[2:3]+=jnp.sum(dx1*o,axis=0,keepdims=True)
        do=dx1*gate1
        db_ref[2:3]+=jnp.sum(do,axis=0,keepdims=True)
        dob=do.astype(bf)
        dzb[r,:]=dob
        t=dot(dob,wout[...],NT).astype(bf)
        for g4 in range(4): dat_ref[g4,r,:]=t[:,g4*256:(g4+1)*256]
    rows_loop(S,128,post)
    def wo(r):
        dwout_ref[r,:]=dot(attnT[r,:],dzb[...])
    rows_loop(D,256,wo)

def kb(R,*a):
    V=pl.BlockSpec(memory_space=pltpu.VMEM); A=pl.BlockSpec(memory_space=pl.ANY)
    sd=jax.ShapeDtypeStruct
    return pl.pallas_call(functools.partial(kb_kernel,R),
      out_shape=(sd((S,D),bf),sd((S,D),f32),sd((4,S,256),bf),sd((NJ,2,D,CH),f32),sd((D,D),f32),sd((8,D),f32),sd((8,D),f32),sd((NJ,1,CH),f32)),
      in_specs=[V]*6+[A], out_specs=[V,V,V,A,V,V,V,V],
      scratch_shapes=[pltpu.VMEM((S,D),bf)]*4+[pltpu.VMEM((S,D),f32)]*3+[pltpu.VMEM((D,D),bf),pltpu.VMEM((2,D,2*CH),bf),pltpu.VMEM((S,CH),bf),pltpu.VMEM((S,CH),bf),
         pltpu.VMEM((2,2,D,CH),f32),pltpu.SemaphoreType.DMA((2,)),pltpu.SemaphoreType.DMA((2,)),pltpu.SemaphoreType.DMA((4,))],
      compiler_params=pltpu.CompilerParams(vmem_limit_bytes=62*2**20), name=f"kb{R}")(*a)

def ka_kernel(tok, mod, bqkv, wall, qkv, attnT, lse, h1T, h1, wbuf, wsem):
    c = LOG2E / 8.0

    def cp(g, slot):
        return pltpu.make_async_copy(wall.at[g, :, 0:768], wbuf.at[slot], wsem.at[slot])

    cp(0, 0).start()
    shift1, scale1 = mod[0:1], mod[1:2]

    def ln(r):
        xh, _ = nrm(tok[r, :].astype(f32))
        h1[r, :] = (xh * (1.0 + scale1) + shift1).astype(bf)

    rows_loop(S, 128, ln)
    for i in range(4):
        r = slice(i * 256, (i + 1) * 256)
        h1T[:, r] = h1[r, :].T

    def group(g, _):
        slot = lax.rem(g, 2)
        when(g < 3, lambda: cp(g + 1, 1 - slot).start())
        cp(g, slot).wait()

        def proj(r):
            qkv[g, r, :] = (dot(h1[r, :], wbuf[slot]) + bqkv[g]).astype(bf)

        rows_loop(S, 256, proj)
        for p in range(2):
            kp = qkv[g, :, 256 + p * 128 : 256 + (p + 1) * 128]
            vT = qkv[g, :, 512 + p * 128 : 512 + (p + 1) * 128].T
            q = qkv[g, :, p * 128 : (p + 1) * 128]
            for h in range(2):
                s = dot(lane_half(kp, h), q, NT)
                m = jnp.max(s, axis=0, keepdims=True)
                e = jnp.exp2((s - m) * c)
                l = jnp.sum(e, axis=0, keepdims=True)
                pr = (e * (1.0 / l)).astype(bf)
                o = dot(vT[h * 64 : (h + 1) * 64], pr)
                lse[g, p * 2 + h : p * 2 + h + 1, :] = m * 0.125 + jnp.log(l)
                attnT[pl.ds(pl.multiple_of(g * 256 + (p * 128 + h * 64), 64), 64), :] = o.astype(bf)
        return 0

    lax.fori_loop(0, 4, group, 0)


def ka(*a):
    return pl.pallas_call(
        ka_kernel,
        out_shape=(sd((4, S, 768), bf), sd((D, S), bf), sd((4, 4, S), f32), sd((D, S), bf)),
        in_specs=[V, V, V, A],
        out_specs=[V] * 4,
        scratch_shapes=[pltpu.VMEM((S, D), bf), pltpu.VMEM((2, D, 768), bf), pltpu.SemaphoreType.DMA((2,))],
        compiler_params=pltpu.CompilerParams(vmem_limit_bytes=60 * 2**20),
        name="attention_forward",
    )(*a)


def kc_kernel(QB, tok, mod, qkv, dat, lse, dx1, h1T, w_h, ig, dw_h, dmod, dbq, dqkv, dk_s, dv_s, dqT_s, dh1, wbuf, dwst, wsem, osem):
    c=LOG2E/8.0
    def cp(g,slot): return pltpu.make_async_copy(w_h.at[g, :, 0:768], wbuf.at[slot], wsem.at[slot])
    def co(g,slot): return pltpu.make_async_copy(dwst.at[slot], dw_h.at[g], osem.at[slot])
    cp(0,0).start()
    dh1[...]=jnp.zeros_like(dh1); dmod[...]=jnp.zeros_like(dmod); dbq[...]=jnp.zeros_like(dbq)
    def group(g,_):
        slot=lax.rem(g,2)
        @pl.when(g<3)
        def _(): cp(g+1,1-slot).start()
        for p in range(2):
            sl=slice(p*128,(p+1)*128); slk=slice(256+p*128,256+(p+1)*128); slv=slice(512+p*128,512+(p+1)*128)
            kp=qkv[g,:,slk]; vp=qkv[g,:,slv]
            ks=[lane_half(kp,h) for h in range(2)]; vs=[lane_half(vp,h) for h in range(2)]
            kT=kp.T
            dk_s[...]=jnp.zeros_like(dk_s); dv_s[...]=jnp.zeros_like(dv_s)
            def qblk(i,_):
                r=pl.ds(pl.multiple_of(i*QB,QB),QB)
                q=qkv[g,r,sl]; da=dat[g,r,sl]
                for h in range(2):
                    s=dot(ks[h],q,NT)
                    pT=jnp.exp2(s*c-lse[g,p*2+h:p*2+h+1,r]*LOG2E)
                    dp=dot(vs[h],da,NT)
                    delta=jnp.sum(pT*dp,axis=0,keepdims=True)
                    ds=(pT*(dp-delta)).astype(bf)
                    dv_s[...]+=dot(pT.astype(bf),lane_half(da,h))
                    dk_s[...]+=dot(ds,lane_half(q,h))
                    dqT_s[h*64:(h+1)*64,r]=dot(kT[h*64:(h+1)*64],ds)
                return 0
            lax.fori_loop(0,S//QB,qblk,0)
            dq=dqT_s[...].T*0.125
            dbq[g,:,sl]=jnp.sum(dq,axis=0,keepdims=True)
            dqkv[:,sl]=dq.astype(bf)
            dqkv[:,slk]=(dk_s[...]*0.125).astype(bf)
            dbq[g,:,slv]=jnp.sum(dv_s[...],axis=0,keepdims=True)
            dqkv[:,slv]=dv_s[...].astype(bf)
        cp(g,slot).wait()
        @pl.when(g>=2)
        def _(): co(g,slot).wait()
        def wrow(r):
            dwst[slot,r,:]=dot(h1T[r,:],dqkv[...])
            dh1[r,:]+=dot(dqkv[r,:],wbuf[slot],NT)
        rows_loop(D,256,wrow)
        co(g,slot).start()
        return 0
    lax.fori_loop(0,4,group,0)
    for s_ in range(2): co(s_,s_).wait()
    scale1=mod[1:2]
    def post(r):
        xh,rstd=nrm(tok[r,:].astype(f32))
        dh=dh1[r,:]
        dmod[0:1]+=jnp.sum(dh,axis=0,keepdims=True)
        dmod[1:2]+=jnp.sum(dh*xh,axis=0,keepdims=True)
        gg=dh*(1.0+scale1)
        ig[r,:]=dx1[r,:]+rstd*(gg-jnp.mean(gg,axis=-1,keepdims=True)-xh*jnp.mean(gg*xh,axis=-1,keepdims=True))
    rows_loop(S,128,post)
def kc(QB,*a):
    return pl.pallas_call(functools.partial(kc_kernel,QB),
      out_shape=(sd((S,D),f32),sd((4,D,768),f32),sd((8,D),f32),sd((4,1,768),f32)),
      in_specs=[V]*7+[A], out_specs=[V,A,V,V],
      scratch_shapes=[pltpu.VMEM((S,768),bf),pltpu.VMEM((S,128),f32),pltpu.VMEM((S,128),f32),pltpu.VMEM((128,S),f32),pltpu.VMEM((S,D),f32),
        pltpu.VMEM((2,D,768),bf),pltpu.VMEM((2,D,768),f32),pltpu.SemaphoreType.DMA((2,)),pltpu.SemaphoreType.DMA((2,))],
      compiler_params=pltpu.CompilerParams(vmem_limit_bytes=60*2**20), name=f"kc{QB}")(*a)
def when(cond, f):
    @pl.when(cond)
    def _():
        f()


class Pair:
    def __init__(self, at, own, theirs, send, recv, credit, count):
        self.at, self.own, self.theirs, self.sems, self.credit, self.count = at, own, theirs, (send, recv), credit, count

    def copy(self, i, part, cols):
        slot = lax.rem(i, 2)
        return remote(self.own.at[slot, :, cols], self.theirs.at[slot, :, cols], self.sems[0].at[slot, part], self.sems[1].at[slot, part], self.at.to_c)

    def start(self, i, part, cols):
        if part == 0:
            when(i >= 2, lambda: pl.semaphore_wait(self.credit, 1))
        self.copy(i, part, cols).start()

    def sent(self, i, parts):
        for part, cols in enumerate(parts):
            self.copy(i, part, cols).wait_send()

    def arrived(self, i, parts):
        for part, cols in enumerate(parts):
            self.copy(i, part, cols).wait_recv()

    def free(self, i):
        when(i + 2 < self.count, lambda: mesh_signal(self.credit, self.at.to_c))


WHOLE = (slice(0, 1024),)
PARTS = (slice(768, 1024), slice(0, 384), slice(384, 768))


class Scatter:
    shapes = [
        pltpu.VMEM((2, 2, 2, 2, 32, 1024), f32),
        pltpu.VMEM((2, 2, 2, 2, 16, 1024), bf),
        pltpu.VMEM((2, 2, 2, 2, 16, 1024), f32),
        pltpu.VMEM((2, 2, 2, 2, 2, 16, 1024), bf),
        pltpu.VMEM((2, 2, 2, 16, 1024), bf),
        pltpu.VMEM((2, 2, 2, 16, 1024), f32),
        pltpu.VMEM((2, 2, 2, 2, 16, 1024), bf),
        pltpu.VMEM((2, 32, 1024), f32),
        pltpu.VMEM((2, 32, 1024), f32),
        pltpu.VMEM((2, 2, 32, 1024), f32),
        pltpu.VMEM((32, 1024), f32),
        pltpu.VMEM((32, 1024), f32),
        pltpu.VMEM((2, 32, 1024), f32),
        pltpu.SemaphoreType.DMA((6,)),
        pltpu.SemaphoreType.DMA((2, 6)),
        pltpu.SemaphoreType.REGULAR((6,)),
    ]

    def __init__(self, at, refs, out, count, gaps=()):
        self.at, self.out, self.count, self.gaps = at, out, count, gaps
        self.acc, self.s2, self.k2, self.r2, self.s3, self.k3, self.r3, self.s4, self.k4, self.r4, self.s5, self.k5, self.r5, self.send, self.recv, self.credit = refs

    def todo(self, stage, slot):
        at = self.at
        if stage == 2:
            return [(0, self.s2.at[0], self.r2.at[slot, 0], at.to_y), (1, self.s2.at[1], self.r2.at[slot, 1], at.to_x)]
        if stage == 3:
            return [(2, self.s3.at[0], self.r3.at[slot, 0], at.to_x), (3, self.s3.at[1], self.r3.at[slot, 1], at.to_y)]
        if stage == 4:
            return [(4, self.s4, self.r4.at[slot], at.to_b)]
        return [(5, self.s5, self.r5.at[slot], at.to_a)]

    def copies(self, stage, i):
        slot = lax.rem(i, 2)
        return [remote(src, dst, self.send.at[q], self.recv.at[slot, q], dev) for q, src, dst, dev in self.todo(stage, slot)]

    def reuse(self, stage, i):
        def go():
            for cp in self.copies(stage, i - 1):
                cp.wait_send()

        when(i >= 1, go)

    def start(self, stage, i):
        def go():
            for q, _, _, _ in self.todo(stage, 0):
                pl.semaphore_wait(self.credit.at[q], 1)

        when(i >= 2, go)
        for cp in self.copies(stage, i):
            cp.start()

    def arrived(self, stage, i):
        for cp in self.copies(stage, i):
            cp.wait_recv()

    def free(self, stage, i):
        def go():
            for q, _, _, dev in self.todo(stage, 0):
                mesh_signal(self.credit.at[q], dev)

        when(i + 2 < self.count, go)

    def two(self, i, acc):
        y, x = self.at.y, self.at.x
        lo, hi = pl.ds(0, 16), pl.ds(16, 16)
        self.reuse(2, i)
        self.s2[0] = acc[:, :, 1 - y, :, lo, :].astype(bf)
        self.s2[1] = acc[:, :, :, 1 - x, hi, :].astype(bf)
        self.start(2, i)
        self.k2[0] = acc[:, :, y, :, lo, :]
        self.k2[1] = acc[:, :, :, x, hi, :]

    def three(self, i):
        y, x = self.at.y, self.at.x
        slot = lax.rem(i, 2)
        self.arrived(2, i)
        self.reuse(3, i)
        self.s3[0] = (self.k2[0, :, :, 1 - x] + self.r2[slot, 0, :, :, 1 - x].astype(f32)).astype(bf)
        self.s3[1] = (self.k2[1, :, :, 1 - y] + self.r2[slot, 1, :, :, 1 - y].astype(f32)).astype(bf)
        self.start(3, i)
        self.k3[0] = self.k2[0, :, :, x] + self.r2[slot, 0, :, :, x].astype(f32)
        self.k3[1] = self.k2[1, :, :, y] + self.r2[slot, 1, :, :, y].astype(f32)
        self.free(2, i)

    def four(self, i):
        b = self.at.b
        slot = lax.rem(i, 2)
        self.arrived(3, i)
        self.reuse(4, i)
        for h in (0, 1):
            rows = slice(16 * h, 16 * h + 16)
            self.s4[:, rows, :] = self.k3[h, :, 1 - b] + self.r3[slot, h, :, 1 - b].astype(f32)
        self.start(4, i)
        for h in (0, 1):
            rows = slice(16 * h, 16 * h + 16)
            self.k4[:, rows, :] = self.k3[h, :, b] + self.r3[slot, h, :, b].astype(f32)
        self.free(3, i)

    def five(self, i):
        a = self.at.a
        slot = lax.rem(i, 2)
        self.arrived(4, i)
        self.reuse(5, i)
        self.s5[...] = self.k4[1 - a] + self.r4[slot, 1 - a]
        self.start(5, i)
        self.k5[...] = self.k4[a] + self.r4[slot, a]
        self.free(4, i)

    def six(self, i):
        slot = lax.rem(i, 2)
        self.arrived(5, i)
        t = self.k5[...] + self.r5[slot]

        def spread(start, src, width):
            self.out[:, pl.ds(pl.multiple_of(start, 128), width)] = t[:, src : src + width]

        def feed_forward():
            spread(4 * D + i * CH, 0, CH)
            spread(4 * D + FF + i * CH, CH, CH)

        def attention():
            g = i - NJ
            for p in range(2):
                for q in range(3):
                    spread(q * D + g * 256 + p * 128, p * 384 + q * 128, 128)
            spread(3 * D + g * 256, 768, 256)

        when(i < NJ, feed_forward)
        when(i >= NJ, attention)
        self.free(5, i)

    def tick(self, t):
        for lag, f in ((4, self.six), (3, self.five), (2, self.four), (1, self.three)):
            u = t - lag
            live = (u >= 0) & (u < self.count + len(self.gaps))
            piece = u
            for gap in self.gaps:
                live = live & (u != gap)
                piece = piece - jnp.where(u > gap, 1, 0)
            when(live, functools.partial(f, piece))

    def finish(self):
        for stage in (2, 3, 4, 5):
            for cp in self.copies(stage, self.count - 1):
                cp.wait_send()


def block_kernel(n, tok, gout, small, weights,
                 bo, ig, gw, bsum, crec, wall, dwh, qkvh, dath,
                 mine, ada, gat, condc, rec, dsrc, dall, esrc, erec, csrc, mod, brow, bqkv, bup, dmod, db, dbup, dbq,
                 attnT, h1T, lse, dob, dx1, own, theirs, halfS,
                 s0, r0, s2, r2, s3, r3, s4, r4, s5, r5, xs, xr, ps, pr, pc, hc, wsem, qsem, osem, stsem, local, send, recv, *sc):
    c = LOG2E / 8.0
    at = Place()
    me = at.me
    gather = Gather(at, mine, wall, local, send, recv, 12)
    pair = Pair(at, own, theirs, ps, pr, pc, NJ + 4)
    scatter = Scatter(at, sc, gw, 12, gaps=(11,))

    def cut(shard):
        load = pltpu.make_async_copy(weights, shard, osem.at[0])
        load.start()
        load.wait()
        for g in range(4):
            for p in range(2):
                for q in range(3):
                    a = q * D + g * 256 + p * 128
                    b = p * 384 + q * 128
                    mine[g, :, b : b + 128] = shard[:, a : a + 128].astype(bf)
            mine[g, :, 768:] = shard[:, 3 * D + g * 256 : 3 * D + (g + 1) * 256].astype(bf)
        gather.start(0, 4)
        for j in range(NJ):
            for q in range(2):
                a = 4 * D + q * FF + j * CH
                mine[4 + j, :, q * CH : (q + 1) * CH] = shard[:, a : a + CH].astype(bf)
        gather.start(4, 12)
        for q in range(6):
            a = 4 * D + 2 * FF + q * D
            ada[at.c, :, q * D : (q + 1) * D] = shard[:, a : a + D].astype(bf)

    greet_all(n, me, lambda: pl.run_scoped(cut, pltpu.VMEM((32, 18 * D), f32)))
    gather.tick(0)
    trade_ada = remote(ada.at[at.c], ada.at[at.c], xs.at[4], xr.at[4], at.to_c)
    trade_ada.start()
    each_peer(n, me, lambda k, to, fr: remote(small, gat.at[me // 2, at.c], s0.at[k], r0.at[k], to).start())
    gat[pl.ds(me // 2, 1), pl.ds(at.c, 1)] = small[...].reshape(1, 1, 16, 128)
    db[...] = jnp.zeros_like(db)
    dmod[...] = jnp.zeros_like(dmod)

    def bias_into(biases, ref, row, start, lead):
        for q in range(lead):
            k = start + q
            ref[row, :, q * 64 : (q + 1) * 64] = biases[k // 7, k % 7 : k % 7 + 1, 0:64]

    def fetch(i, wbuf, slot):
        return pltpu.make_async_copy(wall.at[i], wbuf.at[slot], wsem.at[slot])

    def bias_from(k, piece):
        esrc[k // 7, :, 2 * D + (k % 7) * 64 : 2 * D + (k % 7 + 1) * 64] = piece

    def ada_columns(x, q):
        cols = slice(q * 512, (q + 1) * 512)
        gw[:, 4 * D + 2 * FF + q * 512 : 4 * D + 2 * FF + (q + 1) * 512] = dot(condc[...], x, TN)
        return dot(x, ada[pl.ds(at.c, 1), :, cols].reshape(32, 512), NT)

    def qkv_out(g, qkv):
        return pltpu.make_async_copy(qkv.at[lax.rem(g, 2)], qkvh.at[g], qsem.at[lax.rem(g, 2)])

    def qkv_in(g, qkv):
        return pltpu.make_async_copy(qkvh.at[g], qkv.at[lax.rem(g, 2)], qsem.at[lax.rem(g, 2)])

    def matrix(wbuf, slot, cols):
        return wbuf[slot, :, :, :, :, :, cols].reshape(D, cols.stop - cols.start)

    lead, tail = pl.ds(0, 2 * D), pl.ds(2 * D, 4 * D)

    def attention(h1, wbuf, qkv, part, biases, conds):
        def norm_one(r):
            xh, _ = nrm(tok[r, :].astype(f32))
            dx1[r, :] = xh

        rows_loop(S, 128, norm_one)
        each_peer(n, me, lambda k, to, fr: remote(small, gat.at[fr // 2, lax.rem(fr, 2)], s0.at[k], r0.at[k], to).wait())
        biases[...] = gat[...].astype(f32).reshape(n, 16, 128)[:, 8:16]
        conds[...] = gat[...].astype(f32).reshape(n // 2, 2, 16, 128)[:, :, 0:8]
        lane = lax.broadcasted_iota(jnp.int32, (128, 64), 0)
        want = lax.rem(me // 2, 2) * 64 + lax.broadcasted_iota(jnp.int32, (128, 64), 1)
        pick = jnp.where(lane == want, 1.0, 0.0).astype(bf)
        wanted = conds[:, :, pl.ds(me // 4, 1), :].reshape(n, 128).astype(bf)
        both = dot(wanted, pick)
        condc[...] = jnp.where(at.c == 0, both[:, 0:32], both[:, 32:64]).astype(bf)
        mates = dot(conds[:, pl.ds(at.c, 1), pl.ds(me // 4, 1), :].reshape(n // 2, 128).astype(bf), pick).astype(bf)
        trade_ada.wait_send()
        remote(ada.at[at.c], ada.at[1 - at.c], xs.at[4], xr.at[4], at.to_c).wait_recv()

        def columns(q):
            cols = slice(q * 512, (q + 1) * 512)
            part[:, :, cols] = dot(mates, ada[:, :, cols].reshape(64, 512)).reshape(n // 2, 1, 512)

        for q in range(4):
            columns(q)
        each_mate(n, me, lambda k, to, fr: remote(part.at[to // 2, :, lead], rec.at[me // 2, :, lead], s2.at[0, k], r2.at[0, k], to).start())
        gather.tick(1)
        for q in range(4, 12):
            columns(q)
        rec[pl.ds(me // 2, 1)] = part[pl.ds(me // 2, 1)]
        for q in range(6):
            bias_into(biases, mod, q, 128 + 16 * q, 16)
        bias_into(biases, brow, 0, 32, 16)
        bias_into(biases, brow, 1, 112, 16)
        for j in range(NJ):
            bias_into(biases, bup, j, 48 + 8 * j, 8)
        for g in range(4):
            bqkv[g] = jnp.zeros((1, 768), f32)
            for q in range(4):
                for first, offset in ((0, 0), (16, 256)):
                    k = first + g * 4 + q
                    to = (q // 2) * 384 + offset + (q % 2) * 64
                    bqkv[g, :, to : to + 64] = biases[k // 7, k % 7 : k % 7 + 1, 0:64]
        gather.tick(2)
        each_mate(n, me, lambda k, to, fr: remote(part.at[to // 2, :, lead], rec.at[fr // 2, :, lead], s2.at[0, k], r2.at[0, k], to).wait())
        each_mate(n, me, lambda k, to, fr: remote(part.at[to // 2, :, tail], rec.at[me // 2, :, tail], s2.at[1, k], r2.at[1, k], to).start())
        for q in range(2):
            mod[q] += jnp.sum(rec[:, :, q * D : (q + 1) * D], axis=0)
        shift1, scale1 = mod[0], mod[1]

        def modulate(r):
            h1[r, :] = (dx1[r, :] * (1.0 + scale1) + shift1).astype(bf)

        rows_loop(S, 128, modulate)
        for i in range(4):
            r = slice(i * 256, (i + 1) * 256)
            h1T[:, :, :, r] = h1[r, :].T.reshape(16, 2, 32, 256)
        gather.tick(3, (4,))
        gather.tick(4, (5,))
        fetch(0, wbuf, 0).start()
        gather.tick(3, (3, 2, 1))

        def group(g, _):
            slot = lax.rem(g, 2)
            fetch(g, wbuf, slot).wait()
            when(g >= 2, lambda: qkv_out(g - 2, qkv).wait())
            w = matrix(wbuf, slot, slice(0, 768))

            def proj(r):
                qkv[slot, r, :] = (dot(h1[r, :], w) + bqkv[g]).astype(bf)

            rows_loop(S, 256, proj)
            qkv_out(g, qkv).start()
            when(g == 0, lambda: gather.tick(4, (4, 3, 2, 1)))
            for p in range(2):
                kp = qkv[slot, :, p * 384 + 128 : p * 384 + 256]
                vT = qkv[slot, :, p * 384 + 256 : p * 384 + 384].T
                q = qkv[slot, :, p * 384 : p * 384 + 128]
                scores = [dot(lane_half(kp, h), q, NT) for h in range(2)]
                probs = []
                for h in range(2):
                    m = jnp.max(scores[h], axis=0, keepdims=True)
                    e = jnp.exp2((scores[h] - m) * c)
                    l = jnp.sum(e, axis=0, keepdims=True)
                    probs.append((e * (1.0 / l)).astype(bf))
                    lse[g, p * 2 + h : p * 2 + h + 1, :] = m * 0.125 + jnp.log(l)
                for h in range(2):
                    o = dot(vT[h * 64 : (h + 1) * 64], probs[h])
                    attnT[pl.ds(g * 4 + p * 2 + h, 1)] = o.astype(bf).reshape(1, 2, 32, S)
            gather.tick(5 + g)
            when(g < 3, lambda: fetch(g + 1, wbuf, 1 - slot).start())
            return 0

        lax.fori_loop(0, 4, group, 0)
        for g in (2, 3):
            qkv_out(g, qkv).wait()
        each_mate(n, me, lambda k, to, fr: remote(part.at[to // 2, :, tail], rec.at[fr // 2, :, tail], s2.at[1, k], r2.at[1, k], to).wait())
        for q in range(2, 6):
            mod[q] += jnp.sum(rec[:, :, q * D : (q + 1) * D], axis=0)

    pl.run_scoped(
        attention,
        pltpu.VMEM((S, D), bf),
        pltpu.VMEM((2, 4, 2, 2, 2, 32, 1024), bf),
        pltpu.VMEM((2, S, 768), bf),
        pltpu.VMEM((n // 2, 1, 6 * D), f32),
        pltpu.VMEM((n, 8, 128), f32),
        pltpu.VMEM((n // 2, 2, 8, 128), f32),
    )

    def unstage(i):
        return pltpu.make_async_copy(dwh.at[i], scatter.acc, stsem.at[1])

    def staged(i):
        unstage(i).wait()
        scatter.two(i, scatter.acc)
        when(i + 1 < NJ, lambda: unstage(i + 1).start())

    def mlp(h2, hT, dzT, z, wout, wbuf, accw):
        gate1, shift2, scale2, gate2 = mod[2], mod[3], mod[4], mod[5]

        def stage(i):
            return pltpu.make_async_copy(accw, dwh.at[i], stsem.at[0])

        def co(g):
            return pltpu.make_async_copy(wall.at[g, :, :, :, :, :, 768:1024], wout.at[:, :, :, :, :, g * 256 : (g + 1) * 256], osem.at[g])

        for g in range(4):
            co(g).start()
        fetch(4, wbuf, 0).start()
        for g in range(4):
            co(g).wait()

        def branch(r):
            width = r.size
            return dot(attnT[:, :, :, r].reshape(D, width), wout[...].reshape(D, D), TN) + brow[0]

        def pre(r):
            x1 = tok[r, :].astype(f32) + gate1 * branch(r)
            xh, _ = nrm(x1)
            h2[r, :] = (xh * (1.0 + scale2) + shift2).astype(bf)
            dz = gout[r, :].astype(f32) * gate2
            dob[r, :] = dz.astype(bf)
            db[1] += jnp.sum(dz, axis=0, keepdims=True)

        def pre_block(i, _):
            pre(pl.ds(pl.multiple_of(i * 256, 256), 256))
            when(i == 1, lambda: gather.tick(9, (5, 3)))
            when(i == 3, lambda: gather.tick(9, (4, 2, 1)))
            return 0

        lax.fori_loop(0, 4, pre_block, 0)
        for i in range(4):
            r = slice(i * 256, (i + 1) * 256)
            hT[:, :, :, r] = h2[r, :].T.reshape(16, 2, 32, 256)
            dzT[:, :, :, r] = dob[r, :].T.reshape(16, 2, 32, 256)
        halves = [
            remote(hT.at[:, 1 - at.c], halfS.at[0], xs.at[0], xr.at[0], at.to_c),
            remote(dzT.at[:, 1 - at.c], halfS.at[1], xs.at[1], xr.at[1], at.to_c),
        ]
        for cp in halves:
            cp.start()
        z[...] = jnp.zeros_like(z)
        dx1[...] = jnp.zeros_like(dx1)

        def chunk(j, _):
            when(j >= 1, lambda: gather.tick(9 + j, (4, 2, 1)))

            def forward():
                slot = lax.rem(j, 2)
                when(j + 1 < NJ, lambda: fetch(5 + j, wbuf, 1 - slot).start())
                fetch(4 + j, wbuf, slot).wait()
                when(j >= 2, lambda: pair.sent(j - 2, WHOLE))
                dbup[j] = jnp.zeros((1, CH), f32)

                w_up, w_dn = matrix(wbuf, slot, slice(0, CH)), matrix(wbuf, slot, slice(CH, 2 * CH))
                blocks = (slice(0, 512), slice(512, 1024))
                ups = [dot(h2[r, :], w_up) + bup[j] for r in blocks]
                backs = [dot(dob[r, :], w_dn) for r in blocks]
                for r, u, back_ in zip(blocks, ups, backs):
                    a, sl = gelu_pair(u)
                    ab = a.astype(bf)
                    own[slot, r, CH:] = ab
                    d = back_ * sl
                    dbup[j] += jnp.sum(d, axis=0, keepdims=True)
                    db_ = d.astype(bf)
                    own[slot, r, :CH] = db_
                    z[r, :] += dot(ab, w_dn, NT)
                    dx1[r, :] += dot(db_, w_up, NT)

                pair.start(j, 0, WHOLE[0])

            when(j < NJ, forward)
            gather.tick(10 + j, (5, 3))
            scatter.tick(j - 5)
            when(j >= 5, lambda: staged(j - 5))
            when(j == 4, lambda: unstage(0).start())

            def weights():
                i = j - 1
                slot = lax.rem(i, 2)
                when(j == 1, lambda: [cp.wait_recv() for cp in halves])
                pair.arrived(i, WHOLE)
                when(i >= 1, lambda: stage(i - 1).wait())
                for q, lhs in enumerate((hT, dzT)):
                    cols = slice(q * CH, (q + 1) * CH)
                    t = dot(lhs[:, at.c].reshape(512, S), own[slot, :, cols]) + dot(halfS[q].reshape(512, S), theirs[slot, :, cols])
                    accw[:, :, :, :, :, cols] = t.reshape(2, 2, 2, 2, 32, CH)
                pair.free(i)
                stage(i).start()

            when(j >= 1, weights)
            return 0

        lax.fori_loop(0, NJ + 1, chunk, 0)
        mesh_signal(hc, at.to_c)
        stage(NJ - 1).wait()
        for cp in halves:
            cp.wait_send()

        def post(r):
            g = gout[r, :].astype(f32)
            o = branch(r)
            x1 = tok[r, :].astype(f32) + gate1 * o
            xh, rstd = nrm(x1)
            zz = z[r, :] + brow[1]
            h2[r, :] = (x1 + gate2 * zz).astype(bf)
            dmod[5] += jnp.sum(g * zz, axis=0, keepdims=True)
            dh = dx1[r, :]
            dmod[3] += jnp.sum(dh, axis=0, keepdims=True)
            dmod[4] += jnp.sum(dh * xh, axis=0, keepdims=True)
            gg = dh * (1.0 + scale2)
            dx = g + rstd * (gg - jnp.mean(gg, axis=-1, keepdims=True) - xh * jnp.mean(gg * xh, axis=-1, keepdims=True))
            dx1[r, :] = dx
            dmod[2] += jnp.sum(dx * o, axis=0, keepdims=True)
            do = dx * gate1
            db[0] += jnp.sum(do, axis=0, keepdims=True)
            dob_ = do.astype(bf)
            dob[r, :] = dob_
            own[0, r, :] = dot(dob_, wout[...].reshape(D, D), NT).astype(bf)

        pair.sent(NJ - 2, WHOLE)

        def post_half(h):
            def body(i, _):
                post(pl.ds(pl.multiple_of(h * 512 + i * 256, 256), 256))
                return 0

            lax.fori_loop(0, 2, body, 0)

        post_half(0)
        post_half(1)
        outs = [pltpu.make_async_copy(h2, bo, osem.at[0])]
        outs += [pltpu.make_async_copy(own.at[0, :, g * 256 : (g + 1) * 256], dath.at[g], osem.at[1 + g]) for g in range(4)]
        for cp in outs:
            cp.start()
        for cp in outs:
            cp.wait()

    pl.run_scoped(
        mlp,
        pltpu.VMEM((S, D), bf),
        pltpu.VMEM((16, 2, 32, S), bf),
        pltpu.VMEM((16, 2, 32, S), bf),
        pltpu.VMEM((S, D), f32),
        pltpu.VMEM((4, 2, 2, 2, 32, 1024), bf),
        pltpu.VMEM((2, 4, 2, 2, 2, 32, 1024), bf),
        pltpu.VMEM((2, 2, 2, 2, 32, 1024), f32),
    )

    def back(dh1, wbuf, qkv, dat, dk_s, dv_s, dqT_s, accw):
        def dat_in(g):
            return pltpu.make_async_copy(dath.at[g], dat.at[lax.rem(g, 2)], osem.at[lax.rem(g, 2)])

        def load(g):
            qkv_in(g, qkv).start()
            dat_in(g).start()
            fetch(g, wbuf, lax.rem(g, 2)).start()

        load(0)
        pl.semaphore_wait(hc, 1)
        halves = [
            remote(h1T.at[:, 1 - at.c], halfS.at[0], xs.at[2], xr.at[2], at.to_c),
            remote(attnT.at[:, 1 - at.c], halfS.at[1], xs.at[3], xr.at[3], at.to_c),
        ]
        for cp in halves:
            cp.start()
        scatter.tick(4)
        staged(4)
        for q in range(4):
            dsrc[:, q * D : (q + 1) * D] = dmod[2 + q]
        each_mate(n, me, lambda k, to, fr: remote(dsrc, dall.at[at.c, me // 2], s3.at[k], r3.at[k], to).start())
        dall[pl.ds(at.c, 1), pl.ds(me // 2, 1)] = dsrc[...].reshape(1, 1, 1, 4 * D)
        for q in range(16):
            bias_from(32 + q, db[0, :, q * 64 : (q + 1) * 64])
            bias_from(112 + q, db[1, :, q * 64 : (q + 1) * 64])
        for j in range(NJ):
            for q in range(8):
                bias_from(48 + 8 * j + q, dbup[j, :, q * 64 : (q + 1) * 64])
        for k in range(2, 6):
            for q in range(16):
                bias_from(128 + 16 * k + q, dmod[k, :, q * 64 : (q + 1) * 64])
        dh1[...] = jnp.zeros_like(dh1)

        def group(g, _):
            slot = lax.rem(g, 2)
            when(g < 3, lambda: load(g + 1))
            qkv_in(g, qkv).wait()
            dat_in(g).wait()
            when(g == 1, lambda: pair.sent(NJ - 1, WHOLE))
            when(g >= 2, lambda: pair.sent(NJ + g - 2, PARTS))
            own[slot, :, 768:] = dob[:, pl.ds(pl.multiple_of(g * 256, 256), 256)]
            pair.start(NJ + g, 0, PARTS[0])
            for p in range(2):
                if p == 1:
                    scatter.tick(5 + 2 * g)
                    when(g < 2, lambda: staged(5 + 2 * g))
                    when(g == 2, lambda: scatter.two(9, accw))
                sl = slice(p * 128, (p + 1) * 128)
                slq, slk, slv = (slice(p * 384 + q * 128, p * 384 + (q + 1) * 128) for q in range(3))
                kp, vp, q, da = qkv[slot, :, slk], qkv[slot, :, slv], qkv[slot, :, slq], dat[slot, :, sl]
                kT = kp.T
                for h in range(2):
                    s = dot(lane_half(kp, h), q, NT)
                    pT = jnp.exp2(s * c - lse[g, p * 2 + h : p * 2 + h + 1, :] * LOG2E)
                    dp = dot(lane_half(vp, h), da, NT)
                    weighted = pT * dp
                    ds = (weighted - pT * jnp.sum(weighted, axis=0, keepdims=True)).astype(bf)
                    dv = dot(pT.astype(bf), lane_half(da, h))
                    dk = dot(ds, lane_half(q, h))
                    if h == 0:
                        dv_s[...] = dv
                        dk_s[...] = dk
                    else:
                        dv_s[...] += dv
                        dk_s[...] += dk
                    dqT_s[h * 64 : (h + 1) * 64, :] = dot(kT[h * 64 : (h + 1) * 64], ds)
                dq = dqT_s[...].T * 0.125
                dbq[g, :, sl] = jnp.sum(dq, axis=0, keepdims=True)
                own[slot, :, slq] = dq.astype(bf)
                own[slot, :, slk] = (dk_s[...] * 0.125).astype(bf)
                dbq[g, :, 256 + p * 128 : 256 + (p + 1) * 128] = jnp.sum(dv_s[...], axis=0, keepdims=True)
                own[slot, :, slv] = dv_s[...].astype(bf)
                pair.start(NJ + g, 1 + p, PARTS[1 + p])
            fetch(g, wbuf, slot).wait()
            w = matrix(wbuf, slot, slice(0, 768))

            def wrow(r):
                dh1[r, :] += dot(own[slot, r, :768], w, NT)

            rows_loop(D, 256, wrow)
            scatter.tick(6 + 2 * g)

            def at_first():
                staged(6)
                for cp in halves:
                    cp.wait_recv()

            when(g == 0, at_first)
            when(g == 1, lambda: scatter.two(8, accw))

            def pass_on():
                each_mate(n, me, lambda k, to, fr: remote(dsrc, dall.at[at.c, fr // 2], s3.at[k], r3.at[k], to).wait())
                remote(dall.at[at.c], dall.at[at.c], xs.at[5], xr.at[5], at.to_c).start()

            when(g == 1, pass_on)
            pair.arrived(NJ + g, PARTS)
            for q, lhs in enumerate((h1T, attnT)):
                cols = slice(0, 768) if q == 0 else slice(768, 1024)
                t = dot(lhs[:, at.c].reshape(512, S), own[slot, :, cols]) + dot(halfS[q].reshape(512, S), theirs[slot, :, cols])
                accw[:, :, :, :, :, cols] = t.reshape(2, 2, 2, 2, 32, cols.stop - cols.start)
            pair.free(NJ + g)
            when(g >= 2, lambda: scatter.two(8 + g, accw))
            return 0

        lax.fori_loop(0, 4, group, 0)
        for i in (2, 3):
            pair.sent(NJ + i, PARTS)
        for cp in halves:
            cp.wait_send()
        scale1 = mod[1]

        def post(r):
            xh, rstd = nrm(tok[r, :].astype(f32))
            dh = dh1[r, :]
            dmod[0] += jnp.sum(dh, axis=0, keepdims=True)
            dmod[1] += jnp.sum(dh * xh, axis=0, keepdims=True)
            gg = dh * (1.0 + scale1)
            dx1[r, :] += rstd * (gg - jnp.mean(gg, axis=-1, keepdims=True) - xh * jnp.mean(gg * xh, axis=-1, keepdims=True))

        rows_loop(S, 128, post)

    pl.run_scoped(
        back,
        pltpu.VMEM((S, D), f32),
        pltpu.VMEM((2, 4, 2, 2, 2, 32, 1024), bf),
        pltpu.VMEM((2, S, 768), bf),
        pltpu.VMEM((2, S, 256), bf),
        pltpu.VMEM((S, 128), f32),
        pltpu.VMEM((S, 128), f32),
        pltpu.VMEM((128, S), f32),
        pltpu.VMEM((2, 2, 2, 2, 32, 1024), f32),
    )
    done = pltpu.make_async_copy(dx1, ig, osem.at[0])
    done.start()
    for k in range(2):
        for q in range(16):
            bias_from(128 + 16 * k + q, dmod[k, :, q * 64 : (q + 1) * 64])
    for g in range(4):
        for q in range(4):
            bias_from(g * 4 + q, dbq[g, :, q * 64 : (q + 1) * 64])
            bias_from(16 + g * 4 + q, dbq[g, :, 256 + q * 64 : 256 + (q + 1) * 64])
    for k in range(2):
        esrc[:, :, k * D : (k + 1) * D] = jnp.broadcast_to(dmod[k].reshape(1, 1, D), (n, 1, D))
    each_peer(n, me, lambda k, to, fr: remote(esrc.at[to], erec.at[me], s4.at[k], r4.at[k], to).start())
    erec[pl.ds(me, 1)] = esrc[pl.ds(me, 1)]
    scatter.tick(13)
    remote(dall.at[at.c], dall.at[at.c], xs.at[5], xr.at[5], at.to_c).wait_send()
    remote(dall.at[1 - at.c], dall.at[1 - at.c], xs.at[5], xr.at[5], at.to_c).wait_recv()
    total = jnp.zeros((n, 32), f32)
    for q in range(4, 12):
        cols = slice((q - 4) * 512, (q - 3) * 512)
        halves_ = [dall[k, :, :, cols].reshape(n // 2, 1, 512) for k in range(2)]
        total += ada_columns(jnp.concatenate(halves_, axis=1).reshape(n, 512).astype(bf), q)
    scatter.tick(14)
    each_peer(n, me, lambda k, to, fr: remote(esrc.at[to], erec.at[fr], s4.at[k], r4.at[k], to).wait())
    for q in range(4):
        total += ada_columns(erec[:, :, q * 512 : (q + 1) * 512].reshape(n, 512).astype(bf), q)
    csrc[:, :, 0:32] = total.reshape(n, 1, 32)
    each_peer(n, me, lambda k, to, fr: remote(csrc.at[to], crec.at[me], s5.at[k], r5.at[k], to).start())
    crec[pl.ds(me, 1)] = csrc[pl.ds(me, 1)]
    bsum[...] = jnp.sum(erec[:, :, 2 * D :], axis=0)
    scatter.tick(15)
    each_peer(n, me, lambda k, to, fr: remote(csrc.at[to], crec.at[fr], s5.at[k], r5.at[k], to).wait())
    scatter.tick(16)
    done.wait()
    scatter.finish()
    gather.finish()


def block(n, *a):
    dma = pltpu.SemaphoreType.DMA
    regular = pltpu.SemaphoreType.REGULAR
    vm = pltpu.VMEM
    return pl.pallas_call(
        functools.partial(block_kernel, n),
        out_shape=(sd((S, D), bf), sd((S, D), f32), sd((32, 18 * D), f32), sd((1, 512), f32), sd((n, 1, 128), f32))
        + (sd((12, 4, 2, 2, 2, 32, 1024), bf), sd((NJ, 2, 2, 2, 2, 32, 1024), f32), sd((4, S, 768), bf), sd((4, S, 256), bf)),
        in_specs=[V] * 3 + [A],
        out_specs=[A] * 2 + [V] * 3 + [A] * 4,
        scratch_shapes=[vm((12, 32, 1024), bf), vm((2, 32, 6 * D), bf), vm((n // 2, 2, 16, 128), bf), vm((n, 32), bf)]
        + [vm((n // 2, 1, 6 * D), f32), vm((1, 4 * D), f32), vm((2, n // 2, 1, 4 * D), f32), vm((n, 1, 2560), f32), vm((n, 1, 2560), f32), vm((n, 1, 128), f32)]
        + [vm((6, 1, D), f32), vm((2, 1, D), f32), vm((4, 1, 768), f32), vm((NJ, 1, CH), f32), vm((6, 1, D), f32), vm((2, 1, D), f32), vm((NJ, 1, CH), f32), vm((4, 1, 512), f32)]
        + [vm((16, 2, 32, S), bf), vm((16, 2, 32, S), bf), vm((4, 4, S), f32), vm((S, D), bf), vm((S, D), f32)]
        + [vm((2, S, 1024), bf), vm((2, S, 1024), bf), vm((2, 16, 32, S), bf)]
        + [dma((n,))] * 2
        + [dma((2, n))] * 2
        + [dma((n,))] * 6
        + [dma((6,)), dma((6,)), dma((2, 3)), dma((2, 3)), regular, regular]
        + [dma((2,)), dma((2,)), dma((5,)), dma((2,))]
        + gather_sems(12)
        + Scatter.shapes,
        compiler_params=pltpu.CompilerParams(collective_id=0, has_side_effects=True, vmem_limit_bytes=VMEM_BYTES),
        name="block",
    )(*a)


def adam_step(param, grad, first, second, decay):
    new_first = beta_first * first + (1.0 - beta_first) * grad
    new_second = beta_second * second + (1.0 - beta_second) * grad * grad
    step_size = learn_rate / (1.0 - beta_first**STEP)
    denom = jnp.sqrt(new_second / (1.0 - beta_second**STEP)) + adam_eps
    new_param = param - step_size * new_first / denom - learn_rate * decay * param
    return (new_param, new_first, new_second)


def plain(n, tok, gout, condition, weights, biases):
    me = lax.axis_index("dp")
    rows = D // n
    wb = weights.astype(bf)
    qkvo = wb[:, : 4 * D].reshape(rows, 4, 4, 256).transpose(2, 0, 1, 3).reshape(4, rows, 1024)
    updn = wb[:, 4 * D : 4 * D + 2 * FF].reshape(rows, 2, NJ, CH).transpose(2, 0, 1, 3).reshape(NJ, rows, 1024)
    mine = jnp.concatenate([qkvo, updn], axis=0)
    ada_l = wb[:, 4 * D + 2 * FF :]
    cond_act = jax.nn.silu(condition).astype(bf)
    bias_full = lax.all_gather(biases.astype(bf), "dp", axis=0, tiled=True).astype(f32)
    cond_all = lax.all_gather(cond_act, "dp", axis=0, tiled=True)
    cond_cols = lax.dynamic_slice_in_dim(cond_all, me * rows, rows, 1)
    mod = lax.psum_scatter(jnp.dot(cond_cols, ada_l, preferred_element_type=f32), "dp", scatter_dimension=0, tiled=True)
    mod = jnp.concatenate([(mod[0] + bias_full[4 * D + FF :]).reshape(6, D), jnp.zeros((2, D), f32)], axis=0)
    zrow = jnp.zeros((D,), f32)
    bqkv = jnp.stack([bias_full[:D], zrow, bias_full[D : 2 * D]]).reshape(3, 4, 256).transpose(1, 0, 2).reshape(4, 1, 768)
    brows = jnp.stack([zrow, zrow, bias_full[2 * D : 3 * D], bias_full[3 * D + FF : 4 * D + FF], zrow, zrow, zrow, zrow])
    bup = bias_full[3 * D : 3 * D + FF].reshape(NJ, 1, CH)
    wall = lax.all_gather(mine, "dp", axis=1, tiled=True)
    qkv, attn_t, lse, h1t = ka(tok, mod, bqkv, wall)
    bo, dx1, dat, dw_mlp, dw_out, dmod_b, db, db_up = kb(512, tok, gout, attn_t, mod, brows, bup, wall)
    ig, dw_qkv, dmod_a, db_qkv = kc(1024, tok, mod, qkv, dat, lse, dx1, h1t, wall)
    g_mlp = lax.psum_scatter(dw_mlp, "dp", scatter_dimension=2, tiled=True)
    g_out = lax.psum_scatter(dw_out, "dp", scatter_dimension=0, tiled=True)
    g_qkv = lax.psum_scatter(dw_qkv, "dp", scatter_dimension=1, tiled=True)
    g_qkv = g_qkv.reshape(4, rows, 3, 256).transpose(1, 2, 0, 3).reshape(rows, 3 * D)
    g_mlp = g_mlp.transpose(2, 1, 0, 3).reshape(rows, 2 * FF)
    dmod = (dmod_a + dmod_b)[:6].reshape(1, 6 * D)
    db_qkv = db_qkv.reshape(4, 3, 256).transpose(1, 0, 2).reshape(3, D)
    bias_row = jnp.concatenate([db_qkv[0], db_qkv[2], db[2], db_up.reshape(FF), db[3], dmod[0]])
    bias_grad = lax.psum_scatter(bias_row, "dp", scatter_dimension=0, tiled=True)
    dmod_all = lax.all_gather(dmod.astype(bf), "dp", axis=0, tiled=True)
    g_ada = lax.dot_general(cond_cols, dmod_all, TN, preferred_element_type=f32)
    cond_part = lax.dot_general(dmod_all, ada_l, NT, preferred_element_type=f32)
    cond_grad = lax.all_to_all(cond_part, "dp", split_axis=0, concat_axis=1, tiled=True)
    return bo, ig, cond_grad, jnp.concatenate([g_qkv, g_out, g_mlp, g_ada], axis=1), bias_grad


def on_chips(n, tok, gout, condition, weights, biases):
    cond_act = jax.nn.silu(condition).reshape(8, 128)
    padded = jnp.pad(biases.reshape(7, 64), ((0, 1), (0, 64)))
    bo, ig, weight_grad, bsum, crec = block(n, tok, gout, jnp.concatenate([cond_act, padded]).astype(bf), weights)[:5]
    return bo, ig, crec[:, 0, :32].reshape(1, D), weight_grad, bsum[0, : biases.shape[0]]


def on_device(n, block_in, condition, out_grad, weights, biases, first_moment, second_moment, bias_first, bias_second):
    run = on_chips if n == 32 else plain
    bo, ig, cond_grad, weight_grad, bias_grad = run(n, block_in[0], out_grad[0], condition, weights, biases)
    sigma = jax.nn.sigmoid(condition)
    cond_grad = cond_grad * (sigma * (1.0 + condition * (1.0 - sigma)))
    new_weights, new_first, new_second = adam_step(weights, weight_grad, first_moment, second_moment, weight_decay)
    new_biases, new_bias_first, new_bias_second = adam_step(biases, bias_grad, bias_first, bias_second, 0.0)
    return (bo[None], ig[None], cond_grad, weight_grad, bias_grad, new_weights, new_biases, new_first, new_second, new_bias_first, new_bias_second)


def solution(mesh):
    three, two, one = P("dp", None, None), P("dp", None), P("dp")
    return jax.shard_map(
        functools.partial(on_device, mesh.shape["dp"]),
        mesh=mesh,
        in_specs=(three, two, three, two, one, two, two, one, one),
        out_specs=(three, three, two, two, one, two, one, two, two, one, one),
        check_vma=False,
    )
```

```python
import functools

import jax
import jax.numpy as jnp
from jax import lax
from jax.experimental import pallas as pl
from jax.experimental.pallas import tpu as pltpu
from jax.sharding import PartitionSpec as P

D = 1024
FF = 4096
S = 1024
STEP = 3
CH = 512
NJ = FF // CH
VMEM_BYTES = 64 * 2**20
STEPS = 8
learn_rate = 0.01
beta_first = 0.9
beta_second = 0.95
adam_eps = 1e-08
weight_decay = 0.05
gc = 0.7978845608028654
LOG2E = 1.4426950408889634
f32 = jnp.float32
bf = jnp.bfloat16
NT = (((1,), (1,)), ((), ()))
TN = (((0,), (0,)), ((), ()))
V = pl.BlockSpec(memory_space=pltpu.VMEM)
A = pl.BlockSpec(memory_space=pl.ANY)
sd = jax.ShapeDtypeStruct
MESH = pl.DeviceIdType.MESH


def mesh_signal(sem, dev):
    pl.semaphore_signal(sem, inc=1, device_id=(dev,), device_id_type=MESH)


def remote(src, dst, send, recv, dev):
    return pltpu.make_async_remote_copy(src_ref=src, dst_ref=dst, send_sem=send, recv_sem=recv, device_id=(dev,), device_id_type=MESH)


def greet_all(n, me, between):
    barrier = pltpu.get_barrier_semaphore()

    def go(k, _):
        mesh_signal(barrier, lax.rem(me + k, n))
        return 0

    lax.fori_loop(1, n, go, 0)
    between()
    pl.semaphore_wait(barrier, n - 1)


def each_peer(n, me, f):
    def go(k, _):
        f(k, lax.rem(me + k, n), lax.rem(me + n - k, n))
        return 0

    lax.fori_loop(1, n, go, 0)


def gather_sems(count):
    return [pltpu.SemaphoreType.DMA((count,)), pltpu.SemaphoreType.DMA((count, 12)), pltpu.SemaphoreType.DMA((count, 12))]


def each_mate(n, me, f):
    def go(k, _):
        f(k, lax.rem(me + 2 * k, n), lax.rem(me + n - 2 * k, n))
        return 0

    lax.fori_loop(1, n // 2, go, 0)


class Place:
    def __init__(self):
        me = lax.axis_index("dp")
        self.me = me
        self.z = me // 8
        self.y = lax.rem(me // 4, 2)
        self.x = lax.rem(me // 2, 2)
        self.c = lax.rem(me, 2)
        self.to_c = me + 1 - 2 * self.c
        self.to_x = me + 2 - 4 * self.x
        self.to_y = me + 4 - 8 * self.y
        self.a = self.z // 2
        self.b = lax.rem(self.z, 2)
        self.to_b = me + 8 - 16 * self.b
        self.to_a = me + 16 - 32 * self.a

    def to_z(self, k):
        return lax.rem(self.z + k, 4) * 8 + lax.rem(self.me, 8)


class Gather:
    def __init__(self, at, src, buf, local, send, recv, count):
        self.at, self.src, self.buf, self.local, self.send, self.recv, self.count = at, src, buf, local, send, recv, count

    def step_refs(self, i, step, c):
        at, b = self.at, self.buf.at[i]
        y, x = at.y, at.x
        lo, hi = pl.ds(0, 16), pl.ds(16, 16)
        if step == 1:
            return [b.at[:, y, x, c]]
        if step == 2:
            return [b.at[:, y, 1 - x, c, lo], b.at[:, 1 - y, x, c, hi]]
        return [b.at[:, 1 - y, :, c, lo], b.at[:, :, 1 - x, c, hi]]

    def z_copy(self, i, k):
        at = self.at
        return remote(self.src.at[i], self.buf.at[i, at.z, at.y, at.x, at.c], self.send.at[i, k - 1], self.recv.at[i, k - 1], at.to_z(k))

    def z_landed(self, i, k):
        at = self.at
        zz = lax.rem(at.z + 4 - k, 4)
        return remote(self.src.at[i], self.buf.at[i, zz, at.y, at.x, at.c], self.send.at[i, k - 1], self.recv.at[i, k - 1], at.to_z(k))

    def own(self, i):
        at = self.at
        return pltpu.make_async_copy(self.src.at[i], self.buf.at[i, at.z, at.y, at.x, at.c], self.local.at[i])

    def xy_copies(self, i, step):
        at, b = self.at, self.buf.at[i]
        y, x, c = at.y, at.x, at.c
        lo, hi = pl.ds(0, 16), pl.ds(16, 16)
        if step == 2:
            a, d = b.at[:, y, x, c, lo], b.at[:, y, x, c, hi]
            return [
                remote(a, a, self.send.at[i, 3], self.recv.at[i, 3], at.to_x),
                remote(d, d, self.send.at[i, 4], self.recv.at[i, 4], at.to_y),
            ]
        a, d = b.at[:, y, :, c, lo], b.at[:, :, x, c, hi]
        return [
            remote(a, a, self.send.at[i, 5], self.recv.at[i, 5], at.to_y),
            remote(d, d, self.send.at[i, 6], self.recv.at[i, 6], at.to_x),
        ]

    def xy_landed(self, i, step):
        at, b = self.at, self.buf.at[i]
        refs = self.step_refs(i, step, at.c)
        base = 3 if step == 2 else 5
        return [remote(r, r, self.send.at[i, base + q], self.recv.at[i, base + q], at.to_x) for q, r in enumerate(refs)]

    def core_copies(self, i, step):
        at = self.at
        base = {1: 7, 2: 8, 3: 10}[step]
        return [remote(r, r, self.send.at[i, base + q], self.recv.at[i, base + q], at.to_c) for q, r in enumerate(self.step_refs(i, step, at.c))]

    def core_landed(self, i, step):
        at = self.at
        base = {1: 7, 2: 8, 3: 10}[step]
        return [remote(r, r, self.send.at[i, base + q], self.recv.at[i, base + q], at.to_c) for q, r in enumerate(self.step_refs(i, step, 1 - at.c))]

    def start(self, first, last):
        def go(i, _):
            self.own(i).start()
            return 0

        lax.fori_loop(first, last, go, 0)

    def tick(self, t, parts=(5, 4, 3, 2, 1)):
        def one():
            for k in (1, 2, 3):
                self.z_copy(t, k).start()

        def two():
            i = t - 1
            for k in (1, 2, 3):
                self.z_landed(i, k).wait_recv()
            self.own(i).wait()
            for cp in self.xy_copies(i, 2) + self.core_copies(i, 1):
                cp.start()

        def three():
            i = t - 2
            for cp in self.xy_landed(i, 2):
                cp.wait_recv()
            for cp in self.xy_copies(i, 3) + self.core_copies(i, 2):
                cp.start()

        def four():
            i = t - 3
            for cp in self.xy_landed(i, 3):
                cp.wait_recv()
            for cp in self.core_copies(i, 3):
                cp.start()

        def five():
            i = t - 4
            for step in (1, 2, 3):
                for cp in self.core_landed(i, step):
                    cp.wait_recv()

        for part in parts:
            i = t - part + 1
            when((i >= 0) & (i < self.count), (one, two, three, four, five)[part - 1])

    def finish(self):
        def go(i, _):
            for k in (1, 2, 3):
                self.z_copy(i, k).wait_send()
            for step in (2, 3):
                for cp in self.xy_copies(i, step):
                    cp.wait_send()
            for step in (1, 2, 3):
                for cp in self.core_copies(i, step):
                    cp.wait_send()
            return 0

        lax.fori_loop(0, self.count, go, 0)


def dot(a,b,dn=None):
    if dn is None: return jnp.dot(a,b,preferred_element_type=f32)
    return lax.dot_general(a,b,dn,preferred_element_type=f32)

def lane_half(x, hh):
    lane=lax.broadcasted_iota(jnp.int32, x.shape, 1)
    keep=(lane<64) if hh==0 else (lane>=64)
    return jnp.where(keep, x, jnp.zeros_like(x))

def gelu_pair(u):
    u2=u*u
    t=jnp.tanh(gc*(u+0.044715*u2*u))
    return 0.5*u*(1.0+t), 0.5*(1.0+t)+0.5*u*(1.0-t*t)*gc*(1.0+3.0*0.044715*u2)
def nrm(v):
    c=v-jnp.mean(v,axis=-1,keepdims=True)
    r=lax.rsqrt(jnp.mean(c*c,axis=-1,keepdims=True)+1e-6)
    return c*r,r
def rows_loop(n, R, f):
    def body(i,_):
        f(pl.ds(pl.multiple_of(i*R,R),R)); return 0
    lax.fori_loop(0,n//R,body,0)

def kb_kernel(R, tok, gout, attnT, mod, bias, bup, wall,
      bo_ref, dx1_ref, dat_ref, dw_h, dwout_ref, dmod_ref, db_ref, dbup_ref,
      h2, h2T, dzb, dzT, z, dh2, o_s, wout, wbuf, act, du, dwst, wsem, osem, wosem):
    def co(g): return pltpu.make_async_copy(wall.at[g, :, 768:1024], wout.at[:, g*256:(g+1)*256], wosem.at[g])
    for g in range(4): co(g).start()
    def fetch(j, slot):
        pltpu.make_async_copy(wall.at[4 + j], wbuf.at[slot], wsem.at[slot]).start()
    fetch(0,0)
    shift1=mod[0:1];scale1=mod[1:2];gate1=mod[2:3];shift2=mod[3:4];scale2=mod[4:5];gate2=mod[5:6]
    db_ref[...]=jnp.zeros_like(db_ref); dmod_ref[...]=jnp.zeros_like(dmod_ref)
    for g in range(4): co(g).wait()
    def pre(r):
        o=dot(attnT[:,r],wout[...],TN)+bias[2:3]
        o_s[r,:]=o
        x1=tok[r,:].astype(f32)+gate1*o
        xh,_=nrm(x1)
        h2[r,:]=(xh*(1.0+scale2)+shift2).astype(bf)
        dz=gout[r,:].astype(f32)*gate2
        dzb[r,:]=dz.astype(bf)
        db_ref[3:4]+=jnp.sum(dz,axis=0,keepdims=True)
    rows_loop(S,256,pre)
    for i in range(4):
        r=slice(i*256,(i+1)*256)
        h2T[:,r]=h2[r,:].T
        dzT[:,r]=dzb[r,:].T
    z[...]=jnp.zeros_like(z); dh2[...]=jnp.zeros_like(dh2)
    def chunk(j,_):
        slot=lax.rem(j,2)
        @pl.when(j+1<NJ)
        def _(): fetch(j+1,1-slot)
        pltpu.make_async_copy(wall.at[4 + j], wbuf.at[slot], wsem.at[slot]).wait()
        dbup_ref[j]=jnp.zeros((1,CH),f32)
        def row(r):
            u=dot(h2[r,:],wbuf[slot,:,:CH])+bup[j]
            a,sl=gelu_pair(u)
            ab=a.astype(bf); act[r,:]=ab
            da=dot(dzb[r,:],wbuf[slot,:,CH:])
            d=da*sl
            dbup_ref[j]+=jnp.sum(d,axis=0,keepdims=True)
            db_=d.astype(bf); du[r,:]=db_
            z[r,:]+=dot(ab,wbuf[slot,:,CH:],NT)
            dh2[r,:]+=dot(db_,wbuf[slot,:,:CH],NT)
        rows_loop(S,R,row)
        @pl.when(j>=2)
        def _():
            pltpu.make_async_copy(dwst.at[slot], dw_h.at[j], osem.at[slot]).wait()
        def wrow(r):
            dwst[slot,0,r,:]=dot(h2T[r,:],du[...])
            dwst[slot,1,r,:]=dot(dzT[r,:],act[...])
        rows_loop(D,256,wrow)
        pltpu.make_async_copy(dwst.at[slot], dw_h.at[j], osem.at[slot]).start()
        return 0
    lax.fori_loop(0,NJ,chunk,0)
    for s in range(2): pltpu.make_async_copy(dwst.at[s], dw_h.at[s], osem.at[s]).wait()
    def post(r):
        g=gout[r,:].astype(f32); o=o_s[r,:]
        x1=tok[r,:].astype(f32)+gate1*o
        xh,rstd=nrm(x1)
        zz=z[r,:]+bias[3:4]
        bo_ref[r,:]=(x1+gate2*zz).astype(bf)
        dmod_ref[5:6]+=jnp.sum(g*zz,axis=0,keepdims=True)
        dh=dh2[r,:]
        dmod_ref[3:4]+=jnp.sum(dh,axis=0,keepdims=True)
        dmod_ref[4:5]+=jnp.sum(dh*xh,axis=0,keepdims=True)
        gg=dh*(1.0+scale2)
        dx1=g+rstd*(gg-jnp.mean(gg,axis=-1,keepdims=True)-xh*jnp.mean(gg*xh,axis=-1,keepdims=True))
        dx1_ref[r,:]=dx1
        dmod_ref[2:3]+=jnp.sum(dx1*o,axis=0,keepdims=True)
        do=dx1*gate1
        db_ref[2:3]+=jnp.sum(do,axis=0,keepdims=True)
        dob=do.astype(bf)
        dzb[r,:]=dob
        t=dot(dob,wout[...],NT).astype(bf)
        for g4 in range(4): dat_ref[g4,r,:]=t[:,g4*256:(g4+1)*256]
    rows_loop(S,128,post)
    def wo(r):
        dwout_ref[r,:]=dot(attnT[r,:],dzb[...])
    rows_loop(D,256,wo)

def kb(R,*a):
    V=pl.BlockSpec(memory_space=pltpu.VMEM); A=pl.BlockSpec(memory_space=pl.ANY)
    sd=jax.ShapeDtypeStruct
    return pl.pallas_call(functools.partial(kb_kernel,R),
      out_shape=(sd((S,D),bf),sd((S,D),f32),sd((4,S,256),bf),sd((NJ,2,D,CH),f32),sd((D,D),f32),sd((8,D),f32),sd((8,D),f32),sd((NJ,1,CH),f32)),
      in_specs=[V]*6+[A], out_specs=[V,V,V,A,V,V,V,V],
      scratch_shapes=[pltpu.VMEM((S,D),bf)]*4+[pltpu.VMEM((S,D),f32)]*3+[pltpu.VMEM((D,D),bf),pltpu.VMEM((2,D,2*CH),bf),pltpu.VMEM((S,CH),bf),pltpu.VMEM((S,CH),bf),
         pltpu.VMEM((2,2,D,CH),f32),pltpu.SemaphoreType.DMA((2,)),pltpu.SemaphoreType.DMA((2,)),pltpu.SemaphoreType.DMA((4,))],
      compiler_params=pltpu.CompilerParams(vmem_limit_bytes=62*2**20), name=f"kb{R}")(*a)

def ka_kernel(tok, mod, bqkv, wall, qkv, attnT, lse, h1T, h1, wbuf, wsem):
    c = LOG2E / 8.0

    def cp(g, slot):
        return pltpu.make_async_copy(wall.at[g, :, 0:768], wbuf.at[slot], wsem.at[slot])

    cp(0, 0).start()
    shift1, scale1 = mod[0:1], mod[1:2]

    def ln(r):
        xh, _ = nrm(tok[r, :].astype(f32))
        h1[r, :] = (xh * (1.0 + scale1) + shift1).astype(bf)

    rows_loop(S, 128, ln)
    for i in range(4):
        r = slice(i * 256, (i + 1) * 256)
        h1T[:, r] = h1[r, :].T

    def group(g, _):
        slot = lax.rem(g, 2)
        when(g < 3, lambda: cp(g + 1, 1 - slot).start())
        cp(g, slot).wait()

        def proj(r):
            qkv[g, r, :] = (dot(h1[r, :], wbuf[slot]) + bqkv[g]).astype(bf)

        rows_loop(S, 256, proj)
        for p in range(2):
            kp = qkv[g, :, 256 + p * 128 : 256 + (p + 1) * 128]
            vT = qkv[g, :, 512 + p * 128 : 512 + (p + 1) * 128].T
            q = qkv[g, :, p * 128 : (p + 1) * 128]
            for h in range(2):
                s = dot(lane_half(kp, h), q, NT)
                m = jnp.max(s, axis=0, keepdims=True)
                e = jnp.exp2((s - m) * c)
                l = jnp.sum(e, axis=0, keepdims=True)
                pr = (e * (1.0 / l)).astype(bf)
                o = dot(vT[h * 64 : (h + 1) * 64], pr)
                lse[g, p * 2 + h : p * 2 + h + 1, :] = m * 0.125 + jnp.log(l)
                attnT[pl.ds(pl.multiple_of(g * 256 + (p * 128 + h * 64), 64), 64), :] = o.astype(bf)
        return 0

    lax.fori_loop(0, 4, group, 0)


def ka(*a):
    return pl.pallas_call(
        ka_kernel,
        out_shape=(sd((4, S, 768), bf), sd((D, S), bf), sd((4, 4, S), f32), sd((D, S), bf)),
        in_specs=[V, V, V, A],
        out_specs=[V] * 4,
        scratch_shapes=[pltpu.VMEM((S, D), bf), pltpu.VMEM((2, D, 768), bf), pltpu.SemaphoreType.DMA((2,))],
        compiler_params=pltpu.CompilerParams(vmem_limit_bytes=60 * 2**20),
        name="attention_forward",
    )(*a)


def kc_kernel(QB, tok, mod, qkv, dat, lse, dx1, h1T, w_h, ig, dw_h, dmod, dbq, dqkv, dk_s, dv_s, dqT_s, dh1, wbuf, dwst, wsem, osem):
    c=LOG2E/8.0
    def cp(g,slot): return pltpu.make_async_copy(w_h.at[g, :, 0:768], wbuf.at[slot], wsem.at[slot])
    def co(g,slot): return pltpu.make_async_copy(dwst.at[slot], dw_h.at[g], osem.at[slot])
    cp(0,0).start()
    dh1[...]=jnp.zeros_like(dh1); dmod[...]=jnp.zeros_like(dmod); dbq[...]=jnp.zeros_like(dbq)
    def group(g,_):
        slot=lax.rem(g,2)
        @pl.when(g<3)
        def _(): cp(g+1,1-slot).start()
        for p in range(2):
            sl=slice(p*128,(p+1)*128); slk=slice(256+p*128,256+(p+1)*128); slv=slice(512+p*128,512+(p+1)*128)
            kp=qkv[g,:,slk]; vp=qkv[g,:,slv]
            ks=[lane_half(kp,h) for h in range(2)]; vs=[lane_half(vp,h) for h in range(2)]
            kT=kp.T
            dk_s[...]=jnp.zeros_like(dk_s); dv_s[...]=jnp.zeros_like(dv_s)
            def qblk(i,_):
                r=pl.ds(pl.multiple_of(i*QB,QB),QB)
                q=qkv[g,r,sl]; da=dat[g,r,sl]
                for h in range(2):
                    s=dot(ks[h],q,NT)
                    pT=jnp.exp2(s*c-lse[g,p*2+h:p*2+h+1,r]*LOG2E)
                    dp=dot(vs[h],da,NT)
                    delta=jnp.sum(pT*dp,axis=0,keepdims=True)
                    ds=(pT*(dp-delta)).astype(bf)
                    dv_s[...]+=dot(pT.astype(bf),lane_half(da,h))
                    dk_s[...]+=dot(ds,lane_half(q,h))
                    dqT_s[h*64:(h+1)*64,r]=dot(kT[h*64:(h+1)*64],ds)
                return 0
            lax.fori_loop(0,S//QB,qblk,0)
            dq=dqT_s[...].T*0.125
            dbq[g,:,sl]=jnp.sum(dq,axis=0,keepdims=True)
            dqkv[:,sl]=dq.astype(bf)
            dqkv[:,slk]=(dk_s[...]*0.125).astype(bf)
            dbq[g,:,slv]=jnp.sum(dv_s[...],axis=0,keepdims=True)
            dqkv[:,slv]=dv_s[...].astype(bf)
        cp(g,slot).wait()
        @pl.when(g>=2)
        def _(): co(g,slot).wait()
        def wrow(r):
            dwst[slot,r,:]=dot(h1T[r,:],dqkv[...])
            dh1[r,:]+=dot(dqkv[r,:],wbuf[slot],NT)
        rows_loop(D,256,wrow)
        co(g,slot).start()
        return 0
    lax.fori_loop(0,4,group,0)
    for s_ in range(2): co(s_,s_).wait()
    scale1=mod[1:2]
    def post(r):
        xh,rstd=nrm(tok[r,:].astype(f32))
        dh=dh1[r,:]
        dmod[0:1]+=jnp.sum(dh,axis=0,keepdims=True)
        dmod[1:2]+=jnp.sum(dh*xh,axis=0,keepdims=True)
        gg=dh*(1.0+scale1)
        ig[r,:]=dx1[r,:]+rstd*(gg-jnp.mean(gg,axis=-1,keepdims=True)-xh*jnp.mean(gg*xh,axis=-1,keepdims=True))
    rows_loop(S,128,post)
def kc(QB,*a):
    return pl.pallas_call(functools.partial(kc_kernel,QB),
      out_shape=(sd((S,D),f32),sd((4,D,768),f32),sd((8,D),f32),sd((4,1,768),f32)),
      in_specs=[V]*7+[A], out_specs=[V,A,V,V],
      scratch_shapes=[pltpu.VMEM((S,768),bf),pltpu.VMEM((S,128),f32),pltpu.VMEM((S,128),f32),pltpu.VMEM((128,S),f32),pltpu.VMEM((S,D),f32),
        pltpu.VMEM((2,D,768),bf),pltpu.VMEM((2,D,768),f32),pltpu.SemaphoreType.DMA((2,)),pltpu.SemaphoreType.DMA((2,))],
      compiler_params=pltpu.CompilerParams(vmem_limit_bytes=60*2**20), name=f"kc{QB}")(*a)
def when(cond, f):
    @pl.when(cond)
    def _():
        f()


class Pair:
    def __init__(self, at, own, theirs, send, recv, credit, count):
        self.at, self.own, self.theirs, self.sems, self.credit, self.count = at, own, theirs, (send, recv), credit, count

    def copy(self, i, part, cols):
        slot = lax.rem(i, 2)
        return remote(self.own.at[slot, :, cols], self.theirs.at[slot, :, cols], self.sems[0].at[slot, part], self.sems[1].at[slot, part], self.at.to_c)

    def start(self, i, part, cols):
        if part == 0:
            when(i >= 2, lambda: pl.semaphore_wait(self.credit, 1))
        self.copy(i, part, cols).start()

    def sent(self, i, parts):
        for part, cols in enumerate(parts):
            self.copy(i, part, cols).wait_send()

    def arrived(self, i, parts):
        for part, cols in enumerate(parts):
            self.copy(i, part, cols).wait_recv()

    def free(self, i):
        when(i + 2 < self.count, lambda: mesh_signal(self.credit, self.at.to_c))


WHOLE = (slice(0, 1024),)
PARTS = (slice(768, 1024), slice(0, 384), slice(384, 768))


class Scatter:
    shapes = [
        pltpu.VMEM((2, 2, 2, 2, 32, 1024), f32),
        pltpu.VMEM((2, 2, 2, 2, 16, 1024), bf),
        pltpu.VMEM((2, 2, 2, 2, 16, 1024), f32),
        pltpu.VMEM((2, 2, 2, 2, 2, 16, 1024), bf),
        pltpu.VMEM((2, 2, 2, 16, 1024), bf),
        pltpu.VMEM((2, 2, 2, 16, 1024), f32),
        pltpu.VMEM((2, 2, 2, 2, 16, 1024), bf),
        pltpu.VMEM((2, 32, 1024), f32),
        pltpu.VMEM((2, 32, 1024), f32),
        pltpu.VMEM((2, 2, 32, 1024), f32),
        pltpu.VMEM((32, 1024), f32),
        pltpu.VMEM((32, 1024), f32),
        pltpu.VMEM((2, 32, 1024), f32),
        pltpu.SemaphoreType.DMA((6,)),
        pltpu.SemaphoreType.DMA((2, 6)),
        pltpu.SemaphoreType.REGULAR((6,)),
    ]

    def __init__(self, at, refs, out, count, gaps=()):
        self.at, self.out, self.count, self.gaps = at, out, count, gaps
        self.acc, self.s2, self.k2, self.r2, self.s3, self.k3, self.r3, self.s4, self.k4, self.r4, self.s5, self.k5, self.r5, self.send, self.recv, self.credit = refs

    def todo(self, stage, slot):
        at = self.at
        if stage == 2:
            return [(0, self.s2.at[0], self.r2.at[slot, 0], at.to_y), (1, self.s2.at[1], self.r2.at[slot, 1], at.to_x)]
        if stage == 3:
            return [(2, self.s3.at[0], self.r3.at[slot, 0], at.to_x), (3, self.s3.at[1], self.r3.at[slot, 1], at.to_y)]
        if stage == 4:
            return [(4, self.s4, self.r4.at[slot], at.to_b)]
        return [(5, self.s5, self.r5.at[slot], at.to_a)]

    def copies(self, stage, i):
        slot = lax.rem(i, 2)
        return [remote(src, dst, self.send.at[q], self.recv.at[slot, q], dev) for q, src, dst, dev in self.todo(stage, slot)]

    def reuse(self, stage, i):
        def go():
            for cp in self.copies(stage, i - 1):
                cp.wait_send()

        when(i >= 1, go)

    def start(self, stage, i):
        def go():
            for q, _, _, _ in self.todo(stage, 0):
                pl.semaphore_wait(self.credit.at[q], 1)

        when(i >= 2, go)
        for cp in self.copies(stage, i):
            cp.start()

    def arrived(self, stage, i):
        for cp in self.copies(stage, i):
            cp.wait_recv()

    def free(self, stage, i):
        def go():
            for q, _, _, dev in self.todo(stage, 0):
                mesh_signal(self.credit.at[q], dev)

        when(i + 2 < self.count, go)

    def two(self, i, acc):
        y, x = self.at.y, self.at.x
        lo, hi = pl.ds(0, 16), pl.ds(16, 16)
        self.reuse(2, i)
        self.s2[0] = acc[:, :, 1 - y, :, lo, :].astype(bf)
        self.s2[1] = acc[:, :, :, 1 - x, hi, :].astype(bf)
        self.start(2, i)
        self.k2[0] = acc[:, :, y, :, lo, :]
        self.k2[1] = acc[:, :, :, x, hi, :]

    def three(self, i):
        y, x = self.at.y, self.at.x
        slot = lax.rem(i, 2)
        self.arrived(2, i)
        self.reuse(3, i)
        self.s3[0] = (self.k2[0, :, :, 1 - x] + self.r2[slot, 0, :, :, 1 - x].astype(f32)).astype(bf)
        self.s3[1] = (self.k2[1, :, :, 1 - y] + self.r2[slot, 1, :, :, 1 - y].astype(f32)).astype(bf)
        self.start(3, i)
        self.k3[0] = self.k2[0, :, :, x] + self.r2[slot, 0, :, :, x].astype(f32)
        self.k3[1] = self.k2[1, :, :, y] + self.r2[slot, 1, :, :, y].astype(f32)
        self.free(2, i)

    def four(self, i):
        b = self.at.b
        slot = lax.rem(i, 2)
        self.arrived(3, i)
        self.reuse(4, i)
        for h in (0, 1):
            rows = slice(16 * h, 16 * h + 16)
            self.s4[:, rows, :] = self.k3[h, :, 1 - b] + self.r3[slot, h, :, 1 - b].astype(f32)
        self.start(4, i)
        for h in (0, 1):
            rows = slice(16 * h, 16 * h + 16)
            self.k4[:, rows, :] = self.k3[h, :, b] + self.r3[slot, h, :, b].astype(f32)
        self.free(3, i)

    def five(self, i):
        a = self.at.a
        slot = lax.rem(i, 2)
        self.arrived(4, i)
        self.reuse(5, i)
        self.s5[...] = self.k4[1 - a] + self.r4[slot, 1 - a]
        self.start(5, i)
        self.k5[...] = self.k4[a] + self.r4[slot, a]
        self.free(4, i)

    def six(self, i):
        slot = lax.rem(i, 2)
        self.arrived(5, i)
        t = self.k5[...] + self.r5[slot]

        def spread(start, src, width):
            self.out[:, pl.ds(pl.multiple_of(start, 128), width)] = t[:, src : src + width]

        def feed_forward():
            spread(4 * D + i * CH, 0, CH)
            spread(4 * D + FF + i * CH, CH, CH)

        def attention():
            g = i - NJ
            for p in range(2):
                for q in range(3):
                    spread(q * D + g * 256 + p * 128, p * 384 + q * 128, 128)
            spread(3 * D + g * 256, 768, 256)

        when(i < NJ, feed_forward)
        when(i >= NJ, attention)
        self.free(5, i)

    def tick(self, t):
        for lag, f in ((4, self.six), (3, self.five), (2, self.four), (1, self.three)):
            u = t - lag
            live = (u >= 0) & (u < self.count + len(self.gaps))
            piece = u
            for gap in self.gaps:
                live = live & (u != gap)
                piece = piece - jnp.where(u > gap, 1, 0)
            when(live, functools.partial(f, piece))

    def finish(self):
        for stage in (2, 3, 4, 5):
            for cp in self.copies(stage, self.count - 1):
                cp.wait_send()


def block_kernel(n, tok, gout, small, weights,
                 bo, ig, gw, bsum, dsum, crec, wall, dwh, qkvh, dath,
                 mine, ada, gat, condc, rec, dsrc, dall, lsrc, lall, esrc, erec, csrc, mod, brow, bqkv, bup, dmod, db, dbup, dbq,
                 attnT, h1T, lse, dob, dx1, own, theirs, halfS,
                 s0, r0, s2, r2, s3, r3, s4, r4, s5, r5, s6, r6, xs, xr, ps, pr, pc, hc, wsem, qsem, osem, stsem, local, send, recv, *sc):
    c = LOG2E / 8.0
    at = Place()
    me = at.me
    gather = Gather(at, mine, wall, local, send, recv, 12)
    pair = Pair(at, own, theirs, ps, pr, pc, NJ + 4)
    scatter = Scatter(at, sc, gw, 12, gaps=(11,))

    def cut(shard):
        load = pltpu.make_async_copy(weights, shard, osem.at[0])
        load.start()
        load.wait()
        for g in range(4):
            for p in range(2):
                for q in range(3):
                    a = q * D + g * 256 + p * 128
                    b = p * 384 + q * 128
                    mine[g, :, b : b + 128] = shard[:, a : a + 128].astype(bf)
            mine[g, :, 768:] = shard[:, 3 * D + g * 256 : 3 * D + (g + 1) * 256].astype(bf)
        gather.start(0, 4)
        for j in range(NJ):
            for q in range(2):
                a = 4 * D + q * FF + j * CH
                mine[4 + j, :, q * CH : (q + 1) * CH] = shard[:, a : a + CH].astype(bf)
        gather.start(4, 12)
        for q in range(6):
            a = 4 * D + 2 * FF + q * D
            ada[at.c, :, q * D : (q + 1) * D] = shard[:, a : a + D].astype(bf)

    greet_all(n, me, lambda: pl.run_scoped(cut, pltpu.VMEM((32, 18 * D), f32)))
    gather.tick(0)
    trade_ada = remote(ada.at[at.c], ada.at[at.c], xs.at[4], xr.at[4], at.to_c)
    trade_ada.start()
    each_peer(n, me, lambda k, to, fr: remote(small, gat.at[me // 2, at.c], s0.at[k], r0.at[k], to).start())
    gat[pl.ds(me // 2, 1), pl.ds(at.c, 1)] = small[...].reshape(1, 1, 16, 128)
    db[...] = jnp.zeros_like(db)
    dmod[...] = jnp.zeros_like(dmod)

    def bias_into(biases, ref, row, start, lead):
        for q in range(lead):
            k = start + q
            ref[row, :, q * 64 : (q + 1) * 64] = biases[k // 7, k % 7 : k % 7 + 1, 0:64]

    def fetch(i, wbuf, slot):
        return pltpu.make_async_copy(wall.at[i], wbuf.at[slot], wsem.at[slot])

    def bias_from(k, piece):
        esrc[k // 7, :, (k % 7) * 64 : (k % 7 + 1) * 64] = piece

    def ada_columns(x, q):
        cols = slice(q * 512, (q + 1) * 512)
        gw[:, 4 * D + 2 * FF + q * 512 : 4 * D + 2 * FF + (q + 1) * 512] = dot(condc[...], x, TN)
        return dot(x, ada[pl.ds(at.c, 1), :, cols].reshape(32, 512), NT)

    def qkv_out(g, qkv):
        return pltpu.make_async_copy(qkv.at[lax.rem(g, 2)], qkvh.at[g], qsem.at[lax.rem(g, 2)])

    def qkv_in(g, qkv):
        return pltpu.make_async_copy(qkvh.at[g], qkv.at[lax.rem(g, 2)], qsem.at[lax.rem(g, 2)])

    def matrix(wbuf, slot, cols):
        return wbuf[slot, :, :, :, :, :, cols].reshape(D, cols.stop - cols.start)

    lead, tail = pl.ds(0, 2 * D), pl.ds(2 * D, 4 * D)

    def attention(h1, wbuf, qkv, part, biases, conds):
        def norm_one(r):
            xh, _ = nrm(tok[r, :].astype(f32))
            dx1[r, :] = xh

        rows_loop(S, 256, norm_one)
        each_peer(n, me, lambda k, to, fr: remote(small, gat.at[fr // 2, lax.rem(fr, 2)], s0.at[k], r0.at[k], to).wait())
        biases[...] = gat[...].astype(f32).reshape(n, 16, 128)[:, 8:16]
        conds[...] = gat[...].astype(f32).reshape(n // 2, 2, 16, 128)[:, :, 0:8]
        lane = lax.broadcasted_iota(jnp.int32, (128, 64), 0)
        want = lax.rem(me // 2, 2) * 64 + lax.broadcasted_iota(jnp.int32, (128, 64), 1)
        pick = jnp.where(lane == want, 1.0, 0.0).astype(bf)
        wanted = conds[:, :, pl.ds(me // 4, 1), :].reshape(n, 128).astype(bf)
        both = dot(wanted, pick)
        condc[...] = jnp.where(at.c == 0, both[:, 0:32], both[:, 32:64]).astype(bf)
        mates = dot(conds[:, pl.ds(at.c, 1), pl.ds(me // 4, 1), :].reshape(n // 2, 128).astype(bf), pick).astype(bf)
        trade_ada.wait_send()
        remote(ada.at[at.c], ada.at[1 - at.c], xs.at[4], xr.at[4], at.to_c).wait_recv()

        def columns(q):
            cols = slice(q * 512, (q + 1) * 512)
            part[:, :, cols] = dot(mates, ada[:, :, cols].reshape(64, 512)).reshape(n // 2, 1, 512)

        for q in range(4):
            columns(q)
        each_mate(n, me, lambda k, to, fr: remote(part.at[to // 2, :, lead], rec.at[me // 2, :, lead], s2.at[0, k], r2.at[0, k], to).start())
        gather.tick(1)
        for q in range(4, 12):
            columns(q)
        rec[pl.ds(me // 2, 1)] = part[pl.ds(me // 2, 1)]
        for q in range(6):
            bias_into(biases, mod, q, 128 + 16 * q, 16)
        bias_into(biases, brow, 0, 32, 16)
        bias_into(biases, brow, 1, 112, 16)
        for j in range(NJ):
            bias_into(biases, bup, j, 48 + 8 * j, 8)
        for g in range(4):
            bqkv[g] = jnp.zeros((1, 768), f32)
            for q in range(4):
                for first, offset in ((0, 0), (16, 256)):
                    k = first + g * 4 + q
                    to = (q // 2) * 384 + offset + (q % 2) * 64
                    bqkv[g, :, to : to + 64] = biases[k // 7, k % 7 : k % 7 + 1, 0:64]
        gather.tick(2)
        each_mate(n, me, lambda k, to, fr: remote(part.at[to // 2, :, lead], rec.at[fr // 2, :, lead], s2.at[0, k], r2.at[0, k], to).wait())
        each_mate(n, me, lambda k, to, fr: remote(part.at[to // 2, :, tail], rec.at[me // 2, :, tail], s2.at[1, k], r2.at[1, k], to).start())
        for q in range(2):
            mod[q] += jnp.sum(rec[:, :, q * D : (q + 1) * D], axis=0)
        shift1, scale1 = mod[0], mod[1]

        def modulate(r):
            h1[r, :] = (dx1[r, :] * (1.0 + scale1) + shift1).astype(bf)

        rows_loop(S, 256, modulate)
        for i in range(4):
            r = slice(i * 256, (i + 1) * 256)
            h1T[:, :, :, r] = h1[r, :].T.reshape(16, 2, 32, 256)
        gather.tick(3, (4,))
        gather.tick(4, (5,))
        fetch(0, wbuf, 0).start()
        gather.tick(3, (3, 2, 1))

        def group(g, _):
            slot = lax.rem(g, 2)
            fetch(g, wbuf, slot).wait()
            when(g >= 2, lambda: qkv_out(g - 2, qkv).wait())
            w = matrix(wbuf, slot, slice(0, 768))

            def proj(r):
                qkv[slot, r, :] = (dot(h1[r, :], w) + bqkv[g]).astype(bf)

            for r in (slice(0, 512), slice(512, 1024)):
                proj(r)
            qkv_out(g, qkv).start()
            when(g == 0, lambda: gather.tick(4, (4, 3, 2, 1)))
            for p in range(2):
                kp = qkv[slot, :, p * 384 + 128 : p * 384 + 256]
                vT = qkv[slot, :, p * 384 + 256 : p * 384 + 384].T
                q = qkv[slot, :, p * 384 : p * 384 + 128]
                scores = [dot(lane_half(kp, h), q, NT) for h in range(2)]
                probs = []
                for h in range(2):
                    m = jnp.max(scores[h], axis=0, keepdims=True)
                    e = jnp.exp2((scores[h] - m) * c)
                    l = jnp.sum(e, axis=0, keepdims=True)
                    probs.append((e * (1.0 / l)).astype(bf))
                    lse[g, p * 2 + h : p * 2 + h + 1, :] = m * 0.125 + jnp.log(l)
                for h in range(2):
                    o = dot(vT[h * 64 : (h + 1) * 64], probs[h])
                    attnT[pl.ds(g * 4 + p * 2 + h, 1)] = o.astype(bf).reshape(1, 2, 32, S)
            gather.tick(5 + g)
            when(g < 3, lambda: fetch(g + 1, wbuf, 1 - slot).start())
            return 0

        lax.fori_loop(0, 4, group, 0)
        for g in (2, 3):
            qkv_out(g, qkv).wait()
        each_mate(n, me, lambda k, to, fr: remote(part.at[to // 2, :, tail], rec.at[fr // 2, :, tail], s2.at[1, k], r2.at[1, k], to).wait())
        for q in range(2, 6):
            mod[q] += jnp.sum(rec[:, :, q * D : (q + 1) * D], axis=0)

    pl.run_scoped(
        attention,
        pltpu.VMEM((S, D), bf),
        pltpu.VMEM((2, 4, 2, 2, 2, 32, 1024), bf),
        pltpu.VMEM((2, S, 768), bf),
        pltpu.VMEM((n // 2, 1, 6 * D), f32),
        pltpu.VMEM((n, 8, 128), f32),
        pltpu.VMEM((n // 2, 2, 8, 128), f32),
    )

    def unstage(i):
        return pltpu.make_async_copy(dwh.at[i], scatter.acc, stsem.at[1])

    def staged(i):
        unstage(i).wait()
        scatter.two(i, scatter.acc)
        when(i + 1 < NJ, lambda: unstage(i + 1).start())

    def mlp(h2, hT, dzT, z, wout, wbuf, accw):
        gate1, shift2, scale2, gate2 = mod[2], mod[3], mod[4], mod[5]

        def stage(i):
            return pltpu.make_async_copy(accw, dwh.at[i], stsem.at[0])

        def co(g):
            return pltpu.make_async_copy(wall.at[g, :, :, :, :, :, 768:1024], wout.at[:, :, :, :, :, g * 256 : (g + 1) * 256], osem.at[g])

        for g in range(4):
            co(g).start()
        fetch(4, wbuf, 0).start()
        for g in range(4):
            co(g).wait()

        def branch(r):
            width = r.size
            return dot(attnT[:, :, :, r].reshape(D, width), wout[...].reshape(D, D), TN) + brow[0]

        def pre(r):
            x1 = tok[r, :].astype(f32) + gate1 * branch(r)
            xh, _ = nrm(x1)
            h2[r, :] = (xh * (1.0 + scale2) + shift2).astype(bf)
            dz = gout[r, :].astype(f32) * gate2
            dob[r, :] = dz.astype(bf)
            db[1] += jnp.sum(dz, axis=0, keepdims=True)

        def pre_block(i, _):
            pre(pl.ds(pl.multiple_of(i * 256, 256), 256))
            when(i == 1, lambda: gather.tick(9, (5, 3)))
            when(i == 3, lambda: gather.tick(9, (4, 2, 1)))
            return 0

        lax.fori_loop(0, 4, pre_block, 0)
        for i in range(4):
            r = slice(i * 256, (i + 1) * 256)
            hT[:, :, :, r] = h2[r, :].T.reshape(16, 2, 32, 256)
            dzT[:, :, :, r] = dob[r, :].T.reshape(16, 2, 32, 256)
        halves = [
            remote(hT.at[:, 1 - at.c], halfS.at[0], xs.at[0], xr.at[0], at.to_c),
            remote(dzT.at[:, 1 - at.c], halfS.at[1], xs.at[1], xr.at[1], at.to_c),
        ]
        for cp in halves:
            cp.start()
        z[...] = jnp.zeros_like(z)
        dx1[...] = jnp.zeros_like(dx1)

        def chunk(j, _):
            when(j >= 1, lambda: gather.tick(9 + j, (4, 2, 1)))

            def forward():
                slot = lax.rem(j, 2)
                when(j + 1 < NJ, lambda: fetch(5 + j, wbuf, 1 - slot).start())
                fetch(4 + j, wbuf, slot).wait()
                when(j >= 2, lambda: pair.sent(j - 2, WHOLE))
                dbup[j] = jnp.zeros((1, CH), f32)

                w_up, w_dn = matrix(wbuf, slot, slice(0, CH)), matrix(wbuf, slot, slice(CH, 2 * CH))
                blocks = (slice(0, 512), slice(512, 1024))
                ups = [dot(h2[r, :], w_up) + bup[j] for r in blocks]
                backs = [dot(dob[r, :], w_dn) for r in blocks]
                for r, u, back_ in zip(blocks, ups, backs):
                    a, sl = gelu_pair(u)
                    ab = a.astype(bf)
                    own[slot, r, CH:] = ab
                    d = back_ * sl
                    dbup[j] += jnp.sum(d, axis=0, keepdims=True)
                    db_ = d.astype(bf)
                    own[slot, r, :CH] = db_
                    z[r, :] += dot(ab, w_dn, NT)
                    dx1[r, :] += dot(db_, w_up, NT)

                pair.start(j, 0, WHOLE[0])

            when(j < NJ, forward)
            gather.tick(10 + j, (5, 3))
            scatter.tick(j - 5)
            when(j >= 5, lambda: staged(j - 5))
            when(j == 4, lambda: unstage(0).start())

            def weights():
                i = j - 1
                slot = lax.rem(i, 2)
                when(j == 1, lambda: [cp.wait_recv() for cp in halves])
                pair.arrived(i, WHOLE)
                when(i >= 1, lambda: stage(i - 1).wait())
                for q, lhs in enumerate((hT, dzT)):
                    cols = slice(q * CH, (q + 1) * CH)
                    t = dot(lhs[:, at.c].reshape(512, S), own[slot, :, cols]) + dot(halfS[q].reshape(512, S), theirs[slot, :, cols])
                    accw[:, :, :, :, :, cols] = t.reshape(2, 2, 2, 2, 32, CH)
                pair.free(i)
                stage(i).start()

            when(j >= 1, weights)
            return 0

        lax.fori_loop(0, NJ + 1, chunk, 0)
        mesh_signal(hc, at.to_c)
        stage(NJ - 1).wait()
        for cp in halves:
            cp.wait_send()

        def post(r):
            g = gout[r, :].astype(f32)
            o = branch(r)
            x1 = tok[r, :].astype(f32) + gate1 * o
            xh, rstd = nrm(x1)
            zz = z[r, :] + brow[1]
            h2[r, :] = (x1 + gate2 * zz).astype(bf)
            dmod[5] += jnp.sum(g * zz, axis=0, keepdims=True)
            dh = dx1[r, :]
            dmod[3] += jnp.sum(dh, axis=0, keepdims=True)
            dmod[4] += jnp.sum(dh * xh, axis=0, keepdims=True)
            gg = dh * (1.0 + scale2)
            dx = g + rstd * (gg - jnp.mean(gg, axis=-1, keepdims=True) - xh * jnp.mean(gg * xh, axis=-1, keepdims=True))
            dx1[r, :] = dx
            dmod[2] += jnp.sum(dx * o, axis=0, keepdims=True)
            do = dx * gate1
            db[0] += jnp.sum(do, axis=0, keepdims=True)
            dob_ = do.astype(bf)
            dob[r, :] = dob_
            own[0, r, :] = dot(dob_, wout[...].reshape(D, D), NT).astype(bf)

        pair.sent(NJ - 2, WHOLE)

        def post_half(h):
            def body(i, _):
                post(pl.ds(pl.multiple_of(h * 512 + i * 256, 256), 256))
                return 0

            lax.fori_loop(0, 2, body, 0)

        post_half(0)
        post_half(1)
        outs = [pltpu.make_async_copy(h2, bo, osem.at[0])]
        outs += [pltpu.make_async_copy(own.at[0, :, g * 256 : (g + 1) * 256], dath.at[g], osem.at[1 + g]) for g in range(4)]
        for cp in outs:
            cp.start()
        for cp in outs:
            cp.wait()

    pl.run_scoped(
        mlp,
        pltpu.VMEM((S, D), bf),
        pltpu.VMEM((16, 2, 32, S), bf),
        pltpu.VMEM((16, 2, 32, S), bf),
        pltpu.VMEM((S, D), f32),
        pltpu.VMEM((4, 2, 2, 2, 32, 1024), bf),
        pltpu.VMEM((2, 4, 2, 2, 2, 32, 1024), bf),
        pltpu.VMEM((2, 2, 2, 2, 32, 1024), f32),
    )

    def back(dh1, wbuf, qkv, dat, dk_s, dv_s, dqT_s, accw):
        def dat_in(g):
            return pltpu.make_async_copy(dath.at[g], dat.at[lax.rem(g, 2)], osem.at[lax.rem(g, 2)])

        def load(g):
            qkv_in(g, qkv).start()
            dat_in(g).start()
            fetch(g, wbuf, lax.rem(g, 2)).start()

        load(0)
        pl.semaphore_wait(hc, 1)
        halves = [
            remote(h1T.at[:, 1 - at.c], halfS.at[0], xs.at[2], xr.at[2], at.to_c),
            remote(attnT.at[:, 1 - at.c], halfS.at[1], xs.at[3], xr.at[3], at.to_c),
        ]
        for cp in halves:
            cp.start()
        scatter.tick(4)
        staged(4)
        for q in range(4):
            dsrc[:, q * D : (q + 1) * D] = dmod[2 + q]
        each_mate(n, me, lambda k, to, fr: remote(dsrc, dall.at[at.c, me // 2], s3.at[k], r3.at[k], to).start())
        dall[pl.ds(at.c, 1), pl.ds(me // 2, 1)] = dsrc[...].reshape(1, 1, 1, 4 * D)
        esrc[...] = jnp.zeros_like(esrc)
        for q in range(16):
            bias_from(32 + q, db[0, :, q * 64 : (q + 1) * 64])
            bias_from(112 + q, db[1, :, q * 64 : (q + 1) * 64])
        for j in range(NJ):
            for q in range(8):
                bias_from(48 + 8 * j + q, dbup[j, :, q * 64 : (q + 1) * 64])
        dh1[...] = jnp.zeros_like(dh1)

        def group(g, _):
            slot = lax.rem(g, 2)
            when(g < 3, lambda: load(g + 1))
            qkv_in(g, qkv).wait()
            dat_in(g).wait()
            when(g == 1, lambda: pair.sent(NJ - 1, WHOLE))
            when(g >= 2, lambda: pair.sent(NJ + g - 2, PARTS))
            own[slot, :, 768:] = dob[:, pl.ds(pl.multiple_of(g * 256, 256), 256)]
            pair.start(NJ + g, 0, PARTS[0])
            for p in range(2):
                if p == 1:
                    scatter.tick(5 + 2 * g)
                    when(g < 2, lambda: staged(5 + 2 * g))
                    when(g == 2, lambda: scatter.two(9, accw))
                sl = slice(p * 128, (p + 1) * 128)
                slq, slk, slv = (slice(p * 384 + q * 128, p * 384 + (q + 1) * 128) for q in range(3))
                kp, vp, q, da = qkv[slot, :, slk], qkv[slot, :, slv], qkv[slot, :, slq], dat[slot, :, sl]
                kT = kp.T
                for h in range(2):
                    s = dot(lane_half(kp, h), q, NT)
                    pT = jnp.exp2(s * c - lse[g, p * 2 + h : p * 2 + h + 1, :] * LOG2E)
                    dp = dot(lane_half(vp, h), da, NT)
                    weighted = pT * dp
                    ds = (weighted - pT * jnp.sum(weighted, axis=0, keepdims=True)).astype(bf)
                    dv = dot(pT.astype(bf), lane_half(da, h))
                    dk = dot(ds, lane_half(q, h))
                    if h == 0:
                        dv_s[...] = dv
                        dk_s[...] = dk
                    else:
                        dv_s[...] += dv
                        dk_s[...] += dk
                    dqT_s[h * 64 : (h + 1) * 64, :] = dot(kT[h * 64 : (h + 1) * 64], ds)
                dq = dqT_s[...].T * 0.125
                dbq[g, :, sl] = jnp.sum(dq, axis=0, keepdims=True)
                own[slot, :, slq] = dq.astype(bf)
                own[slot, :, slk] = (dk_s[...] * 0.125).astype(bf)
                dbq[g, :, 256 + p * 128 : 256 + (p + 1) * 128] = jnp.sum(dv_s[...], axis=0, keepdims=True)
                own[slot, :, slv] = dv_s[...].astype(bf)
                pair.start(NJ + g, 1 + p, PARTS[1 + p])
            fetch(g, wbuf, slot).wait()
            w = matrix(wbuf, slot, slice(0, 768))

            def wrow(r):
                dh1[r, :] += dot(own[slot, r, :768], w, NT)

            for r in (slice(0, 512), slice(512, 1024)):
                wrow(r)
            scatter.tick(6 + 2 * g)

            def at_first():
                staged(6)
                for cp in halves:
                    cp.wait_recv()

            when(g == 0, at_first)
            when(g == 1, lambda: scatter.two(8, accw))

            def pass_on():
                each_mate(n, me, lambda k, to, fr: remote(dsrc, dall.at[at.c, fr // 2], s3.at[k], r3.at[k], to).wait())
                remote(dall.at[at.c], dall.at[at.c], xs.at[5], xr.at[5], at.to_c).start()

            when(g == 1, pass_on)
            pair.arrived(NJ + g, PARTS)
            for q, lhs in enumerate((h1T, attnT)):
                cols = slice(0, 768) if q == 0 else slice(768, 1024)
                t = dot(lhs[:, at.c].reshape(512, S), own[slot, :, cols]) + dot(halfS[q].reshape(512, S), theirs[slot, :, cols])
                accw[:, :, :, :, :, cols] = t.reshape(2, 2, 2, 2, 32, cols.stop - cols.start)
            pair.free(NJ + g)
            when(g >= 2, lambda: scatter.two(8 + g, accw))
            return 0

        lax.fori_loop(0, 4, group, 0)
        for g in range(4):
            for q in range(4):
                bias_from(g * 4 + q, dbq[g, :, q * 64 : (q + 1) * 64])
                bias_from(16 + g * 4 + q, dbq[g, :, 256 + q * 64 : 256 + (q + 1) * 64])
        each_peer(n, me, lambda k, to, fr: remote(esrc.at[to], erec.at[me], s4.at[k], r4.at[k], to).start())
        erec[pl.ds(me, 1)] = esrc[pl.ds(me, 1)]
        for i in (2, 3):
            pair.sent(NJ + i, PARTS)
        for cp in halves:
            cp.wait_send()
        scale1 = mod[1]

        def post(r):
            xh, rstd = nrm(tok[r, :].astype(f32))
            dh = dh1[r, :]
            dmod[0] += jnp.sum(dh, axis=0, keepdims=True)
            dmod[1] += jnp.sum(dh * xh, axis=0, keepdims=True)
            gg = dh * (1.0 + scale1)
            dx1[r, :] += rstd * (gg - jnp.mean(gg, axis=-1, keepdims=True) - xh * jnp.mean(gg * xh, axis=-1, keepdims=True))

        rows_loop(S, 256, post)

    pl.run_scoped(
        back,
        pltpu.VMEM((S, D), f32),
        pltpu.VMEM((2, 4, 2, 2, 2, 32, 1024), bf),
        pltpu.VMEM((2, S, 768), bf),
        pltpu.VMEM((2, S, 256), bf),
        pltpu.VMEM((S, 128), f32),
        pltpu.VMEM((S, 128), f32),
        pltpu.VMEM((128, S), f32),
        pltpu.VMEM((2, 2, 2, 2, 32, 1024), f32),
    )
    done = pltpu.make_async_copy(dx1, ig, osem.at[0])
    done.start()
    for k in range(2):
        lsrc[:, k * D : (k + 1) * D] = dmod[k]
    each_mate(n, me, lambda k, to, fr: remote(lsrc, lall.at[at.c, me // 2], s6.at[k], r6.at[k], to).start())
    lall[pl.ds(at.c, 1), pl.ds(me // 2, 1)] = lsrc[...].reshape(1, 1, 1, 2 * D)
    scatter.tick(13)
    passed = [remote(ref.at[at.c], ref.at[at.c], xs.at[5 + q], xr.at[5 + q], at.to_c) for q, ref in enumerate((dall, lall))]
    landed = [remote(ref.at[1 - at.c], ref.at[1 - at.c], xs.at[5 + q], xr.at[5 + q], at.to_c) for q, ref in enumerate((dall, lall))]
    passed[0].wait_send()
    landed[0].wait_recv()

    def latents(ref, first, count):
        total = jnp.zeros((n, 32), f32)
        for q in range(count):
            cols = slice(q * 512, (q + 1) * 512)
            x = jnp.concatenate([ref[k, :, :, cols].reshape(n // 2, 1, 512) for k in range(2)], axis=1).reshape(n, 512)
            dsum[:, (first + q) * 512 : (first + q + 1) * 512] = jnp.sum(x, axis=0, keepdims=True)
            total += ada_columns(x.astype(bf), first + q)
        return total

    total = latents(dall, 4, 8)
    each_mate(n, me, lambda k, to, fr: remote(lsrc, lall.at[at.c, fr // 2], s6.at[k], r6.at[k], to).wait())
    passed[1].start()
    scatter.tick(14)
    passed[1].wait_send()
    landed[1].wait_recv()
    total += latents(lall, 0, 4)
    csrc[:, :, 0:32] = total.reshape(n, 1, 32)
    each_peer(n, me, lambda k, to, fr: remote(csrc.at[to], crec.at[me], s5.at[k], r5.at[k], to).start())
    crec[pl.ds(me, 1)] = csrc[pl.ds(me, 1)]
    each_peer(n, me, lambda k, to, fr: remote(esrc.at[to], erec.at[fr], s4.at[k], r4.at[k], to).wait())
    bsum[...] = jnp.sum(erec[...], axis=0)
    scatter.tick(15)
    each_peer(n, me, lambda k, to, fr: remote(csrc.at[to], crec.at[fr], s5.at[k], r5.at[k], to).wait())
    scatter.tick(16)
    done.wait()
    scatter.finish()
    gather.finish()


def block(n, *a):
    dma = pltpu.SemaphoreType.DMA
    regular = pltpu.SemaphoreType.REGULAR
    vm = pltpu.VMEM
    return pl.pallas_call(
        functools.partial(block_kernel, n),
        out_shape=(sd((S, D), bf), sd((S, D), f32), sd((32, 18 * D), f32), sd((1, 512), f32), sd((1, 6 * D), f32), sd((n, 1, 128), f32))
        + (sd((12, 4, 2, 2, 2, 32, 1024), bf), sd((NJ, 2, 2, 2, 2, 32, 1024), f32), sd((4, S, 768), bf), sd((4, S, 256), bf)),
        in_specs=[V] * 3 + [A],
        out_specs=[A] * 2 + [V] * 4 + [A] * 4,
        scratch_shapes=[vm((12, 32, 1024), bf), vm((2, 32, 6 * D), bf), vm((n // 2, 2, 16, 128), bf), vm((n, 32), bf)]
        + [vm((n // 2, 1, 6 * D), f32), vm((1, 4 * D), f32), vm((2, n // 2, 1, 4 * D), f32), vm((1, 2 * D), f32), vm((2, n // 2, 1, 2 * D), f32), vm((n, 1, 512), f32), vm((n, 1, 512), f32), vm((n, 1, 128), f32)]
        + [vm((6, 1, D), f32), vm((2, 1, D), f32), vm((4, 1, 768), f32), vm((NJ, 1, CH), f32), vm((6, 1, D), f32), vm((2, 1, D), f32), vm((NJ, 1, CH), f32), vm((4, 1, 512), f32)]
        + [vm((16, 2, 32, S), bf), vm((16, 2, 32, S), bf), vm((4, 4, S), f32), vm((S, D), bf), vm((S, D), f32)]
        + [vm((2, S, 1024), bf), vm((2, S, 1024), bf), vm((2, 16, 32, S), bf)]
        + [dma((n,))] * 2
        + [dma((2, n))] * 2
        + [dma((n,))] * 8
        + [dma((7,)), dma((7,)), dma((2, 3)), dma((2, 3)), regular, regular]
        + [dma((2,)), dma((2,)), dma((5,)), dma((2,))]
        + gather_sems(12)
        + Scatter.shapes,
        compiler_params=pltpu.CompilerParams(collective_id=0, has_side_effects=True, vmem_limit_bytes=VMEM_BYTES),
        name="block",
    )(*a)


def adam_step(param, grad, first, second, decay):
    new_first = beta_first * first + (1.0 - beta_first) * grad
    new_second = beta_second * second + (1.0 - beta_second) * grad * grad
    step_size = learn_rate / (1.0 - beta_first**STEP)
    denom = jnp.sqrt(new_second / (1.0 - beta_second**STEP)) + adam_eps
    new_param = param - step_size * new_first / denom - learn_rate * decay * param
    return (new_param, new_first, new_second)


def plain(n, tok, gout, condition, weights, biases):
    me = lax.axis_index("dp")
    rows = D // n
    wb = weights.astype(bf)
    qkvo = wb[:, : 4 * D].reshape(rows, 4, 4, 256).transpose(2, 0, 1, 3).reshape(4, rows, 1024)
    updn = wb[:, 4 * D : 4 * D + 2 * FF].reshape(rows, 2, NJ, CH).transpose(2, 0, 1, 3).reshape(NJ, rows, 1024)
    mine = jnp.concatenate([qkvo, updn], axis=0)
    ada_l = wb[:, 4 * D + 2 * FF :]
    cond_act = jax.nn.silu(condition).astype(bf)
    bias_full = lax.all_gather(biases.astype(bf), "dp", axis=0, tiled=True).astype(f32)
    cond_all = lax.all_gather(cond_act, "dp", axis=0, tiled=True)
    cond_cols = lax.dynamic_slice_in_dim(cond_all, me * rows, rows, 1)
    mod = lax.psum_scatter(jnp.dot(cond_cols, ada_l, preferred_element_type=f32), "dp", scatter_dimension=0, tiled=True)
    mod = jnp.concatenate([(mod[0] + bias_full[4 * D + FF :]).reshape(6, D), jnp.zeros((2, D), f32)], axis=0)
    zrow = jnp.zeros((D,), f32)
    bqkv = jnp.stack([bias_full[:D], zrow, bias_full[D : 2 * D]]).reshape(3, 4, 256).transpose(1, 0, 2).reshape(4, 1, 768)
    brows = jnp.stack([zrow, zrow, bias_full[2 * D : 3 * D], bias_full[3 * D + FF : 4 * D + FF], zrow, zrow, zrow, zrow])
    bup = bias_full[3 * D : 3 * D + FF].reshape(NJ, 1, CH)
    wall = lax.all_gather(mine, "dp", axis=1, tiled=True)
    qkv, attn_t, lse, h1t = ka(tok, mod, bqkv, wall)
    bo, dx1, dat, dw_mlp, dw_out, dmod_b, db, db_up = kb(512, tok, gout, attn_t, mod, brows, bup, wall)
    ig, dw_qkv, dmod_a, db_qkv = kc(1024, tok, mod, qkv, dat, lse, dx1, h1t, wall)
    g_mlp = lax.psum_scatter(dw_mlp, "dp", scatter_dimension=2, tiled=True)
    g_out = lax.psum_scatter(dw_out, "dp", scatter_dimension=0, tiled=True)
    g_qkv = lax.psum_scatter(dw_qkv, "dp", scatter_dimension=1, tiled=True)
    g_qkv = g_qkv.reshape(4, rows, 3, 256).transpose(1, 2, 0, 3).reshape(rows, 3 * D)
    g_mlp = g_mlp.transpose(2, 1, 0, 3).reshape(rows, 2 * FF)
    dmod = (dmod_a + dmod_b)[:6].reshape(1, 6 * D)
    db_qkv = db_qkv.reshape(4, 3, 256).transpose(1, 0, 2).reshape(3, D)
    bias_row = jnp.concatenate([db_qkv[0], db_qkv[2], db[2], db_up.reshape(FF), db[3], dmod[0]])
    bias_grad = lax.psum_scatter(bias_row, "dp", scatter_dimension=0, tiled=True)
    dmod_all = lax.all_gather(dmod.astype(bf), "dp", axis=0, tiled=True)
    g_ada = lax.dot_general(cond_cols, dmod_all, TN, preferred_element_type=f32)
    cond_part = lax.dot_general(dmod_all, ada_l, NT, preferred_element_type=f32)
    cond_grad = lax.all_to_all(cond_part, "dp", split_axis=0, concat_axis=1, tiled=True)
    return bo, ig, cond_grad, jnp.concatenate([g_qkv, g_out, g_mlp, g_ada], axis=1), bias_grad


def finish_kernel(gw, w, m, v, bo, ig, gw_o, w_o, m_o, v_o, bo_o, ig_o):
    grad = gw[...]
    gw_o[...] = grad
    w_o[...], m_o[...], v_o[...] = adam_step(w[...], grad, m[...], v[...], weight_decay)
    bo_o[...] = bo[...]
    ig_o[...] = ig[...]


def finish(steps, *a):
    cols = pl.BlockSpec((32, 18 * D // steps), lambda i: (0, i))
    toks = pl.BlockSpec((S // steps, D), lambda i: (i, 0))
    specs = [cols] * 4 + [toks] * 2
    return pl.pallas_call(
        finish_kernel,
        grid=(steps,),
        out_shape=(sd((32, 18 * D), f32),) * 4 + (sd((S, D), bf), sd((S, D), f32)),
        in_specs=specs,
        out_specs=specs,
        compiler_params=pltpu.CompilerParams(vmem_limit_bytes=VMEM_BYTES),
        name="finish",
    )(*a)


def on_chips(n, tok, gout, condition, weights, biases):
    cond_act = jax.nn.silu(condition).reshape(8, 128)
    padded = jnp.pad(biases.reshape(7, 64), ((0, 1), (0, 64)))
    bo, ig, weight_grad, bsum, dsum, crec = block(n, tok, gout, jnp.concatenate([cond_act, padded]).astype(bf), weights)[:6]
    own = biases.shape[0]
    flat = jnp.concatenate([jnp.zeros((4 * D + FF,), f32), dsum[0]])
    bias_grad = bsum[0, :own] + lax.dynamic_slice_in_dim(flat, lax.axis_index("dp") * own, own, 0)
    return bo, ig, crec[:, 0, :32].reshape(1, D), weight_grad, bias_grad


def on_device(n, block_in, condition, out_grad, weights, biases, first_moment, second_moment, bias_first, bias_second):
    run = on_chips if n == 32 else plain
    bo, ig, cond_grad, weight_grad, bias_grad = run(n, block_in[0], out_grad[0], condition, weights, biases)
    sigma = jax.nn.sigmoid(condition)
    cond_grad = cond_grad * (sigma * (1.0 + condition * (1.0 - sigma)))
    if n == 32:
        weight_grad, new_weights, new_first, new_second, bo, ig = finish(STEPS, weight_grad, weights, first_moment, second_moment, bo, ig)
    else:
        new_weights, new_first, new_second = adam_step(weights, weight_grad, first_moment, second_moment, weight_decay)
    new_biases, new_bias_first, new_bias_second = adam_step(biases, bias_grad, bias_first, bias_second, 0.0)
    return (bo[None], ig[None], cond_grad, weight_grad, bias_grad, new_weights, new_biases, new_first, new_second, new_bias_first, new_bias_second)


def solution(mesh):
    three, two, one = P("dp", None, None), P("dp", None), P("dp")
    return jax.shard_map(
        functools.partial(on_device, mesh.shape["dp"]),
        mesh=mesh,
        in_specs=(three, two, three, two, one, two, two, one, one),
        out_specs=(three, three, two, two, one, two, one, two, two, one, one),
        check_vma=False,
    )
```

```python
import functools

import jax
import jax.numpy as jnp
from jax import lax
from jax.experimental import pallas as pl
from jax.experimental.pallas import tpu as pltpu
from jax.sharding import PartitionSpec as P

D = 1024
FF = 4096
S = 1024
STEP = 3
CH = 512
NJ = FF // CH
VMEM_BYTES = 64 * 2**20
STEPS = 4
learn_rate = 0.01
beta_first = 0.9
beta_second = 0.95
adam_eps = 1e-08
weight_decay = 0.05
gc = 0.7978845608028654
LOG2E = 1.4426950408889634
f32 = jnp.float32
bf = jnp.bfloat16
NT = (((1,), (1,)), ((), ()))
TN = (((0,), (0,)), ((), ()))
V = pl.BlockSpec(memory_space=pltpu.VMEM)
A = pl.BlockSpec(memory_space=pl.ANY)
sd = jax.ShapeDtypeStruct
MESH = pl.DeviceIdType.MESH


def mesh_signal(sem, dev):
    pl.semaphore_signal(sem, inc=1, device_id=(dev,), device_id_type=MESH)


def remote(src, dst, send, recv, dev):
    return pltpu.make_async_remote_copy(src_ref=src, dst_ref=dst, send_sem=send, recv_sem=recv, device_id=(dev,), device_id_type=MESH)


def greet_all(n, me, between):
    barrier = pltpu.get_barrier_semaphore()

    def go(k, _):
        mesh_signal(barrier, lax.rem(me + k, n))
        return 0

    lax.fori_loop(1, n, go, 0)
    between()
    pl.semaphore_wait(barrier, n - 1)


def each_peer(n, me, f):
    def go(k, _):
        f(k, lax.rem(me + k, n), lax.rem(me + n - k, n))
        return 0

    lax.fori_loop(1, n, go, 0)


def gather_sems(count):
    return [pltpu.SemaphoreType.DMA((count,)), pltpu.SemaphoreType.DMA((count, 12)), pltpu.SemaphoreType.DMA((count, 12))]


def each_mate(n, me, f):
    def go(k, _):
        f(k, lax.rem(me + 2 * k, n), lax.rem(me + n - 2 * k, n))
        return 0

    lax.fori_loop(1, n // 2, go, 0)


class Place:
    def __init__(self):
        me = lax.axis_index("dp")
        self.me = me
        self.z = me // 8
        self.y = lax.rem(me // 4, 2)
        self.x = lax.rem(me // 2, 2)
        self.c = lax.rem(me, 2)
        self.to_c = me + 1 - 2 * self.c
        self.to_x = me + 2 - 4 * self.x
        self.to_y = me + 4 - 8 * self.y
        self.a = self.z // 2
        self.b = lax.rem(self.z, 2)
        self.to_b = me + 8 - 16 * self.b
        self.to_a = me + 16 - 32 * self.a

    def to_z(self, k):
        return lax.rem(self.z + k, 4) * 8 + lax.rem(self.me, 8)


class Gather:
    def __init__(self, at, src, buf, local, send, recv, count):
        self.at, self.src, self.buf, self.local, self.send, self.recv, self.count = at, src, buf, local, send, recv, count

    def step_refs(self, i, step, c):
        at, b = self.at, self.buf.at[i]
        y, x = at.y, at.x
        lo, hi = pl.ds(0, 16), pl.ds(16, 16)
        if step == 1:
            return [b.at[:, y, x, c]]
        if step == 2:
            return [b.at[:, y, 1 - x, c, lo], b.at[:, 1 - y, x, c, hi]]
        return [b.at[:, 1 - y, :, c, lo], b.at[:, :, 1 - x, c, hi]]

    def z_copy(self, i, k):
        at = self.at
        return remote(self.src.at[i], self.buf.at[i, at.z, at.y, at.x, at.c], self.send.at[i, k - 1], self.recv.at[i, k - 1], at.to_z(k))

    def z_landed(self, i, k):
        at = self.at
        zz = lax.rem(at.z + 4 - k, 4)
        return remote(self.src.at[i], self.buf.at[i, zz, at.y, at.x, at.c], self.send.at[i, k - 1], self.recv.at[i, k - 1], at.to_z(k))

    def own(self, i):
        at = self.at
        return pltpu.make_async_copy(self.src.at[i], self.buf.at[i, at.z, at.y, at.x, at.c], self.local.at[i])

    def xy_copies(self, i, step):
        at, b = self.at, self.buf.at[i]
        y, x, c = at.y, at.x, at.c
        lo, hi = pl.ds(0, 16), pl.ds(16, 16)
        if step == 2:
            a, d = b.at[:, y, x, c, lo], b.at[:, y, x, c, hi]
            return [
                remote(a, a, self.send.at[i, 3], self.recv.at[i, 3], at.to_x),
                remote(d, d, self.send.at[i, 4], self.recv.at[i, 4], at.to_y),
            ]
        a, d = b.at[:, y, :, c, lo], b.at[:, :, x, c, hi]
        return [
            remote(a, a, self.send.at[i, 5], self.recv.at[i, 5], at.to_y),
            remote(d, d, self.send.at[i, 6], self.recv.at[i, 6], at.to_x),
        ]

    def xy_landed(self, i, step):
        at, b = self.at, self.buf.at[i]
        refs = self.step_refs(i, step, at.c)
        base = 3 if step == 2 else 5
        return [remote(r, r, self.send.at[i, base + q], self.recv.at[i, base + q], at.to_x) for q, r in enumerate(refs)]

    def core_copies(self, i, step):
        at = self.at
        base = {1: 7, 2: 8, 3: 10}[step]
        return [remote(r, r, self.send.at[i, base + q], self.recv.at[i, base + q], at.to_c) for q, r in enumerate(self.step_refs(i, step, at.c))]

    def core_landed(self, i, step):
        at = self.at
        base = {1: 7, 2: 8, 3: 10}[step]
        return [remote(r, r, self.send.at[i, base + q], self.recv.at[i, base + q], at.to_c) for q, r in enumerate(self.step_refs(i, step, 1 - at.c))]

    def start(self, first, last):
        def go(i, _):
            self.own(i).start()
            return 0

        lax.fori_loop(first, last, go, 0)

    def tick(self, t, parts=(5, 4, 3, 2, 1)):
        def one():
            for k in (1, 2, 3):
                self.z_copy(t, k).start()

        def two():
            i = t - 1
            for k in (1, 2, 3):
                self.z_landed(i, k).wait_recv()
            self.own(i).wait()
            for cp in self.xy_copies(i, 2) + self.core_copies(i, 1):
                cp.start()

        def three():
            i = t - 2
            for cp in self.xy_landed(i, 2):
                cp.wait_recv()
            for cp in self.xy_copies(i, 3) + self.core_copies(i, 2):
                cp.start()

        def four():
            i = t - 3
            for cp in self.xy_landed(i, 3):
                cp.wait_recv()
            for cp in self.core_copies(i, 3):
                cp.start()

        def five():
            i = t - 4
            for step in (1, 2, 3):
                for cp in self.core_landed(i, step):
                    cp.wait_recv()

        for part in parts:
            i = t - part + 1
            when((i >= 0) & (i < self.count), (one, two, three, four, five)[part - 1])

    def finish(self):
        def go(i, _):
            for k in (1, 2, 3):
                self.z_copy(i, k).wait_send()
            for step in (2, 3):
                for cp in self.xy_copies(i, step):
                    cp.wait_send()
            for step in (1, 2, 3):
                for cp in self.core_copies(i, step):
                    cp.wait_send()
            return 0

        lax.fori_loop(0, self.count, go, 0)


def dot(a,b,dn=None):
    if dn is None: return jnp.dot(a,b,preferred_element_type=f32)
    return lax.dot_general(a,b,dn,preferred_element_type=f32)

def lane_half(x, hh):
    lane=lax.broadcasted_iota(jnp.int32, x.shape, 1)
    keep=(lane<64) if hh==0 else (lane>=64)
    return jnp.where(keep, x, jnp.zeros_like(x))

def gelu_pair(u):
    u2=u*u
    t=jnp.tanh(gc*(u+0.044715*u2*u))
    return 0.5*u*(1.0+t), 0.5*(1.0+t)+0.5*u*(1.0-t*t)*gc*(1.0+3.0*0.044715*u2)
def nrm(v):
    c=v-jnp.mean(v,axis=-1,keepdims=True)
    r=lax.rsqrt(jnp.mean(c*c,axis=-1,keepdims=True)+1e-6)
    return c*r,r
def rows_loop(n, R, f):
    def body(i,_):
        f(pl.ds(pl.multiple_of(i*R,R),R)); return 0
    lax.fori_loop(0,n//R,body,0)

def kb_kernel(R, tok, gout, attnT, mod, bias, bup, wall,
      bo_ref, dx1_ref, dat_ref, dw_h, dwout_ref, dmod_ref, db_ref, dbup_ref,
      h2, h2T, dzb, dzT, z, dh2, o_s, wout, wbuf, act, du, dwst, wsem, osem, wosem):
    def co(g): return pltpu.make_async_copy(wall.at[g, :, 768:1024], wout.at[:, g*256:(g+1)*256], wosem.at[g])
    for g in range(4): co(g).start()
    def fetch(j, slot):
        pltpu.make_async_copy(wall.at[4 + j], wbuf.at[slot], wsem.at[slot]).start()
    fetch(0,0)
    shift1=mod[0:1];scale1=mod[1:2];gate1=mod[2:3];shift2=mod[3:4];scale2=mod[4:5];gate2=mod[5:6]
    db_ref[...]=jnp.zeros_like(db_ref); dmod_ref[...]=jnp.zeros_like(dmod_ref)
    for g in range(4): co(g).wait()
    def pre(r):
        o=dot(attnT[:,r],wout[...],TN)+bias[2:3]
        o_s[r,:]=o
        x1=tok[r,:].astype(f32)+gate1*o
        xh,_=nrm(x1)
        h2[r,:]=(xh*(1.0+scale2)+shift2).astype(bf)
        dz=gout[r,:].astype(f32)*gate2
        dzb[r,:]=dz.astype(bf)
        db_ref[3:4]+=jnp.sum(dz,axis=0,keepdims=True)
    rows_loop(S,256,pre)
    for i in range(4):
        r=slice(i*256,(i+1)*256)
        h2T[:,r]=h2[r,:].T
        dzT[:,r]=dzb[r,:].T
    z[...]=jnp.zeros_like(z); dh2[...]=jnp.zeros_like(dh2)
    def chunk(j,_):
        slot=lax.rem(j,2)
        @pl.when(j+1<NJ)
        def _(): fetch(j+1,1-slot)
        pltpu.make_async_copy(wall.at[4 + j], wbuf.at[slot], wsem.at[slot]).wait()
        dbup_ref[j]=jnp.zeros((1,CH),f32)
        def row(r):
            u=dot(h2[r,:],wbuf[slot,:,:CH])+bup[j]
            a,sl=gelu_pair(u)
            ab=a.astype(bf); act[r,:]=ab
            da=dot(dzb[r,:],wbuf[slot,:,CH:])
            d=da*sl
            dbup_ref[j]+=jnp.sum(d,axis=0,keepdims=True)
            db_=d.astype(bf); du[r,:]=db_
            z[r,:]+=dot(ab,wbuf[slot,:,CH:],NT)
            dh2[r,:]+=dot(db_,wbuf[slot,:,:CH],NT)
        rows_loop(S,R,row)
        @pl.when(j>=2)
        def _():
            pltpu.make_async_copy(dwst.at[slot], dw_h.at[j], osem.at[slot]).wait()
        def wrow(r):
            dwst[slot,0,r,:]=dot(h2T[r,:],du[...])
            dwst[slot,1,r,:]=dot(dzT[r,:],act[...])
        rows_loop(D,256,wrow)
        pltpu.make_async_copy(dwst.at[slot], dw_h.at[j], osem.at[slot]).start()
        return 0
    lax.fori_loop(0,NJ,chunk,0)
    for s in range(2): pltpu.make_async_copy(dwst.at[s], dw_h.at[s], osem.at[s]).wait()
    def post(r):
        g=gout[r,:].astype(f32); o=o_s[r,:]
        x1=tok[r,:].astype(f32)+gate1*o
        xh,rstd=nrm(x1)
        zz=z[r,:]+bias[3:4]
        bo_ref[r,:]=(x1+gate2*zz).astype(bf)
        dmod_ref[5:6]+=jnp.sum(g*zz,axis=0,keepdims=True)
        dh=dh2[r,:]
        dmod_ref[3:4]+=jnp.sum(dh,axis=0,keepdims=True)
        dmod_ref[4:5]+=jnp.sum(dh*xh,axis=0,keepdims=True)
        gg=dh*(1.0+scale2)
        dx1=g+rstd*(gg-jnp.mean(gg,axis=-1,keepdims=True)-xh*jnp.mean(gg*xh,axis=-1,keepdims=True))
        dx1_ref[r,:]=dx1
        dmod_ref[2:3]+=jnp.sum(dx1*o,axis=0,keepdims=True)
        do=dx1*gate1
        db_ref[2:3]+=jnp.sum(do,axis=0,keepdims=True)
        dob=do.astype(bf)
        dzb[r,:]=dob
        t=dot(dob,wout[...],NT).astype(bf)
        for g4 in range(4): dat_ref[g4,r,:]=t[:,g4*256:(g4+1)*256]
    rows_loop(S,128,post)
    def wo(r):
        dwout_ref[r,:]=dot(attnT[r,:],dzb[...])
    rows_loop(D,256,wo)

def kb(R,*a):
    V=pl.BlockSpec(memory_space=pltpu.VMEM); A=pl.BlockSpec(memory_space=pl.ANY)
    sd=jax.ShapeDtypeStruct
    return pl.pallas_call(functools.partial(kb_kernel,R),
      out_shape=(sd((S,D),bf),sd((S,D),f32),sd((4,S,256),bf),sd((NJ,2,D,CH),f32),sd((D,D),f32),sd((8,D),f32),sd((8,D),f32),sd((NJ,1,CH),f32)),
      in_specs=[V]*6+[A], out_specs=[V,V,V,A,V,V,V,V],
      scratch_shapes=[pltpu.VMEM((S,D),bf)]*4+[pltpu.VMEM((S,D),f32)]*3+[pltpu.VMEM((D,D),bf),pltpu.VMEM((2,D,2*CH),bf),pltpu.VMEM((S,CH),bf),pltpu.VMEM((S,CH),bf),
         pltpu.VMEM((2,2,D,CH),f32),pltpu.SemaphoreType.DMA((2,)),pltpu.SemaphoreType.DMA((2,)),pltpu.SemaphoreType.DMA((4,))],
      compiler_params=pltpu.CompilerParams(vmem_limit_bytes=62*2**20), name=f"kb{R}")(*a)

def ka_kernel(tok, mod, bqkv, wall, qkv, attnT, lse, h1T, h1, wbuf, wsem):
    c = LOG2E / 8.0

    def cp(g, slot):
        return pltpu.make_async_copy(wall.at[g, :, 0:768], wbuf.at[slot], wsem.at[slot])

    cp(0, 0).start()
    shift1, scale1 = mod[0:1], mod[1:2]

    def ln(r):
        xh, _ = nrm(tok[r, :].astype(f32))
        h1[r, :] = (xh * (1.0 + scale1) + shift1).astype(bf)

    rows_loop(S, 128, ln)
    for i in range(4):
        r = slice(i * 256, (i + 1) * 256)
        h1T[:, r] = h1[r, :].T

    def group(g, _):
        slot = lax.rem(g, 2)
        when(g < 3, lambda: cp(g + 1, 1 - slot).start())
        cp(g, slot).wait()

        def proj(r):
            qkv[g, r, :] = (dot(h1[r, :], wbuf[slot]) + bqkv[g]).astype(bf)

        rows_loop(S, 256, proj)
        for p in range(2):
            kp = qkv[g, :, 256 + p * 128 : 256 + (p + 1) * 128]
            vT = qkv[g, :, 512 + p * 128 : 512 + (p + 1) * 128].T
            q = qkv[g, :, p * 128 : (p + 1) * 128]
            for h in range(2):
                s = dot(lane_half(kp, h), q, NT)
                m = jnp.max(s, axis=0, keepdims=True)
                e = jnp.exp2((s - m) * c)
                l = jnp.sum(e, axis=0, keepdims=True)
                pr = (e * (1.0 / l)).astype(bf)
                o = dot(vT[h * 64 : (h + 1) * 64], pr)
                lse[g, p * 2 + h : p * 2 + h + 1, :] = m * 0.125 + jnp.log(l)
                attnT[pl.ds(pl.multiple_of(g * 256 + (p * 128 + h * 64), 64), 64), :] = o.astype(bf)
        return 0

    lax.fori_loop(0, 4, group, 0)


def ka(*a):
    return pl.pallas_call(
        ka_kernel,
        out_shape=(sd((4, S, 768), bf), sd((D, S), bf), sd((4, 4, S), f32), sd((D, S), bf)),
        in_specs=[V, V, V, A],
        out_specs=[V] * 4,
        scratch_shapes=[pltpu.VMEM((S, D), bf), pltpu.VMEM((2, D, 768), bf), pltpu.SemaphoreType.DMA((2,))],
        compiler_params=pltpu.CompilerParams(vmem_limit_bytes=60 * 2**20),
        name="attention_forward",
    )(*a)


def kc_kernel(QB, tok, mod, qkv, dat, lse, dx1, h1T, w_h, ig, dw_h, dmod, dbq, dqkv, dk_s, dv_s, dqT_s, dh1, wbuf, dwst, wsem, osem):
    c=LOG2E/8.0
    def cp(g,slot): return pltpu.make_async_copy(w_h.at[g, :, 0:768], wbuf.at[slot], wsem.at[slot])
    def co(g,slot): return pltpu.make_async_copy(dwst.at[slot], dw_h.at[g], osem.at[slot])
    cp(0,0).start()
    dh1[...]=jnp.zeros_like(dh1); dmod[...]=jnp.zeros_like(dmod); dbq[...]=jnp.zeros_like(dbq)
    def group(g,_):
        slot=lax.rem(g,2)
        @pl.when(g<3)
        def _(): cp(g+1,1-slot).start()
        for p in range(2):
            sl=slice(p*128,(p+1)*128); slk=slice(256+p*128,256+(p+1)*128); slv=slice(512+p*128,512+(p+1)*128)
            kp=qkv[g,:,slk]; vp=qkv[g,:,slv]
            ks=[lane_half(kp,h) for h in range(2)]; vs=[lane_half(vp,h) for h in range(2)]
            kT=kp.T
            dk_s[...]=jnp.zeros_like(dk_s); dv_s[...]=jnp.zeros_like(dv_s)
            def qblk(i,_):
                r=pl.ds(pl.multiple_of(i*QB,QB),QB)
                q=qkv[g,r,sl]; da=dat[g,r,sl]
                for h in range(2):
                    s=dot(ks[h],q,NT)
                    pT=jnp.exp2(s*c-lse[g,p*2+h:p*2+h+1,r]*LOG2E)
                    dp=dot(vs[h],da,NT)
                    delta=jnp.sum(pT*dp,axis=0,keepdims=True)
                    ds=(pT*(dp-delta)).astype(bf)
                    dv_s[...]+=dot(pT.astype(bf),lane_half(da,h))
                    dk_s[...]+=dot(ds,lane_half(q,h))
                    dqT_s[h*64:(h+1)*64,r]=dot(kT[h*64:(h+1)*64],ds)
                return 0
            lax.fori_loop(0,S//QB,qblk,0)
            dq=dqT_s[...].T*0.125
            dbq[g,:,sl]=jnp.sum(dq,axis=0,keepdims=True)
            dqkv[:,sl]=dq.astype(bf)
            dqkv[:,slk]=(dk_s[...]*0.125).astype(bf)
            dbq[g,:,slv]=jnp.sum(dv_s[...],axis=0,keepdims=True)
            dqkv[:,slv]=dv_s[...].astype(bf)
        cp(g,slot).wait()
        @pl.when(g>=2)
        def _(): co(g,slot).wait()
        def wrow(r):
            dwst[slot,r,:]=dot(h1T[r,:],dqkv[...])
            dh1[r,:]+=dot(dqkv[r,:],wbuf[slot],NT)
        rows_loop(D,256,wrow)
        co(g,slot).start()
        return 0
    lax.fori_loop(0,4,group,0)
    for s_ in range(2): co(s_,s_).wait()
    scale1=mod[1:2]
    def post(r):
        xh,rstd=nrm(tok[r,:].astype(f32))
        dh=dh1[r,:]
        dmod[0:1]+=jnp.sum(dh,axis=0,keepdims=True)
        dmod[1:2]+=jnp.sum(dh*xh,axis=0,keepdims=True)
        gg=dh*(1.0+scale1)
        ig[r,:]=dx1[r,:]+rstd*(gg-jnp.mean(gg,axis=-1,keepdims=True)-xh*jnp.mean(gg*xh,axis=-1,keepdims=True))
    rows_loop(S,128,post)
def kc(QB,*a):
    return pl.pallas_call(functools.partial(kc_kernel,QB),
      out_shape=(sd((S,D),f32),sd((4,D,768),f32),sd((8,D),f32),sd((4,1,768),f32)),
      in_specs=[V]*7+[A], out_specs=[V,A,V,V],
      scratch_shapes=[pltpu.VMEM((S,768),bf),pltpu.VMEM((S,128),f32),pltpu.VMEM((S,128),f32),pltpu.VMEM((128,S),f32),pltpu.VMEM((S,D),f32),
        pltpu.VMEM((2,D,768),bf),pltpu.VMEM((2,D,768),f32),pltpu.SemaphoreType.DMA((2,)),pltpu.SemaphoreType.DMA((2,))],
      compiler_params=pltpu.CompilerParams(vmem_limit_bytes=60*2**20), name=f"kc{QB}")(*a)
def when(cond, f):
    @pl.when(cond)
    def _():
        f()


class Pair:
    def __init__(self, at, own, theirs, send, recv, credit, count):
        self.at, self.own, self.theirs, self.sems, self.credit, self.count = at, own, theirs, (send, recv), credit, count

    def copy(self, i, part, cols):
        slot = lax.rem(i, 2)
        return remote(self.own.at[slot, :, cols], self.theirs.at[slot, :, cols], self.sems[0].at[slot, part], self.sems[1].at[slot, part], self.at.to_c)

    def start(self, i, part, cols):
        if part == 0:
            when(i >= 2, lambda: pl.semaphore_wait(self.credit, 1))
        self.copy(i, part, cols).start()

    def sent(self, i, parts):
        for part, cols in enumerate(parts):
            self.copy(i, part, cols).wait_send()

    def arrived(self, i, parts):
        for part, cols in enumerate(parts):
            self.copy(i, part, cols).wait_recv()

    def free(self, i):
        when(i + 2 < self.count, lambda: mesh_signal(self.credit, self.at.to_c))


WHOLE = (slice(0, 1024),)
PARTS = (slice(768, 1024), slice(0, 384), slice(384, 768))


class Scatter:
    shapes = [
        pltpu.VMEM((2, 2, 2, 2, 32, 1024), f32),
        pltpu.VMEM((2, 2, 2, 2, 16, 1024), bf),
        pltpu.VMEM((2, 2, 2, 2, 16, 1024), f32),
        pltpu.VMEM((2, 2, 2, 2, 2, 16, 1024), bf),
        pltpu.VMEM((2, 2, 2, 16, 1024), bf),
        pltpu.VMEM((2, 2, 2, 16, 1024), f32),
        pltpu.VMEM((2, 2, 2, 2, 16, 1024), bf),
        pltpu.VMEM((2, 32, 1024), f32),
        pltpu.VMEM((2, 32, 1024), f32),
        pltpu.VMEM((2, 2, 32, 1024), f32),
        pltpu.VMEM((32, 1024), f32),
        pltpu.VMEM((32, 1024), f32),
        pltpu.VMEM((2, 32, 1024), f32),
        pltpu.SemaphoreType.DMA((6,)),
        pltpu.SemaphoreType.DMA((2, 6)),
        pltpu.SemaphoreType.REGULAR((6,)),
    ]

    def __init__(self, at, refs, out, count, gaps=()):
        self.at, self.out, self.count, self.gaps = at, out, count, gaps
        self.acc, self.s2, self.k2, self.r2, self.s3, self.k3, self.r3, self.s4, self.k4, self.r4, self.s5, self.k5, self.r5, self.send, self.recv, self.credit = refs

    def todo(self, stage, slot):
        at = self.at
        if stage == 2:
            return [(0, self.s2.at[0], self.r2.at[slot, 0], at.to_y), (1, self.s2.at[1], self.r2.at[slot, 1], at.to_x)]
        if stage == 3:
            return [(2, self.s3.at[0], self.r3.at[slot, 0], at.to_x), (3, self.s3.at[1], self.r3.at[slot, 1], at.to_y)]
        if stage == 4:
            return [(4, self.s4, self.r4.at[slot], at.to_b)]
        return [(5, self.s5, self.r5.at[slot], at.to_a)]

    def copies(self, stage, i):
        slot = lax.rem(i, 2)
        return [remote(src, dst, self.send.at[q], self.recv.at[slot, q], dev) for q, src, dst, dev in self.todo(stage, slot)]

    def reuse(self, stage, i):
        def go():
            for cp in self.copies(stage, i - 1):
                cp.wait_send()

        when(i >= 1, go)

    def start(self, stage, i):
        def go():
            for q, _, _, _ in self.todo(stage, 0):
                pl.semaphore_wait(self.credit.at[q], 1)

        when(i >= 2, go)
        for cp in self.copies(stage, i):
            cp.start()

    def arrived(self, stage, i):
        for cp in self.copies(stage, i):
            cp.wait_recv()

    def free(self, stage, i):
        def go():
            for q, _, _, dev in self.todo(stage, 0):
                mesh_signal(self.credit.at[q], dev)

        when(i + 2 < self.count, go)

    def two(self, i, acc):
        y, x = self.at.y, self.at.x
        lo, hi = pl.ds(0, 16), pl.ds(16, 16)
        self.reuse(2, i)
        self.s2[0] = acc[:, :, 1 - y, :, lo, :].astype(bf)
        self.s2[1] = acc[:, :, :, 1 - x, hi, :].astype(bf)
        self.start(2, i)
        self.k2[0] = acc[:, :, y, :, lo, :]
        self.k2[1] = acc[:, :, :, x, hi, :]

    def three(self, i):
        y, x = self.at.y, self.at.x
        slot = lax.rem(i, 2)
        self.arrived(2, i)
        self.reuse(3, i)
        self.s3[0] = (self.k2[0, :, :, 1 - x] + self.r2[slot, 0, :, :, 1 - x].astype(f32)).astype(bf)
        self.s3[1] = (self.k2[1, :, :, 1 - y] + self.r2[slot, 1, :, :, 1 - y].astype(f32)).astype(bf)
        self.start(3, i)
        self.k3[0] = self.k2[0, :, :, x] + self.r2[slot, 0, :, :, x].astype(f32)
        self.k3[1] = self.k2[1, :, :, y] + self.r2[slot, 1, :, :, y].astype(f32)
        self.free(2, i)

    def four(self, i):
        b = self.at.b
        slot = lax.rem(i, 2)
        self.arrived(3, i)
        self.reuse(4, i)
        for h in (0, 1):
            rows = slice(16 * h, 16 * h + 16)
            self.s4[:, rows, :] = self.k3[h, :, 1 - b] + self.r3[slot, h, :, 1 - b].astype(f32)
        self.start(4, i)
        for h in (0, 1):
            rows = slice(16 * h, 16 * h + 16)
            self.k4[:, rows, :] = self.k3[h, :, b] + self.r3[slot, h, :, b].astype(f32)
        self.free(3, i)

    def five(self, i):
        a = self.at.a
        slot = lax.rem(i, 2)
        self.arrived(4, i)
        self.reuse(5, i)
        self.s5[...] = self.k4[1 - a] + self.r4[slot, 1 - a]
        self.start(5, i)
        self.k5[...] = self.k4[a] + self.r4[slot, a]
        self.free(4, i)

    def six(self, i):
        slot = lax.rem(i, 2)
        self.arrived(5, i)
        t = self.k5[...] + self.r5[slot]

        def spread(start, src, width):
            self.out[:, pl.ds(pl.multiple_of(start, 128), width)] = t[:, src : src + width]

        def feed_forward():
            spread(4 * D + i * CH, 0, CH)
            spread(4 * D + FF + i * CH, CH, CH)

        def attention():
            g = i - NJ
            for p in range(2):
                for q in range(3):
                    spread(q * D + g * 256 + p * 128, p * 384 + q * 128, 128)
            spread(3 * D + g * 256, 768, 256)

        when(i < NJ, feed_forward)
        when(i >= NJ, attention)
        self.free(5, i)

    def tick(self, t):
        for lag, f in ((4, self.six), (3, self.five), (2, self.four), (1, self.three)):
            u = t - lag
            live = (u >= 0) & (u < self.count + len(self.gaps))
            piece = u
            for gap in self.gaps:
                live = live & (u != gap)
                piece = piece - jnp.where(u > gap, 1, 0)
            when(live, functools.partial(f, piece))

    def finish(self):
        for stage in (2, 3, 4, 5):
            for cp in self.copies(stage, self.count - 1):
                cp.wait_send()


def block_kernel(n, tok, gout, small, weights,
                 bo, ig, gw, bsum, dsum, crec, wall, dwh, qkvh, dath,
                 mine, ada, gat, condc, rec, dsrc, dall, lsrc, lall, esrc, erec, csrc, mod, brow, bqkv, bup, dmod, db, dbup, dbq,
                 attnT, h1T, lse, dob, dx1, own, theirs, halfS,
                 s0, r0, s2, r2, s3, r3, s4, r4, s5, r5, s6, r6, xs, xr, ps, pr, pc, hc, wsem, qsem, osem, stsem, local, send, recv, *sc):
    c = LOG2E / 8.0
    at = Place()
    me = at.me
    gather = Gather(at, mine, wall, local, send, recv, 12)
    pair = Pair(at, own, theirs, ps, pr, pc, NJ + 4)
    scatter = Scatter(at, sc, gw, 12, gaps=(11,))

    def cut(shard):
        load = pltpu.make_async_copy(weights, shard, osem.at[0])
        load.start()
        load.wait()
        for g in range(4):
            for p in range(2):
                for q in range(3):
                    a = q * D + g * 256 + p * 128
                    b = p * 384 + q * 128
                    mine[g, :, b : b + 128] = shard[:, a : a + 128].astype(bf)
            mine[g, :, 768:] = shard[:, 3 * D + g * 256 : 3 * D + (g + 1) * 256].astype(bf)
        gather.start(0, 4)
        for j in range(NJ):
            for q in range(2):
                a = 4 * D + q * FF + j * CH
                mine[4 + j, :, q * CH : (q + 1) * CH] = shard[:, a : a + CH].astype(bf)
        gather.start(4, 12)
        for q in range(6):
            a = 4 * D + 2 * FF + q * D
            ada[at.c, :, q * D : (q + 1) * D] = shard[:, a : a + D].astype(bf)

    greet_all(n, me, lambda: pl.run_scoped(cut, pltpu.VMEM((32, 18 * D), f32)))
    gather.tick(0)
    trade_ada = remote(ada.at[at.c], ada.at[at.c], xs.at[4], xr.at[4], at.to_c)
    trade_ada.start()
    each_peer(n, me, lambda k, to, fr: remote(small, gat.at[me // 2, at.c], s0.at[k], r0.at[k], to).start())
    gat[pl.ds(me // 2, 1), pl.ds(at.c, 1)] = small[...].reshape(1, 1, 16, 128)
    db[...] = jnp.zeros_like(db)
    dmod[...] = jnp.zeros_like(dmod)

    def bias_into(biases, ref, row, start, lead):
        for q in range(lead):
            k = start + q
            ref[row, :, q * 64 : (q + 1) * 64] = biases[k // 7, k % 7 : k % 7 + 1, 0:64]

    def fetch(i, wbuf, slot):
        return pltpu.make_async_copy(wall.at[i], wbuf.at[slot], wsem.at[slot])

    def bias_from(k, piece):
        esrc[k // 7, :, (k % 7) * 64 : (k % 7 + 1) * 64] = piece

    def ada_columns(x, q):
        cols = slice(q * 512, (q + 1) * 512)
        gw[:, 4 * D + 2 * FF + q * 512 : 4 * D + 2 * FF + (q + 1) * 512] = dot(condc[...], x, TN)
        return dot(x, ada[pl.ds(at.c, 1), :, cols].reshape(32, 512), NT)

    def qkv_out(g, qkv):
        return pltpu.make_async_copy(qkv.at[lax.rem(g, 2)], qkvh.at[g], qsem.at[lax.rem(g, 2)])

    def qkv_in(g, qkv):
        return pltpu.make_async_copy(qkvh.at[g], qkv.at[lax.rem(g, 2)], qsem.at[lax.rem(g, 2)])

    def matrix(wbuf, slot, cols):
        return wbuf[slot, :, :, :, :, :, cols].reshape(D, cols.stop - cols.start)

    lead, tail = pl.ds(0, 2 * D), pl.ds(2 * D, 4 * D)

    def attention(h1, wbuf, qkv, part, biases, conds):
        def norm_one(r):
            xh, _ = nrm(tok[r, :].astype(f32))
            dx1[r, :] = xh

        rows_loop(S, 256, norm_one)
        each_peer(n, me, lambda k, to, fr: remote(small, gat.at[fr // 2, lax.rem(fr, 2)], s0.at[k], r0.at[k], to).wait())
        biases[...] = gat[...].astype(f32).reshape(n, 16, 128)[:, 8:16]
        conds[...] = gat[...].astype(f32).reshape(n // 2, 2, 16, 128)[:, :, 0:8]
        lane = lax.broadcasted_iota(jnp.int32, (128, 64), 0)
        want = lax.rem(me // 2, 2) * 64 + lax.broadcasted_iota(jnp.int32, (128, 64), 1)
        pick = jnp.where(lane == want, 1.0, 0.0).astype(bf)
        wanted = conds[:, :, pl.ds(me // 4, 1), :].reshape(n, 128).astype(bf)
        both = dot(wanted, pick)
        condc[...] = jnp.where(at.c == 0, both[:, 0:32], both[:, 32:64]).astype(bf)
        mates = dot(conds[:, pl.ds(at.c, 1), pl.ds(me // 4, 1), :].reshape(n // 2, 128).astype(bf), pick).astype(bf)
        trade_ada.wait_send()
        remote(ada.at[at.c], ada.at[1 - at.c], xs.at[4], xr.at[4], at.to_c).wait_recv()

        def columns(q):
            cols = slice(q * 512, (q + 1) * 512)
            part[:, :, cols] = dot(mates, ada[:, :, cols].reshape(64, 512)).reshape(n // 2, 1, 512)

        for q in range(4):
            columns(q)
        each_mate(n, me, lambda k, to, fr: remote(part.at[to // 2, :, lead], rec.at[me // 2, :, lead], s2.at[0, k], r2.at[0, k], to).start())
        gather.tick(1)
        for q in range(4, 12):
            columns(q)
        rec[pl.ds(me // 2, 1)] = part[pl.ds(me // 2, 1)]
        for q in range(6):
            bias_into(biases, mod, q, 128 + 16 * q, 16)
        bias_into(biases, brow, 0, 32, 16)
        bias_into(biases, brow, 1, 112, 16)
        for j in range(NJ):
            bias_into(biases, bup, j, 48 + 8 * j, 8)
        for g in range(4):
            bqkv[g] = jnp.zeros((1, 768), f32)
            for q in range(4):
                for first, offset in ((0, 0), (16, 256)):
                    k = first + g * 4 + q
                    to = (q // 2) * 384 + offset + (q % 2) * 64
                    bqkv[g, :, to : to + 64] = biases[k // 7, k % 7 : k % 7 + 1, 0:64]
        gather.tick(2)
        each_mate(n, me, lambda k, to, fr: remote(part.at[to // 2, :, lead], rec.at[fr // 2, :, lead], s2.at[0, k], r2.at[0, k], to).wait())
        each_mate(n, me, lambda k, to, fr: remote(part.at[to // 2, :, tail], rec.at[me // 2, :, tail], s2.at[1, k], r2.at[1, k], to).start())
        for q in range(2):
            mod[q] += jnp.sum(rec[:, :, q * D : (q + 1) * D], axis=0)
        shift1, scale1 = mod[0], mod[1]

        def modulate(r):
            h1[r, :] = (dx1[r, :] * (1.0 + scale1) + shift1).astype(bf)

        rows_loop(S, 256, modulate)
        for i in range(4):
            r = slice(i * 256, (i + 1) * 256)
            h1T[:, :, :, r] = h1[r, :].T.reshape(16, 2, 32, 256)
        gather.tick(3, (4,))
        gather.tick(4, (5,))
        fetch(0, wbuf, 0).start()
        gather.tick(3, (3, 2, 1))

        def group(g, _):
            slot = lax.rem(g, 2)
            fetch(g, wbuf, slot).wait()
            when(g >= 2, lambda: qkv_out(g - 2, qkv).wait())
            w = matrix(wbuf, slot, slice(0, 768))

            def proj(r):
                qkv[slot, r, :] = (dot(h1[r, :], w) + bqkv[g]).astype(bf)

            for r in (slice(0, 512), slice(512, 1024)):
                proj(r)
            qkv_out(g, qkv).start()
            when(g == 0, lambda: gather.tick(4, (4, 3, 2, 1)))
            for p in range(2):
                kp = qkv[slot, :, p * 384 + 128 : p * 384 + 256]
                vT = qkv[slot, :, p * 384 + 256 : p * 384 + 384].T
                q = qkv[slot, :, p * 384 : p * 384 + 128]
                if p == 1:
                    gather.tick(5 + g, (3,))
                scores = [dot(lane_half(kp, h), q, NT) for h in range(2)]
                probs = []
                for h in range(2):
                    m = jnp.max(scores[h], axis=0, keepdims=True)
                    e = jnp.exp2((scores[h] - m) * c)
                    l = jnp.sum(e, axis=0, keepdims=True)
                    probs.append((e * (1.0 / l)).astype(bf))
                    lse[g, p * 2 + h : p * 2 + h + 1, :] = m * 0.125 + jnp.log(l)
                for h in range(2):
                    o = dot(vT[h * 64 : (h + 1) * 64], probs[h])
                    attnT[pl.ds(g * 4 + p * 2 + h, 1)] = o.astype(bf).reshape(1, 2, 32, S)
            gather.tick(5 + g, (5, 4, 2, 1))
            when(g < 3, lambda: fetch(g + 1, wbuf, 1 - slot).start())
            return 0

        lax.fori_loop(0, 4, group, 0)
        for g in (2, 3):
            qkv_out(g, qkv).wait()
        each_mate(n, me, lambda k, to, fr: remote(part.at[to // 2, :, tail], rec.at[fr // 2, :, tail], s2.at[1, k], r2.at[1, k], to).wait())
        for q in range(2, 6):
            mod[q] += jnp.sum(rec[:, :, q * D : (q + 1) * D], axis=0)

    pl.run_scoped(
        attention,
        pltpu.VMEM((S, D), bf),
        pltpu.VMEM((2, 4, 2, 2, 2, 32, 1024), bf),
        pltpu.VMEM((2, S, 768), bf),
        pltpu.VMEM((n // 2, 1, 6 * D), f32),
        pltpu.VMEM((n, 8, 128), f32),
        pltpu.VMEM((n // 2, 2, 8, 128), f32),
    )

    def unstage(i):
        return pltpu.make_async_copy(dwh.at[i], scatter.acc, stsem.at[1])

    def staged(i):
        unstage(i).wait()
        scatter.two(i, scatter.acc)
        when(i + 1 < NJ, lambda: unstage(i + 1).start())

    def mlp(h2, hT, dzT, z, wout, wbuf, accw):
        gate1, shift2, scale2, gate2 = mod[2], mod[3], mod[4], mod[5]

        def stage(i):
            return pltpu.make_async_copy(accw, dwh.at[i], stsem.at[0])

        def co(g):
            return pltpu.make_async_copy(wall.at[g, :, :, :, :, :, 768:1024], wout.at[:, :, :, :, :, g * 256 : (g + 1) * 256], osem.at[g])

        for g in range(4):
            co(g).start()
        fetch(4, wbuf, 0).start()
        for g in range(4):
            co(g).wait()

        def branch(r):
            width = r.size
            return dot(attnT[:, :, :, r].reshape(D, width), wout[...].reshape(D, D), TN) + brow[0]

        def pre(r):
            x1 = tok[r, :].astype(f32) + gate1 * branch(r)
            xh, _ = nrm(x1)
            h2[r, :] = (xh * (1.0 + scale2) + shift2).astype(bf)
            dz = gout[r, :].astype(f32) * gate2
            dob[r, :] = dz.astype(bf)
            db[1] += jnp.sum(dz, axis=0, keepdims=True)

        def pre_block(i, _):
            pre(pl.ds(pl.multiple_of(i * 256, 256), 256))
            when(i == 1, lambda: gather.tick(9, (5, 3)))
            when(i == 3, lambda: gather.tick(9, (4, 2, 1)))
            return 0

        lax.fori_loop(0, 4, pre_block, 0)
        for i in range(4):
            r = slice(i * 256, (i + 1) * 256)
            hT[:, :, :, r] = h2[r, :].T.reshape(16, 2, 32, 256)
            dzT[:, :, :, r] = dob[r, :].T.reshape(16, 2, 32, 256)
        halves = [
            remote(hT.at[:, 1 - at.c], halfS.at[0], xs.at[0], xr.at[0], at.to_c),
            remote(dzT.at[:, 1 - at.c], halfS.at[1], xs.at[1], xr.at[1], at.to_c),
        ]
        for cp in halves:
            cp.start()
        z[...] = jnp.zeros_like(z)
        dx1[...] = jnp.zeros_like(dx1)

        def chunk(j, _):
            when(j >= 1, lambda: gather.tick(9 + j, (4, 2, 1)))

            def forward():
                slot = lax.rem(j, 2)
                when(j + 1 < NJ, lambda: fetch(5 + j, wbuf, 1 - slot).start())
                fetch(4 + j, wbuf, slot).wait()
                when(j >= 2, lambda: pair.sent(j - 2, WHOLE))
                dbup[j] = jnp.zeros((1, CH), f32)

                w_up, w_dn = matrix(wbuf, slot, slice(0, CH)), matrix(wbuf, slot, slice(CH, 2 * CH))
                blocks = (slice(0, 512), slice(512, 1024))
                ups = [dot(h2[r, :], w_up) + bup[j] for r in blocks]
                backs = [dot(dob[r, :], w_dn) for r in blocks]
                for r, u, back_ in zip(blocks, ups, backs):
                    a, sl = gelu_pair(u)
                    ab = a.astype(bf)
                    own[slot, r, CH:] = ab
                    d = back_ * sl
                    dbup[j] += jnp.sum(d, axis=0, keepdims=True)
                    db_ = d.astype(bf)
                    own[slot, r, :CH] = db_
                    z[r, :] += dot(ab, w_dn, NT)
                    dx1[r, :] += dot(db_, w_up, NT)

                pair.start(j, 0, WHOLE[0])

            when(j < NJ, forward)
            gather.tick(10 + j, (5, 3))
            scatter.tick(j - 5)
            when(j >= 5, lambda: staged(j - 5))
            when(j == 4, lambda: unstage(0).start())

            def weights():
                i = j - 1
                slot = lax.rem(i, 2)
                when(j == 1, lambda: [cp.wait_recv() for cp in halves])
                pair.arrived(i, WHOLE)
                when(i >= 1, lambda: stage(i - 1).wait())
                for q, lhs in enumerate((hT, dzT)):
                    cols = slice(q * CH, (q + 1) * CH)
                    t = dot(lhs[:, at.c].reshape(512, S), own[slot, :, cols]) + dot(halfS[q].reshape(512, S), theirs[slot, :, cols])
                    accw[:, :, :, :, :, cols] = t.reshape(2, 2, 2, 2, 32, CH)
                pair.free(i)
                stage(i).start()

            when(j >= 1, weights)
            return 0

        lax.fori_loop(0, NJ + 1, chunk, 0)
        mesh_signal(hc, at.to_c)
        stage(NJ - 1).wait()
        for cp in halves:
            cp.wait_send()

        def post(r):
            g = gout[r, :].astype(f32)
            o = branch(r)
            x1 = tok[r, :].astype(f32) + gate1 * o
            xh, rstd = nrm(x1)
            zz = z[r, :] + brow[1]
            h2[r, :] = (x1 + gate2 * zz).astype(bf)
            dmod[5] += jnp.sum(g * zz, axis=0, keepdims=True)
            dh = dx1[r, :]
            dmod[3] += jnp.sum(dh, axis=0, keepdims=True)
            dmod[4] += jnp.sum(dh * xh, axis=0, keepdims=True)
            gg = dh * (1.0 + scale2)
            dx = g + rstd * (gg - jnp.mean(gg, axis=-1, keepdims=True) - xh * jnp.mean(gg * xh, axis=-1, keepdims=True))
            dx1[r, :] = dx
            dmod[2] += jnp.sum(dx * o, axis=0, keepdims=True)
            do = dx * gate1
            db[0] += jnp.sum(do, axis=0, keepdims=True)
            dob_ = do.astype(bf)
            dob[r, :] = dob_
            own[0, r, :] = dot(dob_, wout[...].reshape(D, D), NT).astype(bf)

        pair.sent(NJ - 2, WHOLE)

        def post_half(h):
            def body(i, _):
                post(pl.ds(pl.multiple_of(h * 512 + i * 256, 256), 256))
                return 0

            lax.fori_loop(0, 2, body, 0)

        post_half(0)
        post_half(1)
        outs = [pltpu.make_async_copy(h2, bo, osem.at[0])]
        outs += [pltpu.make_async_copy(own.at[0, :, g * 256 : (g + 1) * 256], dath.at[g], osem.at[1 + g]) for g in range(4)]
        for cp in outs:
            cp.start()
        for cp in outs:
            cp.wait()

    pl.run_scoped(
        mlp,
        pltpu.VMEM((S, D), bf),
        pltpu.VMEM((16, 2, 32, S), bf),
        pltpu.VMEM((16, 2, 32, S), bf),
        pltpu.VMEM((S, D), f32),
        pltpu.VMEM((4, 2, 2, 2, 32, 1024), bf),
        pltpu.VMEM((2, 4, 2, 2, 2, 32, 1024), bf),
        pltpu.VMEM((2, 2, 2, 2, 32, 1024), f32),
    )

    def back(dh1, wbuf, qkv, dat, dk_s, dv_s, dqT_s, accw):
        def dat_in(g):
            return pltpu.make_async_copy(dath.at[g], dat.at[lax.rem(g, 2)], osem.at[lax.rem(g, 2)])

        def load(g):
            qkv_in(g, qkv).start()
            dat_in(g).start()
            fetch(g, wbuf, lax.rem(g, 2)).start()

        load(0)
        pl.semaphore_wait(hc, 1)
        halves = [
            remote(h1T.at[:, 1 - at.c], halfS.at[0], xs.at[2], xr.at[2], at.to_c),
            remote(attnT.at[:, 1 - at.c], halfS.at[1], xs.at[3], xr.at[3], at.to_c),
        ]
        for cp in halves:
            cp.start()
        scatter.tick(4)
        staged(4)
        for q in range(4):
            dsrc[:, q * D : (q + 1) * D] = dmod[2 + q]
        each_mate(n, me, lambda k, to, fr: remote(dsrc, dall.at[at.c, me // 2], s3.at[k], r3.at[k], to).start())
        dall[pl.ds(at.c, 1), pl.ds(me // 2, 1)] = dsrc[...].reshape(1, 1, 1, 4 * D)
        esrc[...] = jnp.zeros_like(esrc)
        for q in range(16):
            bias_from(32 + q, db[0, :, q * 64 : (q + 1) * 64])
            bias_from(112 + q, db[1, :, q * 64 : (q + 1) * 64])
        for j in range(NJ):
            for q in range(8):
                bias_from(48 + 8 * j + q, dbup[j, :, q * 64 : (q + 1) * 64])
        dh1[...] = jnp.zeros_like(dh1)

        def group(g, _):
            slot = lax.rem(g, 2)
            when(g < 3, lambda: load(g + 1))
            qkv_in(g, qkv).wait()
            dat_in(g).wait()
            when(g == 1, lambda: pair.sent(NJ - 1, WHOLE))
            when(g >= 2, lambda: pair.sent(NJ + g - 2, PARTS))
            own[slot, :, 768:] = dob[:, pl.ds(pl.multiple_of(g * 256, 256), 256)]
            pair.start(NJ + g, 0, PARTS[0])
            for p in range(2):
                if p == 1:
                    scatter.tick(5 + 2 * g)
                    when(g < 2, lambda: staged(5 + 2 * g))
                    when(g == 2, lambda: scatter.two(9, accw))
                sl = slice(p * 128, (p + 1) * 128)
                slq, slk, slv = (slice(p * 384 + q * 128, p * 384 + (q + 1) * 128) for q in range(3))
                kp, vp, q, da = qkv[slot, :, slk], qkv[slot, :, slv], qkv[slot, :, slq], dat[slot, :, sl]
                kT = kp.T
                for h in range(2):
                    s = dot(lane_half(kp, h), q, NT)
                    pT = jnp.exp2(s * c - lse[g, p * 2 + h : p * 2 + h + 1, :] * LOG2E)
                    dp = dot(lane_half(vp, h), da, NT)
                    weighted = pT * dp
                    ds = (weighted - pT * jnp.sum(weighted, axis=0, keepdims=True)).astype(bf)
                    dv = dot(pT.astype(bf), lane_half(da, h))
                    dk = dot(ds, lane_half(q, h))
                    if h == 0:
                        dv_s[...] = dv
                        dk_s[...] = dk
                    else:
                        dv_s[...] += dv
                        dk_s[...] += dk
                    dqT_s[h * 64 : (h + 1) * 64, :] = dot(kT[h * 64 : (h + 1) * 64], ds)
                dq = dqT_s[...].T * 0.125
                dbq[g, :, sl] = jnp.sum(dq, axis=0, keepdims=True)
                own[slot, :, slq] = dq.astype(bf)
                own[slot, :, slk] = (dk_s[...] * 0.125).astype(bf)
                dbq[g, :, 256 + p * 128 : 256 + (p + 1) * 128] = jnp.sum(dv_s[...], axis=0, keepdims=True)
                own[slot, :, slv] = dv_s[...].astype(bf)
                pair.start(NJ + g, 1 + p, PARTS[1 + p])
            fetch(g, wbuf, slot).wait()
            w = matrix(wbuf, slot, slice(0, 768))

            def wrow(r):
                dh1[r, :] += dot(own[slot, r, :768], w, NT)

            for r in (slice(0, 512), slice(512, 1024)):
                wrow(r)
            scatter.tick(6 + 2 * g)

            def at_first():
                staged(6)
                for cp in halves:
                    cp.wait_recv()

            when(g == 0, at_first)
            when(g == 1, lambda: scatter.two(8, accw))

            def pass_on():
                each_mate(n, me, lambda k, to, fr: remote(dsrc, dall.at[at.c, fr // 2], s3.at[k], r3.at[k], to).wait())
                remote(dall.at[at.c], dall.at[at.c], xs.at[5], xr.at[5], at.to_c).start()

            when(g == 1, pass_on)
            pair.arrived(NJ + g, PARTS)
            for q, lhs in enumerate((h1T, attnT)):
                cols = slice(0, 768) if q == 0 else slice(768, 1024)
                t = dot(lhs[:, at.c].reshape(512, S), own[slot, :, cols]) + dot(halfS[q].reshape(512, S), theirs[slot, :, cols])
                accw[:, :, :, :, :, cols] = t.reshape(2, 2, 2, 2, 32, cols.stop - cols.start)
            pair.free(NJ + g)
            when(g >= 2, lambda: scatter.two(8 + g, accw))
            return 0

        lax.fori_loop(0, 4, group, 0)
        for g in range(4):
            for q in range(4):
                bias_from(g * 4 + q, dbq[g, :, q * 64 : (q + 1) * 64])
                bias_from(16 + g * 4 + q, dbq[g, :, 256 + q * 64 : 256 + (q + 1) * 64])
        each_peer(n, me, lambda k, to, fr: remote(esrc.at[to], erec.at[me], s4.at[k], r4.at[k], to).start())
        erec[pl.ds(me, 1)] = esrc[pl.ds(me, 1)]
        for i in (2, 3):
            pair.sent(NJ + i, PARTS)
        for cp in halves:
            cp.wait_send()
        scale1 = mod[1]

        def post(r):
            xh, rstd = nrm(tok[r, :].astype(f32))
            dh = dh1[r, :]
            dmod[0] += jnp.sum(dh, axis=0, keepdims=True)
            dmod[1] += jnp.sum(dh * xh, axis=0, keepdims=True)
            gg = dh * (1.0 + scale1)
            dx1[r, :] += rstd * (gg - jnp.mean(gg, axis=-1, keepdims=True) - xh * jnp.mean(gg * xh, axis=-1, keepdims=True))

        rows_loop(S, 256, post)

    pl.run_scoped(
        back,
        pltpu.VMEM((S, D), f32),
        pltpu.VMEM((2, 4, 2, 2, 2, 32, 1024), bf),
        pltpu.VMEM((2, S, 768), bf),
        pltpu.VMEM((2, S, 256), bf),
        pltpu.VMEM((S, 128), f32),
        pltpu.VMEM((S, 128), f32),
        pltpu.VMEM((128, S), f32),
        pltpu.VMEM((2, 2, 2, 2, 32, 1024), f32),
    )
    done = pltpu.make_async_copy(dx1, ig, osem.at[0])
    done.start()
    for k in range(2):
        lsrc[:, k * D : (k + 1) * D] = dmod[k]
    each_mate(n, me, lambda k, to, fr: remote(lsrc, lall.at[at.c, me // 2], s6.at[k], r6.at[k], to).start())
    lall[pl.ds(at.c, 1), pl.ds(me // 2, 1)] = lsrc[...].reshape(1, 1, 1, 2 * D)
    scatter.tick(13)
    passed = [remote(ref.at[at.c], ref.at[at.c], xs.at[5 + q], xr.at[5 + q], at.to_c) for q, ref in enumerate((dall, lall))]
    landed = [remote(ref.at[1 - at.c], ref.at[1 - at.c], xs.at[5 + q], xr.at[5 + q], at.to_c) for q, ref in enumerate((dall, lall))]
    passed[0].wait_send()
    landed[0].wait_recv()

    def latents(ref, first, count):
        total = jnp.zeros((n, 32), f32)
        for q in range(count):
            cols = slice(q * 512, (q + 1) * 512)
            x = jnp.concatenate([ref[k, :, :, cols].reshape(n // 2, 1, 512) for k in range(2)], axis=1).reshape(n, 512)
            dsum[:, (first + q) * 512 : (first + q + 1) * 512] = jnp.sum(x, axis=0, keepdims=True)
            total += ada_columns(x.astype(bf), first + q)
        return total

    total = latents(dall, 4, 8)
    each_mate(n, me, lambda k, to, fr: remote(lsrc, lall.at[at.c, fr // 2], s6.at[k], r6.at[k], to).wait())
    passed[1].start()
    scatter.tick(14)
    passed[1].wait_send()
    landed[1].wait_recv()
    total += latents(lall, 0, 4)
    csrc[:, :, 0:32] = total.reshape(n, 1, 32)
    each_peer(n, me, lambda k, to, fr: remote(csrc.at[to], crec.at[me], s5.at[k], r5.at[k], to).start())
    crec[pl.ds(me, 1)] = csrc[pl.ds(me, 1)]
    each_peer(n, me, lambda k, to, fr: remote(esrc.at[to], erec.at[fr], s4.at[k], r4.at[k], to).wait())
    bsum[...] = jnp.sum(erec[...], axis=0)
    scatter.tick(15)
    each_peer(n, me, lambda k, to, fr: remote(csrc.at[to], crec.at[fr], s5.at[k], r5.at[k], to).wait())
    scatter.tick(16)
    done.wait()
    scatter.finish()
    gather.finish()


def block(n, *a):
    dma = pltpu.SemaphoreType.DMA
    regular = pltpu.SemaphoreType.REGULAR
    vm = pltpu.VMEM
    return pl.pallas_call(
        functools.partial(block_kernel, n),
        out_shape=(sd((S, D), bf), sd((S, D), f32), sd((32, 18 * D), f32), sd((1, 512), f32), sd((1, 6 * D), f32), sd((n, 1, 128), f32))
        + (sd((12, 4, 2, 2, 2, 32, 1024), bf), sd((NJ, 2, 2, 2, 2, 32, 1024), f32), sd((4, S, 768), bf), sd((4, S, 256), bf)),
        in_specs=[V] * 3 + [A],
        out_specs=[A] * 2 + [V] * 4 + [A] * 4,
        scratch_shapes=[vm((12, 32, 1024), bf), vm((2, 32, 6 * D), bf), vm((n // 2, 2, 16, 128), bf), vm((n, 32), bf)]
        + [vm((n // 2, 1, 6 * D), f32), vm((1, 4 * D), f32), vm((2, n // 2, 1, 4 * D), f32), vm((1, 2 * D), f32), vm((2, n // 2, 1, 2 * D), f32), vm((n, 1, 512), f32), vm((n, 1, 512), f32), vm((n, 1, 128), f32)]
        + [vm((6, 1, D), f32), vm((2, 1, D), f32), vm((4, 1, 768), f32), vm((NJ, 1, CH), f32), vm((6, 1, D), f32), vm((2, 1, D), f32), vm((NJ, 1, CH), f32), vm((4, 1, 512), f32)]
        + [vm((16, 2, 32, S), bf), vm((16, 2, 32, S), bf), vm((4, 4, S), f32), vm((S, D), bf), vm((S, D), f32)]
        + [vm((2, S, 1024), bf), vm((2, S, 1024), bf), vm((2, 16, 32, S), bf)]
        + [dma((n,))] * 2
        + [dma((2, n))] * 2
        + [dma((n,))] * 8
        + [dma((7,)), dma((7,)), dma((2, 3)), dma((2, 3)), regular, regular]
        + [dma((2,)), dma((2,)), dma((5,)), dma((2,))]
        + gather_sems(12)
        + Scatter.shapes,
        compiler_params=pltpu.CompilerParams(collective_id=0, has_side_effects=True, vmem_limit_bytes=VMEM_BYTES),
        name="block",
    )(*a)


def adam_step(param, grad, first, second, decay):
    new_first = beta_first * first + (1.0 - beta_first) * grad
    new_second = beta_second * second + (1.0 - beta_second) * grad * grad
    step_size = learn_rate / (1.0 - beta_first**STEP)
    denom = jnp.sqrt(new_second / (1.0 - beta_second**STEP)) + adam_eps
    new_param = param - step_size * new_first / denom - learn_rate * decay * param
    return (new_param, new_first, new_second)


def plain(n, tok, gout, condition, weights, biases):
    me = lax.axis_index("dp")
    rows = D // n
    wb = weights.astype(bf)
    qkvo = wb[:, : 4 * D].reshape(rows, 4, 4, 256).transpose(2, 0, 1, 3).reshape(4, rows, 1024)
    updn = wb[:, 4 * D : 4 * D + 2 * FF].reshape(rows, 2, NJ, CH).transpose(2, 0, 1, 3).reshape(NJ, rows, 1024)
    mine = jnp.concatenate([qkvo, updn], axis=0)
    ada_l = wb[:, 4 * D + 2 * FF :]
    cond_act = jax.nn.silu(condition).astype(bf)
    bias_full = lax.all_gather(biases.astype(bf), "dp", axis=0, tiled=True).astype(f32)
    cond_all = lax.all_gather(cond_act, "dp", axis=0, tiled=True)
    cond_cols = lax.dynamic_slice_in_dim(cond_all, me * rows, rows, 1)
    mod = lax.psum_scatter(jnp.dot(cond_cols, ada_l, preferred_element_type=f32), "dp", scatter_dimension=0, tiled=True)
    mod = jnp.concatenate([(mod[0] + bias_full[4 * D + FF :]).reshape(6, D), jnp.zeros((2, D), f32)], axis=0)
    zrow = jnp.zeros((D,), f32)
    bqkv = jnp.stack([bias_full[:D], zrow, bias_full[D : 2 * D]]).reshape(3, 4, 256).transpose(1, 0, 2).reshape(4, 1, 768)
    brows = jnp.stack([zrow, zrow, bias_full[2 * D : 3 * D], bias_full[3 * D + FF : 4 * D + FF], zrow, zrow, zrow, zrow])
    bup = bias_full[3 * D : 3 * D + FF].reshape(NJ, 1, CH)
    wall = lax.all_gather(mine, "dp", axis=1, tiled=True)
    qkv, attn_t, lse, h1t = ka(tok, mod, bqkv, wall)
    bo, dx1, dat, dw_mlp, dw_out, dmod_b, db, db_up = kb(512, tok, gout, attn_t, mod, brows, bup, wall)
    ig, dw_qkv, dmod_a, db_qkv = kc(1024, tok, mod, qkv, dat, lse, dx1, h1t, wall)
    g_mlp = lax.psum_scatter(dw_mlp, "dp", scatter_dimension=2, tiled=True)
    g_out = lax.psum_scatter(dw_out, "dp", scatter_dimension=0, tiled=True)
    g_qkv = lax.psum_scatter(dw_qkv, "dp", scatter_dimension=1, tiled=True)
    g_qkv = g_qkv.reshape(4, rows, 3, 256).transpose(1, 2, 0, 3).reshape(rows, 3 * D)
    g_mlp = g_mlp.transpose(2, 1, 0, 3).reshape(rows, 2 * FF)
    dmod = (dmod_a + dmod_b)[:6].reshape(1, 6 * D)
    db_qkv = db_qkv.reshape(4, 3, 256).transpose(1, 0, 2).reshape(3, D)
    bias_row = jnp.concatenate([db_qkv[0], db_qkv[2], db[2], db_up.reshape(FF), db[3], dmod[0]])
    bias_grad = lax.psum_scatter(bias_row, "dp", scatter_dimension=0, tiled=True)
    dmod_all = lax.all_gather(dmod.astype(bf), "dp", axis=0, tiled=True)
    g_ada = lax.dot_general(cond_cols, dmod_all, TN, preferred_element_type=f32)
    cond_part = lax.dot_general(dmod_all, ada_l, NT, preferred_element_type=f32)
    cond_grad = lax.all_to_all(cond_part, "dp", split_axis=0, concat_axis=1, tiled=True)
    return bo, ig, cond_grad, jnp.concatenate([g_qkv, g_out, g_mlp, g_ada], axis=1), bias_grad


def finish_kernel(gw, w, m, v, bo, ig, gw_o, w_o, m_o, v_o, bo_o, ig_o):
    grad = gw[...]
    gw_o[...] = grad
    w_o[...], m_o[...], v_o[...] = adam_step(w[...], grad, m[...], v[...], weight_decay)
    bo_o[...] = bo[...]
    ig_o[...] = ig[...]


def finish(steps, *a):
    cols = pl.BlockSpec((32, 18 * D // steps), lambda i: (0, i))
    toks = pl.BlockSpec((S // steps, D), lambda i: (i, 0))
    specs = [cols] * 4 + [toks] * 2
    return pl.pallas_call(
        finish_kernel,
        grid=(steps,),
        out_shape=(sd((32, 18 * D), f32),) * 4 + (sd((S, D), bf), sd((S, D), f32)),
        in_specs=specs,
        out_specs=specs,
        compiler_params=pltpu.CompilerParams(vmem_limit_bytes=VMEM_BYTES),
        name="finish",
    )(*a)


def on_chips(n, tok, gout, condition, weights, biases):
    cond_act = jax.nn.silu(condition).reshape(8, 128)
    padded = jnp.pad(biases.reshape(7, 64), ((0, 1), (0, 64)))
    bo, ig, weight_grad, bsum, dsum, crec = block(n, tok, gout, jnp.concatenate([cond_act, padded]).astype(bf), weights)[:6]
    own = biases.shape[0]
    flat = jnp.concatenate([jnp.zeros((4 * D + FF,), f32), dsum[0]])
    bias_grad = bsum[0, :own] + lax.dynamic_slice_in_dim(flat, lax.axis_index("dp") * own, own, 0)
    return bo, ig, crec[:, 0, :32].reshape(1, D), weight_grad, bias_grad


def on_device(n, block_in, condition, out_grad, weights, biases, first_moment, second_moment, bias_first, bias_second):
    run = on_chips if n == 32 else plain
    bo, ig, cond_grad, weight_grad, bias_grad = run(n, block_in[0], out_grad[0], condition, weights, biases)
    sigma = jax.nn.sigmoid(condition)
    cond_grad = cond_grad * (sigma * (1.0 + condition * (1.0 - sigma)))
    if n == 32:
        weight_grad, new_weights, new_first, new_second, bo, ig = finish(STEPS, weight_grad, weights, first_moment, second_moment, bo, ig)
    else:
        new_weights, new_first, new_second = adam_step(weights, weight_grad, first_moment, second_moment, weight_decay)
    new_biases, new_bias_first, new_bias_second = adam_step(biases, bias_grad, bias_first, bias_second, 0.0)
    return (bo[None], ig[None], cond_grad, weight_grad, bias_grad, new_weights, new_biases, new_first, new_second, new_bias_first, new_bias_second)


def solution(mesh):
    three, two, one = P("dp", None, None), P("dp", None), P("dp")
    return jax.shard_map(
        functools.partial(on_device, mesh.shape["dp"]),
        mesh=mesh,
        in_specs=(three, two, three, two, one, two, two, one, one),
        out_specs=(three, three, two, two, one, two, one, two, two, one, one),
        check_vma=False,
    )
```
